32 devices in a mesh: ctx: 8 (over y, x, core), fsdp: 4 (over z).
Axes of the slice: x: 2, y: 2, z: 4, core: 2. Of those that a mesh axis runs over, the one named last changes fastest.
Arguments:
- tokens: bfloat16 [4, 4096, 512], P('fsdp', 'ctx'), may hold values from -6 to 6
- cotangent: bfloat16 [4, 4096, 512], P('fsdp', 'ctx'), may hold values from -6 to 6
- block_table: int32 [16], replicated, may hold values from 0 to 15, as said below
- seg_ids: int32 [4, 4096], P('fsdp'), may hold values from 0 to 2, as said below
- group_ids: int32 [4, 4096], P('fsdp', 'ctx'), may hold values from 0 to 127, as said below
- w_qkv: bfloat16 [512, 1536], P('fsdp'), may hold values from -0.375 to 0.375
- w_out: bfloat16 [512, 512], P('fsdp'), may hold values from -1.5 to 1.5
- w_router: bfloat16 [512, 8], P('fsdp'), may hold values from -0.1875 to 0.1875
- ln_gain: bfloat16 [512], P('fsdp'), may hold values from 0.5 to 1.5
- ln_bias: bfloat16 [512], P('fsdp'), may hold values from -1 to 1
- w_up: bfloat16 [8, 512, 2048], P('fsdp'), may hold values from -2 to 2
- w_down: bfloat16 [8, 2048, 512], P('fsdp'), may hold values from -1.5 to 1.5
Outputs:
- layer_out: float32 [4, 4096, 512], P('fsdp', 'ctx')
- grad_tokens: float32 [4, 4096, 512], P('fsdp', 'ctx')
- grad_qkv: float32 [512, 1536], P('fsdp')
- grad_out: float32 [512, 512], P('fsdp')
- grad_router: float32 [512, 8], P('fsdp')
- grad_gain: float32 [512], P('fsdp')
- grad_bias: float32 [512], P('fsdp')
- grad_up: float32 [8, 512, 2048], P('fsdp')
- grad_down: float32 [8, 2048, 512], P('fsdp')
The draws below stay inside these ranges and needn't reach their ends.
Inputs may be any that keep to these rules, and one draw needn't show every extreme that they name: `block_table`: a permutation; each index c of ctx holds stored blocks 2c and 2c + 1, which are sequence blocks j and 15 - j for some j. `seg_ids`: in sequence order each batch is the prompt (segment 0) followed by continuations 1 to 2, each a nonempty run of positions. `group_ids`: every group has exactly 32 tokens; the tokens of ctx index c have groups c * 16 to (c + 1) * 16 - 1.
All inputs are finite; a program needn't handle non-finite values.
Results may differ from the reference program's by a relative error of at most 0.019.
Values may be sent and summed in bfloat16 or wider, within the bound.
A program may use at most 256 MiB of HBM per device.

```python
import jax
import jax.numpy as jnp
from jax import lax

D = 512
HEADS = 8
HEAD = 64
FFN = 2048
EXPERTS = 8
GROUP_SIZE = 32
TOK_DEV = 512
CONT_LEN = 1024
QUERY_BLOCK = 512
BATCHES = 4
GROUP_TOK = 4096
BLK = 256
NB = 16
PROMPT = 2048
NCONT = 2
GPD = 16


def deal_table(key):
    base = jax.random.fold_in(key, 11)
    pair_count = NB // 2
    order = jax.random.permutation(jax.random.fold_in(base, 1), pair_count)
    flips = jax.random.randint(jax.random.fold_in(base, 2), (pair_count,), 0, 2)
    first = jnp.where(flips == 0, order, NB - 1 - order)
    second = NB - 1 - first
    return jnp.stack([first, second], axis=1).reshape(NB).astype(jnp.int32)


def draw_block_table(key, part):
    return deal_table(key)


def draw_seg_ids(key, part):
    table = deal_table(key)
    quarter = CONT_LEN // 4
    shifts = jax.random.randint(jax.random.fold_in(key, 23), (BATCHES, NCONT), -quarter, quarter + 1)
    bounds = PROMPT + jnp.arange(NCONT, dtype=jnp.int32)[None, :] * CONT_LEN + shifts
    row_ids = jnp.arange(GROUP_TOK, dtype=jnp.int32)
    positions = jnp.take(table, row_ids // BLK) * BLK + row_ids % BLK
    segment = jnp.sum((positions[None, :, None] >= bounds[:, None, :]).astype(jnp.int32), axis=-1)
    return segment.astype(jnp.int32)


def draw_group_ids(key, part):
    base = jax.random.fold_in(key, 37)
    shard_count = GROUP_TOK // TOK_DEV
    subkeys = jax.random.split(base, BATCHES * shard_count)
    orders = jax.vmap(lambda subkey: jax.random.permutation(subkey, TOK_DEV))(subkeys)
    offsets = jnp.arange(BATCHES * shard_count, dtype=jnp.int32) % shard_count * GPD
    groups = orders // GROUP_SIZE + offsets[:, None]
    return groups.reshape(BATCHES, GROUP_TOK).astype(jnp.int32)


def block_levels(rng, dims, cuts, low, high):
    loudness, own = 1.0, jax.random.fold_in(rng, 6)
    for dim, parts in cuts:
        steps = jnp.exp(jax.random.uniform(jax.random.fold_in(own, dim), (parts,), jnp.float32, low / len(cuts), high / len(cuts)))
        loudness = loudness * jnp.repeat(steps, dims[dim] // parts).reshape([-1 if axis == dim else 1 for axis in range(len(dims))])
    return loudness


def centred(own_key, shape, width, limit, pieces=(), held_as=jnp.bfloat16):
    array = width * jax.random.normal(own_key, shape, jnp.float32)
    if pieces:
        array = array * block_levels(own_key, shape, pieces, -0.22, 0.18)
    return jnp.clip(array, -limit, limit).astype(held_as)


def setup_inputs(seed: int = 0) -> dict:
    splits = jax.random.split(jax.random.key(seed), 13)
    return {
        "tokens": centred(splits[0], (BATCHES, GROUP_TOK, D), 1.0, 6.0, ((0, 4), (1, 8))),
        "cotangent": centred(splits[1], (BATCHES, GROUP_TOK, D), 1.0, 6.0, ((0, 4), (1, 8))),
        "block_table": draw_block_table(jax.random.fold_in(splits[12], 71), 0),
        "seg_ids": draw_seg_ids(jax.random.fold_in(splits[12], 71), 0),
        "group_ids": draw_group_ids(jax.random.fold_in(splits[12], 71), 0),
        "w_qkv": centred(splits[5], (D, 3 * D), (D // 2) ** -0.5, 0.375, ((0, 4),)),
        "w_out": centred(splits[6], (D, D), (D // 32) ** -0.5, 1.5, ((0, 4),)),
        "w_router": centred(splits[7], (D, EXPERTS), (2 * D) ** -0.5, 0.1875, ((0, 4),)),
        "ln_gain": jnp.clip(1.0 + 0.1 * jax.random.normal(splits[8], (D,), jnp.float32), 0.5, 1.5).astype(jnp.bfloat16),
        "ln_bias": centred(splits[9], (D,), 0.2, 1.0, ((0, 4),)),
        "w_up": centred(splits[10], (EXPERTS, D, FFN), (D // 64) ** -0.5, 2.0, ((0, 4),)),
        "w_down": centred(splits[11], (EXPERTS, FFN, D), (FFN // 128) ** -0.5, 1.5, ((0, 4),)),
    }


@jax.custom_vjp
def low(v):
    return lax.optimization_barrier(v.astype(jnp.bfloat16)).astype(jnp.float32)

@jax.custom_vjp
def low_back(v):
    return v

def low_keep(v):
    return (low(v), None)

def low_pass(kept, grad):
    return (grad,)

def back_keep(v):
    return (v, None)

def back_low(kept, grad):
    return (low(grad),)
low.defvjp(low_keep, low_pass)
low_back.defvjp(back_keep, back_low)
highest = lax.Precision.HIGHEST

def round_both(value):
    return low(low_back(value))

def attention_block(items, key_heads, val_heads, key_pos, key_seg):
    query_block, pos_block, seg_block = items
    scale = HEAD ** (-0.5)
    scores = low_back(jnp.einsum('qhd,khd->hqk', query_block, key_heads, precision=highest) * scale)
    allowed = (key_pos[None, :] <= pos_block[:, None]) & ((key_seg[None, :] == 0) | (key_seg[None, :] == seg_block[:, None]))
    allowed = allowed[None]
    masked = jnp.where(allowed, scores, -1e+30)
    peak = lax.optimization_barrier(jnp.max(masked, axis=-1, keepdims=True))
    weights = jnp.where(allowed, jnp.exp(masked - peak), 0.0)
    probs = low(weights / lax.optimization_barrier(jnp.sum(weights, axis=-1, keepdims=True)))
    return jnp.einsum('hqk,khd->qhd', probs, val_heads, precision=highest)

def batch_forward(weights, tok_rows, seg_row, group_row, positions):
    w_qkv, w_out, w_router, ln_gain, ln_bias, w_up, w_down = weights
    row_count = tok_rows.shape[0]
    qkv = round_both(jnp.dot(tok_rows, w_qkv, precision=highest))
    query = qkv[:, :D].reshape(row_count, HEADS, HEAD)
    key_heads = qkv[:, D:2 * D].reshape(row_count, HEADS, HEAD)
    val_heads = qkv[:, 2 * D:].reshape(row_count, HEADS, HEAD)
    blocks = row_count // QUERY_BLOCK

    def attend(items):
        return attention_block(items, key_heads, val_heads, positions, seg_row)
    attended = lax.map(jax.checkpoint(attend), (query.reshape(blocks, QUERY_BLOCK, HEADS, HEAD), positions.reshape(blocks, QUERY_BLOCK), seg_row.reshape(blocks, QUERY_BLOCK)))
    attended = round_both(attended.reshape(row_count, D))
    branch = low_back(jnp.dot(attended, w_out, precision=highest))
    hidden = tok_rows + branch
    center = hidden - lax.optimization_barrier(jnp.mean(hidden, axis=-1, keepdims=True))
    unit = center * lax.rsqrt(lax.optimization_barrier(jnp.mean(center * center, axis=-1, keepdims=True)) + 1e-05)
    normed = low(unit * ln_gain + ln_bias)
    logits = low_back(jnp.dot(normed, w_router, precision=highest))
    group_count = row_count // GROUP_SIZE
    expo = jnp.exp(logits)
    group_total = jax.ops.segment_sum(expo, group_row, num_segments=group_count)
    mix_low = low(expo / jnp.take(group_total, group_row, axis=0))
    mixed = jax.ops.segment_sum(mix_low[:, :, None] * normed[:, None, :], group_row, num_segments=group_count)
    mixed = round_both(mixed)
    pre = low_back(jnp.einsum('ged,edh->geh', mixed, w_up, precision=highest))
    active = low(jax.nn.gelu(pre, approximate=True))
    expert_out = round_both(jnp.einsum('geh,ehd->ged', active, w_down, precision=highest))
    spread = jnp.einsum('te,ted->td', mix_low, jnp.take(expert_out, group_row, axis=0), precision=highest)
    return hidden + spread

def reference(tokens, cotangent, block_table, seg_ids, group_ids, w_qkv, w_out, w_router, ln_gain, ln_bias, w_up, w_down):
    row_ids = jnp.arange(GROUP_TOK, dtype=jnp.int32)
    positions = (jnp.take(block_table, row_ids // BLK) * BLK + row_ids % BLK).astype(jnp.int32)
    floats = [value.astype(jnp.float32) for value in (tokens, w_qkv, w_out, w_router, ln_gain, ln_bias, w_up, w_down)]

    def forward(tok_all, qkv_weight, out_weight, router_weight, gain, bias, up_weight, down_weight):
        weights = (qkv_weight, out_weight, router_weight, gain, bias, up_weight, down_weight)

        def one_batch(items):
            tok_rows, seg_row, group_row = items
            return batch_forward(weights, tok_rows, seg_row, group_row, positions)
        return lax.map(one_batch, (tok_all, seg_ids, group_ids))
    result, pullback = jax.vjp(forward, *floats)
    grads = pullback(cotangent.astype(jnp.float32))
    return (result, grads[0], grads[1], grads[2], grads[3], grads[4], grads[5], grads[6], grads[7])
```

```python
import functools

import jax
import jax.numpy as jnp
from jax import lax
from jax.experimental import pallas as pl
from jax.experimental.pallas import tpu as pltpu
from jax.sharding import PartitionSpec as P

HEADS = 8
HEAD = 64
GROUP_SIZE = 32
KEY_BLOCK = 2048


highest = lax.Precision.HIGHEST
neg_large = -1e30
epsilon = 1e-05
gelu_coef = 0.7978845608028654
gelu_cubic = 0.044715


def contract_rows(left, right):
    return lax.dot_general(
        left, right, (((0,), (0,)), ((), ())), preferred_element_type=jnp.float32
    )


def contract_cols(left, right):
    return lax.dot_general(
        left, right, (((1,), (1,)), ((), ())), preferred_element_type=jnp.float32
    )


def gelu_slope(value):
    inner = gelu_coef * (value + gelu_cubic * value * value * value)
    tangent = jnp.tanh(inner)
    return 0.5 * (1.0 + tangent) + 0.5 * value * (1.0 - tangent * tangent) * gelu_coef * (
        1.0 + 3.0 * gelu_cubic * value * value
    )


def expert_forward(mixed_low, up_weight, down_weight):
    pre = jnp.einsum("ged,edh->geh", mixed_low, up_weight, preferred_element_type=jnp.float32)
    active = jax.nn.gelu(pre, approximate=True).astype(jnp.bfloat16)
    result = jnp.einsum("geh,ehd->ged", active, down_weight, preferred_element_type=jnp.float32)
    return (pre, active, result.astype(jnp.bfloat16))


def expert_backward(mixed_low, pre, active, grad_result, up_weight, down_weight):
    grad_act = jnp.einsum(
        "ged,ehd->geh", grad_result, down_weight, preferred_element_type=jnp.float32
    )
    grad_pre = (grad_act * gelu_slope(pre)).astype(jnp.bfloat16)
    grad_down_part = jnp.einsum(
        "geh,ged->ehd", active, grad_result, preferred_element_type=jnp.float32
    )
    grad_up_part = jnp.einsum(
        "ged,geh->edh", mixed_low, grad_pre, preferred_element_type=jnp.float32
    )
    grad_mixed = jnp.einsum("geh,edh->ged", grad_pre, up_weight, preferred_element_type=jnp.float32)
    return (grad_up_part, grad_down_part, grad_mixed.astype(jnp.bfloat16))


def on_device(
    tokens,
    cotangent,
    block_table,
    seg_ids,
    group_ids,
    w_qkv,
    w_out,
    w_router,
    ln_gain,
    ln_bias,
    w_up,
    w_down,
):
    tok_rows = tokens[0]
    tok_count = tok_rows.shape[0]
    width = tok_rows.shape[1]
    expert_count = w_router.shape[1]
    ctx_index = lax.axis_index("ctx")
    full_rows = seg_ids.shape[1]
    block_len = full_rows // block_table.shape[0]
    row_ids = jnp.arange(full_rows, dtype=jnp.int32)
    key_pos = jnp.take(block_table, row_ids // block_len) * block_len + row_ids % block_len
    key_seg = seg_ids[0]
    pos_rows = lax.dynamic_slice_in_dim(key_pos, ctx_index * tok_count, tok_count)
    seg_rows = lax.dynamic_slice_in_dim(key_seg, ctx_index * tok_count, tok_count)
    scale = HEAD ** (-0.5)
    qkv_full, out_full, router_full, gain_full, bias_full = (
        lax.all_gather(w_qkv, "fsdp", axis=0, tiled=True),
        lax.all_gather(w_out, "fsdp", axis=0, tiled=True),
        lax.all_gather(w_router, "fsdp", axis=0, tiled=True),
        lax.all_gather(ln_gain, "fsdp", axis=0, tiled=True),
        lax.all_gather(ln_bias, "fsdp", axis=0, tiled=True),
    )
    qkv = jnp.dot(tok_rows, qkv_full, preferred_element_type=jnp.float32).astype(jnp.bfloat16)
    query_heads = qkv[:, :width].reshape(tok_count, HEADS, HEAD)
    key_all, val_all = (
        lax.all_gather(qkv[:, width : 2 * width], "ctx", axis=0, tiled=True),
        lax.all_gather(qkv[:, 2 * width :], "ctx", axis=0, tiled=True),
    )
    key_heads = key_all.reshape(full_rows, HEADS, HEAD)
    val_heads = val_all.reshape(full_rows, HEADS, HEAD)
    block_count = full_rows // KEY_BLOCK
    block_ids = jnp.arange(block_count, dtype=jnp.int32)

    def block_scores(index):
        start = index * KEY_BLOCK
        key_block = lax.dynamic_slice_in_dim(key_heads, start, KEY_BLOCK, 0)
        val_block = lax.dynamic_slice_in_dim(val_heads, start, KEY_BLOCK, 0)
        pos_block = lax.dynamic_slice_in_dim(key_pos, start, KEY_BLOCK, 0)
        seg_block = lax.dynamic_slice_in_dim(key_seg, start, KEY_BLOCK, 0)
        scores = (
            jnp.einsum("qhd,khd->hqk", query_heads, key_block, preferred_element_type=jnp.float32)
            * scale
        )
        allowed = (pos_block[None, :] <= pos_rows[:, None]) & (
            (seg_block[None, :] == 0) | (seg_block[None, :] == seg_rows[:, None])
        )
        return (scores, allowed[None], key_block, val_block)

    def lse_step(carry, index):
        top, total = carry
        scores, allowed, key_block, val_block = block_scores(index)
        masked = jnp.where(allowed, scores, neg_large)
        new_top = jnp.maximum(top, jnp.max(masked, axis=-1))
        weights = jnp.where(allowed, jnp.exp(masked - new_top[..., None]), 0.0)
        return ((new_top, total * jnp.exp(top - new_top) + jnp.sum(weights, axis=-1)), None)

    start_top = jnp.full((HEADS, tok_count), neg_large, jnp.float32)
    (top, total), unused = lax.scan(
        lse_step, (start_top, jnp.zeros((HEADS, tok_count), jnp.float32)), block_ids
    )
    log_total = top + jnp.log(total)

    def block_probs(index):
        scores, allowed, key_block, val_block = block_scores(index)
        probs = jnp.where(allowed, jnp.exp(scores - log_total[..., None]), 0.0)
        return (probs, key_block, val_block)

    def value_step(accum, index):
        probs, key_block, val_block = block_probs(index)
        return (
            accum
            + jnp.einsum(
                "hqk,khd->qhd",
                probs.astype(jnp.bfloat16),
                val_block,
                preferred_element_type=jnp.float32,
            ),
            None,
        )

    accum, unused = lax.scan(
        value_step, jnp.zeros((tok_count, HEADS, HEAD), jnp.float32), block_ids
    )
    attended = accum.reshape(tok_count, width).astype(jnp.bfloat16)
    hidden = tok_rows.astype(jnp.float32) + jnp.dot(
        attended, out_full, preferred_element_type=jnp.float32
    )
    center = hidden - jnp.mean(hidden, axis=-1, keepdims=True)
    inv_dev = lax.rsqrt(jnp.mean(center * center, axis=-1, keepdims=True) + epsilon)
    unit = center * inv_dev
    gain_f = gain_full.astype(jnp.float32)
    normed_low = (unit * gain_f + bias_full.astype(jnp.float32)).astype(jnp.bfloat16)
    logits = jnp.dot(normed_low, router_full, preferred_element_type=jnp.float32)
    groups_dev = tok_count // GROUP_SIZE
    local_group = group_ids[0] - ctx_index * groups_dev
    member = (local_group[:, None] == jnp.arange(groups_dev, dtype=jnp.int32)[None, :]).astype(
        jnp.float32
    )
    expo = jnp.exp(logits)
    group_total = jnp.dot(member.T, expo, precision=highest)
    mix_weights = expo / jnp.dot(member, group_total, precision=highest)
    weights_low = mix_weights.astype(jnp.bfloat16)
    mixing = member.astype(jnp.bfloat16).T[:, None, :] * weights_low.T[None, :, :]
    mixing_flat = mixing.reshape(groups_dev * expert_count, tok_count)
    mixed_low = jnp.dot(mixing_flat, normed_low, preferred_element_type=jnp.float32).astype(
        jnp.bfloat16
    )
    mixed_low = mixed_low.reshape(groups_dev, expert_count, width)
    owner_mixed = lax.all_to_all(mixed_low, "fsdp", split_axis=1, concat_axis=0, tiled=True)
    pre, active, owner_out = expert_forward(owner_mixed, w_up, w_down)
    expert_out = lax.all_to_all(owner_out, "fsdp", split_axis=0, concat_axis=1, tiled=True)
    expert_flat = expert_out.reshape(groups_dev * expert_count, width)
    spread = contract_rows(mixing_flat, expert_flat)
    layer_out = hidden + spread
    cot_rows = cotangent[0]
    cot_f = cot_rows.astype(jnp.float32)
    grad_expert = jnp.dot(mixing_flat, cot_rows, preferred_element_type=jnp.float32).astype(
        jnp.bfloat16
    )
    grad_expert = grad_expert.reshape(groups_dev, expert_count, width)
    coef = contract_cols(cot_rows, expert_flat).reshape(tok_count, groups_dev, expert_count)
    grad_mix_spread = jnp.sum(coef * member[:, :, None], axis=1)
    owner_grad = lax.all_to_all(grad_expert, "fsdp", split_axis=1, concat_axis=0, tiled=True)
    grad_up_own, grad_down_own, owner_back = expert_backward(
        owner_mixed, pre, active, owner_grad, w_up, w_down
    )
    grad_mixed = lax.all_to_all(owner_back, "fsdp", split_axis=0, concat_axis=1, tiled=True)
    grad_mixed_flat = grad_mixed.reshape(groups_dev * expert_count, width)
    grad_norm_mix = contract_rows(mixing_flat, grad_mixed_flat)
    grad_mixing = contract_cols(grad_mixed_flat, normed_low).reshape(
        groups_dev, expert_count, tok_count
    )
    grad_mix_mixing = jnp.sum(grad_mixing * member.T[:, None, :], axis=0).T
    grad_mix = grad_mix_spread + grad_mix_mixing
    product = mix_weights * grad_mix
    token_dot = jnp.dot(member, jnp.dot(member.T, product, precision=highest), precision=highest)
    grad_logits = (product - mix_weights * token_dot).astype(jnp.bfloat16)
    grad_router_part = contract_rows(normed_low, grad_logits)
    grad_norm_router = contract_cols(grad_logits, router_full)
    grad_normed = grad_norm_mix + grad_norm_router
    grad_gain_part = jnp.sum(grad_normed * unit, axis=0)
    grad_bias_part = jnp.sum(grad_normed, axis=0)
    scaled = grad_normed * gain_f
    grad_hidden = cot_f + inv_dev * (
        scaled
        - jnp.mean(scaled, axis=-1, keepdims=True)
        - unit * jnp.mean(scaled * unit, axis=-1, keepdims=True)
    )
    grad_branch = grad_hidden.astype(jnp.bfloat16)
    grad_out_part = contract_rows(attended, grad_branch)
    grad_heads = (
        contract_cols(grad_branch, out_full).astype(jnp.bfloat16).reshape(tok_count, HEADS, HEAD)
    )
    delta = jnp.sum(grad_heads.astype(jnp.float32) * accum, axis=-1).T

    def grad_step(grad_query, index):
        probs, key_block, val_block = block_probs(index)
        grad_probs = jnp.einsum(
            "qhd,khd->hqk", grad_heads, val_block, preferred_element_type=jnp.float32
        )
        grad_scores = (probs * (grad_probs - delta[..., None])).astype(jnp.bfloat16)
        grad_query = (
            grad_query
            + jnp.einsum("hqk,khd->qhd", grad_scores, key_block, preferred_element_type=jnp.float32)
            * scale
        )
        grad_key = (
            jnp.einsum("hqk,qhd->khd", grad_scores, query_heads, preferred_element_type=jnp.float32)
            * scale
        )
        grad_val = jnp.einsum(
            "hqk,qhd->khd",
            probs.astype(jnp.bfloat16),
            grad_heads,
            preferred_element_type=jnp.float32,
        )
        return (grad_query, (grad_key, grad_val))

    grad_query, (grad_keys, grad_vals) = lax.scan(
        grad_step, jnp.zeros((tok_count, HEADS, HEAD), jnp.float32), block_ids
    )
    grad_key_own, grad_val_own = (
        lax.psum_scatter(
            grad_keys.reshape(full_rows, width), "ctx", scatter_dimension=0, tiled=True
        ),
        lax.psum_scatter(
            grad_vals.reshape(full_rows, width), "ctx", scatter_dimension=0, tiled=True
        ),
    )
    grad_qkv_low = jnp.concatenate(
        [grad_query.reshape(tok_count, width), grad_key_own, grad_val_own], axis=1
    ).astype(jnp.bfloat16)
    grad_qkv_part = contract_rows(tok_rows, grad_qkv_low)
    grad_tokens = grad_hidden + contract_cols(grad_qkv_low, qkv_full)
    dense = (
        lax.psum_scatter(grad_qkv_part, "fsdp", scatter_dimension=0, tiled=True),
        lax.psum_scatter(grad_out_part, "fsdp", scatter_dimension=0, tiled=True),
        lax.psum_scatter(grad_router_part, "fsdp", scatter_dimension=0, tiled=True),
        lax.psum_scatter(grad_gain_part, "fsdp", scatter_dimension=0, tiled=True),
        lax.psum_scatter(grad_bias_part, "fsdp", scatter_dimension=0, tiled=True),
    )
    totals = lax.psum(
        (dense[0], dense[1], dense[2], dense[3], dense[4], grad_up_own, grad_down_own), "ctx"
    )
    return (
        layer_out[None],
        grad_tokens[None],
        totals[0],
        totals[1],
        totals[2],
        totals[3],
        totals[4],
        totals[5],
        totals[6],
    )


LOG2E = 1.4426950408889634
HIDE = -1e30
SUPER = 512
VMEM = pl.BlockSpec(memory_space=pltpu.VMEM)
SMEM = pl.BlockSpec(memory_space=pltpu.SMEM)
ANY = pl.BlockSpec(memory_space=pl.ANY)
LIMIT = 60 << 20


def dot_nn(left, right):
    return lax.dot_general(left, right, (((1,), (0,)), ((), ())), preferred_element_type=jnp.float32)


def dot_nt(left, right):
    return lax.dot_general(left, right, (((1,), (1,)), ((), ())), preferred_element_type=jnp.float32)


def dot_tn(left, right):
    return lax.dot_general(left, right, (((0,), (0,)), ((), ())), preferred_element_type=jnp.float32)


def split3(value):
    one = value.astype(jnp.bfloat16)
    rest = value - one.astype(jnp.float32)
    two = rest.astype(jnp.bfloat16)
    three = (rest - two.astype(jnp.float32)).astype(jnp.bfloat16)
    return one, two, three


def read_order(table_ref, seg_ref, inv_ref, first_ref, last_ref, blocks, block_len, per):
    for t in range(blocks):
        inv_ref[table_ref[t]] = t
    for s in range(blocks // per):
        first_ref[s] = seg_ref[inv_ref[s * per], 0]
        last_ref[s] = seg_ref[inv_ref[s * per + per - 1], block_len - 1]


def count_below(ref, limit, n):
    total = jnp.int32(0)
    for s in range(n):
        total = total + (ref[s] < limit).astype(jnp.int32)
    return total


def fwd_body(blocks, block_len, table_ref, seg_ref, tok_ref, w_ref, segrow_ref, att_ref, qf_ref, kf_ref, vf_ref, kp_ref, stat_ref,
             inv_ref, first_ref, last_ref):
    per = SUPER // block_len
    runs = blocks // per
    read_order(table_ref, seg_ref, inv_ref, first_ref, last_ref, blocks, block_len, per)
    weight = w_ref[...].reshape(w_ref.shape[0] * w_ref.shape[1], w_ref.shape[2])
    factor = HEAD ** (-0.5) * LOG2E
    ids = lax.broadcasted_iota(jnp.int32, (8, 1), 0) + 1
    eye = (lax.broadcasted_iota(jnp.int32, (8, HEAD), 0) == lax.broadcasted_iota(jnp.int32, (8, HEAD), 1)).astype(jnp.bfloat16)
    lane = lax.broadcasted_iota(jnp.int32, (block_len, HEAD), 1)
    ones_k = ((lane >= 8) & (lane < 11)).astype(jnp.float32)
    ones_v = (lane < 3).astype(jnp.bfloat16)

    def project(s, carry):
        t = inv_ref[s]
        rows = tok_ref[pl.ds(pl.multiple_of(t * block_len, block_len), block_len), :]
        qkv = dot_nn(rows, weight).astype(jnp.bfloat16)
        q, k, v = qkv[:, :HEAD], qkv[:, HEAD:2 * HEAD], qkv[:, 2 * HEAD:]
        one, two, three = split3(k.astype(jnp.float32) * factor)
        same = segrow_ref[pl.ds(t, 1), :] == ids
        other = dot_tn(jnp.where(same, 0.0, 1.0).astype(jnp.bfloat16), eye).astype(jnp.bfloat16)
        hidden = (dot_tn(jnp.where(same, HIDE, 0.0).astype(jnp.bfloat16), eye) + ones_k).astype(jnp.bfloat16)
        at = pl.ds(pl.multiple_of(s * block_len, block_len), block_len)
        qf_ref[at, :] = jnp.concatenate([q, q, q, other], axis=1)
        kf_ref[at, :] = jnp.concatenate([one, two, three, hidden], axis=1)
        vf_ref[at, :] = jnp.concatenate([v, ones_v], axis=1)
        kp_ref[at, :] = jnp.concatenate([k, k], axis=1)
        return carry

    lax.fori_loop(0, blocks, project, 0)
    start_hidden = count_below(first_ref, 1, runs)
    row = lax.broadcasted_iota(jnp.int32, (SUPER, SUPER), 0)
    col = lax.broadcasted_iota(jnp.int32, (SUPER, SUPER), 1)
    causal = col <= row

    def query_run(run, carry):
        at_q = pl.ds(pl.multiple_of(run * SUPER, SUPER), SUPER)
        query = qf_ref[at_q, :]
        skip = jnp.maximum(count_below(last_ref, first_ref[run], runs) - start_hidden, 0)

        def tile(index, diagonal, state):
            top, acc = state
            at_k = pl.ds(pl.multiple_of(index * SUPER, SUPER), SUPER)
            scores = dot_nt(query, kf_ref[at_k, :])
            if diagonal:
                scores = jnp.where(causal, scores, HIDE)
            new_top = jnp.maximum(top, jnp.max(scores, axis=1, keepdims=True))
            weights = jnp.exp2(scores - new_top)
            acc = acc * jnp.exp2(top - new_top) + dot_nn(weights.astype(jnp.bfloat16), vf_ref[at_k, :])
            return new_top, acc

        def step(n, state):
            return tile(jnp.where(n < start_hidden, n, n + skip), False, state)

        state = (jnp.full((SUPER, 1), HIDE, jnp.float32), jnp.zeros((SUPER, 2 * HEAD), jnp.float32))
        state = lax.fori_loop(0, run - skip, step, state)
        top, acc = tile(run, True, state)
        total = acc[:, HEAD:HEAD + 1]
        lse = top + jnp.log2(total)
        out = acc[:, :HEAD] / total
        stat_ref[at_q, :] = jnp.concatenate([out, jnp.broadcast_to(lse, (SUPER, HEAD))], axis=1)
        return carry

    lax.fori_loop(0, runs, query_run, 0)
    for c in range(blocks // 2):
        parts = []
        for half in range(2):
            s = table_ref[2 * c + half]
            parts.append(stat_ref[pl.ds(pl.multiple_of(s * block_len, block_len), block_len), :HEAD])
        att_ref[c] = jnp.concatenate(parts, axis=1).astype(jnp.bfloat16)


def attn_fwd(tokens_all, weight, table, segs):
    rows = tokens_all.shape[0]
    blocks, block_len = segs.shape
    runs = rows // SUPER
    return pl.pallas_call(
        functools.partial(fwd_body, blocks, block_len),
        out_shape=(
            jax.ShapeDtypeStruct((blocks // 2, block_len, 2 * HEAD), jnp.bfloat16),
            jax.ShapeDtypeStruct((rows, 4 * HEAD), jnp.bfloat16),
            jax.ShapeDtypeStruct((rows, 4 * HEAD), jnp.bfloat16),
            jax.ShapeDtypeStruct((rows, 2 * HEAD), jnp.bfloat16),
            jax.ShapeDtypeStruct((rows, 2 * HEAD), jnp.bfloat16),
            jax.ShapeDtypeStruct((rows, 2 * HEAD), jnp.float32),
        ),
        in_specs=[SMEM, SMEM, VMEM, VMEM, VMEM],
        out_specs=(VMEM,) * 6,
        scratch_shapes=[pltpu.SMEM((blocks,), jnp.int32), pltpu.SMEM((runs,), jnp.int32), pltpu.SMEM((runs,), jnp.int32)],
        compiler_params=pltpu.CompilerParams(vmem_limit_bytes=LIMIT),
        name="attention",
    )(table, segs, tokens_all, weight, segs)


def bwd_body(blocks, block_len, table_ref, seg_ref, do_ref, qf_ref, kf_ref, vf_ref, kp_ref, stat_ref, out_ref,
             inv_ref, first_ref, last_ref, qs_ref, dof_ref, dq_ref, dk_ref, dv_ref):
    per = SUPER // block_len
    runs = blocks // per
    read_order(table_ref, seg_ref, inv_ref, first_ref, last_ref, blocks, block_len, per)
    lane = lax.broadcasted_iota(jnp.int32, (block_len, HEAD), 1)
    zero = jnp.zeros((), jnp.bfloat16)

    def spread(value, offset):
        one, two, three = (jnp.broadcast_to(part, (block_len, HEAD)) for part in split3(value))
        out = jnp.where(lane == offset, one, zero)
        out = jnp.where(lane == offset + 1, two, out)
        return jnp.where(lane == offset + 2, three, out)

    def prepare(s, carry):
        t = inv_ref[s]
        at = pl.ds(pl.multiple_of(s * block_len, block_len), block_len)
        both = do_ref[t // 2]
        grad = jnp.where(t % 2 == 0, both[:, :HEAD], both[:, HEAD:])
        stat = stat_ref[at, :]
        delta = jnp.sum(grad.astype(jnp.float32) * stat[:, :HEAD], axis=1, keepdims=True)
        dof_ref[at, :] = jnp.concatenate([grad, spread(-delta, 0)], axis=1)
        old = qf_ref[at, :]
        tail = jnp.where(lane < 8, old[:, 3 * HEAD:], spread(-stat[:, HEAD:HEAD + 1], 8))
        qs_ref[at, :] = jnp.concatenate([old[:, :3 * HEAD], tail], axis=1)
        dq_ref[at, :] = jnp.zeros((block_len, 2 * HEAD), jnp.float32)
        return carry

    lax.fori_loop(0, blocks, prepare, 0)
    causal = lax.broadcasted_iota(jnp.int32, (SUPER, SUPER), 0) <= lax.broadcasted_iota(jnp.int32, (SUPER, SUPER), 1)

    def key_run(run, carry):
        at_k = pl.ds(pl.multiple_of(run * SUPER, SUPER), SUPER)
        end = jnp.where(first_ref[run] == 0, runs, count_below(first_ref, last_ref[run] + 1, runs))

        def tile(index, diagonal):
            at_q = pl.ds(pl.multiple_of(index * SUPER, SUPER), SUPER)
            scores = dot_nt(kf_ref[at_k, :], qs_ref[at_q, :])
            probs = jnp.exp2(scores)
            if diagonal:
                probs = jnp.where(causal, probs, 0.0)
            slope = dot_nt(vf_ref[at_k, :], dof_ref[at_q, :])
            grad = (probs * slope).astype(jnp.bfloat16)
            dv = dot_nn(probs.astype(jnp.bfloat16), dof_ref[at_q, :])
            dk = dot_nn(grad, qs_ref[at_q, :2 * HEAD])
            if diagonal:
                dv_ref[...] = dv
                dk_ref[...] = dk
            else:
                dv_ref[...] += dv
                dk_ref[...] += dk
            dq_ref[at_q, :] += dot_tn(grad, kp_ref[at_k, :])

        tile(run, True)

        def step(index, inner):
            tile(index, False)
            return inner

        lax.fori_loop(run + 1, end, step, 0)
        scale = HEAD ** (-0.5)
        stat_dk = (dk_ref[:, :HEAD] * scale).astype(jnp.bfloat16)
        stat_dv = dv_ref[:, :HEAD].astype(jnp.bfloat16)
        stat_dq = (dq_ref[at_k, :HEAD] * scale).astype(jnp.bfloat16)
        for part in range(per):
            t = inv_ref[run * per + part]
            rows = slice(part * block_len, (part + 1) * block_len)
            pieces = (stat_dq[rows], stat_dk[rows], stat_dv[rows])
            for parity in range(2):
                @pl.when(t % 2 == parity)
                def _():
                    for kind in range(3):
                        low = kind * 2 * HEAD + parity * HEAD
                        out_ref[t // 2, :, low:low + HEAD] = pieces[kind]
        return carry

    lax.fori_loop(0, runs, key_run, 0)


def attn_bwd(grad, saved, table, segs):
    blocks, block_len = segs.shape
    rows = blocks * block_len
    runs = rows // SUPER
    return pl.pallas_call(
        functools.partial(bwd_body, blocks, block_len),
        out_shape=jax.ShapeDtypeStruct((blocks // 2, block_len, 6 * HEAD), jnp.bfloat16),
        in_specs=[SMEM, SMEM] + [VMEM] * 6,
        out_specs=VMEM,
        scratch_shapes=[
            pltpu.SMEM((blocks,), jnp.int32), pltpu.SMEM((runs,), jnp.int32), pltpu.SMEM((runs,), jnp.int32),
            pltpu.VMEM((rows, 4 * HEAD), jnp.bfloat16), pltpu.VMEM((rows, 2 * HEAD), jnp.bfloat16),
            pltpu.VMEM((rows, 2 * HEAD), jnp.float32), pltpu.VMEM((SUPER, 2 * HEAD), jnp.float32),
            pltpu.VMEM((SUPER, 2 * HEAD), jnp.float32),
        ],
        compiler_params=pltpu.CompilerParams(vmem_limit_bytes=LIMIT),
        name="attention_grad",
    )(table, segs, grad, *saved)


MESH = pl.DeviceIdType.MESH


def flip(index, bit):
    return index + bit - 2 * bit * lax.rem(index // bit, 2)


def meet(devices):
    barrier = pltpu.get_barrier_semaphore()
    for device in devices:
        pl.semaphore_signal(barrier, inc=1, device_id=device, device_id_type=MESH)
    pl.semaphore_wait(barrier, len(devices))


def push(src, dst, send_sem, recv_sem, device):
    return pltpu.make_async_remote_copy(
        src_ref=src, dst_ref=dst, send_sem=send_sem, recv_sem=recv_sem, device_id=device, device_id_type=MESH
    )


def exchange_body(axis, count, x_ref, out_ref, own_sem, send_sem, recv_sem):
    spot = {"ctx": lax.axis_index("ctx"), "fsdp": lax.axis_index("fsdp")}
    me = spot[axis]
    others = [lax.rem(me + k, count) for k in range(1, count)]
    meet([(other, spot["fsdp"]) if axis == "ctx" else (spot["ctx"], other) for other in others])
    own = pltpu.make_async_copy(x_ref.at[me], out_ref.at[me], own_sem)
    own.start()
    copies = []
    for k, other in enumerate(others):
        device = (other, spot["fsdp"]) if axis == "ctx" else (spot["ctx"], other)
        copies.append(push(x_ref.at[other], out_ref.at[me], send_sem.at[k], recv_sem.at[k], device))
        copies[-1].start()
    own.wait()
    for copy in copies:
        copy.wait()


def exchange(x, axis, collective_id, name):
    count = x.shape[0]
    return pl.pallas_call(
        functools.partial(exchange_body, axis, count),
        out_shape=jax.ShapeDtypeStruct(x.shape, x.dtype),
        in_specs=[ANY],
        out_specs=ANY,
        scratch_shapes=[pltpu.SemaphoreType.DMA, pltpu.SemaphoreType.DMA((count - 1,)), pltpu.SemaphoreType.DMA((count - 1,))],
        compiler_params=pltpu.CompilerParams(collective_id=collective_id, has_side_effects=True),
        name=name,
    )(x)


def gather_body(zs, tok_ref, *refs):
    count = (len(refs) - 9) // 2
    shards, toks_ref, wholes = refs[:count], refs[count], refs[count + 1:2 * count + 1]
    own_sem, z_send, z_recv, far_send, near_send, own_recv, diag_recv, near_recv = refs[2 * count + 1:]
    me, z = lax.axis_index("ctx"), lax.axis_index("fsdp")
    sib, xn, yn, diag = flip(me, 1), flip(me, 2), flip(me, 4), flip(flip(me, 2), 4)
    z_peers = [lax.rem(z + k, zs) for k in range(1, zs)]
    meet([(sib, z), (xn, z), (yn, z)] + [(me, other) for other in z_peers])
    half = tok_ref.shape[0] // 2

    def part(device, k):
        return toks_ref.at[device, pl.ds(k * half, half)]

    started = []

    def go(copy):
        copy.start()
        started.append(copy)

    for k in (0, 1):
        rows = tok_ref.at[pl.ds(k * half, half)]
        go(push(rows, part(me, k), far_send.at[0, k], own_recv.at[0, k], (xn, z)))
        rows = tok_ref.at[pl.ds((1 - k) * half, half)]
        go(push(rows, part(me, 1 - k), far_send.at[1, 1 - k], own_recv.at[1, 1 - k], (yn, z)))
    for i, (shard, whole) in enumerate(zip(shards, wholes)):
        for k, other in enumerate(z_peers):
            go(push(shard, whole.at[z], z_send.at[i, k], z_recv.at[i, k], (me, other)))
    for k in (0, 1):
        rows = tok_ref.at[pl.ds(k * half, half)]
        go(push(rows, part(me, k), near_send.at[0, k], near_recv.at[0, k], (sib, z)))
    locals_ = [pltpu.make_async_copy(tok_ref, toks_ref.at[me], own_sem.at[0])]
    for i, (shard, whole) in enumerate(zip(shards, wholes)):
        locals_.append(pltpu.make_async_copy(shard, whole.at[z], own_sem.at[i + 1]))
    for copy in locals_:
        copy.start()

    def arrived(device, k, sem):
        push(part(device, k), part(device, k), far_send.at[0, 0], sem, (sib, z)).wait_recv()

    def relay(device, k, i):
        go(push(part(device, k), part(device, k), near_send.at[i, k], near_recv.at[i, k], (sib, z)))

    arrived(xn, 0, own_recv.at[0, 0])
    go(push(part(xn, 0), part(xn, 0), far_send.at[2, 0], diag_recv.at[0], (yn, z)))
    relay(xn, 0, 1)
    arrived(yn, 1, own_recv.at[1, 1])
    go(push(part(yn, 1), part(yn, 1), far_send.at[2, 1], diag_recv.at[1], (xn, z)))
    relay(yn, 1, 2)
    arrived(xn, 1, own_recv.at[0, 1])
    relay(xn, 1, 1)
    arrived(yn, 0, own_recv.at[1, 0])
    relay(yn, 0, 2)
    for k in (0, 1):
        arrived(diag, k, diag_recv.at[k])
        relay(diag, k, 3)
    for k in (0, 1):
        for i, device in enumerate((sib, flip(xn, 1), flip(yn, 1), flip(diag, 1))):
            arrived(device, k, near_recv.at[i, k])
    for i, whole in enumerate(wholes):
        for k in range(zs - 1):
            other = lax.rem(z + zs - 1 - k, zs)
            push(whole.at[other], whole.at[other], z_send.at[i, k], z_recv.at[i, k], (me, other)).wait_recv()
    for copy in locals_:
        copy.wait()
    for copy in started:
        copy.wait_send()


def gather(tokens, shards, ctx_count, z_count):
    outs = [jax.ShapeDtypeStruct((ctx_count,) + tokens.shape, tokens.dtype)]
    outs += [jax.ShapeDtypeStruct((z_count,) + shard.shape, shard.dtype) for shard in shards]
    dma = pltpu.SemaphoreType.DMA
    return pl.pallas_call(
        functools.partial(gather_body, z_count),
        out_shape=outs,
        in_specs=[ANY] * (1 + len(shards)),
        out_specs=[ANY] * (1 + len(shards)),
        scratch_shapes=[
            dma((1 + len(shards),)), dma((len(shards), z_count - 1)), dma((len(shards), z_count - 1)), dma((3, 2)), dma((4, 2)),
            dma((2, 2)), dma((2,)), dma((4, 2)),
        ],
        compiler_params=pltpu.CompilerParams(collective_id=1, has_side_effects=True),
        name="gather_tokens",
    )(tokens, *shards)


def norm_parts(hidden):
    center = hidden - jnp.mean(hidden, axis=-1, keepdims=True)
    inv_dev = lax.rsqrt(jnp.mean(center * center, axis=-1, keepdims=True) + epsilon)
    return center * inv_dev, inv_dev


def small_rows(pack_ref):
    return jnp.concatenate([pack_ref[z] for z in range(pack_ref.shape[0])], axis=1)


def mix_body(experts, groups, att_ref, tok_ref, cot_ref, wo_ref, pack_ref, gid_ref, hidden_ref, normed_ref, mix_ref, attended_ref, send_ref):
    heads = att_ref.shape[0]
    halves = [jnp.concatenate([att_ref[h, :, HEAD * p:HEAD * (p + 1)] for h in range(heads)], axis=1) for p in range(2)]
    attended = jnp.concatenate(halves, axis=0)
    attended_ref[...] = attended
    width = tok_ref.shape[1]
    hidden = tok_ref[...].astype(jnp.float32) + dot_nn(attended, wo_ref[...].reshape(width, width))
    hidden_ref[...] = hidden
    unit, inv_dev = norm_parts(hidden)
    small = small_rows(pack_ref)
    gain, bias = small[experts:experts + 1].astype(jnp.float32), small[experts + 1:experts + 2].astype(jnp.float32)
    normed = (unit * gain + bias).astype(jnp.bfloat16)
    normed_ref[...] = normed
    expo = jnp.exp(dot_nt(small, normed)[:experts])
    rows = tok_ref.shape[0]
    expo = jnp.broadcast_to(expo[:, None, :], (experts, groups, rows)).reshape(experts * groups, rows)
    member = lax.rem(lax.broadcasted_iota(jnp.int32, (experts * groups, 1), 0), groups) == lax.rem(gid_ref[...], groups)
    expo = jnp.where(member, expo, 0.0)
    mix = expo / jnp.sum(expo, axis=1, keepdims=True)
    mix_ref[...] = mix
    low = mix.astype(jnp.bfloat16)
    owners = send_ref.shape[0]
    per = experts * groups // owners
    send_ref[:, 0] = dot_nn(low, normed).astype(jnp.bfloat16).reshape(owners, per, width)
    send_ref[:, 1] = dot_nn(low, cot_ref[...]).astype(jnp.bfloat16).reshape(owners, per, width)


def mix_tokens(att, tokens, cot, w_out, pack, gid_row, experts, groups, owners):
    rows, width = tokens.shape
    return pl.pallas_call(
        functools.partial(mix_body, experts, groups),
        out_shape=(
            jax.ShapeDtypeStruct((rows, width), jnp.float32),
            jax.ShapeDtypeStruct((rows, width), jnp.bfloat16),
            jax.ShapeDtypeStruct((experts * groups, rows), jnp.float32),
            jax.ShapeDtypeStruct((rows, width), jnp.bfloat16),
            jax.ShapeDtypeStruct((owners, 2, experts * groups // owners, width), jnp.bfloat16),
        ),
        in_specs=[VMEM] * 6,
        out_specs=(VMEM,) * 5,
        compiler_params=pltpu.CompilerParams(vmem_limit_bytes=LIMIT),
        name="mix_tokens",
    )(att, tokens, cot, w_out, pack, gid_row)


def expert_body(groups, got_ref, up_ref, down_ref, back_ref, out_acc, grad_acc):
    own, part = pl.program_id(0), pl.program_id(1)
    at = pl.ds(pl.multiple_of(own * groups, groups), groups)
    sources, width = got_ref.shape[0], got_ref.shape[3]
    mixed = got_ref[:, 0, at, :].reshape(sources * groups, width)
    grad_out = got_ref[:, 1, at, :].reshape(sources * groups, width)
    up, down = up_ref[0], down_ref[0]
    pre = dot_nn(mixed, up)
    active = jax.nn.gelu(pre, approximate=True).astype(jnp.bfloat16)
    grad_pre = (dot_nt(grad_out, down) * gelu_slope(pre)).astype(jnp.bfloat16)
    out, grad = dot_nn(active, down), dot_nt(grad_pre, up)

    @pl.when(part == 0)
    def _():
        out_acc[...] = out
        grad_acc[...] = grad

    @pl.when(part != 0)
    def _():
        out_acc[...] += out
        grad_acc[...] += grad

    @pl.when(part == pl.num_programs(1) - 1)
    def _():
        back_ref[:, 0, at, :] = out_acc[...].astype(jnp.bfloat16).reshape(sources, groups, width)
        back_ref[:, 1, at, :] = grad_acc[...].astype(jnp.bfloat16).reshape(sources, groups, width)


def run_experts(got, w_up, w_down, groups):
    own, width, ffn = w_up.shape
    step = 1024
    rows = got.shape[0] * groups
    return pl.pallas_call(
        functools.partial(expert_body, groups),
        grid=(own, ffn // step),
        out_shape=jax.ShapeDtypeStruct(got.shape, jnp.bfloat16),
        in_specs=[
            pl.BlockSpec(got.shape, lambda e, f: (0, 0, 0, 0)),
            pl.BlockSpec((1, width, step), lambda e, f: (e, 0, f)),
            pl.BlockSpec((1, step, width), lambda e, f: (e, f, 0)),
        ],
        out_specs=pl.BlockSpec(got.shape, lambda e, f: (0, 0, 0, 0)),
        scratch_shapes=[pltpu.VMEM((rows, width), jnp.float32)] * 2,
        compiler_params=pltpu.CompilerParams(vmem_limit_bytes=LIMIT),
        name="experts",
    )(got, w_up, w_down)


def expert_grad_body(mixed_ref, grad_ref, up_ref, down_ref, gup_ref, gdown_ref):
    width = up_ref.shape[1]
    mixed, grad_out = mixed_ref[...].reshape(-1, width), grad_ref[...].reshape(-1, width)
    pre = dot_nn(mixed, up_ref[0])
    active = jax.nn.gelu(pre, approximate=True).astype(jnp.bfloat16)
    grad_pre = (dot_nt(grad_out, down_ref[0]) * gelu_slope(pre)).astype(jnp.bfloat16)
    gup_ref[0] = dot_tn(mixed, grad_pre)
    gdown_ref[0] = dot_tn(active, grad_out)


def expert_grads(gathered, w_up, w_down, groups):
    own, width, ffn = w_up.shape
    step = 512
    sources = gathered.shape[0]
    view = gathered.reshape(sources, 2, own, groups, width)
    return pl.pallas_call(
        expert_grad_body,
        grid=(own, ffn // step),
        out_shape=(jax.ShapeDtypeStruct(w_up.shape, jnp.float32), jax.ShapeDtypeStruct(w_down.shape, jnp.float32)),
        in_specs=[
            pl.BlockSpec((sources, 1, 1, groups, width), lambda e, f: (0, 0, e, 0, 0)),
            pl.BlockSpec((sources, 1, 1, groups, width), lambda e, f: (0, 1, e, 0, 0)),
            pl.BlockSpec((1, width, step), lambda e, f: (e, 0, f)),
            pl.BlockSpec((1, step, width), lambda e, f: (e, f, 0)),
        ],
        out_specs=(pl.BlockSpec((1, width, step), lambda e, f: (e, 0, f)), pl.BlockSpec((1, step, width), lambda e, f: (e, f, 0))),
        compiler_params=pltpu.CompilerParams(vmem_limit_bytes=LIMIT),
        name="expert_grads",
    )(view, view, w_up, w_down)


def unmix_body(experts, groups, heads, hidden_ref, normed_ref, mix_ref, attended_ref, cot_ref, wo_ref, pack_ref, back_ref,
               layer_ref, ghidden_ref, gout_ref, small_ref, ghead_ref):
    rows, width = hidden_ref.shape
    hidden, normed, mix, cot = hidden_ref[...], normed_ref[...], mix_ref[...], cot_ref[...]
    low = mix.astype(jnp.bfloat16)
    flat = experts * groups
    expert_out, grad_mixed = back_ref[:, 0].reshape(flat, width), back_ref[:, 1].reshape(flat, width)
    layer_ref[...] = hidden + dot_tn(low, expert_out)
    product = mix * (dot_nt(expert_out, cot) + dot_nt(grad_mixed, normed))
    grad_logits = product - mix * jnp.sum(product, axis=1, keepdims=True)
    grad_logits = jnp.sum(grad_logits.reshape(experts, groups, rows), axis=1).astype(jnp.bfloat16)
    small = small_rows(pack_ref)
    pad = jnp.zeros((small.shape[0] - experts, rows), jnp.bfloat16)
    grad_logits = jnp.concatenate([grad_logits, pad], axis=0)
    grad_normed = dot_tn(jnp.concatenate([low, grad_logits], axis=0), jnp.concatenate([grad_mixed, small], axis=0))
    gain = small[experts:experts + 1].astype(jnp.float32)
    unit, inv_dev = norm_parts(hidden)
    small_ref[...] = dot_nn(grad_logits, normed)
    small_ref[experts:experts + 1] = jnp.sum(grad_normed * unit, axis=0, keepdims=True)
    small_ref[experts + 1:experts + 2] = jnp.sum(grad_normed, axis=0, keepdims=True)
    scaled = grad_normed * gain
    mean = jnp.mean(scaled, axis=-1, keepdims=True)
    grad_hidden = cot.astype(jnp.float32) + inv_dev * (scaled - mean - unit * jnp.mean(scaled * unit, axis=-1, keepdims=True))
    ghidden_ref[...] = grad_hidden
    branch = grad_hidden.astype(jnp.bfloat16)
    gout_ref[...] = dot_tn(attended_ref[...], branch)
    grad_heads = dot_nt(branch, wo_ref[...].reshape(width, width)).astype(jnp.bfloat16)
    half = rows // 2
    for h in range(heads):
        at = slice(HEAD * h, HEAD * (h + 1))
        ghead_ref[h] = jnp.concatenate([grad_heads[:half, at], grad_heads[half:, at]], axis=1)


def unmix_tokens(hidden, normed, mix, attended, cot, w_out, pack, back, experts, groups, heads):
    rows, width = hidden.shape
    return pl.pallas_call(
        functools.partial(unmix_body, experts, groups, heads),
        out_shape=(
            jax.ShapeDtypeStruct((rows, width), jnp.float32),
            jax.ShapeDtypeStruct((rows, width), jnp.float32),
            jax.ShapeDtypeStruct((width, width), jnp.float32),
            jax.ShapeDtypeStruct((pack.shape[1], width), jnp.float32),
            jax.ShapeDtypeStruct((heads, rows // 2, 2 * HEAD), jnp.bfloat16),
        ),
        in_specs=[VMEM] * 8,
        out_specs=(VMEM,) * 5,
        compiler_params=pltpu.CompilerParams(vmem_limit_bytes=LIMIT),
        name="unmix_tokens",
    )(hidden, normed, mix, attended, cot, w_out, pack, back)


def head_weight_body(z_count, toks_ref, grad_ref, out_ref, acc_ref):
    step = pl.program_id(0)
    half = grad_ref.shape[1]
    total = None
    for p in range(2):
        columns = [grad_ref[0, :, HEAD * (2 * kind + p):HEAD * (2 * kind + p + 1)] for kind in range(3)]
        part = dot_tn(jnp.concatenate(columns, axis=1), toks_ref[0, p * half:(p + 1) * half, :])
        total = part if total is None else total + part

    @pl.when(step == 0)
    def _():
        acc_ref[...] = total

    @pl.when(step != 0)
    def _():
        acc_ref[...] += total

    @pl.when(step == pl.num_programs(0) - 1)
    def _():
        out_ref[...] = acc_ref[...].T


def head_weight(tokens_all, grad, z_count):
    count, rows, width = tokens_all.shape
    return pl.pallas_call(
        functools.partial(head_weight_body, z_count),
        grid=(count,),
        out_shape=jax.ShapeDtypeStruct((width, 3 * HEAD), jnp.float32),
        in_specs=[
            pl.BlockSpec((1, rows, width), lambda i: (i, 0, 0)),
            pl.BlockSpec((1,) + grad.shape[1:], lambda i: (i, 0, 0)),
        ],
        out_specs=pl.BlockSpec((width, 3 * HEAD), lambda i: (0, 0)),
        scratch_shapes=[pltpu.VMEM((3 * HEAD, width), jnp.float32)],
        compiler_params=pltpu.CompilerParams(vmem_limit_bytes=LIMIT),
        name="head_weight",
    )(tokens_all, grad)


def token_grad_body(grad_ref, weight_ref, ghidden_ref, out_ref):
    heads, half = grad_ref.shape[0], grad_ref.shape[1]
    for p in range(2):
        columns = [grad_ref[h, :, HEAD * (2 * kind + p):HEAD * (2 * kind + p + 1)] for kind in range(3) for h in range(heads)]
        at = slice(p * half, (p + 1) * half)
        out_ref[at, :] = ghidden_ref[at, :] + dot_nt(jnp.concatenate(columns, axis=1), weight_ref[...])


def token_grad(grad, weight, ghidden):
    return pl.pallas_call(
        token_grad_body,
        out_shape=jax.ShapeDtypeStruct(ghidden.shape, jnp.float32),
        in_specs=[VMEM] * 3,
        out_specs=VMEM,
        compiler_params=pltpu.CompilerParams(vmem_limit_bytes=LIMIT),
        name="token_grad",
    )(grad, weight, ghidden)


def fast_device(
    tokens, cotangent, block_table, seg_ids, group_ids, w_qkv, w_out, w_router, ln_gain, ln_bias, w_up, w_down
):
    ctx_count, z_count = lax.axis_size("ctx"), lax.axis_size("fsdp")
    ctx_index, z_index = lax.axis_index("ctx"), lax.axis_index("fsdp")
    tok_rows, cot_rows = tokens[0], cotangent[0]
    rows, width = tok_rows.shape
    experts = w_router.shape[1]
    groups = rows // GROUP_SIZE
    shard = w_qkv.shape[0]
    segs = seg_ids[0].reshape(block_table.shape[0], -1)
    head_cols = lax.dynamic_slice_in_dim(w_qkv.reshape(shard, 3, ctx_count, HEAD), ctx_index, 1, 2).reshape(shard, 3 * HEAD)
    pack = jnp.concatenate(
        [w_router.T, ln_gain[None], ln_bias[None], jnp.zeros((16 - experts - 2, shard), jnp.bfloat16)], axis=0
    )
    tokens_all, head_weights, out_full, pack_full = gather(tok_rows, [head_cols, w_out, pack], ctx_count, z_count)
    qkv_full = lax.all_gather(w_qkv, "fsdp", axis=0, tiled=True)
    att, *saved = attn_fwd(tokens_all.reshape(ctx_count * rows, width), head_weights, block_table, segs)
    att = exchange(att, "ctx", 2, "exchange_attended")
    hidden, normed, mix, attended, mixed = mix_tokens(
        att, tok_rows, cot_rows, out_full, pack_full, group_ids, experts, groups, z_count
    )
    got = exchange(mixed, "fsdp", 3, "exchange_mixed")
    back = exchange(run_experts(got, w_up, w_down, groups), "fsdp", 4, "exchange_back")
    gathered = lax.all_gather(got, "ctx", axis=0, tiled=True)
    layer_out, grad_hidden, gout_part, small_part, grad_heads = unmix_tokens(
        hidden, normed, mix, attended, cot_rows, out_full, pack_full, back, experts, groups, ctx_count
    )
    grad_heads = exchange(grad_heads, "ctx", 5, "exchange_grad")
    grad_out = lax.psum(lax.psum_scatter(gout_part, "fsdp", scatter_dimension=0, tiled=True), "ctx")
    small = lax.psum(small_part, ("ctx", "fsdp"))
    grad_qkv_all = attn_bwd(grad_heads, saved, block_table, segs)
    grad_rows = exchange(grad_qkv_all, "ctx", 6, "exchange_qkv")
    grad_up, grad_down = expert_grads(gathered, w_up, w_down, groups)
    own_cols = head_weight(tokens_all, grad_qkv_all, z_count)
    own_cols = lax.psum_scatter(own_cols, "fsdp", scatter_dimension=0, tiled=True)
    cols = lax.all_gather(own_cols.reshape(shard, 3, 1, HEAD), "ctx", axis=2, tiled=True)
    grad_tokens = token_grad(grad_rows, qkv_full, grad_hidden)
    mine = lax.dynamic_slice_in_dim(small, z_index * shard, shard, 1)
    return (
        layer_out[None],
        grad_tokens[None],
        cols.reshape(shard, 3 * width),
        grad_out,
        mine[:experts].T,
        mine[experts],
        mine[experts + 1],
        grad_up,
        grad_down,
    )


def solution(mesh):
    placed = (
        P("fsdp", "ctx", None),
        P("fsdp", "ctx", None),
        P(),
        P("fsdp", None),
        P("fsdp", "ctx"),
        P("fsdp", None),
        P("fsdp", None),
        P("fsdp", None),
        P("fsdp"),
        P("fsdp"),
        P("fsdp", None, None),
        P("fsdp", None, None),
    )
    step = fast_device if mesh.shape["ctx"] == HEADS else on_device
    return jax.shard_map(
        step,
        mesh=mesh,
        in_specs=placed,
        out_specs=(
            P("fsdp", "ctx", None),
            P("fsdp", "ctx", None),
            P("fsdp", None),
            P("fsdp", None),
            P("fsdp", None),
            P("fsdp"),
            P("fsdp"),
            P("fsdp", None, None),
            P("fsdp", None, None),
        ),
        check_vma=False,
    )
```

```python
import functools

import jax
import jax.numpy as jnp
from jax import lax
from jax.experimental import pallas as pl
from jax.experimental.pallas import tpu as pltpu
from jax.sharding import PartitionSpec as P

HEADS = 8
HEAD = 64
GROUP_SIZE = 32
KEY_BLOCK = 2048


highest = lax.Precision.HIGHEST
neg_large = -1e30
epsilon = 1e-05
gelu_coef = 0.7978845608028654
gelu_cubic = 0.044715


def contract_rows(left, right):
    return lax.dot_general(
        left, right, (((0,), (0,)), ((), ())), preferred_element_type=jnp.float32
    )


def contract_cols(left, right):
    return lax.dot_general(
        left, right, (((1,), (1,)), ((), ())), preferred_element_type=jnp.float32
    )


def gelu_slope(value):
    inner = gelu_coef * (value + gelu_cubic * value * value * value)
    tangent = jnp.tanh(inner)
    return 0.5 * (1.0 + tangent) + 0.5 * value * (1.0 - tangent * tangent) * gelu_coef * (
        1.0 + 3.0 * gelu_cubic * value * value
    )


def expert_forward(mixed_low, up_weight, down_weight):
    pre = jnp.einsum("ged,edh->geh", mixed_low, up_weight, preferred_element_type=jnp.float32)
    active = jax.nn.gelu(pre, approximate=True).astype(jnp.bfloat16)
    result = jnp.einsum("geh,ehd->ged", active, down_weight, preferred_element_type=jnp.float32)
    return (pre, active, result.astype(jnp.bfloat16))


def expert_backward(mixed_low, pre, active, grad_result, up_weight, down_weight):
    grad_act = jnp.einsum(
        "ged,ehd->geh", grad_result, down_weight, preferred_element_type=jnp.float32
    )
    grad_pre = (grad_act * gelu_slope(pre)).astype(jnp.bfloat16)
    grad_down_part = jnp.einsum(
        "geh,ged->ehd", active, grad_result, preferred_element_type=jnp.float32
    )
    grad_up_part = jnp.einsum(
        "ged,geh->edh", mixed_low, grad_pre, preferred_element_type=jnp.float32
    )
    grad_mixed = jnp.einsum("geh,edh->ged", grad_pre, up_weight, preferred_element_type=jnp.float32)
    return (grad_up_part, grad_down_part, grad_mixed.astype(jnp.bfloat16))


def on_device(
    tokens,
    cotangent,
    block_table,
    seg_ids,
    group_ids,
    w_qkv,
    w_out,
    w_router,
    ln_gain,
    ln_bias,
    w_up,
    w_down,
):
    tok_rows = tokens[0]
    tok_count = tok_rows.shape[0]
    width = tok_rows.shape[1]
    expert_count = w_router.shape[1]
    ctx_index = lax.axis_index("ctx")
    full_rows = seg_ids.shape[1]
    block_len = full_rows // block_table.shape[0]
    row_ids = jnp.arange(full_rows, dtype=jnp.int32)
    key_pos = jnp.take(block_table, row_ids // block_len) * block_len + row_ids % block_len
    key_seg = seg_ids[0]
    pos_rows = lax.dynamic_slice_in_dim(key_pos, ctx_index * tok_count, tok_count)
    seg_rows = lax.dynamic_slice_in_dim(key_seg, ctx_index * tok_count, tok_count)
    scale = HEAD ** (-0.5)
    qkv_full, out_full, router_full, gain_full, bias_full = (
        lax.all_gather(w_qkv, "fsdp", axis=0, tiled=True),
        lax.all_gather(w_out, "fsdp", axis=0, tiled=True),
        lax.all_gather(w_router, "fsdp", axis=0, tiled=True),
        lax.all_gather(ln_gain, "fsdp", axis=0, tiled=True),
        lax.all_gather(ln_bias, "fsdp", axis=0, tiled=True),
    )
    qkv = jnp.dot(tok_rows, qkv_full, preferred_element_type=jnp.float32).astype(jnp.bfloat16)
    query_heads = qkv[:, :width].reshape(tok_count, HEADS, HEAD)
    key_all, val_all = (
        lax.all_gather(qkv[:, width : 2 * width], "ctx", axis=0, tiled=True),
        lax.all_gather(qkv[:, 2 * width :], "ctx", axis=0, tiled=True),
    )
    key_heads = key_all.reshape(full_rows, HEADS, HEAD)
    val_heads = val_all.reshape(full_rows, HEADS, HEAD)
    block_count = full_rows // KEY_BLOCK
    block_ids = jnp.arange(block_count, dtype=jnp.int32)

    def block_scores(index):
        start = index * KEY_BLOCK
        key_block = lax.dynamic_slice_in_dim(key_heads, start, KEY_BLOCK, 0)
        val_block = lax.dynamic_slice_in_dim(val_heads, start, KEY_BLOCK, 0)
        pos_block = lax.dynamic_slice_in_dim(key_pos, start, KEY_BLOCK, 0)
        seg_block = lax.dynamic_slice_in_dim(key_seg, start, KEY_BLOCK, 0)
        scores = (
            jnp.einsum("qhd,khd->hqk", query_heads, key_block, preferred_element_type=jnp.float32)
            * scale
        )
        allowed = (pos_block[None, :] <= pos_rows[:, None]) & (
            (seg_block[None, :] == 0) | (seg_block[None, :] == seg_rows[:, None])
        )
        return (scores, allowed[None], key_block, val_block)

    def lse_step(carry, index):
        top, total = carry
        scores, allowed, key_block, val_block = block_scores(index)
        masked = jnp.where(allowed, scores, neg_large)
        new_top = jnp.maximum(top, jnp.max(masked, axis=-1))
        weights = jnp.where(allowed, jnp.exp(masked - new_top[..., None]), 0.0)
        return ((new_top, total * jnp.exp(top - new_top) + jnp.sum(weights, axis=-1)), None)

    start_top = jnp.full((HEADS, tok_count), neg_large, jnp.float32)
    (top, total), unused = lax.scan(
        lse_step, (start_top, jnp.zeros((HEADS, tok_count), jnp.float32)), block_ids
    )
    log_total = top + jnp.log(total)

    def block_probs(index):
        scores, allowed, key_block, val_block = block_scores(index)
        probs = jnp.where(allowed, jnp.exp(scores - log_total[..., None]), 0.0)
        return (probs, key_block, val_block)

    def value_step(accum, index):
        probs, key_block, val_block = block_probs(index)
        return (
            accum
            + jnp.einsum(
                "hqk,khd->qhd",
                probs.astype(jnp.bfloat16),
                val_block,
                preferred_element_type=jnp.float32,
            ),
            None,
        )

    accum, unused = lax.scan(
        value_step, jnp.zeros((tok_count, HEADS, HEAD), jnp.float32), block_ids
    )
    attended = accum.reshape(tok_count, width).astype(jnp.bfloat16)
    hidden = tok_rows.astype(jnp.float32) + jnp.dot(
        attended, out_full, preferred_element_type=jnp.float32
    )
    center = hidden - jnp.mean(hidden, axis=-1, keepdims=True)
    inv_dev = lax.rsqrt(jnp.mean(center * center, axis=-1, keepdims=True) + epsilon)
    unit = center * inv_dev
    gain_f = gain_full.astype(jnp.float32)
    normed_low = (unit * gain_f + bias_full.astype(jnp.float32)).astype(jnp.bfloat16)
    logits = jnp.dot(normed_low, router_full, preferred_element_type=jnp.float32)
    groups_dev = tok_count // GROUP_SIZE
    local_group = group_ids[0] - ctx_index * groups_dev
    member = (local_group[:, None] == jnp.arange(groups_dev, dtype=jnp.int32)[None, :]).astype(
        jnp.float32
    )
    expo = jnp.exp(logits)
    group_total = jnp.dot(member.T, expo, precision=highest)
    mix_weights = expo / jnp.dot(member, group_total, precision=highest)
    weights_low = mix_weights.astype(jnp.bfloat16)
    mixing = member.astype(jnp.bfloat16).T[:, None, :] * weights_low.T[None, :, :]
    mixing_flat = mixing.reshape(groups_dev * expert_count, tok_count)
    mixed_low = jnp.dot(mixing_flat, normed_low, preferred_element_type=jnp.float32).astype(
        jnp.bfloat16
    )
    mixed_low = mixed_low.reshape(groups_dev, expert_count, width)
    owner_mixed = lax.all_to_all(mixed_low, "fsdp", split_axis=1, concat_axis=0, tiled=True)
    pre, active, owner_out = expert_forward(owner_mixed, w_up, w_down)
    expert_out = lax.all_to_all(owner_out, "fsdp", split_axis=0, concat_axis=1, tiled=True)
    expert_flat = expert_out.reshape(groups_dev * expert_count, width)
    spread = contract_rows(mixing_flat, expert_flat)
    layer_out = hidden + spread
    cot_rows = cotangent[0]
    cot_f = cot_rows.astype(jnp.float32)
    grad_expert = jnp.dot(mixing_flat, cot_rows, preferred_element_type=jnp.float32).astype(
        jnp.bfloat16
    )
    grad_expert = grad_expert.reshape(groups_dev, expert_count, width)
    coef = contract_cols(cot_rows, expert_flat).reshape(tok_count, groups_dev, expert_count)
    grad_mix_spread = jnp.sum(coef * member[:, :, None], axis=1)
    owner_grad = lax.all_to_all(grad_expert, "fsdp", split_axis=1, concat_axis=0, tiled=True)
    grad_up_own, grad_down_own, owner_back = expert_backward(
        owner_mixed, pre, active, owner_grad, w_up, w_down
    )
    grad_mixed = lax.all_to_all(owner_back, "fsdp", split_axis=0, concat_axis=1, tiled=True)
    grad_mixed_flat = grad_mixed.reshape(groups_dev * expert_count, width)
    grad_norm_mix = contract_rows(mixing_flat, grad_mixed_flat)
    grad_mixing = contract_cols(grad_mixed_flat, normed_low).reshape(
        groups_dev, expert_count, tok_count
    )
    grad_mix_mixing = jnp.sum(grad_mixing * member.T[:, None, :], axis=0).T
    grad_mix = grad_mix_spread + grad_mix_mixing
    product = mix_weights * grad_mix
    token_dot = jnp.dot(member, jnp.dot(member.T, product, precision=highest), precision=highest)
    grad_logits = (product - mix_weights * token_dot).astype(jnp.bfloat16)
    grad_router_part = contract_rows(normed_low, grad_logits)
    grad_norm_router = contract_cols(grad_logits, router_full)
    grad_normed = grad_norm_mix + grad_norm_router
    grad_gain_part = jnp.sum(grad_normed * unit, axis=0)
    grad_bias_part = jnp.sum(grad_normed, axis=0)
    scaled = grad_normed * gain_f
    grad_hidden = cot_f + inv_dev * (
        scaled
        - jnp.mean(scaled, axis=-1, keepdims=True)
        - unit * jnp.mean(scaled * unit, axis=-1, keepdims=True)
    )
    grad_branch = grad_hidden.astype(jnp.bfloat16)
    grad_out_part = contract_rows(attended, grad_branch)
    grad_heads = (
        contract_cols(grad_branch, out_full).astype(jnp.bfloat16).reshape(tok_count, HEADS, HEAD)
    )
    delta = jnp.sum(grad_heads.astype(jnp.float32) * accum, axis=-1).T

    def grad_step(grad_query, index):
        probs, key_block, val_block = block_probs(index)
        grad_probs = jnp.einsum(
            "qhd,khd->hqk", grad_heads, val_block, preferred_element_type=jnp.float32
        )
        grad_scores = (probs * (grad_probs - delta[..., None])).astype(jnp.bfloat16)
        grad_query = (
            grad_query
            + jnp.einsum("hqk,khd->qhd", grad_scores, key_block, preferred_element_type=jnp.float32)
            * scale
        )
        grad_key = (
            jnp.einsum("hqk,qhd->khd", grad_scores, query_heads, preferred_element_type=jnp.float32)
            * scale
        )
        grad_val = jnp.einsum(
            "hqk,qhd->khd",
            probs.astype(jnp.bfloat16),
            grad_heads,
            preferred_element_type=jnp.float32,
        )
        return (grad_query, (grad_key, grad_val))

    grad_query, (grad_keys, grad_vals) = lax.scan(
        grad_step, jnp.zeros((tok_count, HEADS, HEAD), jnp.float32), block_ids
    )
    grad_key_own, grad_val_own = (
        lax.psum_scatter(
            grad_keys.reshape(full_rows, width), "ctx", scatter_dimension=0, tiled=True
        ),
        lax.psum_scatter(
            grad_vals.reshape(full_rows, width), "ctx", scatter_dimension=0, tiled=True
        ),
    )
    grad_qkv_low = jnp.concatenate(
        [grad_query.reshape(tok_count, width), grad_key_own, grad_val_own], axis=1
    ).astype(jnp.bfloat16)
    grad_qkv_part = contract_rows(tok_rows, grad_qkv_low)
    grad_tokens = grad_hidden + contract_cols(grad_qkv_low, qkv_full)
    dense = (
        lax.psum_scatter(grad_qkv_part, "fsdp", scatter_dimension=0, tiled=True),
        lax.psum_scatter(grad_out_part, "fsdp", scatter_dimension=0, tiled=True),
        lax.psum_scatter(grad_router_part, "fsdp", scatter_dimension=0, tiled=True),
        lax.psum_scatter(grad_gain_part, "fsdp", scatter_dimension=0, tiled=True),
        lax.psum_scatter(grad_bias_part, "fsdp", scatter_dimension=0, tiled=True),
    )
    totals = lax.psum(
        (dense[0], dense[1], dense[2], dense[3], dense[4], grad_up_own, grad_down_own), "ctx"
    )
    return (
        layer_out[None],
        grad_tokens[None],
        totals[0],
        totals[1],
        totals[2],
        totals[3],
        totals[4],
        totals[5],
        totals[6],
    )


LOG2E = 1.4426950408889634
HIDE = -1e30
SUPER = 512
VMEM = pl.BlockSpec(memory_space=pltpu.VMEM)
SMEM = pl.BlockSpec(memory_space=pltpu.SMEM)
ANY = pl.BlockSpec(memory_space=pl.ANY)
LIMIT = 60 << 20


def dot_nn(left, right):
    return lax.dot_general(left, right, (((1,), (0,)), ((), ())), preferred_element_type=jnp.float32)


def dot_nt(left, right):
    return lax.dot_general(left, right, (((1,), (1,)), ((), ())), preferred_element_type=jnp.float32)


def dot_tn(left, right):
    return lax.dot_general(left, right, (((0,), (0,)), ((), ())), preferred_element_type=jnp.float32)


def split3(value):
    one = value.astype(jnp.bfloat16)
    rest = value - one.astype(jnp.float32)
    two = rest.astype(jnp.bfloat16)
    three = (rest - two.astype(jnp.float32)).astype(jnp.bfloat16)
    return one, two, three


def read_order(table_ref, seg_ref, inv_ref, first_ref, last_ref, blocks, block_len, per):
    for t in range(blocks):
        inv_ref[table_ref[t]] = t
    for s in range(blocks // per):
        first_ref[s] = seg_ref[inv_ref[s * per], 0]
        last_ref[s] = seg_ref[inv_ref[s * per + per - 1], block_len - 1]


def count_below(ref, limit, n):
    total = jnp.int32(0)
    for s in range(n):
        total = total + (ref[s] < limit).astype(jnp.int32)
    return total


def fwd_body(blocks, block_len, table_ref, seg_ref, tok_ref, w_ref, segrow_ref, att_ref, qf_ref, kf_ref, vf_ref, kp_ref, stat_ref,
             inv_ref, first_ref, last_ref):
    per = SUPER // block_len
    runs = blocks // per
    read_order(table_ref, seg_ref, inv_ref, first_ref, last_ref, blocks, block_len, per)
    weight = w_ref[...].reshape(w_ref.shape[0] * w_ref.shape[1], w_ref.shape[2])
    factor = HEAD ** (-0.5) * LOG2E
    ids = lax.broadcasted_iota(jnp.int32, (8, 1), 0) + 1
    eye = (lax.broadcasted_iota(jnp.int32, (8, HEAD), 0) == lax.broadcasted_iota(jnp.int32, (8, HEAD), 1)).astype(jnp.bfloat16)
    lane = lax.broadcasted_iota(jnp.int32, (block_len, HEAD), 1)
    ones_k = ((lane >= 8) & (lane < 11)).astype(jnp.float32)
    ones_v = (lane < 3).astype(jnp.bfloat16)

    def project(s, carry):
        t = inv_ref[s]
        rows = tok_ref[pl.ds(pl.multiple_of(t * block_len, block_len), block_len), :]
        qkv = dot_nn(rows, weight).astype(jnp.bfloat16)
        q, k, v = qkv[:, :HEAD], qkv[:, HEAD:2 * HEAD], qkv[:, 2 * HEAD:]
        one, two, three = split3(k.astype(jnp.float32) * factor)
        same = segrow_ref[pl.ds(t, 1), :] == ids
        other = dot_tn(jnp.where(same, 0.0, 1.0).astype(jnp.bfloat16), eye).astype(jnp.bfloat16)
        hidden = (dot_tn(jnp.where(same, HIDE, 0.0).astype(jnp.bfloat16), eye) + ones_k).astype(jnp.bfloat16)
        at = pl.ds(pl.multiple_of(s * block_len, block_len), block_len)
        qf_ref[at, :] = jnp.concatenate([q, q, q, other], axis=1)
        kf_ref[at, :] = jnp.concatenate([one, two, three, hidden], axis=1)
        vf_ref[at, :] = jnp.concatenate([v, ones_v], axis=1)
        kp_ref[at, :] = jnp.concatenate([k, k], axis=1)
        return carry

    lax.fori_loop(0, blocks, project, 0)
    start_hidden = count_below(first_ref, 1, runs)
    row = lax.broadcasted_iota(jnp.int32, (SUPER, SUPER), 0)
    col = lax.broadcasted_iota(jnp.int32, (SUPER, SUPER), 1)
    causal = col <= row

    def query_run(run, carry):
        at_q = pl.ds(pl.multiple_of(run * SUPER, SUPER), SUPER)
        query = qf_ref[at_q, :]
        skip = jnp.maximum(count_below(last_ref, first_ref[run], runs) - start_hidden, 0)

        def tile(index, diagonal, state):
            top, acc = state
            at_k = pl.ds(pl.multiple_of(index * SUPER, SUPER), SUPER)
            scores = dot_nt(query, kf_ref[at_k, :])
            if diagonal:
                scores = jnp.where(causal, scores, HIDE)
            new_top = jnp.maximum(top, jnp.max(scores, axis=1, keepdims=True))
            weights = jnp.exp2(scores - new_top)
            acc = acc * jnp.exp2(top - new_top) + dot_nn(weights.astype(jnp.bfloat16), vf_ref[at_k, :])
            return new_top, acc

        def step(n, state):
            return tile(jnp.where(n < start_hidden, n, n + skip), False, state)

        state = (jnp.full((SUPER, 1), HIDE, jnp.float32), jnp.zeros((SUPER, 2 * HEAD), jnp.float32))
        state = lax.fori_loop(0, run - skip, step, state)
        top, acc = tile(run, True, state)
        total = acc[:, HEAD:HEAD + 1]
        lse = top + jnp.log2(total)
        out = acc[:, :HEAD] / total
        stat_ref[at_q, :] = jnp.concatenate([out, jnp.broadcast_to(lse, (SUPER, HEAD))], axis=1)
        return carry

    lax.fori_loop(0, runs, query_run, 0)
    for c in range(blocks // 2):
        parts = []
        for half in range(2):
            s = table_ref[2 * c + half]
            parts.append(stat_ref[pl.ds(pl.multiple_of(s * block_len, block_len), block_len), :HEAD])
        att_ref[c] = jnp.concatenate(parts, axis=1).astype(jnp.bfloat16)


def attn_fwd(tokens_all, weight, table, segs):
    rows = tokens_all.shape[0]
    blocks, block_len = segs.shape
    runs = rows // SUPER
    return pl.pallas_call(
        functools.partial(fwd_body, blocks, block_len),
        out_shape=(
            jax.ShapeDtypeStruct((blocks // 2, block_len, 2 * HEAD), jnp.bfloat16),
            jax.ShapeDtypeStruct((rows, 4 * HEAD), jnp.bfloat16),
            jax.ShapeDtypeStruct((rows, 4 * HEAD), jnp.bfloat16),
            jax.ShapeDtypeStruct((rows, 2 * HEAD), jnp.bfloat16),
            jax.ShapeDtypeStruct((rows, 2 * HEAD), jnp.bfloat16),
            jax.ShapeDtypeStruct((rows, 2 * HEAD), jnp.float32),
        ),
        in_specs=[SMEM, SMEM, VMEM, VMEM, VMEM],
        out_specs=(VMEM,) * 6,
        scratch_shapes=[pltpu.SMEM((blocks,), jnp.int32), pltpu.SMEM((runs,), jnp.int32), pltpu.SMEM((runs,), jnp.int32)],
        compiler_params=pltpu.CompilerParams(vmem_limit_bytes=LIMIT),
        cost_estimate=cost(35),
        name="attention",
    )(table, segs, tokens_all, weight, segs)


def bwd_body(blocks, block_len, table_ref, seg_ref, do_ref, qf_ref, kf_ref, vf_ref, kp_ref, stat_ref, out_ref,
             inv_ref, first_ref, last_ref, qs_ref, dof_ref, dq_ref, dk_ref, dv_ref):
    per = SUPER // block_len
    runs = blocks // per
    read_order(table_ref, seg_ref, inv_ref, first_ref, last_ref, blocks, block_len, per)
    lane = lax.broadcasted_iota(jnp.int32, (block_len, HEAD), 1)
    zero = jnp.zeros((), jnp.bfloat16)

    def spread(value, offset):
        one, two, three = (jnp.broadcast_to(part, (block_len, HEAD)) for part in split3(value))
        out = jnp.where(lane == offset, one, zero)
        out = jnp.where(lane == offset + 1, two, out)
        return jnp.where(lane == offset + 2, three, out)

    def prepare(s, carry):
        t = inv_ref[s]
        at = pl.ds(pl.multiple_of(s * block_len, block_len), block_len)
        both = do_ref[t // 2]
        grad = jnp.where(t % 2 == 0, both[:, :HEAD], both[:, HEAD:])
        stat = stat_ref[at, :]
        delta = jnp.sum(grad.astype(jnp.float32) * stat[:, :HEAD], axis=1, keepdims=True)
        dof_ref[at, :] = jnp.concatenate([grad, spread(-delta, 0)], axis=1)
        old = qf_ref[at, :]
        tail = jnp.where(lane < 8, old[:, 3 * HEAD:], spread(-stat[:, HEAD:HEAD + 1], 8))
        qs_ref[at, :] = jnp.concatenate([old[:, :3 * HEAD], tail], axis=1)
        dq_ref[at, :] = jnp.zeros((block_len, 2 * HEAD), jnp.float32)
        return carry

    lax.fori_loop(0, blocks, prepare, 0)
    causal = lax.broadcasted_iota(jnp.int32, (SUPER, SUPER), 0) <= lax.broadcasted_iota(jnp.int32, (SUPER, SUPER), 1)

    def key_run(run, carry):
        at_k = pl.ds(pl.multiple_of(run * SUPER, SUPER), SUPER)
        end = jnp.where(first_ref[run] == 0, runs, count_below(first_ref, last_ref[run] + 1, runs))

        def tile(index, diagonal):
            at_q = pl.ds(pl.multiple_of(index * SUPER, SUPER), SUPER)
            scores = dot_nt(kf_ref[at_k, :], qs_ref[at_q, :])
            probs = jnp.exp2(scores)
            if diagonal:
                probs = jnp.where(causal, probs, 0.0)
            slope = dot_nt(vf_ref[at_k, :], dof_ref[at_q, :])
            grad = (probs * slope).astype(jnp.bfloat16)
            dv = dot_nn(probs.astype(jnp.bfloat16), dof_ref[at_q, :])
            dk = dot_nn(grad, qs_ref[at_q, :2 * HEAD])
            if diagonal:
                dv_ref[...] = dv
                dk_ref[...] = dk
            else:
                dv_ref[...] += dv
                dk_ref[...] += dk
            dq_ref[at_q, :] += dot_tn(grad, kp_ref[at_k, :])

        tile(run, True)

        def step(index, inner):
            tile(index, False)
            return inner

        lax.fori_loop(run + 1, end, step, 0)
        scale = HEAD ** (-0.5)
        stat_dk = (dk_ref[:, :HEAD] * scale).astype(jnp.bfloat16)
        stat_dv = dv_ref[:, :HEAD].astype(jnp.bfloat16)
        stat_dq = (dq_ref[at_k, :HEAD] * scale).astype(jnp.bfloat16)
        for part in range(per):
            t = inv_ref[run * per + part]
            rows = slice(part * block_len, (part + 1) * block_len)
            pieces = (stat_dq[rows], stat_dk[rows], stat_dv[rows])
            for parity in range(2):
                @pl.when(t % 2 == parity)
                def _():
                    for kind in range(3):
                        low = kind * 2 * HEAD + parity * HEAD
                        out_ref[t // 2, :, low:low + HEAD] = pieces[kind]
        return carry

    lax.fori_loop(0, runs, key_run, 0)


def attn_bwd(grad, saved, table, segs):
    blocks, block_len = segs.shape
    rows = blocks * block_len
    runs = rows // SUPER
    return pl.pallas_call(
        functools.partial(bwd_body, blocks, block_len),
        out_shape=jax.ShapeDtypeStruct((blocks // 2, block_len, 6 * HEAD), jnp.bfloat16),
        in_specs=[SMEM, SMEM] + [VMEM] * 6,
        out_specs=VMEM,
        scratch_shapes=[
            pltpu.SMEM((blocks,), jnp.int32), pltpu.SMEM((runs,), jnp.int32), pltpu.SMEM((runs,), jnp.int32),
            pltpu.VMEM((rows, 4 * HEAD), jnp.bfloat16), pltpu.VMEM((rows, 2 * HEAD), jnp.bfloat16),
            pltpu.VMEM((rows, 2 * HEAD), jnp.float32), pltpu.VMEM((SUPER, 2 * HEAD), jnp.float32),
            pltpu.VMEM((SUPER, 2 * HEAD), jnp.float32),
        ],
        compiler_params=pltpu.CompilerParams(vmem_limit_bytes=LIMIT),
        cost_estimate=cost(40),
        name="attention_grad",
    )(table, segs, grad, *saved)


MESH = pl.DeviceIdType.MESH


def cost(microseconds):
    return pl.CostEstimate(flops=int(microseconds * 1.15e9), bytes_accessed=1 << 20, transcendentals=0)


def flip(index, bit):
    return index + bit - 2 * bit * lax.rem(index // bit, 2)


def meet(devices):
    barrier = pltpu.get_barrier_semaphore()
    for device in devices:
        pl.semaphore_signal(barrier, inc=1, device_id=device, device_id_type=MESH)
    pl.semaphore_wait(barrier, len(devices))


def push(src, dst, send_sem, recv_sem, device):
    return pltpu.make_async_remote_copy(
        src_ref=src, dst_ref=dst, send_sem=send_sem, recv_sem=recv_sem, device_id=device, device_id_type=MESH
    )


def exchange_body(axis, count, x_ref, out_ref, own_sem, send_sem, recv_sem):
    spot = {"ctx": lax.axis_index("ctx"), "fsdp": lax.axis_index("fsdp")}
    me = spot[axis]
    others = [lax.rem(me + k, count) for k in range(1, count)]
    meet([(other, spot["fsdp"]) if axis == "ctx" else (spot["ctx"], other) for other in others])
    own = pltpu.make_async_copy(x_ref.at[me], out_ref.at[me], own_sem)
    own.start()
    copies = []
    for k, other in enumerate(others):
        device = (other, spot["fsdp"]) if axis == "ctx" else (spot["ctx"], other)
        copies.append(push(x_ref.at[other], out_ref.at[me], send_sem.at[k], recv_sem.at[k], device))
        copies[-1].start()
    own.wait()
    for copy in copies:
        copy.wait()


def exchange(x, axis, collective_id, name):
    count = x.shape[0]
    return pl.pallas_call(
        functools.partial(exchange_body, axis, count),
        out_shape=jax.ShapeDtypeStruct(x.shape, x.dtype),
        in_specs=[ANY],
        out_specs=ANY,
        scratch_shapes=[pltpu.SemaphoreType.DMA, pltpu.SemaphoreType.DMA((count - 1,)), pltpu.SemaphoreType.DMA((count - 1,))],
        compiler_params=pltpu.CompilerParams(collective_id=collective_id, has_side_effects=True),
        cost_estimate=cost(9),
        name=name,
    )(x)


def gather_body(zs, tok_ref, *refs):
    count = (len(refs) - 9) // 2
    shards, toks_ref, wholes = refs[:count], refs[count], refs[count + 1:2 * count + 1]
    own_sem, z_send, z_recv, far_send, near_send, own_recv, diag_recv, near_recv = refs[2 * count + 1:]
    me, z = lax.axis_index("ctx"), lax.axis_index("fsdp")
    sib, xn, yn, diag = flip(me, 1), flip(me, 2), flip(me, 4), flip(flip(me, 2), 4)
    z_peers = [lax.rem(z + k, zs) for k in range(1, zs)]
    meet([(sib, z), (xn, z), (yn, z)] + [(me, other) for other in z_peers])
    half = tok_ref.shape[0] // 2

    def part(device, k):
        return toks_ref.at[device, pl.ds(k * half, half)]

    started = []

    def go(copy):
        copy.start()
        started.append(copy)

    for k in (0, 1):
        rows = tok_ref.at[pl.ds(k * half, half)]
        go(push(rows, part(me, k), far_send.at[0, k], own_recv.at[0, k], (xn, z)))
        rows = tok_ref.at[pl.ds((1 - k) * half, half)]
        go(push(rows, part(me, 1 - k), far_send.at[1, 1 - k], own_recv.at[1, 1 - k], (yn, z)))
    for i, (shard, whole) in enumerate(zip(shards, wholes)):
        for k, other in enumerate(z_peers):
            go(push(shard, whole.at[z], z_send.at[i, k], z_recv.at[i, k], (me, other)))
    for k in (0, 1):
        rows = tok_ref.at[pl.ds(k * half, half)]
        go(push(rows, part(me, k), near_send.at[0, k], near_recv.at[0, k], (sib, z)))
    locals_ = [pltpu.make_async_copy(tok_ref, toks_ref.at[me], own_sem.at[0])]
    for i, (shard, whole) in enumerate(zip(shards, wholes)):
        locals_.append(pltpu.make_async_copy(shard, whole.at[z], own_sem.at[i + 1]))
    for copy in locals_:
        copy.start()

    def arrived(device, k, sem):
        push(part(device, k), part(device, k), far_send.at[0, 0], sem, (sib, z)).wait_recv()

    def relay(device, k, i):
        go(push(part(device, k), part(device, k), near_send.at[i, k], near_recv.at[i, k], (sib, z)))

    arrived(xn, 0, own_recv.at[0, 0])
    go(push(part(xn, 0), part(xn, 0), far_send.at[2, 0], diag_recv.at[0], (yn, z)))
    relay(xn, 0, 1)
    arrived(yn, 1, own_recv.at[1, 1])
    go(push(part(yn, 1), part(yn, 1), far_send.at[2, 1], diag_recv.at[1], (xn, z)))
    relay(yn, 1, 2)
    arrived(xn, 1, own_recv.at[0, 1])
    relay(xn, 1, 1)
    arrived(yn, 0, own_recv.at[1, 0])
    relay(yn, 0, 2)
    for k in (0, 1):
        arrived(diag, k, diag_recv.at[k])
        relay(diag, k, 3)
    for k in (0, 1):
        for i, device in enumerate((sib, flip(xn, 1), flip(yn, 1), flip(diag, 1))):
            arrived(device, k, near_recv.at[i, k])
    for i, whole in enumerate(wholes):
        for k in range(zs - 1):
            other = lax.rem(z + zs - 1 - k, zs)
            push(whole.at[other], whole.at[other], z_send.at[i, k], z_recv.at[i, k], (me, other)).wait_recv()
    for copy in locals_:
        copy.wait()
    for copy in started:
        copy.wait_send()


def gather(tokens, shards, ctx_count, z_count):
    outs = [jax.ShapeDtypeStruct((ctx_count,) + tokens.shape, tokens.dtype)]
    outs += [jax.ShapeDtypeStruct((z_count,) + shard.shape, shard.dtype) for shard in shards]
    dma = pltpu.SemaphoreType.DMA
    return pl.pallas_call(
        functools.partial(gather_body, z_count),
        out_shape=outs,
        in_specs=[ANY] * (1 + len(shards)),
        out_specs=[ANY] * (1 + len(shards)),
        scratch_shapes=[
            dma((1 + len(shards),)), dma((len(shards), z_count - 1)), dma((len(shards), z_count - 1)), dma((3, 2)), dma((4, 2)),
            dma((2, 2)), dma((2,)), dma((4, 2)),
        ],
        compiler_params=pltpu.CompilerParams(collective_id=1, has_side_effects=True),
        cost_estimate=cost(24),
        name="gather_tokens",
    )(tokens, *shards)


def norm_parts(hidden):
    center = hidden - jnp.mean(hidden, axis=-1, keepdims=True)
    inv_dev = lax.rsqrt(jnp.mean(center * center, axis=-1, keepdims=True) + epsilon)
    return center * inv_dev, inv_dev


def small_rows(pack_ref):
    return jnp.concatenate([pack_ref[z] for z in range(pack_ref.shape[0])], axis=1)


def mix_body(experts, groups, att_ref, tok_ref, cot_ref, wo_ref, pack_ref, gid_ref, hidden_ref, normed_ref, mix_ref, attended_ref, send_ref):
    heads = att_ref.shape[0]
    halves = [jnp.concatenate([att_ref[h, :, HEAD * p:HEAD * (p + 1)] for h in range(heads)], axis=1) for p in range(2)]
    attended = jnp.concatenate(halves, axis=0)
    attended_ref[...] = attended
    width = tok_ref.shape[1]
    hidden = tok_ref[...].astype(jnp.float32) + dot_nn(attended, wo_ref[...].reshape(width, width))
    hidden_ref[...] = hidden
    unit, inv_dev = norm_parts(hidden)
    small = small_rows(pack_ref)
    gain, bias = small[experts:experts + 1].astype(jnp.float32), small[experts + 1:experts + 2].astype(jnp.float32)
    normed = (unit * gain + bias).astype(jnp.bfloat16)
    normed_ref[...] = normed
    expo = jnp.exp(dot_nt(small, normed)[:experts])
    rows = tok_ref.shape[0]
    expo = jnp.broadcast_to(expo[:, None, :], (experts, groups, rows)).reshape(experts * groups, rows)
    member = lax.rem(lax.broadcasted_iota(jnp.int32, (experts * groups, 1), 0), groups) == lax.rem(gid_ref[...], groups)
    expo = jnp.where(member, expo, 0.0)
    mix = expo / jnp.sum(expo, axis=1, keepdims=True)
    mix_ref[...] = mix
    low = mix.astype(jnp.bfloat16)
    owners = send_ref.shape[0]
    per = experts * groups // owners
    send_ref[:, 0] = dot_nn(low, normed).astype(jnp.bfloat16).reshape(owners, per, width)
    send_ref[:, 1] = dot_nn(low, cot_ref[...]).astype(jnp.bfloat16).reshape(owners, per, width)


def mix_tokens(att, tokens, cot, w_out, pack, gid_row, experts, groups, owners):
    rows, width = tokens.shape
    return pl.pallas_call(
        functools.partial(mix_body, experts, groups),
        out_shape=(
            jax.ShapeDtypeStruct((rows, width), jnp.float32),
            jax.ShapeDtypeStruct((rows, width), jnp.bfloat16),
            jax.ShapeDtypeStruct((experts * groups, rows), jnp.float32),
            jax.ShapeDtypeStruct((rows, width), jnp.bfloat16),
            jax.ShapeDtypeStruct((owners, 2, experts * groups // owners, width), jnp.bfloat16),
        ),
        in_specs=[VMEM] * 6,
        out_specs=(VMEM,) * 5,
        compiler_params=pltpu.CompilerParams(vmem_limit_bytes=LIMIT),
        cost_estimate=cost(4),
        name="mix_tokens",
    )(att, tokens, cot, w_out, pack, gid_row)


def expert_body(groups, got_ref, up_ref, down_ref, back_ref, out_acc, grad_acc):
    own, part = pl.program_id(0), pl.program_id(1)
    at = pl.ds(pl.multiple_of(own * groups, groups), groups)
    sources, width = got_ref.shape[0], got_ref.shape[3]
    mixed = got_ref[:, 0, at, :].reshape(sources * groups, width)
    grad_out = got_ref[:, 1, at, :].reshape(sources * groups, width)
    up, down = up_ref[0], down_ref[0]
    pre = dot_nn(mixed, up)
    active = jax.nn.gelu(pre, approximate=True).astype(jnp.bfloat16)
    grad_pre = (dot_nt(grad_out, down) * gelu_slope(pre)).astype(jnp.bfloat16)
    out, grad = dot_nn(active, down), dot_nt(grad_pre, up)

    @pl.when(part == 0)
    def _():
        out_acc[...] = out
        grad_acc[...] = grad

    @pl.when(part != 0)
    def _():
        out_acc[...] += out
        grad_acc[...] += grad

    @pl.when(part == pl.num_programs(1) - 1)
    def _():
        back_ref[:, 0, at, :] = out_acc[...].astype(jnp.bfloat16).reshape(sources, groups, width)
        back_ref[:, 1, at, :] = grad_acc[...].astype(jnp.bfloat16).reshape(sources, groups, width)


def run_experts(got, w_up, w_down, groups):
    own, width, ffn = w_up.shape
    step = 1024
    rows = got.shape[0] * groups
    return pl.pallas_call(
        functools.partial(expert_body, groups),
        grid=(own, ffn // step),
        out_shape=jax.ShapeDtypeStruct(got.shape, jnp.bfloat16),
        in_specs=[
            pl.BlockSpec(got.shape, lambda e, f: (0, 0, 0, 0)),
            pl.BlockSpec((1, width, step), lambda e, f: (e, 0, f)),
            pl.BlockSpec((1, step, width), lambda e, f: (e, f, 0)),
        ],
        out_specs=pl.BlockSpec(got.shape, lambda e, f: (0, 0, 0, 0)),
        scratch_shapes=[pltpu.VMEM((rows, width), jnp.float32)] * 2,
        compiler_params=pltpu.CompilerParams(vmem_limit_bytes=LIMIT),
        cost_estimate=cost(8),
        name="experts",
    )(got, w_up, w_down)


def unmix_body(experts, groups, heads, hidden_ref, normed_ref, mix_ref, attended_ref, cot_ref, wo_ref, pack_ref, back_ref,
               layer_ref, ghidden_ref, rows_ref, ghead_ref):
    rows, width = hidden_ref.shape
    hidden, normed, mix, cot = hidden_ref[...], normed_ref[...], mix_ref[...], cot_ref[...]
    low = mix.astype(jnp.bfloat16)
    flat = experts * groups
    expert_out, grad_mixed = back_ref[:, 0].reshape(flat, width), back_ref[:, 1].reshape(flat, width)
    layer_ref[...] = hidden + dot_tn(low, expert_out)
    product = mix * (dot_nt(expert_out, cot) + dot_nt(grad_mixed, normed))
    grad_logits = product - mix * jnp.sum(product, axis=1, keepdims=True)
    grad_logits = jnp.sum(grad_logits.reshape(experts, groups, rows), axis=1).astype(jnp.bfloat16)
    small = small_rows(pack_ref)
    pad = jnp.zeros((small.shape[0] - experts, rows), jnp.bfloat16)
    grad_logits = jnp.concatenate([grad_logits, pad], axis=0)
    grad_normed = dot_tn(jnp.concatenate([low, grad_logits], axis=0), jnp.concatenate([grad_mixed, small], axis=0))
    gain = small[experts:experts + 1].astype(jnp.float32)
    unit, inv_dev = norm_parts(hidden)
    small_grad = jnp.concatenate(
        [
            dot_nn(grad_logits, normed)[:experts],
            jnp.sum(grad_normed * unit, axis=0, keepdims=True),
            jnp.sum(grad_normed, axis=0, keepdims=True),
            jnp.zeros((small.shape[0] - experts - 2, width), jnp.float32),
        ],
        axis=0,
    )
    scaled = grad_normed * gain
    mean = jnp.mean(scaled, axis=-1, keepdims=True)
    grad_hidden = cot.astype(jnp.float32) + inv_dev * (scaled - mean - unit * jnp.mean(scaled * unit, axis=-1, keepdims=True))
    ghidden_ref[...] = grad_hidden
    branch = grad_hidden.astype(jnp.bfloat16)
    gout = dot_tn(attended_ref[...], branch)
    owners, count = pack_ref.shape[0], rows_ref.shape[0]
    own = width // (owners * count)
    for c in range(count):
        for z in range(owners):
            low = (z * count + c) * own
            rows_ref[c, z * own:(z + 1) * own, :] = gout[low:low + own]
        rows_ref[c, owners * own:, :] = jnp.zeros((16, width), jnp.float32)
        rows_ref[c, owners * own:owners * own + 2, :] = small_grad[2 * c:2 * c + 2]
    grad_heads = dot_nt(branch, wo_ref[...].reshape(width, width)).astype(jnp.bfloat16)
    half = rows // 2
    for h in range(heads):
        at = slice(HEAD * h, HEAD * (h + 1))
        ghead_ref[h] = jnp.concatenate([grad_heads[:half, at], grad_heads[half:, at]], axis=1)


def unmix_tokens(hidden, normed, mix, attended, cot, w_out, pack, back, experts, groups, heads):
    rows, width = hidden.shape
    return pl.pallas_call(
        functools.partial(unmix_body, experts, groups, heads),
        out_shape=(
            jax.ShapeDtypeStruct((rows, width), jnp.float32),
            jax.ShapeDtypeStruct((rows, width), jnp.float32),
            jax.ShapeDtypeStruct((heads, width // heads + 16, width), jnp.float32),
            jax.ShapeDtypeStruct((heads, rows // 2, 2 * HEAD), jnp.bfloat16),
        ),
        in_specs=[VMEM] * 8,
        out_specs=(VMEM,) * 4,
        compiler_params=pltpu.CompilerParams(vmem_limit_bytes=LIMIT),
        cost_estimate=cost(5),
        name="unmix_tokens",
    )(hidden, normed, mix, attended, cot, w_out, pack, back)


def head_columns(ref, p, index=None):
    columns = []
    for kind in range(3):
        at = slice(HEAD * (2 * kind + p), HEAD * (2 * kind + p + 1))
        columns.append(ref[index, :, at])
    return jnp.concatenate(columns, axis=1)


def closing_body(
    owners, grads_ref, toks_ref, rows_ref, weight_ref, ghidden_ref, gathered_ref, up_ref, down_ref,
    gtok_ref, gq_ref, gout_ref, small_ref, act_ref, gpre_ref,
    held_grads, held_toks, held_rows, held_weight, held_hidden, held_mixed, held_up, held_down, act_buf, gpre_buf,
    landing, zsend, zone, total_ref, all_ref,
    load_sem, store_sem, a_send, a_recv, z_send, z_recv, c_send, c_recv,
):
    me, z = lax.axis_index("ctx"), lax.axis_index("fsdp")
    count, half = grads_ref.shape[0], grads_ref.shape[1]
    width = toks_ref.shape[2]
    own_experts, ffn = up_ref.shape[0], up_ref.shape[2]
    pairs = [
        (grads_ref, held_grads), (toks_ref, held_toks), (rows_ref, held_rows), (gathered_ref, held_mixed), (up_ref, held_up),
        (down_ref, held_down), (weight_ref, held_weight), (ghidden_ref, held_hidden),
    ]
    loads = [pltpu.make_async_copy(src, dst, load_sem.at[i]) for i, (src, dst) in enumerate(pairs)]
    for copy in loads:
        copy.start()
    z_peers = [(me, lax.rem(z + k, owners)) for k in range(1, owners)]
    c_peers = [(jnp.bitwise_xor(me, k), z) for k in range(1, count)]
    meet(z_peers + c_peers)
    swaps = []
    for k, device in enumerate(c_peers):
        swaps.append(push(grads_ref.at[device[0]], landing.at[me], a_send.at[k], a_recv.at[k], device))
        swaps[-1].start()
    own_swap = pltpu.make_async_copy(grads_ref.at[me], landing.at[me], store_sem.at[0])
    own_swap.start()

    loads[0].wait()
    loads[1].wait()
    total = None
    for device in range(count):
        for p in range(2):
            part = dot_tn(head_columns(held_grads, p, device), held_toks[device, p * half:(p + 1) * half, :])
            total = part if total is None else total + part
    loads[2].wait()
    lanes = width // owners
    small = held_rows.shape[0] - 16
    own = small // owners
    for c in range(owners):
        at = slice(c * lanes, (c + 1) * lanes)
        zsend[c, :3 * HEAD, :] = total[:, at].astype(jnp.bfloat16)
        zsend[c, 3 * HEAD:3 * HEAD + 16, :] = held_rows[small:, at].astype(jnp.bfloat16)
        for j in range(width // lanes):
            low = 3 * HEAD + 16 + own * j
            zsend[c, low:low + own, :] = held_rows[own * c:own * (c + 1), lanes * j:lanes * (j + 1)].astype(jnp.bfloat16)
    z_copies = []
    for k, device in enumerate(z_peers):
        z_copies.append(push(zsend.at[device[1]], zone.at[z], z_send.at[k], z_recv.at[k], device))
        z_copies[-1].start()
    zone[z] = zsend[z]
    for i in (3, 4, 5):
        loads[i].wait()

    step = 512

    def expert_part(own_expert):
        mixed = held_mixed[:, 0, own_expert].reshape(-1, width)
        grad_out = held_mixed[:, 1, own_expert].reshape(-1, width)

        def chunk(i, carry):
            at = pl.ds(pl.multiple_of(i * step, step), step)
            pre = dot_nn(mixed, held_up[own_expert, :, at])
            act_buf[own_expert, :, at] = jax.nn.gelu(pre, approximate=True).astype(jnp.bfloat16)
            slope = dot_nt(grad_out, held_down[own_expert, at, :])
            gpre_buf[own_expert, :, at] = (slope * gelu_slope(pre)).astype(jnp.bfloat16)
            return carry

        lax.fori_loop(0, ffn // step, chunk, 0)
        stores = [
            pltpu.make_async_copy(act_buf.at[own_expert], act_ref.at[own_expert], store_sem.at[1 + 2 * own_expert]),
            pltpu.make_async_copy(gpre_buf.at[own_expert], gpre_ref.at[own_expert], store_sem.at[2 + 2 * own_expert]),
        ]
        for copy in stores:
            copy.start()
        return stores

    stores = expert_part(0)
    for copy in z_copies:
        copy.wait()
    total = zone[0].astype(jnp.float32)
    for k in range(1, owners):
        total = total + zone[k].astype(jnp.float32)
    total_ref[...] = total.astype(jnp.bfloat16)
    c_copies = []
    for k, device in enumerate(c_peers):
        c_copies.append(push(total_ref, all_ref.at[me], c_send.at[k], c_recv.at[k], device))
        c_copies[-1].start()
    all_ref[me] = total_ref[...]
    for own_expert in range(1, own_experts):
        stores += expert_part(own_expert)
    loads[6].wait()
    loads[7].wait()
    own_swap.wait()
    for copy in swaps:
        copy.wait()
    for p in range(2):
        columns = [landing[h, :, HEAD * (2 * kind + p):HEAD * (2 * kind + p + 1)] for kind in range(3) for h in range(count)]
        at = slice(p * half, (p + 1) * half)
        gtok_ref[at, :] = held_hidden[at, :] + dot_nt(jnp.concatenate(columns, axis=1), held_weight[...])
    for copy in c_copies:
        copy.wait()
    per = lanes // count
    smalls = []
    turned = []
    for c in range(count):
        turned.append(all_ref[c, :3 * HEAD, :].astype(jnp.float32).T)
        smalls.append(all_ref[c, 3 * HEAD:3 * HEAD + 16, :].astype(jnp.float32)[:2])
        for j in range(width // lanes):
            low = 3 * HEAD + 16 + per * j
            gout_ref[per * c:per * (c + 1), lanes * j:lanes * (j + 1)] = all_ref[c, low:low + per, :].astype(jnp.float32)
    for kind in range(3):
        at = slice(HEAD * kind, HEAD * (kind + 1))
        gq_ref[:, HEAD * count * kind:HEAD * count * (kind + 1)] = jnp.concatenate([part[:, at] for part in turned], axis=1)
    small_ref[...] = jnp.concatenate(smalls, axis=0)
    for copy in stores:
        copy.wait()


def closing(grads, tokens_all, rows, weight, ghidden, gathered, w_up, w_down, groups, owners):
    count, width = tokens_all.shape[0], tokens_all.shape[2]
    lanes = width // owners
    own = (rows.shape[0] - 16) // owners
    height = 3 * HEAD + 16 + own * (width // lanes)
    own_experts, _, ffn = w_up.shape
    sources = gathered.shape[0]
    view = gathered.reshape(sources, 2, own_experts, groups, width)
    wide = (own_experts, sources * groups, ffn)
    dma = pltpu.SemaphoreType.DMA
    held = [grads, tokens_all, rows, weight, ghidden, view, w_up, w_down]
    return pl.pallas_call(
        functools.partial(closing_body, owners),
        out_shape=(
            jax.ShapeDtypeStruct(ghidden.shape, jnp.float32),
            jax.ShapeDtypeStruct((lanes, 3 * width), jnp.float32),
            jax.ShapeDtypeStruct((lanes, width), jnp.float32),
            jax.ShapeDtypeStruct((2 * count, lanes), jnp.float32),
            jax.ShapeDtypeStruct(wide, jnp.bfloat16),
            jax.ShapeDtypeStruct(wide, jnp.bfloat16),
        ),
        in_specs=[ANY] * 8,
        out_specs=(VMEM,) * 4 + (ANY,) * 2,
        scratch_shapes=[pltpu.VMEM(x.shape, x.dtype) for x in held] + [
            pltpu.VMEM(wide, jnp.bfloat16), pltpu.VMEM(wide, jnp.bfloat16), pltpu.VMEM(grads.shape, jnp.bfloat16),
            pltpu.VMEM((owners, height, lanes), jnp.bfloat16), pltpu.VMEM((owners, height, lanes), jnp.bfloat16),
            pltpu.VMEM((height, lanes), jnp.bfloat16), pltpu.VMEM((count, height, lanes), jnp.bfloat16),
            dma((8,)), dma((1 + 2 * own_experts,)), dma((count - 1,)), dma((count - 1,)), dma((owners - 1,)), dma((owners - 1,)),
            dma((count - 1,)), dma((count - 1,)),
        ],
        compiler_params=pltpu.CompilerParams(collective_id=6, has_side_effects=True, vmem_limit_bytes=LIMIT),
        cost_estimate=cost(24),
        name="closing",
    )(*held)


def expert_grad_body(mixed_ref, grad_ref, act_ref, gpre_ref, gup_ref, gdown_ref):
    width = gup_ref.shape[1]
    gup_ref[0] = dot_tn(mixed_ref[...].reshape(-1, width), gpre_ref[0])
    gdown_ref[0] = dot_tn(act_ref[0], grad_ref[...].reshape(-1, width))


def expert_grads(gathered, active, grad_pre, groups):
    own, rows, ffn = active.shape
    step = 512
    sources, width = gathered.shape[0], gathered.shape[3]
    view = gathered.reshape(sources, 2, own, groups, width)
    return pl.pallas_call(
        expert_grad_body,
        grid=(own, ffn // step),
        out_shape=(jax.ShapeDtypeStruct((own, width, ffn), jnp.float32), jax.ShapeDtypeStruct((own, ffn, width), jnp.float32)),
        in_specs=[
            pl.BlockSpec((sources, 1, 1, groups, width), lambda e, f: (0, 0, e, 0, 0)),
            pl.BlockSpec((sources, 1, 1, groups, width), lambda e, f: (0, 1, e, 0, 0)),
            pl.BlockSpec((1, rows, step), lambda e, f: (e, 0, f)),
            pl.BlockSpec((1, rows, step), lambda e, f: (e, 0, f)),
        ],
        out_specs=(pl.BlockSpec((1, width, step), lambda e, f: (e, 0, f)), pl.BlockSpec((1, step, width), lambda e, f: (e, f, 0))),
        compiler_params=pltpu.CompilerParams(vmem_limit_bytes=LIMIT),
        cost_estimate=cost(8),
        name="expert_grads",
    )(view, view, active, grad_pre)


def fast_device(
    tokens, cotangent, block_table, seg_ids, group_ids, w_qkv, w_out, w_router, ln_gain, ln_bias, w_up, w_down
):
    ctx_count, z_count = lax.axis_size("ctx"), lax.axis_size("fsdp")
    ctx_index = lax.axis_index("ctx")
    tok_rows, cot_rows = tokens[0], cotangent[0]
    rows, width = tok_rows.shape
    experts = w_router.shape[1]
    groups = rows // GROUP_SIZE
    shard = w_qkv.shape[0]
    segs = seg_ids[0].reshape(block_table.shape[0], -1)
    head_cols = lax.dynamic_slice_in_dim(w_qkv.reshape(shard, 3, ctx_count, HEAD), ctx_index, 1, 2).reshape(shard, 3 * HEAD)
    pack = jnp.concatenate(
        [w_router.T, ln_gain[None], ln_bias[None], jnp.zeros((16 - experts - 2, shard), jnp.bfloat16)], axis=0
    )
    tokens_all, head_weights, out_full, pack_full = gather(tok_rows, [head_cols, w_out, pack], ctx_count, z_count)
    qkv_full = lax.all_gather(w_qkv, "fsdp", axis=0, tiled=True)
    att, *saved = attn_fwd(tokens_all.reshape(ctx_count * rows, width), head_weights, block_table, segs)
    att = exchange(att, "ctx", 2, "exchange_attended")
    hidden, normed, mix, attended, mixed = mix_tokens(
        att, tok_rows, cot_rows, out_full, pack_full, group_ids, experts, groups, z_count
    )
    got = exchange(mixed, "fsdp", 3, "exchange_mixed")
    back = exchange(run_experts(got, w_up, w_down, groups), "fsdp", 4, "exchange_back")
    gathered = lax.all_gather(got, "ctx", axis=0, tiled=True)
    layer_out, grad_hidden, part_rows, grad_heads = unmix_tokens(
        hidden, normed, mix, attended, cot_rows, out_full, pack_full, back, experts, groups, ctx_count
    )
    grad_heads = exchange(grad_heads, "ctx", 5, "exchange_grad")
    sum_rows = lax.psum_scatter(part_rows.reshape(-1, width), "ctx", scatter_dimension=0, tiled=True)
    grads = attn_bwd(grad_heads, saved, block_table, segs)
    grad_tokens, grad_qkv, grad_out, small, active, grad_pre = closing(
        grads, tokens_all, sum_rows, qkv_full, grad_hidden, gathered, w_up, w_down, groups, z_count
    )
    grad_up, grad_down = expert_grads(gathered, active, grad_pre, groups)
    return (
        layer_out[None],
        grad_tokens[None],
        grad_qkv,
        grad_out,
        small[:experts].T,
        small[experts],
        small[experts + 1],
        grad_up,
        grad_down,
    )


def solution(mesh):
    placed = (
        P("fsdp", "ctx", None),
        P("fsdp", "ctx", None),
        P(),
        P("fsdp", None),
        P("fsdp", "ctx"),
        P("fsdp", None),
        P("fsdp", None),
        P("fsdp", None),
        P("fsdp"),
        P("fsdp"),
        P("fsdp", None, None),
        P("fsdp", None, None),
    )
    step = fast_device if mesh.shape["ctx"] == HEADS else on_device
    return jax.shard_map(
        step,
        mesh=mesh,
        in_specs=placed,
        out_specs=(
            P("fsdp", "ctx", None),
            P("fsdp", "ctx", None),
            P("fsdp", None),
            P("fsdp", None),
            P("fsdp", None),
            P("fsdp"),
            P("fsdp"),
            P("fsdp", None, None),
            P("fsdp", None, None),
        ),
        check_vma=False,
    )
```

```python
import functools

import jax
import jax.numpy as jnp
from jax import lax
from jax.experimental import pallas as pl
from jax.experimental.pallas import tpu as pltpu
from jax.sharding import PartitionSpec as P

HEADS = 8
HEAD = 64
GROUP_SIZE = 32
KEY_BLOCK = 2048


highest = lax.Precision.HIGHEST
neg_large = -1e30
epsilon = 1e-05
gelu_coef = 0.7978845608028654
gelu_cubic = 0.044715


def contract_rows(left, right):
    return lax.dot_general(
        left, right, (((0,), (0,)), ((), ())), preferred_element_type=jnp.float32
    )


def contract_cols(left, right):
    return lax.dot_general(
        left, right, (((1,), (1,)), ((), ())), preferred_element_type=jnp.float32
    )


def gelu_slope(value):
    inner = gelu_coef * (value + gelu_cubic * value * value * value)
    tangent = jnp.tanh(inner)
    return 0.5 * (1.0 + tangent) + 0.5 * value * (1.0 - tangent * tangent) * gelu_coef * (
        1.0 + 3.0 * gelu_cubic * value * value
    )


def expert_forward(mixed_low, up_weight, down_weight):
    pre = jnp.einsum("ged,edh->geh", mixed_low, up_weight, preferred_element_type=jnp.float32)
    active = jax.nn.gelu(pre, approximate=True).astype(jnp.bfloat16)
    result = jnp.einsum("geh,ehd->ged", active, down_weight, preferred_element_type=jnp.float32)
    return (pre, active, result.astype(jnp.bfloat16))


def expert_backward(mixed_low, pre, active, grad_result, up_weight, down_weight):
    grad_act = jnp.einsum(
        "ged,ehd->geh", grad_result, down_weight, preferred_element_type=jnp.float32
    )
    grad_pre = (grad_act * gelu_slope(pre)).astype(jnp.bfloat16)
    grad_down_part = jnp.einsum(
        "geh,ged->ehd", active, grad_result, preferred_element_type=jnp.float32
    )
    grad_up_part = jnp.einsum(
        "ged,geh->edh", mixed_low, grad_pre, preferred_element_type=jnp.float32
    )
    grad_mixed = jnp.einsum("geh,edh->ged", grad_pre, up_weight, preferred_element_type=jnp.float32)
    return (grad_up_part, grad_down_part, grad_mixed.astype(jnp.bfloat16))


def on_device(
    tokens,
    cotangent,
    block_table,
    seg_ids,
    group_ids,
    w_qkv,
    w_out,
    w_router,
    ln_gain,
    ln_bias,
    w_up,
    w_down,
):
    tok_rows = tokens[0]
    tok_count = tok_rows.shape[0]
    width = tok_rows.shape[1]
    expert_count = w_router.shape[1]
    ctx_index = lax.axis_index("ctx")
    full_rows = seg_ids.shape[1]
    block_len = full_rows // block_table.shape[0]
    row_ids = jnp.arange(full_rows, dtype=jnp.int32)
    key_pos = jnp.take(block_table, row_ids // block_len) * block_len + row_ids % block_len
    key_seg = seg_ids[0]
    pos_rows = lax.dynamic_slice_in_dim(key_pos, ctx_index * tok_count, tok_count)
    seg_rows = lax.dynamic_slice_in_dim(key_seg, ctx_index * tok_count, tok_count)
    scale = HEAD ** (-0.5)
    qkv_full, out_full, router_full, gain_full, bias_full = (
        lax.all_gather(w_qkv, "fsdp", axis=0, tiled=True),
        lax.all_gather(w_out, "fsdp", axis=0, tiled=True),
        lax.all_gather(w_router, "fsdp", axis=0, tiled=True),
        lax.all_gather(ln_gain, "fsdp", axis=0, tiled=True),
        lax.all_gather(ln_bias, "fsdp", axis=0, tiled=True),
    )
    qkv = jnp.dot(tok_rows, qkv_full, preferred_element_type=jnp.float32).astype(jnp.bfloat16)
    query_heads = qkv[:, :width].reshape(tok_count, HEADS, HEAD)
    key_all, val_all = (
        lax.all_gather(qkv[:, width : 2 * width], "ctx", axis=0, tiled=True),
        lax.all_gather(qkv[:, 2 * width :], "ctx", axis=0, tiled=True),
    )
    key_heads = key_all.reshape(full_rows, HEADS, HEAD)
    val_heads = val_all.reshape(full_rows, HEADS, HEAD)
    block_count = full_rows // KEY_BLOCK
    block_ids = jnp.arange(block_count, dtype=jnp.int32)

    def block_scores(index):
        start = index * KEY_BLOCK
        key_block = lax.dynamic_slice_in_dim(key_heads, start, KEY_BLOCK, 0)
        val_block = lax.dynamic_slice_in_dim(val_heads, start, KEY_BLOCK, 0)
        pos_block = lax.dynamic_slice_in_dim(key_pos, start, KEY_BLOCK, 0)
        seg_block = lax.dynamic_slice_in_dim(key_seg, start, KEY_BLOCK, 0)
        scores = (
            jnp.einsum("qhd,khd->hqk", query_heads, key_block, preferred_element_type=jnp.float32)
            * scale
        )
        allowed = (pos_block[None, :] <= pos_rows[:, None]) & (
            (seg_block[None, :] == 0) | (seg_block[None, :] == seg_rows[:, None])
        )
        return (scores, allowed[None], key_block, val_block)

    def lse_step(carry, index):
        top, total = carry
        scores, allowed, key_block, val_block = block_scores(index)
        masked = jnp.where(allowed, scores, neg_large)
        new_top = jnp.maximum(top, jnp.max(masked, axis=-1))
        weights = jnp.where(allowed, jnp.exp(masked - new_top[..., None]), 0.0)
        return ((new_top, total * jnp.exp(top - new_top) + jnp.sum(weights, axis=-1)), None)

    start_top = jnp.full((HEADS, tok_count), neg_large, jnp.float32)
    (top, total), unused = lax.scan(
        lse_step, (start_top, jnp.zeros((HEADS, tok_count), jnp.float32)), block_ids
    )
    log_total = top + jnp.log(total)

    def block_probs(index):
        scores, allowed, key_block, val_block = block_scores(index)
        probs = jnp.where(allowed, jnp.exp(scores - log_total[..., None]), 0.0)
        return (probs, key_block, val_block)

    def value_step(accum, index):
        probs, key_block, val_block = block_probs(index)
        return (
            accum
            + jnp.einsum(
                "hqk,khd->qhd",
                probs.astype(jnp.bfloat16),
                val_block,
                preferred_element_type=jnp.float32,
            ),
            None,
        )

    accum, unused = lax.scan(
        value_step, jnp.zeros((tok_count, HEADS, HEAD), jnp.float32), block_ids
    )
    attended = accum.reshape(tok_count, width).astype(jnp.bfloat16)
    hidden = tok_rows.astype(jnp.float32) + jnp.dot(
        attended, out_full, preferred_element_type=jnp.float32
    )
    center = hidden - jnp.mean(hidden, axis=-1, keepdims=True)
    inv_dev = lax.rsqrt(jnp.mean(center * center, axis=-1, keepdims=True) + epsilon)
    unit = center * inv_dev
    gain_f = gain_full.astype(jnp.float32)
    normed_low = (unit * gain_f + bias_full.astype(jnp.float32)).astype(jnp.bfloat16)
    logits = jnp.dot(normed_low, router_full, preferred_element_type=jnp.float32)
    groups_dev = tok_count // GROUP_SIZE
    local_group = group_ids[0] - ctx_index * groups_dev
    member = (local_group[:, None] == jnp.arange(groups_dev, dtype=jnp.int32)[None, :]).astype(
        jnp.float32
    )
    expo = jnp.exp(logits)
    group_total = jnp.dot(member.T, expo, precision=highest)
    mix_weights = expo / jnp.dot(member, group_total, precision=highest)
    weights_low = mix_weights.astype(jnp.bfloat16)
    mixing = member.astype(jnp.bfloat16).T[:, None, :] * weights_low.T[None, :, :]
    mixing_flat = mixing.reshape(groups_dev * expert_count, tok_count)
    mixed_low = jnp.dot(mixing_flat, normed_low, preferred_element_type=jnp.float32).astype(
        jnp.bfloat16
    )
    mixed_low = mixed_low.reshape(groups_dev, expert_count, width)
    owner_mixed = lax.all_to_all(mixed_low, "fsdp", split_axis=1, concat_axis=0, tiled=True)
    pre, active, owner_out = expert_forward(owner_mixed, w_up, w_down)
    expert_out = lax.all_to_all(owner_out, "fsdp", split_axis=0, concat_axis=1, tiled=True)
    expert_flat = expert_out.reshape(groups_dev * expert_count, width)
    spread = contract_rows(mixing_flat, expert_flat)
    layer_out = hidden + spread
    cot_rows = cotangent[0]
    cot_f = cot_rows.astype(jnp.float32)
    grad_expert = jnp.dot(mixing_flat, cot_rows, preferred_element_type=jnp.float32).astype(
        jnp.bfloat16
    )
    grad_expert = grad_expert.reshape(groups_dev, expert_count, width)
    coef = contract_cols(cot_rows, expert_flat).reshape(tok_count, groups_dev, expert_count)
    grad_mix_spread = jnp.sum(coef * member[:, :, None], axis=1)
    owner_grad = lax.all_to_all(grad_expert, "fsdp", split_axis=1, concat_axis=0, tiled=True)
    grad_up_own, grad_down_own, owner_back = expert_backward(
        owner_mixed, pre, active, owner_grad, w_up, w_down
    )
    grad_mixed = lax.all_to_all(owner_back, "fsdp", split_axis=0, concat_axis=1, tiled=True)
    grad_mixed_flat = grad_mixed.reshape(groups_dev * expert_count, width)
    grad_norm_mix = contract_rows(mixing_flat, grad_mixed_flat)
    grad_mixing = contract_cols(grad_mixed_flat, normed_low).reshape(
        groups_dev, expert_count, tok_count
    )
    grad_mix_mixing = jnp.sum(grad_mixing * member.T[:, None, :], axis=0).T
    grad_mix = grad_mix_spread + grad_mix_mixing
    product = mix_weights * grad_mix
    token_dot = jnp.dot(member, jnp.dot(member.T, product, precision=highest), precision=highest)
    grad_logits = (product - mix_weights * token_dot).astype(jnp.bfloat16)
    grad_router_part = contract_rows(normed_low, grad_logits)
    grad_norm_router = contract_cols(grad_logits, router_full)
    grad_normed = grad_norm_mix + grad_norm_router
    grad_gain_part = jnp.sum(grad_normed * unit, axis=0)
    grad_bias_part = jnp.sum(grad_normed, axis=0)
    scaled = grad_normed * gain_f
    grad_hidden = cot_f + inv_dev * (
        scaled
        - jnp.mean(scaled, axis=-1, keepdims=True)
        - unit * jnp.mean(scaled * unit, axis=-1, keepdims=True)
    )
    grad_branch = grad_hidden.astype(jnp.bfloat16)
    grad_out_part = contract_rows(attended, grad_branch)
    grad_heads = (
        contract_cols(grad_branch, out_full).astype(jnp.bfloat16).reshape(tok_count, HEADS, HEAD)
    )
    delta = jnp.sum(grad_heads.astype(jnp.float32) * accum, axis=-1).T

    def grad_step(grad_query, index):
        probs, key_block, val_block = block_probs(index)
        grad_probs = jnp.einsum(
            "qhd,khd->hqk", grad_heads, val_block, preferred_element_type=jnp.float32
        )
        grad_scores = (probs * (grad_probs - delta[..., None])).astype(jnp.bfloat16)
        grad_query = (
            grad_query
            + jnp.einsum("hqk,khd->qhd", grad_scores, key_block, preferred_element_type=jnp.float32)
            * scale
        )
        grad_key = (
            jnp.einsum("hqk,qhd->khd", grad_scores, query_heads, preferred_element_type=jnp.float32)
            * scale
        )
        grad_val = jnp.einsum(
            "hqk,qhd->khd",
            probs.astype(jnp.bfloat16),
            grad_heads,
            preferred_element_type=jnp.float32,
        )
        return (grad_query, (grad_key, grad_val))

    grad_query, (grad_keys, grad_vals) = lax.scan(
        grad_step, jnp.zeros((tok_count, HEADS, HEAD), jnp.float32), block_ids
    )
    grad_key_own, grad_val_own = (
        lax.psum_scatter(
            grad_keys.reshape(full_rows, width), "ctx", scatter_dimension=0, tiled=True
        ),
        lax.psum_scatter(
            grad_vals.reshape(full_rows, width), "ctx", scatter_dimension=0, tiled=True
        ),
    )
    grad_qkv_low = jnp.concatenate(
        [grad_query.reshape(tok_count, width), grad_key_own, grad_val_own], axis=1
    ).astype(jnp.bfloat16)
    grad_qkv_part = contract_rows(tok_rows, grad_qkv_low)
    grad_tokens = grad_hidden + contract_cols(grad_qkv_low, qkv_full)
    dense = (
        lax.psum_scatter(grad_qkv_part, "fsdp", scatter_dimension=0, tiled=True),
        lax.psum_scatter(grad_out_part, "fsdp", scatter_dimension=0, tiled=True),
        lax.psum_scatter(grad_router_part, "fsdp", scatter_dimension=0, tiled=True),
        lax.psum_scatter(grad_gain_part, "fsdp", scatter_dimension=0, tiled=True),
        lax.psum_scatter(grad_bias_part, "fsdp", scatter_dimension=0, tiled=True),
    )
    totals = lax.psum(
        (dense[0], dense[1], dense[2], dense[3], dense[4], grad_up_own, grad_down_own), "ctx"
    )
    return (
        layer_out[None],
        grad_tokens[None],
        totals[0],
        totals[1],
        totals[2],
        totals[3],
        totals[4],
        totals[5],
        totals[6],
    )


LOG2E = 1.4426950408889634
HIDE = -1e30
SUPER = 512
VMEM = pl.BlockSpec(memory_space=pltpu.VMEM)
SMEM = pl.BlockSpec(memory_space=pltpu.SMEM)
ANY = pl.BlockSpec(memory_space=pl.ANY)
LIMIT = 60 << 20


def dot_nn(left, right):
    return lax.dot_general(left, right, (((1,), (0,)), ((), ())), preferred_element_type=jnp.float32)


def dot_nt(left, right):
    return lax.dot_general(left, right, (((1,), (1,)), ((), ())), preferred_element_type=jnp.float32)


def dot_tn(left, right):
    return lax.dot_general(left, right, (((0,), (0,)), ((), ())), preferred_element_type=jnp.float32)


def split3(value):
    one = value.astype(jnp.bfloat16)
    rest = value - one.astype(jnp.float32)
    two = rest.astype(jnp.bfloat16)
    three = (rest - two.astype(jnp.float32)).astype(jnp.bfloat16)
    return one, two, three


def read_order(table_ref, seg_ref, inv_ref, first_ref, last_ref, blocks, block_len, per):
    for t in range(blocks):
        inv_ref[table_ref[t]] = t
    for s in range(blocks // per):
        first_ref[s] = seg_ref[inv_ref[s * per], 0]
        last_ref[s] = seg_ref[inv_ref[s * per + per - 1], block_len - 1]


def count_below(ref, limit, n):
    total = jnp.int32(0)
    for s in range(n):
        total = total + (ref[s] < limit).astype(jnp.int32)
    return total


def fwd_body(blocks, block_len, table_ref, seg_ref, tok_ref, w_ref, segrow_ref, att_ref, qf_ref, kf_ref, vf_ref, kp_ref, stat_ref,
             inv_ref, first_ref, last_ref):
    per = SUPER // block_len
    runs = blocks // per
    read_order(table_ref, seg_ref, inv_ref, first_ref, last_ref, blocks, block_len, per)
    weight = w_ref[...].reshape(w_ref.shape[0] * w_ref.shape[1], w_ref.shape[2])
    factor = HEAD ** (-0.5) * LOG2E
    ids = lax.broadcasted_iota(jnp.int32, (8, 1), 0) + 1
    eye = (lax.broadcasted_iota(jnp.int32, (8, HEAD), 0) == lax.broadcasted_iota(jnp.int32, (8, HEAD), 1)).astype(jnp.bfloat16)
    lane = lax.broadcasted_iota(jnp.int32, (block_len, HEAD), 1)
    ones_k = ((lane >= 8) & (lane < 11)).astype(jnp.float32)
    ones_v = (lane < 3).astype(jnp.bfloat16)

    def project(s, carry):
        t = inv_ref[s]
        rows = tok_ref[pl.ds(pl.multiple_of(t * block_len, block_len), block_len), :]
        qkv = dot_nn(rows, weight).astype(jnp.bfloat16)
        q, k, v = qkv[:, :HEAD], qkv[:, HEAD:2 * HEAD], qkv[:, 2 * HEAD:]
        one, two, three = split3(k.astype(jnp.float32) * factor)
        same = segrow_ref[pl.ds(t, 1), :] == ids
        other = dot_tn(jnp.where(same, 0.0, 1.0).astype(jnp.bfloat16), eye).astype(jnp.bfloat16)
        hidden = (dot_tn(jnp.where(same, HIDE, 0.0).astype(jnp.bfloat16), eye) + ones_k).astype(jnp.bfloat16)
        at = pl.ds(pl.multiple_of(s * block_len, block_len), block_len)
        qf_ref[at, :] = jnp.concatenate([q, q, q, other], axis=1)
        kf_ref[at, :] = jnp.concatenate([one, two, three, hidden], axis=1)
        vf_ref[at, :] = jnp.concatenate([v, ones_v], axis=1)
        kp_ref[at, :] = jnp.concatenate([k, k], axis=1)
        return carry

    lax.fori_loop(0, blocks, project, 0)
    start_hidden = count_below(first_ref, 1, runs)
    row = lax.broadcasted_iota(jnp.int32, (SUPER, SUPER), 0)
    col = lax.broadcasted_iota(jnp.int32, (SUPER, SUPER), 1)
    causal = col <= row

    def query_run(run, carry):
        at_q = pl.ds(pl.multiple_of(run * SUPER, SUPER), SUPER)
        query = qf_ref[at_q, :]
        skip = jnp.maximum(count_below(last_ref, first_ref[run], runs) - start_hidden, 0)

        def tile(index, diagonal, state):
            top, acc = state
            at_k = pl.ds(pl.multiple_of(index * SUPER, SUPER), SUPER)
            scores = dot_nt(query, kf_ref[at_k, :])
            if diagonal:
                scores = jnp.where(causal, scores, HIDE)
            new_top = jnp.maximum(top, jnp.max(scores, axis=1, keepdims=True))
            weights = jnp.exp2(scores - new_top)
            acc = acc * jnp.exp2(top - new_top) + dot_nn(weights.astype(jnp.bfloat16), vf_ref[at_k, :])
            return new_top, acc

        def step(n, state):
            return tile(jnp.where(n < start_hidden, n, n + skip), False, state)

        state = (jnp.full((SUPER, 1), HIDE, jnp.float32), jnp.zeros((SUPER, 2 * HEAD), jnp.float32))
        state = lax.fori_loop(0, run - skip, step, state)
        top, acc = tile(run, True, state)
        total = acc[:, HEAD:HEAD + 1]
        lse = top + jnp.log2(total)
        out = acc[:, :HEAD] / total
        stat_ref[at_q, :] = jnp.concatenate([out, jnp.broadcast_to(lse, (SUPER, HEAD))], axis=1)
        return carry

    lax.fori_loop(0, runs, query_run, 0)
    for c in range(blocks // 2):
        parts = []
        for half in range(2):
            s = table_ref[2 * c + half]
            parts.append(stat_ref[pl.ds(pl.multiple_of(s * block_len, block_len), block_len), :HEAD])
        att_ref[c] = jnp.concatenate(parts, axis=1).astype(jnp.bfloat16)


def attn_fwd(tokens_all, weight, table, segs):
    rows = tokens_all.shape[0]
    blocks, block_len = segs.shape
    runs = rows // SUPER
    return pl.pallas_call(
        functools.partial(fwd_body, blocks, block_len),
        out_shape=(
            jax.ShapeDtypeStruct((blocks // 2, block_len, 2 * HEAD), jnp.bfloat16),
            jax.ShapeDtypeStruct((rows, 4 * HEAD), jnp.bfloat16),
            jax.ShapeDtypeStruct((rows, 4 * HEAD), jnp.bfloat16),
            jax.ShapeDtypeStruct((rows, 2 * HEAD), jnp.bfloat16),
            jax.ShapeDtypeStruct((rows, 2 * HEAD), jnp.bfloat16),
            jax.ShapeDtypeStruct((rows, 2 * HEAD), jnp.float32),
        ),
        in_specs=[SMEM, SMEM, VMEM, VMEM, VMEM],
        out_specs=(VMEM,) * 6,
        scratch_shapes=[pltpu.SMEM((blocks,), jnp.int32), pltpu.SMEM((runs,), jnp.int32), pltpu.SMEM((runs,), jnp.int32)],
        compiler_params=pltpu.CompilerParams(vmem_limit_bytes=LIMIT),
        cost_estimate=cost(35),
        name="attention",
    )(table, segs, tokens_all, weight, segs)


def bwd_body(blocks, block_len, table_ref, seg_ref, do_ref, qf_ref, kf_ref, vf_ref, kp_ref, stat_ref, out_ref,
             inv_ref, first_ref, last_ref, qs_ref, dof_ref, dq_ref, dk_ref, dv_ref):
    per = SUPER // block_len
    runs = blocks // per
    read_order(table_ref, seg_ref, inv_ref, first_ref, last_ref, blocks, block_len, per)
    lane = lax.broadcasted_iota(jnp.int32, (block_len, HEAD), 1)
    zero = jnp.zeros((), jnp.bfloat16)

    def spread(value, offset):
        one, two, three = (jnp.broadcast_to(part, (block_len, HEAD)) for part in split3(value))
        out = jnp.where(lane == offset, one, zero)
        out = jnp.where(lane == offset + 1, two, out)
        return jnp.where(lane == offset + 2, three, out)

    def prepare(s, carry):
        t = inv_ref[s]
        at = pl.ds(pl.multiple_of(s * block_len, block_len), block_len)
        both = do_ref[t // 2]
        grad = jnp.where(t % 2 == 0, both[:, :HEAD], both[:, HEAD:])
        stat = stat_ref[at, :]
        delta = jnp.sum(grad.astype(jnp.float32) * stat[:, :HEAD], axis=1, keepdims=True)
        dof_ref[at, :] = jnp.concatenate([grad, spread(-delta, 0)], axis=1)
        old = qf_ref[at, :]
        tail = jnp.where(lane < 8, old[:, 3 * HEAD:], spread(-stat[:, HEAD:HEAD + 1], 8))
        qs_ref[at, :] = jnp.concatenate([old[:, :3 * HEAD], tail], axis=1)
        dq_ref[at, :] = jnp.zeros((block_len, 2 * HEAD), jnp.float32)
        return carry

    lax.fori_loop(0, blocks, prepare, 0)
    causal = lax.broadcasted_iota(jnp.int32, (SUPER, SUPER), 0) <= lax.broadcasted_iota(jnp.int32, (SUPER, SUPER), 1)

    def key_run(run, carry):
        at_k = pl.ds(pl.multiple_of(run * SUPER, SUPER), SUPER)
        end = jnp.where(first_ref[run] == 0, runs, count_below(first_ref, last_ref[run] + 1, runs))

        def tile(index, diagonal):
            at_q = pl.ds(pl.multiple_of(index * SUPER, SUPER), SUPER)
            scores = dot_nt(kf_ref[at_k, :], qs_ref[at_q, :])
            probs = jnp.exp2(scores)
            if diagonal:
                probs = jnp.where(causal, probs, 0.0)
            slope = dot_nt(vf_ref[at_k, :], dof_ref[at_q, :])
            grad = (probs * slope).astype(jnp.bfloat16)
            dv = dot_nn(probs.astype(jnp.bfloat16), dof_ref[at_q, :])
            dk = dot_nn(grad, qs_ref[at_q, :2 * HEAD])
            if diagonal:
                dv_ref[...] = dv
                dk_ref[...] = dk
            else:
                dv_ref[...] += dv
                dk_ref[...] += dk
            dq_ref[at_q, :] += dot_tn(grad, kp_ref[at_k, :])

        tile(run, True)

        def step(index, inner):
            tile(index, False)
            return inner

        lax.fori_loop(run + 1, end, step, 0)
        scale = HEAD ** (-0.5)
        stat_dk = (dk_ref[:, :HEAD] * scale).astype(jnp.bfloat16)
        stat_dv = dv_ref[:, :HEAD].astype(jnp.bfloat16)
        stat_dq = (dq_ref[at_k, :HEAD] * scale).astype(jnp.bfloat16)
        for part in range(per):
            t = inv_ref[run * per + part]
            rows = slice(part * block_len, (part + 1) * block_len)
            pieces = (stat_dq[rows], stat_dk[rows], stat_dv[rows])
            for parity in range(2):
                @pl.when(t % 2 == parity)
                def _():
                    for kind in range(3):
                        low = kind * 2 * HEAD + parity * HEAD
                        out_ref[t // 2, :, low:low + HEAD] = pieces[kind]
        return carry

    lax.fori_loop(0, runs, key_run, 0)


def attn_bwd(grad, saved, table, segs):
    blocks, block_len = segs.shape
    rows = blocks * block_len
    runs = rows // SUPER
    return pl.pallas_call(
        functools.partial(bwd_body, blocks, block_len),
        out_shape=jax.ShapeDtypeStruct((blocks // 2, block_len, 6 * HEAD), jnp.bfloat16),
        in_specs=[SMEM, SMEM] + [VMEM] * 6,
        out_specs=VMEM,
        scratch_shapes=[
            pltpu.SMEM((blocks,), jnp.int32), pltpu.SMEM((runs,), jnp.int32), pltpu.SMEM((runs,), jnp.int32),
            pltpu.VMEM((rows, 4 * HEAD), jnp.bfloat16), pltpu.VMEM((rows, 2 * HEAD), jnp.bfloat16),
            pltpu.VMEM((rows, 2 * HEAD), jnp.float32), pltpu.VMEM((SUPER, 2 * HEAD), jnp.float32),
            pltpu.VMEM((SUPER, 2 * HEAD), jnp.float32),
        ],
        compiler_params=pltpu.CompilerParams(vmem_limit_bytes=LIMIT),
        cost_estimate=cost(40),
        name="attention_grad",
    )(table, segs, grad, *saved)


MESH = pl.DeviceIdType.MESH


def cost(microseconds):
    return pl.CostEstimate(flops=int(microseconds * 1.15e9), bytes_accessed=1 << 20, transcendentals=0)


def flip(index, bit):
    return index + bit - 2 * bit * lax.rem(index // bit, 2)


def meet(devices):
    barrier = pltpu.get_barrier_semaphore()
    for device in devices:
        pl.semaphore_signal(barrier, inc=1, device_id=device, device_id_type=MESH)
    pl.semaphore_wait(barrier, len(devices))


def push(src, dst, send_sem, recv_sem, device):
    return pltpu.make_async_remote_copy(
        src_ref=src, dst_ref=dst, send_sem=send_sem, recv_sem=recv_sem, device_id=device, device_id_type=MESH
    )


def gather_body(zs, tok_ref, *refs):
    count = (len(refs) - 9) // 2
    shards, toks_ref, wholes = refs[:count], refs[count], refs[count + 1:2 * count + 1]
    own_sem, z_send, z_recv, far_send, near_send, own_recv, diag_recv, near_recv = refs[2 * count + 1:]
    me, z = lax.axis_index("ctx"), lax.axis_index("fsdp")
    sib, xn, yn, diag = flip(me, 1), flip(me, 2), flip(me, 4), flip(flip(me, 2), 4)
    z_peers = [lax.rem(z + k, zs) for k in range(1, zs)]
    meet([(sib, z), (xn, z), (yn, z)] + [(me, other) for other in z_peers])
    half = tok_ref.shape[0] // 2

    def part(device, k):
        return toks_ref.at[device, pl.ds(k * half, half)]

    started = []

    def go(copy):
        copy.start()
        started.append(copy)

    for k in (0, 1):
        rows = tok_ref.at[pl.ds(k * half, half)]
        go(push(rows, part(me, k), far_send.at[0, k], own_recv.at[0, k], (xn, z)))
        rows = tok_ref.at[pl.ds((1 - k) * half, half)]
        go(push(rows, part(me, 1 - k), far_send.at[1, 1 - k], own_recv.at[1, 1 - k], (yn, z)))
    for i, (shard, whole) in enumerate(zip(shards, wholes)):
        for k, other in enumerate(z_peers):
            go(push(shard, whole.at[z], z_send.at[i, k], z_recv.at[i, k], (me, other)))
    for k in (0, 1):
        rows = tok_ref.at[pl.ds(k * half, half)]
        go(push(rows, part(me, k), near_send.at[0, k], near_recv.at[0, k], (sib, z)))
    locals_ = [pltpu.make_async_copy(tok_ref, toks_ref.at[me], own_sem.at[0])]
    for i, (shard, whole) in enumerate(zip(shards, wholes)):
        locals_.append(pltpu.make_async_copy(shard, whole.at[z], own_sem.at[i + 1]))
    for copy in locals_:
        copy.start()

    def arrived(device, k, sem):
        push(part(device, k), part(device, k), far_send.at[0, 0], sem, (sib, z)).wait_recv()

    def relay(device, k, i):
        go(push(part(device, k), part(device, k), near_send.at[i, k], near_recv.at[i, k], (sib, z)))

    arrived(xn, 0, own_recv.at[0, 0])
    go(push(part(xn, 0), part(xn, 0), far_send.at[2, 0], diag_recv.at[0], (yn, z)))
    relay(xn, 0, 1)
    arrived(yn, 1, own_recv.at[1, 1])
    go(push(part(yn, 1), part(yn, 1), far_send.at[2, 1], diag_recv.at[1], (xn, z)))
    relay(yn, 1, 2)
    arrived(xn, 1, own_recv.at[0, 1])
    relay(xn, 1, 1)
    arrived(yn, 0, own_recv.at[1, 0])
    relay(yn, 0, 2)
    for k in (0, 1):
        arrived(diag, k, diag_recv.at[k])
        relay(diag, k, 3)
    for k in (0, 1):
        for i, device in enumerate((sib, flip(xn, 1), flip(yn, 1), flip(diag, 1))):
            arrived(device, k, near_recv.at[i, k])
    for i, whole in enumerate(wholes):
        for k in range(zs - 1):
            other = lax.rem(z + zs - 1 - k, zs)
            push(whole.at[other], whole.at[other], z_send.at[i, k], z_recv.at[i, k], (me, other)).wait_recv()
    for copy in locals_:
        copy.wait()
    for copy in started:
        copy.wait_send()


def gather(tokens, shards, ctx_count, z_count):
    outs = [jax.ShapeDtypeStruct((ctx_count,) + tokens.shape, tokens.dtype)]
    outs += [jax.ShapeDtypeStruct((z_count,) + shard.shape, shard.dtype) for shard in shards]
    dma = pltpu.SemaphoreType.DMA
    return pl.pallas_call(
        functools.partial(gather_body, z_count),
        out_shape=outs,
        in_specs=[ANY] * (1 + len(shards)),
        out_specs=[ANY] * (1 + len(shards)),
        scratch_shapes=[
            dma((1 + len(shards),)), dma((len(shards), z_count - 1)), dma((len(shards), z_count - 1)), dma((3, 2)), dma((4, 2)),
            dma((2, 2)), dma((2,)), dma((4, 2)),
        ],
        compiler_params=pltpu.CompilerParams(collective_id=1, has_side_effects=True),
        cost_estimate=cost(24),
        name="gather_tokens",
    )(tokens, *shards)


def norm_parts(hidden):
    center = hidden - jnp.mean(hidden, axis=-1, keepdims=True)
    inv_dev = lax.rsqrt(jnp.mean(center * center, axis=-1, keepdims=True) + epsilon)
    return center * inv_dev, inv_dev


def middle_body(
    experts, groups, att_ref, tok_ref, cot_ref, wo_ref, pack_ref, gid_ref, up_ref, down_ref, later_ref,
    layer_ref, ghidden_ref, gout_ref, small_ref, all_ref, ghead_ref,
    tok, cot, wo, pack, up, down, att, zsend, zin, bsend, bin_, ghead,
    load_sem, own_sem, a_send, a_recv, m_send, m_recv, b_send, b_recv, g_send, g_recv, r_send, r_recv, h_send, h_recv,
):
    me, z = lax.axis_index("ctx"), lax.axis_index("fsdp")
    count, half = att_ref.shape[0], att_ref.shape[1]
    rows, width = tok_ref.shape
    owners, own_experts = zsend.shape[0], up_ref.shape[0]
    flat, per = experts * groups, experts * groups // owners
    pairs = [(tok_ref, tok), (wo_ref, wo), (pack_ref, pack), (cot_ref, cot)]
    for e in range(own_experts):
        pairs += [(up_ref.at[e], up.at[e]), (down_ref.at[e], down.at[e])]
    loads = [pltpu.make_async_copy(src, dst, load_sem.at[i]) for i, (src, dst) in enumerate(pairs)]
    for copy in loads:
        copy.start()
    sib, same_core = flip(me, 1), [flip(me, 2), flip(me, 4), flip(flip(me, 2), 4)]
    z_peers = [(me, lax.rem(z + k, owners)) for k in range(1, owners)]
    c_peers = [(jnp.bitwise_xor(me, k), z) for k in range(1, count)]
    meet(z_peers + c_peers)

    def start(copies):
        for copy in copies:
            copy.start()
        return copies

    def wait(copies):
        for copy in copies:
            copy.wait()

    swap = start([push(att_ref.at[d[0]], att.at[me], a_send.at[k], a_recv.at[k], d) for k, d in enumerate(c_peers)])
    own = start([pltpu.make_async_copy(att_ref.at[me], att.at[me], own_sem.at[0])])
    small_in = None
    wait(own + swap)
    wait(loads[:4])
    halves = [jnp.concatenate([att[h, :, HEAD * p:HEAD * (p + 1)] for h in range(count)], axis=1) for p in range(2)]
    attended = jnp.concatenate(halves, axis=0)
    weight = wo[...].reshape(width, width)
    hidden = tok[...].astype(jnp.float32) + dot_nn(attended, weight)
    unit, inv_dev = norm_parts(hidden)
    small_in = jnp.concatenate([pack[k] for k in range(owners)], axis=1)
    gain, bias = small_in[experts:experts + 1].astype(jnp.float32), small_in[experts + 1:experts + 2].astype(jnp.float32)
    normed = (unit * gain + bias).astype(jnp.bfloat16)
    expo = jnp.exp(dot_nt(small_in, normed)[:experts])
    expo = jnp.broadcast_to(expo[:, None, :], (experts, groups, rows)).reshape(flat, rows)
    member = lax.rem(lax.broadcasted_iota(jnp.int32, (flat, 1), 0), groups) == lax.rem(gid_ref[...], groups)
    expo = jnp.where(member, expo, 0.0)
    mix = expo / jnp.sum(expo, axis=1, keepdims=True)
    low = mix.astype(jnp.bfloat16)

    def to_owners(kind, value):
        zsend[:, kind] = value.astype(jnp.bfloat16).reshape(owners, per, width)
        zin[z, kind] = zsend[z, kind]
        return start([
            push(zsend.at[d[1], kind], zin.at[z, kind], m_send.at[kind, k], m_recv.at[kind, k], d) for k, d in enumerate(z_peers)
        ])

    mixed_copies = to_owners(0, dot_nn(low, normed))
    grad_copies = to_owners(1, dot_nn(low, cot[...]))
    wait(loads[4:])
    wait(mixed_copies)

    def from_sources(kind, e):
        return zin[:, kind, e * groups:(e + 1) * groups, :].reshape(owners * groups, width)

    def to_sources(kind, e, value):
        bsend[:, kind, e * groups:(e + 1) * groups, :] = value.astype(jnp.bfloat16).reshape(owners, groups, width)

    def send_back(kind):
        bin_[z, kind] = bsend[z, kind]
        return start([
            push(bsend.at[d[1], kind], bin_.at[z, kind], b_send.at[kind, k], b_recv.at[kind, k], d) for k, d in enumerate(z_peers)
        ])

    pres = []
    for e in range(own_experts):
        pre = dot_nn(from_sources(0, e), up[e])
        pres.append(pre)
        active = jax.nn.gelu(pre, approximate=True).astype(jnp.bfloat16)
        to_sources(0, e, dot_nn(active, down[e]))
    out_copies = send_back(0)
    wait(grad_copies)
    gather_copies = start([push(zin, all_ref.at[me], g_send.at[k], g_recv.at[k], (d, z)) for k, d in enumerate(same_core)])
    relays = start([push(zin, all_ref.at[me], r_send.at[0], r_recv.at[0], (sib, z))])
    own = start([pltpu.make_async_copy(zin, all_ref.at[me], own_sem.at[1])])
    for e in range(own_experts):
        grad_pre = (dot_nt(from_sources(1, e), down[e]) * gelu_slope(pres[e])).astype(jnp.bfloat16)
        to_sources(1, e, dot_nt(grad_pre, up[e]))
    back_copies = send_back(1)
    wait(out_copies)
    expert_out = bin_[:, 0].reshape(flat, width)
    layer_ref[...] = hidden + dot_tn(low, expert_out)
    grad_mix = dot_nt(expert_out, cot[...])
    wait(back_copies)
    grad_mixed = bin_[:, 1].reshape(flat, width)
    product = mix * (grad_mix + dot_nt(grad_mixed, normed))
    grad_logits = product - mix * jnp.sum(product, axis=1, keepdims=True)
    grad_logits = jnp.sum(grad_logits.reshape(experts, groups, rows), axis=1).astype(jnp.bfloat16)
    pad = jnp.zeros((small_in.shape[0] - experts, rows), jnp.bfloat16)
    grad_logits = jnp.concatenate([grad_logits, pad], axis=0)
    grad_normed = dot_tn(jnp.concatenate([low, grad_logits], axis=0), jnp.concatenate([grad_mixed, small_in], axis=0))
    scaled = grad_normed * gain
    mean = jnp.mean(scaled, axis=-1, keepdims=True)
    grad_hidden = cot[...].astype(jnp.float32) + inv_dev * (scaled - mean - unit * jnp.mean(scaled * unit, axis=-1, keepdims=True))
    branch = grad_hidden.astype(jnp.bfloat16)
    grad_heads = dot_nt(branch, weight).astype(jnp.bfloat16)
    for h in range(count):
        at = slice(HEAD * h, HEAD * (h + 1))
        ghead[h] = jnp.concatenate([grad_heads[:half, at], grad_heads[half:, at]], axis=1)
    swap = start([push(ghead.at[d[0]], ghead_ref.at[me], h_send.at[k], h_recv.at[k], d) for k, d in enumerate(c_peers)])
    last = start([pltpu.make_async_copy(ghead.at[me], ghead_ref.at[me], own_sem.at[2])])
    for k, d in enumerate(same_core):
        gather_copies[k].wait_recv()
        relays += start([push(all_ref.at[d], all_ref.at[d], r_send.at[k + 1], r_recv.at[k + 1], (sib, z))])
    ghidden_ref[...] = grad_hidden
    gout_ref[...] = dot_tn(attended, branch).astype(jnp.bfloat16).reshape(gout_ref.shape)
    small_ref[...] = jnp.concatenate(
        [
            dot_nn(grad_logits, normed)[:experts],
            jnp.sum(grad_normed * unit, axis=0, keepdims=True),
            jnp.sum(grad_normed, axis=0, keepdims=True),
            jnp.zeros((small_in.shape[0] - experts - 2, width), jnp.float32),
        ],
        axis=0,
    )
    for copy in gather_copies:
        copy.wait_send()
    wait(own + last + relays + swap)


def middle(att, tokens, cot, w_out, pack, gid_row, w_up, w_down, later, experts, groups):
    rows, width = tokens.shape
    count, owners, own = att.shape[0], pack.shape[0], w_up.shape[0]
    sent = (owners, 2, experts * groups // owners, width)
    dma = pltpu.SemaphoreType.DMA
    low, full = jnp.bfloat16, jnp.float32
    return pl.pallas_call(
        functools.partial(middle_body, experts, groups),
        out_shape=(
            jax.ShapeDtypeStruct((rows, width), full),
            jax.ShapeDtypeStruct((rows, width), full),
            jax.ShapeDtypeStruct((owners, width // owners, width), low),
            jax.ShapeDtypeStruct((pack.shape[1], width), full),
            jax.ShapeDtypeStruct((count,) + sent, low),
            jax.ShapeDtypeStruct(att.shape, low),
        ),
        in_specs=[ANY] * 5 + [VMEM] + [ANY] * 3,
        out_specs=(VMEM,) * 4 + (ANY,) * 2,
        scratch_shapes=[pltpu.VMEM(x.shape, x.dtype) for x in (tokens, cot, w_out, pack, w_up, w_down, att)] + [
            pltpu.VMEM(sent, low), pltpu.VMEM(sent, low), pltpu.VMEM(sent, low), pltpu.VMEM(sent, low), pltpu.VMEM(att.shape, low),
            dma((4 + 2 * own,)), dma((3,)), dma((count - 1,)), dma((count - 1,)), dma((2, owners - 1)), dma((2, owners - 1)),
            dma((2, owners - 1)), dma((2, owners - 1)), dma((3,)), dma((3,)), dma((4,)), dma((4,)), dma((count - 1,)),
            dma((count - 1,)),
        ],
        compiler_params=pltpu.CompilerParams(collective_id=2, has_side_effects=True, vmem_limit_bytes=LIMIT),
        cost_estimate=cost(35),
        name="middle",
    )(att, tokens, cot, w_out, pack, gid_row, w_up, w_down, later)


def head_columns(ref, p, index=None):
    columns = []
    for kind in range(3):
        at = slice(HEAD * (2 * kind + p), HEAD * (2 * kind + p + 1))
        columns.append(ref[index, :, at])
    return jnp.concatenate(columns, axis=1)


def closing_body(
    owners, grads_ref, toks_ref, small_in_ref, out_ref, weight_ref, ghidden_ref, gathered_ref, up_ref, down_ref,
    gtok_ref, gq_ref, gout_ref, small_ref, act_ref, gpre_ref,
    held_grads, held_toks, held_small, held_weight, held_hidden, held_mixed, held_up, held_down, act_buf, gpre_buf,
    landing, zsend, zone, total_ref, all_ref, out_zone, out_sum, out_part, out_own, out_all,
    load_sem, store_sem, a_send, a_recv, z_send, z_recv, c_send, c_recv, o_send, o_recv,
):
    me, z = lax.axis_index("ctx"), lax.axis_index("fsdp")
    count, half = grads_ref.shape[0], grads_ref.shape[1]
    width = toks_ref.shape[2]
    own_experts, ffn = up_ref.shape[0], up_ref.shape[2]
    pairs = [
        (grads_ref, held_grads), (toks_ref, held_toks), (small_in_ref, held_small), (gathered_ref, held_mixed), (up_ref, held_up),
        (down_ref, held_down), (weight_ref, held_weight), (ghidden_ref, held_hidden),
    ]
    loads = [pltpu.make_async_copy(src, dst, load_sem.at[i]) for i, (src, dst) in enumerate(pairs)]
    for copy in loads:
        copy.start()
    z_peers = [(me, lax.rem(z + k, owners)) for k in range(1, owners)]
    c_peers = [(jnp.bitwise_xor(me, k), z) for k in range(1, count)]
    meet(z_peers + c_peers)
    swaps = []
    for k, device in enumerate(c_peers):
        swaps.append(push(grads_ref.at[device[0]], landing.at[me], a_send.at[k], a_recv.at[k], device))
        swaps[-1].start()
    own_swap = pltpu.make_async_copy(grads_ref.at[me], landing.at[me], store_sem.at[0])
    own_swap.start()
    out_copies = []
    for k, device in enumerate(z_peers):
        out_copies.append(push(out_ref.at[device[1]], out_zone.at[z], o_send.at[0, k], o_recv.at[0, k], device))
        out_copies[-1].start()
    own_out = pltpu.make_async_copy(out_ref.at[z], out_zone.at[z], store_sem.at[1])
    own_out.start()

    loads[0].wait()
    loads[1].wait()
    total = None
    for device in range(count):
        for p in range(2):
            part = dot_tn(head_columns(held_grads, p, device), held_toks[device, p * half:(p + 1) * half, :])
            total = part if total is None else total + part
    loads[2].wait()
    lanes = width // owners
    for c in range(owners):
        at = slice(c * lanes, (c + 1) * lanes)
        zsend[c, :3 * HEAD, :] = total[:, at].astype(jnp.bfloat16)
        zsend[c, 3 * HEAD:, :] = held_small[:, at].astype(jnp.bfloat16)
    z_copies = []
    for k, device in enumerate(z_peers):
        z_copies.append(push(zsend.at[device[1]], zone.at[z], z_send.at[k], z_recv.at[k], device))
        z_copies[-1].start()
    zone[z] = zsend[z]
    for i in (3, 4, 5):
        loads[i].wait()

    step = 512

    def expert_part(own_expert):
        mixed = held_mixed[:, 0, own_expert].reshape(-1, width)
        grad_out = held_mixed[:, 1, own_expert].reshape(-1, width)

        def chunk(i, carry):
            at = pl.ds(pl.multiple_of(i * step, step), step)
            pre = dot_nn(mixed, held_up[own_expert, :, at])
            act_buf[own_expert, :, at] = jax.nn.gelu(pre, approximate=True).astype(jnp.bfloat16)
            slope = dot_nt(grad_out, held_down[own_expert, at, :])
            gpre_buf[own_expert, :, at] = (slope * gelu_slope(pre)).astype(jnp.bfloat16)
            return carry

        lax.fori_loop(0, ffn // step, chunk, 0)
        stores = [
            pltpu.make_async_copy(act_buf.at[own_expert], act_ref.at[own_expert], store_sem.at[2 + 2 * own_expert]),
            pltpu.make_async_copy(gpre_buf.at[own_expert], gpre_ref.at[own_expert], store_sem.at[3 + 2 * own_expert]),
        ]
        for copy in stores:
            copy.start()
        return stores

    stores = expert_part(0)
    for copy in z_copies:
        copy.wait()
    total = zone[0].astype(jnp.float32)
    for k in range(1, owners):
        total = total + zone[k].astype(jnp.float32)
    total_ref[...] = total.astype(jnp.bfloat16)
    c_copies = []
    for k, device in enumerate(c_peers):
        c_copies.append(push(total_ref, all_ref.at[me], c_send.at[k], c_recv.at[k], device))
        c_copies[-1].start()
    all_ref[me] = total_ref[...]
    own_out.wait()
    for copy in out_copies:
        copy.wait()
    total = out_zone[0].astype(jnp.float32)
    for k in range(1, owners):
        total = total + out_zone[k].astype(jnp.float32)
    per = lanes // count
    out_sum[...] = total.astype(jnp.bfloat16).reshape(out_sum.shape)
    part_copies = []
    for k, device in enumerate(c_peers):
        part_copies.append(push(out_sum.at[device[0]], out_part.at[me], o_send.at[1, k], o_recv.at[1, k], device))
        part_copies[-1].start()
    out_part[me] = out_sum[me]
    for own_expert in range(1, own_experts):
        stores += expert_part(own_expert)
    for copy in part_copies:
        copy.wait()
    total = out_part[0].astype(jnp.float32)
    for k in range(1, count):
        total = total + out_part[k].astype(jnp.float32)
    out_own[...] = total.astype(jnp.bfloat16)
    last_copies = []
    for k, device in enumerate(c_peers):
        last_copies.append(push(out_own, out_all.at[me], o_send.at[2, k], o_recv.at[2, k], device))
        last_copies[-1].start()
    out_all[me] = out_own[...]
    loads[6].wait()
    loads[7].wait()
    own_swap.wait()
    for copy in swaps:
        copy.wait()
    for p in range(2):
        columns = [landing[h, :, HEAD * (2 * kind + p):HEAD * (2 * kind + p + 1)] for kind in range(3) for h in range(count)]
        at = slice(p * half, (p + 1) * half)
        gtok_ref[at, :] = held_hidden[at, :] + dot_nt(jnp.concatenate(columns, axis=1), held_weight[...])
    for copy in c_copies:
        copy.wait()
    small = None
    turned = []
    for c in range(count):
        turned.append(all_ref[c, :3 * HEAD, :].astype(jnp.float32).T)
        part = all_ref[c, 3 * HEAD:, :].astype(jnp.float32)
        small = part if small is None else small + part
    small_ref[...] = small
    for kind in range(3):
        at = slice(HEAD * kind, HEAD * (kind + 1))
        gq_ref[:, HEAD * count * kind:HEAD * count * (kind + 1)] = jnp.concatenate([part[:, at] for part in turned], axis=1)
    for copy in last_copies:
        copy.wait()
    gout_ref[...] = out_all[...].astype(jnp.float32).reshape(gout_ref.shape)
    for copy in stores:
        copy.wait()


def closing(grads, tokens_all, small, gout, weight, ghidden, gathered, w_up, w_down, groups, owners):
    count, width = tokens_all.shape[0], tokens_all.shape[2]
    lanes = width // owners
    height = 3 * HEAD + small.shape[0]
    own_experts, _, ffn = w_up.shape
    sources = gathered.shape[0]
    view = gathered.reshape(sources, 2, own_experts, groups, width)
    wide = (own_experts, sources * groups, ffn)
    dma = pltpu.SemaphoreType.DMA
    held = [grads, tokens_all, small, weight, ghidden, view, w_up, w_down]
    part = (count, lanes // count, width)
    return pl.pallas_call(
        functools.partial(closing_body, owners),
        out_shape=(
            jax.ShapeDtypeStruct(ghidden.shape, jnp.float32),
            jax.ShapeDtypeStruct((lanes, 3 * width), jnp.float32),
            jax.ShapeDtypeStruct((lanes, width), jnp.float32),
            jax.ShapeDtypeStruct((small.shape[0], lanes), jnp.float32),
            jax.ShapeDtypeStruct(wide, jnp.bfloat16),
            jax.ShapeDtypeStruct(wide, jnp.bfloat16),
        ),
        in_specs=[ANY] * 9,
        out_specs=(VMEM,) * 4 + (ANY,) * 2,
        scratch_shapes=[pltpu.VMEM(x.shape, x.dtype) for x in held] + [
            pltpu.VMEM(wide, jnp.bfloat16), pltpu.VMEM(wide, jnp.bfloat16), pltpu.VMEM(grads.shape, jnp.bfloat16),
            pltpu.VMEM((owners, height, lanes), jnp.bfloat16), pltpu.VMEM((owners, height, lanes), jnp.bfloat16),
            pltpu.VMEM((height, lanes), jnp.bfloat16), pltpu.VMEM((count, height, lanes), jnp.bfloat16),
            pltpu.VMEM(gout.shape, jnp.bfloat16), pltpu.VMEM(part, jnp.bfloat16), pltpu.VMEM(part, jnp.bfloat16),
            pltpu.VMEM(part[1:], jnp.bfloat16), pltpu.VMEM(part, jnp.bfloat16),
            dma((8,)), dma((2 + 2 * own_experts,)), dma((count - 1,)), dma((count - 1,)), dma((owners - 1,)), dma((owners - 1,)),
            dma((count - 1,)), dma((count - 1,)), dma((3, count - 1)), dma((3, count - 1)),
        ],
        compiler_params=pltpu.CompilerParams(collective_id=6, has_side_effects=True, vmem_limit_bytes=LIMIT),
        cost_estimate=cost(28),
        name="closing",
    )(*held[:3], gout, *held[3:])


def expert_grad_body(mixed_ref, grad_ref, act_ref, gpre_ref, gup_ref, gdown_ref):
    width = gup_ref.shape[1]
    gup_ref[0] = dot_tn(mixed_ref[...].reshape(-1, width), gpre_ref[0])
    gdown_ref[0] = dot_tn(act_ref[0], grad_ref[...].reshape(-1, width))


def expert_grads(gathered, active, grad_pre, groups):
    own, rows, ffn = active.shape
    step = 512
    sources, width = gathered.shape[0], gathered.shape[3]
    view = gathered.reshape(sources, 2, own, groups, width)
    return pl.pallas_call(
        expert_grad_body,
        grid=(own, ffn // step),
        out_shape=(jax.ShapeDtypeStruct((own, width, ffn), jnp.float32), jax.ShapeDtypeStruct((own, ffn, width), jnp.float32)),
        in_specs=[
            pl.BlockSpec((sources, 1, 1, groups, width), lambda e, f: (0, 0, e, 0, 0)),
            pl.BlockSpec((sources, 1, 1, groups, width), lambda e, f: (0, 1, e, 0, 0)),
            pl.BlockSpec((1, rows, step), lambda e, f: (e, 0, f)),
            pl.BlockSpec((1, rows, step), lambda e, f: (e, 0, f)),
        ],
        out_specs=(pl.BlockSpec((1, width, step), lambda e, f: (e, 0, f)), pl.BlockSpec((1, step, width), lambda e, f: (e, f, 0))),
        compiler_params=pltpu.CompilerParams(vmem_limit_bytes=LIMIT),
        cost_estimate=cost(8),
        name="expert_grads",
    )(view, view, active, grad_pre)


def fast_device(
    tokens, cotangent, block_table, seg_ids, group_ids, w_qkv, w_out, w_router, ln_gain, ln_bias, w_up, w_down
):
    ctx_count, z_count = lax.axis_size("ctx"), lax.axis_size("fsdp")
    ctx_index = lax.axis_index("ctx")
    tok_rows, cot_rows = tokens[0], cotangent[0]
    rows, width = tok_rows.shape
    experts = w_router.shape[1]
    groups = rows // GROUP_SIZE
    shard = w_qkv.shape[0]
    segs = seg_ids[0].reshape(block_table.shape[0], -1)
    head_cols = lax.dynamic_slice_in_dim(w_qkv.reshape(shard, 3, ctx_count, HEAD), ctx_index, 1, 2).reshape(shard, 3 * HEAD)
    pack = jnp.concatenate(
        [w_router.T, ln_gain[None], ln_bias[None], jnp.zeros((16 - experts - 2, shard), jnp.bfloat16)], axis=0
    )
    tokens_all, head_weights, out_full, pack_full = gather(tok_rows, [head_cols, w_out, pack], ctx_count, z_count)
    later, tokens_all = lax.optimization_barrier((w_qkv, tokens_all))
    qkv_full = lax.all_gather(later, "fsdp", axis=0, tiled=True)
    att, *saved = attn_fwd(tokens_all.reshape(ctx_count * rows, width), head_weights, block_table, segs)
    layer_out, grad_hidden, gout, small, gathered, grad_heads = middle(
        att, tok_rows, cot_rows, out_full, pack_full, group_ids, w_up, w_down, qkv_full, experts, groups
    )
    gathered = gathered.reshape((ctx_count * z_count,) + gathered.shape[2:])
    grads = attn_bwd(grad_heads, saved, block_table, segs)
    grad_tokens, grad_qkv, grad_out, small, active, grad_pre = closing(
        grads, tokens_all, small, gout, qkv_full, grad_hidden, gathered, w_up, w_down, groups, z_count
    )
    grad_up, grad_down = expert_grads(gathered, active, grad_pre, groups)
    return (
        layer_out[None],
        grad_tokens[None],
        grad_qkv,
        grad_out,
        small[:experts].T,
        small[experts],
        small[experts + 1],
        grad_up,
        grad_down,
    )


def solution(mesh):
    placed = (
        P("fsdp", "ctx", None),
        P("fsdp", "ctx", None),
        P(),
        P("fsdp", None),
        P("fsdp", "ctx"),
        P("fsdp", None),
        P("fsdp", None),
        P("fsdp", None),
        P("fsdp"),
        P("fsdp"),
        P("fsdp", None, None),
        P("fsdp", None, None),
    )
    step = fast_device if mesh.shape["ctx"] == HEADS else on_device
    return jax.shard_map(
        step,
        mesh=mesh,
        in_specs=placed,
        out_specs=(
            P("fsdp", "ctx", None),
            P("fsdp", "ctx", None),
            P("fsdp", None),
            P("fsdp", None),
            P("fsdp", None),
            P("fsdp"),
            P("fsdp"),
            P("fsdp", None, None),
            P("fsdp", None, None),
        ),
        check_vma=False,
    )
```

```python
import functools

import jax
import jax.numpy as jnp
from jax import lax
from jax.experimental import pallas as pl
from jax.experimental.pallas import tpu as pltpu
from jax.sharding import PartitionSpec as P

HEADS = 8
HEAD = 64
GROUP_SIZE = 32
KEY_BLOCK = 2048


highest = lax.Precision.HIGHEST
neg_large = -1e30
epsilon = 1e-05
gelu_coef = 0.7978845608028654
gelu_cubic = 0.044715


def contract_rows(left, right):
    return lax.dot_general(
        left, right, (((0,), (0,)), ((), ())), preferred_element_type=jnp.float32
    )


def contract_cols(left, right):
    return lax.dot_general(
        left, right, (((1,), (1,)), ((), ())), preferred_element_type=jnp.float32
    )


def gelu_slope(value):
    inner = gelu_coef * (value + gelu_cubic * value * value * value)
    tangent = jnp.tanh(inner)
    return 0.5 * (1.0 + tangent) + 0.5 * value * (1.0 - tangent * tangent) * gelu_coef * (
        1.0 + 3.0 * gelu_cubic * value * value
    )


def expert_forward(mixed_low, up_weight, down_weight):
    pre = jnp.einsum("ged,edh->geh", mixed_low, up_weight, preferred_element_type=jnp.float32)
    active = jax.nn.gelu(pre, approximate=True).astype(jnp.bfloat16)
    result = jnp.einsum("geh,ehd->ged", active, down_weight, preferred_element_type=jnp.float32)
    return (pre, active, result.astype(jnp.bfloat16))


def expert_backward(mixed_low, pre, active, grad_result, up_weight, down_weight):
    grad_act = jnp.einsum(
        "ged,ehd->geh", grad_result, down_weight, preferred_element_type=jnp.float32
    )
    grad_pre = (grad_act * gelu_slope(pre)).astype(jnp.bfloat16)
    grad_down_part = jnp.einsum(
        "geh,ged->ehd", active, grad_result, preferred_element_type=jnp.float32
    )
    grad_up_part = jnp.einsum(
        "ged,geh->edh", mixed_low, grad_pre, preferred_element_type=jnp.float32
    )
    grad_mixed = jnp.einsum("geh,edh->ged", grad_pre, up_weight, preferred_element_type=jnp.float32)
    return (grad_up_part, grad_down_part, grad_mixed.astype(jnp.bfloat16))


def on_device(
    tokens,
    cotangent,
    block_table,
    seg_ids,
    group_ids,
    w_qkv,
    w_out,
    w_router,
    ln_gain,
    ln_bias,
    w_up,
    w_down,
):
    tok_rows = tokens[0]
    tok_count = tok_rows.shape[0]
    width = tok_rows.shape[1]
    expert_count = w_router.shape[1]
    ctx_index = lax.axis_index("ctx")
    full_rows = seg_ids.shape[1]
    block_len = full_rows // block_table.shape[0]
    row_ids = jnp.arange(full_rows, dtype=jnp.int32)
    key_pos = jnp.take(block_table, row_ids // block_len) * block_len + row_ids % block_len
    key_seg = seg_ids[0]
    pos_rows = lax.dynamic_slice_in_dim(key_pos, ctx_index * tok_count, tok_count)
    seg_rows = lax.dynamic_slice_in_dim(key_seg, ctx_index * tok_count, tok_count)
    scale = HEAD ** (-0.5)
    qkv_full, out_full, router_full, gain_full, bias_full = (
        lax.all_gather(w_qkv, "fsdp", axis=0, tiled=True),
        lax.all_gather(w_out, "fsdp", axis=0, tiled=True),
        lax.all_gather(w_router, "fsdp", axis=0, tiled=True),
        lax.all_gather(ln_gain, "fsdp", axis=0, tiled=True),
        lax.all_gather(ln_bias, "fsdp", axis=0, tiled=True),
    )
    qkv = jnp.dot(tok_rows, qkv_full, preferred_element_type=jnp.float32).astype(jnp.bfloat16)
    query_heads = qkv[:, :width].reshape(tok_count, HEADS, HEAD)
    key_all, val_all = (
        lax.all_gather(qkv[:, width : 2 * width], "ctx", axis=0, tiled=True),
        lax.all_gather(qkv[:, 2 * width :], "ctx", axis=0, tiled=True),
    )
    key_heads = key_all.reshape(full_rows, HEADS, HEAD)
    val_heads = val_all.reshape(full_rows, HEADS, HEAD)
    block_count = full_rows // KEY_BLOCK
    block_ids = jnp.arange(block_count, dtype=jnp.int32)

    def block_scores(index):
        start = index * KEY_BLOCK
        key_block = lax.dynamic_slice_in_dim(key_heads, start, KEY_BLOCK, 0)
        val_block = lax.dynamic_slice_in_dim(val_heads, start, KEY_BLOCK, 0)
        pos_block = lax.dynamic_slice_in_dim(key_pos, start, KEY_BLOCK, 0)
        seg_block = lax.dynamic_slice_in_dim(key_seg, start, KEY_BLOCK, 0)
        scores = (
            jnp.einsum("qhd,khd->hqk", query_heads, key_block, preferred_element_type=jnp.float32)
            * scale
        )
        allowed = (pos_block[None, :] <= pos_rows[:, None]) & (
            (seg_block[None, :] == 0) | (seg_block[None, :] == seg_rows[:, None])
        )
        return (scores, allowed[None], key_block, val_block)

    def lse_step(carry, index):
        top, total = carry
        scores, allowed, key_block, val_block = block_scores(index)
        masked = jnp.where(allowed, scores, neg_large)
        new_top = jnp.maximum(top, jnp.max(masked, axis=-1))
        weights = jnp.where(allowed, jnp.exp(masked - new_top[..., None]), 0.0)
        return ((new_top, total * jnp.exp(top - new_top) + jnp.sum(weights, axis=-1)), None)

    start_top = jnp.full((HEADS, tok_count), neg_large, jnp.float32)
    (top, total), unused = lax.scan(
        lse_step, (start_top, jnp.zeros((HEADS, tok_count), jnp.float32)), block_ids
    )
    log_total = top + jnp.log(total)

    def block_probs(index):
        scores, allowed, key_block, val_block = block_scores(index)
        probs = jnp.where(allowed, jnp.exp(scores - log_total[..., None]), 0.0)
        return (probs, key_block, val_block)

    def value_step(accum, index):
        probs, key_block, val_block = block_probs(index)
        return (
            accum
            + jnp.einsum(
                "hqk,khd->qhd",
                probs.astype(jnp.bfloat16),
                val_block,
                preferred_element_type=jnp.float32,
            ),
            None,
        )

    accum, unused = lax.scan(
        value_step, jnp.zeros((tok_count, HEADS, HEAD), jnp.float32), block_ids
    )
    attended = accum.reshape(tok_count, width).astype(jnp.bfloat16)
    hidden = tok_rows.astype(jnp.float32) + jnp.dot(
        attended, out_full, preferred_element_type=jnp.float32
    )
    center = hidden - jnp.mean(hidden, axis=-1, keepdims=True)
    inv_dev = lax.rsqrt(jnp.mean(center * center, axis=-1, keepdims=True) + epsilon)
    unit = center * inv_dev
    gain_f = gain_full.astype(jnp.float32)
    normed_low = (unit * gain_f + bias_full.astype(jnp.float32)).astype(jnp.bfloat16)
    logits = jnp.dot(normed_low, router_full, preferred_element_type=jnp.float32)
    groups_dev = tok_count // GROUP_SIZE
    local_group = group_ids[0] - ctx_index * groups_dev
    member = (local_group[:, None] == jnp.arange(groups_dev, dtype=jnp.int32)[None, :]).astype(
        jnp.float32
    )
    expo = jnp.exp(logits)
    group_total = jnp.dot(member.T, expo, precision=highest)
    mix_weights = expo / jnp.dot(member, group_total, precision=highest)
    weights_low = mix_weights.astype(jnp.bfloat16)
    mixing = member.astype(jnp.bfloat16).T[:, None, :] * weights_low.T[None, :, :]
    mixing_flat = mixing.reshape(groups_dev * expert_count, tok_count)
    mixed_low = jnp.dot(mixing_flat, normed_low, preferred_element_type=jnp.float32).astype(
        jnp.bfloat16
    )
    mixed_low = mixed_low.reshape(groups_dev, expert_count, width)
    owner_mixed = lax.all_to_all(mixed_low, "fsdp", split_axis=1, concat_axis=0, tiled=True)
    pre, active, owner_out = expert_forward(owner_mixed, w_up, w_down)
    expert_out = lax.all_to_all(owner_out, "fsdp", split_axis=0, concat_axis=1, tiled=True)
    expert_flat = expert_out.reshape(groups_dev * expert_count, width)
    spread = contract_rows(mixing_flat, expert_flat)
    layer_out = hidden + spread
    cot_rows = cotangent[0]
    cot_f = cot_rows.astype(jnp.float32)
    grad_expert = jnp.dot(mixing_flat, cot_rows, preferred_element_type=jnp.float32).astype(
        jnp.bfloat16
    )
    grad_expert = grad_expert.reshape(groups_dev, expert_count, width)
    coef = contract_cols(cot_rows, expert_flat).reshape(tok_count, groups_dev, expert_count)
    grad_mix_spread = jnp.sum(coef * member[:, :, None], axis=1)
    owner_grad = lax.all_to_all(grad_expert, "fsdp", split_axis=1, concat_axis=0, tiled=True)
    grad_up_own, grad_down_own, owner_back = expert_backward(
        owner_mixed, pre, active, owner_grad, w_up, w_down
    )
    grad_mixed = lax.all_to_all(owner_back, "fsdp", split_axis=0, concat_axis=1, tiled=True)
    grad_mixed_flat = grad_mixed.reshape(groups_dev * expert_count, width)
    grad_norm_mix = contract_rows(mixing_flat, grad_mixed_flat)
    grad_mixing = contract_cols(grad_mixed_flat, normed_low).reshape(
        groups_dev, expert_count, tok_count
    )
    grad_mix_mixing = jnp.sum(grad_mixing * member.T[:, None, :], axis=0).T
    grad_mix = grad_mix_spread + grad_mix_mixing
    product = mix_weights * grad_mix
    token_dot = jnp.dot(member, jnp.dot(member.T, product, precision=highest), precision=highest)
    grad_logits = (product - mix_weights * token_dot).astype(jnp.bfloat16)
    grad_router_part = contract_rows(normed_low, grad_logits)
    grad_norm_router = contract_cols(grad_logits, router_full)
    grad_normed = grad_norm_mix + grad_norm_router
    grad_gain_part = jnp.sum(grad_normed * unit, axis=0)
    grad_bias_part = jnp.sum(grad_normed, axis=0)
    scaled = grad_normed * gain_f
    grad_hidden = cot_f + inv_dev * (
        scaled
        - jnp.mean(scaled, axis=-1, keepdims=True)
        - unit * jnp.mean(scaled * unit, axis=-1, keepdims=True)
    )
    grad_branch = grad_hidden.astype(jnp.bfloat16)
    grad_out_part = contract_rows(attended, grad_branch)
    grad_heads = (
        contract_cols(grad_branch, out_full).astype(jnp.bfloat16).reshape(tok_count, HEADS, HEAD)
    )
    delta = jnp.sum(grad_heads.astype(jnp.float32) * accum, axis=-1).T

    def grad_step(grad_query, index):
        probs, key_block, val_block = block_probs(index)
        grad_probs = jnp.einsum(
            "qhd,khd->hqk", grad_heads, val_block, preferred_element_type=jnp.float32
        )
        grad_scores = (probs * (grad_probs - delta[..., None])).astype(jnp.bfloat16)
        grad_query = (
            grad_query
            + jnp.einsum("hqk,khd->qhd", grad_scores, key_block, preferred_element_type=jnp.float32)
            * scale
        )
        grad_key = (
            jnp.einsum("hqk,qhd->khd", grad_scores, query_heads, preferred_element_type=jnp.float32)
            * scale
        )
        grad_val = jnp.einsum(
            "hqk,qhd->khd",
            probs.astype(jnp.bfloat16),
            grad_heads,
            preferred_element_type=jnp.float32,
        )
        return (grad_query, (grad_key, grad_val))

    grad_query, (grad_keys, grad_vals) = lax.scan(
        grad_step, jnp.zeros((tok_count, HEADS, HEAD), jnp.float32), block_ids
    )
    grad_key_own, grad_val_own = (
        lax.psum_scatter(
            grad_keys.reshape(full_rows, width), "ctx", scatter_dimension=0, tiled=True
        ),
        lax.psum_scatter(
            grad_vals.reshape(full_rows, width), "ctx", scatter_dimension=0, tiled=True
        ),
    )
    grad_qkv_low = jnp.concatenate(
        [grad_query.reshape(tok_count, width), grad_key_own, grad_val_own], axis=1
    ).astype(jnp.bfloat16)
    grad_qkv_part = contract_rows(tok_rows, grad_qkv_low)
    grad_tokens = grad_hidden + contract_cols(grad_qkv_low, qkv_full)
    dense = (
        lax.psum_scatter(grad_qkv_part, "fsdp", scatter_dimension=0, tiled=True),
        lax.psum_scatter(grad_out_part, "fsdp", scatter_dimension=0, tiled=True),
        lax.psum_scatter(grad_router_part, "fsdp", scatter_dimension=0, tiled=True),
        lax.psum_scatter(grad_gain_part, "fsdp", scatter_dimension=0, tiled=True),
        lax.psum_scatter(grad_bias_part, "fsdp", scatter_dimension=0, tiled=True),
    )
    totals = lax.psum(
        (dense[0], dense[1], dense[2], dense[3], dense[4], grad_up_own, grad_down_own), "ctx"
    )
    return (
        layer_out[None],
        grad_tokens[None],
        totals[0],
        totals[1],
        totals[2],
        totals[3],
        totals[4],
        totals[5],
        totals[6],
    )


def cost(microseconds):
    return pl.CostEstimate(flops=int(microseconds * 1.15e9), bytes_accessed=1 << 20, transcendentals=0)


LOG2E = 1.4426950408889634
HIDE = -1e30
SAFE = 100.0
RUN = 1024
HALF = 512
VMEM = pl.BlockSpec(memory_space=pltpu.VMEM)
SMEM = pl.BlockSpec(memory_space=pltpu.SMEM)
ANY = pl.BlockSpec(memory_space=pl.ANY)
LIMIT = 60 << 20


def dot_nn(left, right):
    return lax.dot_general(left, right, (((1,), (0,)), ((), ())), preferred_element_type=jnp.float32)


def dot_nt(left, right):
    return lax.dot_general(left, right, (((1,), (1,)), ((), ())), preferred_element_type=jnp.float32)


def dot_tn(left, right):
    return lax.dot_general(left, right, (((0,), (0,)), ((), ())), preferred_element_type=jnp.float32)


def split3(value):
    one = value.astype(jnp.bfloat16)
    rest = value - one.astype(jnp.float32)
    two = rest.astype(jnp.bfloat16)
    three = (rest - two.astype(jnp.float32)).astype(jnp.bfloat16)
    return one, two, three


def span(index, size, width=None):
    return pl.ds(pl.multiple_of(index * size, size), size if width is None else width)


def flipped(value):
    return value.astype(jnp.float32).T.astype(value.dtype)


def boundaries(seg_ref, lane):
    segs = seg_ref[...]
    begin = jnp.zeros(lane.shape, jnp.int32)
    end = jnp.zeros(lane.shape, jnp.int32)
    for c in range(1, 10):
        below = (segs < c).astype(jnp.int32)
        total = jnp.sum(jnp.sum(below, axis=1, keepdims=True), axis=0, keepdims=True)
        begin = jnp.where(lane == HEAD - 1 + c, total, begin)
        end = jnp.where(lane == HEAD - 2 + c, total, end)
    return begin, jnp.where(lane == HEAD + 8, 0, end)


def fwd_body(blocks, block_len, table_ref, tok_ref, w_ref, seg_ref, att_ref, qf_ref, kf_ref, vf_ref, stat_ref, vt_ref, inv_ref):
    rows = blocks * block_len
    for t in range(blocks):
        inv_ref[table_ref[t]] = t
    weight = w_ref[...].reshape(w_ref.shape[0] * w_ref.shape[1], w_ref.shape[2])
    weight = jnp.concatenate([weight, jnp.zeros((weight.shape[0], HEAD), weight.dtype)], axis=1)
    lane = lax.broadcasted_iota(jnp.int32, (1, 2 * HEAD), 1)
    begin, end = boundaries(seg_ref, lane)
    is_flag = (lane >= HEAD) & (lane < HEAD + 8)
    is_one = (lane >= HEAD + 8) & (lane < HEAD + 11)
    pair = (lax.broadcasted_iota(jnp.int32, (2 * HEAD, 2 * HEAD), 0) // HEAD == lane // HEAD).astype(jnp.bfloat16)
    ones_v = ((lane >= HEAD) & (lane < HEAD + 3)).astype(jnp.float32)

    def project(s, sizes):
        t = inv_ref[s]
        qkv = dot_nn(tok_ref[span(t, block_len), :], weight)
        both = qkv[:, :2 * HEAD].astype(jnp.bfloat16).astype(jnp.float32)
        turned = pltpu.roll(both, HEAD, 1)
        value = qkv[:, 2 * HEAD:]
        place = lax.broadcasted_iota(jnp.int32, (block_len, 2 * HEAD), 0) + s * block_len
        own = (place >= begin) & (place < end)
        at = span(s, block_len)
        flag_q = jnp.where(is_flag & jnp.logical_not(own), 1.0, 0.0)
        flag_k = jnp.where(own, HIDE, jnp.where(is_one, 1.0, 0.0))
        qf_ref[at, :] = jnp.where(lane < HEAD, both, flag_q).astype(jnp.bfloat16)
        kf_ref[at, :] = jnp.where(lane < HEAD, turned, flag_k).astype(jnp.bfloat16)
        vf_ref[at, :] = (value + ones_v).astype(jnp.bfloat16)
        vt_ref[:, at] = jnp.where(lane < HEAD, value, 1.0).T.astype(jnp.bfloat16)
        return jnp.maximum(sizes, dot_nn((both * both).astype(jnp.bfloat16), pair))

    sizes = lax.fori_loop(0, blocks, project, jnp.zeros((block_len, 2 * HEAD), jnp.float32), unroll=4)
    scale = HEAD ** (-0.5) * LOG2E
    q_size, k_size = jnp.max(sizes[:, :HEAD]), jnp.max(sizes[:, HEAD:])
    small = q_size * k_size <= (SAFE / scale) ** 2
    causal = lax.broadcasted_iota(jnp.int32, (HALF, HALF), 0) <= lax.broadcasted_iota(jnp.int32, (HALF, HALF), 1)

    def query_run(online, run):
        def tile(state, q_at, k_at, diagonal):
            scores = dot_nt(kf_ref[k_at, :], qf_ref[q_at, :]) * scale
            if diagonal:
                scores = jnp.where(causal, scores, HIDE)
            top, acc = state
            if online:
                new_top = jnp.maximum(top, jnp.max(scores, axis=0, keepdims=True))
                acc = acc * jnp.exp2(top - new_top)
                scores, top = scores - new_top, new_top
            return top, acc + dot_nn(vt_ref[:, k_at], jnp.exp2(scores).astype(jnp.bfloat16))

        start = (jnp.full((1, RUN), HIDE if online else 0.0, jnp.float32), jnp.zeros((2 * HEAD, RUN), jnp.float32))
        whole = lax.fori_loop(0, run, lambda n, state: tile(state, span(run, RUN), span(n, RUN), False), start)
        early, late = span(2 * run, HALF), span(2 * run + 1, HALF)
        first = tile([part[:, :HALF] for part in whole], early, early, True)
        second = tile([part[:, HALF:] for part in whole], late, early, False)
        second = tile(second, late, late, True)
        for at, (top, acc) in ((early, first), (late, second)):
            total = acc[HEAD:]
            stat = jnp.concatenate([acc[:HEAD] / total, top + jnp.log2(total)], axis=0).T
            stat_ref[at, :] = stat
            one, two, three = split3(stat * (-1.0 / scale))
            old = qf_ref[at, :]
            old = jnp.where(lane == HEAD + 8, one, old)
            old = jnp.where(lane == HEAD + 9, two, old)
            qf_ref[at, :] = jnp.where(lane == HEAD + 10, three, old)

    for online in (False, True):
        @pl.when(small != online)
        def _():
            @pl.loop(0, rows // RUN)
            def _(run):
                query_run(online, run)

    for c in range(blocks // 2):
        parts = [stat_ref[span(table_ref[2 * c + half], block_len), :HEAD] for half in range(2)]
        att_ref[c] = jnp.concatenate(parts, axis=1).astype(jnp.bfloat16)


def attn_fwd(tokens_all, weight, table, segs):
    rows = tokens_all.shape[0]
    blocks, block_len = segs.shape
    low = jnp.bfloat16
    return pl.pallas_call(
        functools.partial(fwd_body, blocks, block_len),
        out_shape=(
            jax.ShapeDtypeStruct((blocks // 2, block_len, 2 * HEAD), low),
            jax.ShapeDtypeStruct((rows, 2 * HEAD), low),
            jax.ShapeDtypeStruct((rows, 2 * HEAD), low),
            jax.ShapeDtypeStruct((rows, 2 * HEAD), low),
            jax.ShapeDtypeStruct((rows, 2 * HEAD), jnp.float32),
        ),
        in_specs=[SMEM, VMEM, VMEM, VMEM],
        out_specs=(VMEM,) * 5,
        scratch_shapes=[pltpu.VMEM((2 * HEAD, rows), low), pltpu.SMEM((blocks,), jnp.int32)],
        compiler_params=pltpu.CompilerParams(vmem_limit_bytes=LIMIT),
        cost_estimate=cost(30),
        name="attention",
    )(table, tokens_all, weight, segs)


def bwd_body(blocks, block_len, table_ref, do_ref, qf_ref, kf_ref, vf_ref, stat_ref, out_ref,
             inv_ref, dof_ref, qt_ref, dot_ref, dq_ref, dk_ref, dv_ref):
    rows = blocks * block_len
    for t in range(blocks):
        inv_ref[table_ref[t]] = t
    lane = lax.broadcasted_iota(jnp.int32, (1, 2 * HEAD), 1)

    def prepare(s, carry):
        t = inv_ref[s]
        at = span(s, block_len)
        both = do_ref[t // 2].astype(jnp.float32)
        both = jnp.where(t % 2 == 0, both, pltpu.roll(both, HEAD, 1))
        grad = jnp.where(lane < HEAD, both, 0.0)
        delta = jnp.sum(grad * stat_ref[at, :], axis=1, keepdims=True)
        one, two, three = split3(jnp.broadcast_to(-delta, grad.shape))
        wide = jnp.where(lane == HEAD, one, grad.astype(jnp.bfloat16))
        wide = jnp.where(lane == HEAD + 1, two, wide)
        dof_ref[at, :] = jnp.where(lane == HEAD + 2, three, wide)
        turned = jnp.where(lane < HEAD, both, pltpu.roll(qf_ref[at, :].astype(jnp.float32), HEAD, 1)).T.astype(jnp.bfloat16)
        dot_ref[:, at] = turned[:HEAD]
        qt_ref[:, at] = turned[HEAD:]
        return carry

    lax.fori_loop(0, blocks, prepare, 0, unroll=2)
    causal = lax.broadcasted_iota(jnp.int32, (HALF, HALF), 1) <= lax.broadcasted_iota(jnp.int32, (HALF, HALF), 0)
    scale = HEAD ** (-0.5)

    @pl.loop(0, rows // RUN)
    def _(run):
        def tile(q_at, k_at, k_low, k_size, diagonal, first_k, first_q):
            scores = dot_nt(qf_ref[q_at, :], kf_ref[k_at, :]) * (scale * LOG2E)
            if diagonal:
                scores = jnp.where(causal, scores, HIDE)
            probs = jnp.exp2(scores)
            grad = (probs * dot_nt(dof_ref[q_at, :], vf_ref[k_at, :])).astype(jnp.bfloat16)
            dv = dot_nn(dot_ref[:, q_at], probs.astype(jnp.bfloat16))
            dk = dot_nn(qt_ref[:, q_at], grad)
            dq = dot_nn(grad, kf_ref[k_at, :])
            at = slice(k_low, k_low + k_size)
            if first_k:
                dv_ref[:, at] = dv
                dk_ref[:, at] = dk
            else:
                dv_ref[:, at] += dv
                dk_ref[:, at] += dk
            if first_q:
                @pl.when(run == 0)
                def _():
                    dq_ref[q_at, :] = dq

                @pl.when(run != 0)
                def _():
                    dq_ref[q_at, :] += dq
            else:
                dq_ref[q_at, :] += dq

        early, late = span(2 * run, HALF), span(2 * run + 1, HALF)
        tile(early, early, 0, HALF, True, True, True)
        tile(late, early, 0, HALF, False, False, True)
        tile(late, late, HALF, HALF, True, True, False)

        @pl.loop(run + 1, rows // RUN)
        def _(index):
            tile(span(index, RUN), span(run, RUN), 0, RUN, False, False, True)

        dk, dv = (dk_ref[...] * scale).T.astype(jnp.bfloat16), dv_ref[...].T.astype(jnp.bfloat16)
        dq = (dq_ref[span(run, RUN), :HEAD] * scale).astype(jnp.bfloat16)
        for part in range(RUN // block_len):
            t = inv_ref[run * (RUN // block_len) + part]
            at = slice(part * block_len, (part + 1) * block_len)
            for parity in range(2):
                @pl.when(t % 2 == parity)
                def _():
                    for kind, value in enumerate((dq, dk, dv)):
                        low = kind * 2 * HEAD + parity * HEAD
                        out_ref[t // 2, :, low:low + HEAD] = value[at]


def attn_bwd(grad, saved, table, segs):
    blocks, block_len = segs.shape
    rows = blocks * block_len
    low, full = jnp.bfloat16, jnp.float32
    return pl.pallas_call(
        functools.partial(bwd_body, blocks, block_len),
        out_shape=jax.ShapeDtypeStruct((blocks // 2, block_len, 6 * HEAD), low),
        in_specs=[SMEM] + [VMEM] * 5,
        out_specs=VMEM,
        scratch_shapes=[
            pltpu.SMEM((blocks,), jnp.int32), pltpu.VMEM((rows, 2 * HEAD), low),
            pltpu.VMEM((HEAD, rows), low), pltpu.VMEM((HEAD, rows), low), pltpu.VMEM((rows, 2 * HEAD), full),
            pltpu.VMEM((HEAD, RUN), full), pltpu.VMEM((HEAD, RUN), full),
        ],
        compiler_params=pltpu.CompilerParams(vmem_limit_bytes=LIMIT),
        cost_estimate=cost(35),
        name="attention_grad",
    )(table, grad, *saved)


MESH = pl.DeviceIdType.MESH


def flip(index, bit):
    return index + bit - 2 * bit * lax.rem(index // bit, 2)


def meet(devices):
    barrier = pltpu.get_barrier_semaphore()
    for device in devices:
        pl.semaphore_signal(barrier, inc=1, device_id=device, device_id_type=MESH)
    pl.semaphore_wait(barrier, len(devices))


def push(src, dst, send_sem, recv_sem, device):
    return pltpu.make_async_remote_copy(
        src_ref=src, dst_ref=dst, send_sem=send_sem, recv_sem=recv_sem, device_id=device, device_id_type=MESH
    )


def gather_body(
    zs, tok_ref, wq_ref, wo_ref, router_ref, gain_ref, bias_ref, toks_ref, heads_ref, wos_ref, packs_ref, parts_ref,
    head_buf, pack_buf, own_sem, z_send, z_recv, far_send, near_send, own_recv, diag_recv, near_recv,
):
    me, z = lax.axis_index("ctx"), lax.axis_index("fsdp")
    sib, xn, yn, diag = flip(me, 1), flip(me, 2), flip(me, 4), flip(flip(me, 2), 4)
    z_peers = [lax.rem(z + k, zs) for k in range(1, zs)]
    meet([(sib, z), (xn, z), (yn, z)] + [(me, other) for other in z_peers])
    half = tok_ref.shape[0] // 2
    count = toks_ref.shape[0]

    def part(device, k):
        return toks_ref.at[device, pl.ds(k * half, half)]

    started, locals_ = [], []

    def go(copy):
        copy.start()
        started.append(copy)

    for k in (0, 1):
        rows = tok_ref.at[pl.ds(k * half, half)]
        go(push(rows, part(me, k), far_send.at[0, k], own_recv.at[0, k], (xn, z)))
        rows = tok_ref.at[pl.ds((1 - k) * half, half)]
        go(push(rows, part(me, 1 - k), far_send.at[1, 1 - k], own_recv.at[1, 1 - k], (yn, z)))

    def share(i, shard, whole):
        for k, other in enumerate(z_peers):
            go(push(shard, whole.at[z], z_send.at[i, k], z_recv.at[i, k], (me, other)))
        locals_.append(pltpu.make_async_copy(shard, whole.at[z], own_sem.at[i]))
        locals_[-1].start()

    depth = wq_ref.shape[0] // count
    width = wq_ref.shape[1] // 3
    for h in range(count):
        @pl.when(me == h)
        def _():
            cols = [wq_ref[:, width * kind + HEAD * h:width * kind + HEAD * (h + 1)] for kind in range(3)]
            head_buf[...] = jnp.concatenate(cols, axis=1)

    share(0, head_buf, heads_ref)
    share(1, wo_ref, wos_ref)
    experts = router_ref.shape[1]
    rows = [router_ref[...].astype(jnp.float32).T, gain_ref[...].astype(jnp.float32), bias_ref[...].astype(jnp.float32)]
    rows.append(jnp.zeros((pack_buf.shape[0] - experts - 2, pack_buf.shape[1]), jnp.float32))
    pack_buf[...] = jnp.concatenate(rows, axis=0).astype(jnp.bfloat16)
    share(2, pack_buf, packs_ref)
    share(3, wq_ref.at[pl.ds(pl.multiple_of(me * depth, depth), depth)], parts_ref)
    for k in (0, 1):
        rows = tok_ref.at[pl.ds(k * half, half)]
        go(push(rows, part(me, k), near_send.at[0, k], near_recv.at[0, k], (sib, z)))
    locals_.append(pltpu.make_async_copy(tok_ref, toks_ref.at[me], own_sem.at[4]))
    locals_[-1].start()

    def arrived(device, k, sem):
        push(part(device, k), part(device, k), far_send.at[0, 0], sem, (sib, z)).wait_recv()

    def relay(device, k, i):
        go(push(part(device, k), part(device, k), near_send.at[i, k], near_recv.at[i, k], (sib, z)))

    arrived(xn, 0, own_recv.at[0, 0])
    go(push(part(xn, 0), part(xn, 0), far_send.at[2, 0], diag_recv.at[0], (yn, z)))
    relay(xn, 0, 1)
    arrived(yn, 1, own_recv.at[1, 1])
    go(push(part(yn, 1), part(yn, 1), far_send.at[2, 1], diag_recv.at[1], (xn, z)))
    relay(yn, 1, 2)
    arrived(xn, 1, own_recv.at[0, 1])
    relay(xn, 1, 1)
    arrived(yn, 0, own_recv.at[1, 0])
    relay(yn, 0, 2)
    for k in (0, 1):
        arrived(diag, k, diag_recv.at[k])
        relay(diag, k, 3)
    for k in (0, 1):
        for i, device in enumerate((sib, flip(xn, 1), flip(yn, 1), flip(diag, 1))):
            arrived(device, k, near_recv.at[i, k])
    for i, whole in enumerate((heads_ref, wos_ref, packs_ref, parts_ref)):
        for k in range(zs - 1):
            other = lax.rem(z + zs - 1 - k, zs)
            push(whole.at[other], whole.at[other], z_send.at[i, k], z_recv.at[i, k], (me, other)).wait_recv()
    for copy in locals_:
        copy.wait()
    for copy in started:
        copy.wait_send()


def gather(tokens, w_qkv, w_out, w_router, ln_gain, ln_bias, ctx_count, z_count):
    shard, wide = w_qkv.shape
    low = jnp.bfloat16
    outs = [
        (ctx_count,) + tokens.shape, (z_count, shard, 3 * HEAD), (z_count,) + w_out.shape, (z_count, 16, shard),
        (z_count, shard // ctx_count, wide),
    ]
    dma = pltpu.SemaphoreType.DMA
    return pl.pallas_call(
        functools.partial(gather_body, z_count),
        out_shape=[jax.ShapeDtypeStruct(out, low) for out in outs],
        in_specs=[VMEM] * 6,
        out_specs=[ANY] * 5,
        scratch_shapes=[
            pltpu.VMEM((shard, 3 * HEAD), low), pltpu.VMEM((16, shard), low),
            dma((5,)), dma((4, z_count - 1)), dma((4, z_count - 1)), dma((3, 2)), dma((4, 2)), dma((2, 2)), dma((2,)), dma((4, 2)),
        ],
        compiler_params=pltpu.CompilerParams(collective_id=1, has_side_effects=True, vmem_limit_bytes=LIMIT),
        cost_estimate=cost(24),
        name="gather_tokens",
    )(tokens, w_qkv, w_out, w_router, ln_gain[None], ln_bias[None])


def gelu_parts(value):
    square = value * value
    tangent = jnp.tanh(value * (square * (gelu_coef * gelu_cubic) + gelu_coef))
    half = 0.5 * tangent + 0.5
    rise = value * (square * (3.0 * gelu_coef * gelu_cubic) + gelu_coef)
    return value * half, half + half * (1.0 - tangent) * rise


def norm_parts(hidden):
    center = hidden - jnp.mean(hidden, axis=-1, keepdims=True)
    inv_dev = lax.rsqrt(jnp.mean(center * center, axis=-1, keepdims=True) + epsilon)
    return center * inv_dev, inv_dev


def middle_body(
    experts, groups, att_ref, tok_ref, cot_ref, wo_ref, pack_ref, gid_ref, up_ref, down_ref, wq_ref,
    layer_ref, ghidden_ref, gout_ref, small_ref, all_ref, ghead_ref, wqs_ref,
    tok, cot, wo, pack, up, down, att, zsend, zin, bsend, bin_, ghead,
    load_sem, own_sem, a_send, a_recv, m_send, m_recv, b_send, b_recv, g_send, g_recv, r_send, r_recv, h_send, h_recv, w_send, w_recv, v_send, v_recv,
):
    me, z = lax.axis_index("ctx"), lax.axis_index("fsdp")
    count, half = att_ref.shape[0], att_ref.shape[1]
    rows, width = tok_ref.shape
    owners, own_experts = zsend.shape[0], up_ref.shape[0]
    flat, per = experts * groups, experts * groups // owners
    pairs = [(tok_ref, tok), (wo_ref, wo), (pack_ref, pack), (cot_ref, cot)]
    for e in range(own_experts):
        pairs += [(up_ref.at[e], up.at[e]), (down_ref.at[e], down.at[e])]
    loads = [pltpu.make_async_copy(src, dst, load_sem.at[i]) for i, (src, dst) in enumerate(pairs)]
    for copy in loads:
        copy.start()
    sib, same_core = flip(me, 1), [flip(me, 2), flip(me, 4), flip(flip(me, 2), 4)]
    z_peers = [(me, lax.rem(z + k, owners)) for k in range(1, owners)]
    c_peers = [(jnp.bitwise_xor(me, k), z) for k in range(1, count)]
    meet(z_peers + c_peers)

    def start(copies):
        for copy in copies:
            copy.start()
        return copies

    def wait(copies):
        for copy in copies:
            copy.wait()

    swap = start([push(att_ref.at[d[0]], att.at[me], a_send.at[k], a_recv.at[k], d) for k, d in enumerate(c_peers)])
    own = start([pltpu.make_async_copy(att_ref.at[me], att.at[me], own_sem.at[0])])
    small_in = None
    wait(own + swap)
    weights = start([push(wq_ref, wqs_ref.at[me], w_send.at[k], w_recv.at[k], (d, z)) for k, d in enumerate(same_core)])
    shares = start([push(wq_ref, wqs_ref.at[me], v_send.at[3], v_recv.at[3], (sib, z))])
    own_weight = start([pltpu.make_async_copy(wq_ref, wqs_ref.at[me], own_sem.at[3])])
    wait(loads[:4])
    halves = [jnp.concatenate([att[h, :, HEAD * p:HEAD * (p + 1)] for h in range(count)], axis=1) for p in range(2)]
    attended = jnp.concatenate(halves, axis=0)
    weight = wo[...].reshape(width, width)
    hidden = tok[...].astype(jnp.float32) + dot_nn(attended, weight)
    unit, inv_dev = norm_parts(hidden)
    small_in = jnp.concatenate([pack[k] for k in range(owners)], axis=1)
    gain, bias = small_in[experts:experts + 1].astype(jnp.float32), small_in[experts + 1:experts + 2].astype(jnp.float32)
    normed = (unit * gain + bias).astype(jnp.bfloat16)
    expo = jnp.exp(dot_nt(small_in, normed)[:experts])
    expo = jnp.broadcast_to(expo[:, None, :], (experts, groups, rows)).reshape(flat, rows)
    member = lax.rem(lax.broadcasted_iota(jnp.int32, (flat, 1), 0), groups) == lax.rem(gid_ref[...], groups)
    expo = jnp.where(member, expo, 0.0)
    mix = expo / jnp.sum(expo, axis=1, keepdims=True)
    low = mix.astype(jnp.bfloat16)

    def to_owners(kind, value):
        zsend[:, kind] = value.astype(jnp.bfloat16).reshape(owners, per, width)
        zin[z, kind] = zsend[z, kind]
        return start([
            push(zsend.at[d[1], kind], zin.at[z, kind], m_send.at[kind, k], m_recv.at[kind, k], d) for k, d in enumerate(z_peers)
        ])

    mixed_copies = to_owners(0, dot_nn(low, normed))
    grad_experts = dot_nn(low, cot[...])
    wait(loads[4:])
    wait(mixed_copies)
    grad_copies = to_owners(1, grad_experts)

    def from_sources(kind, e):
        return zin[:, kind, e * groups:(e + 1) * groups, :].reshape(owners * groups, width)

    def to_sources(kind, e, value):
        bsend[:, kind, e * groups:(e + 1) * groups, :] = value.astype(jnp.bfloat16).reshape(owners, groups, width)

    def send_back(kind):
        bin_[z, kind] = bsend[z, kind]
        return start([
            push(bsend.at[d[1], kind], bin_.at[z, kind], b_send.at[kind, k], b_recv.at[kind, k], d) for k, d in enumerate(z_peers)
        ])

    slopes = []
    for e in range(own_experts):
        pre = dot_nn(from_sources(0, e), up[e])
        active, slope = gelu_parts(pre)
        slopes.append(slope)
        to_sources(0, e, dot_nn(active.astype(jnp.bfloat16), down[e]))
    out_copies = send_back(0)
    wait(grad_copies)
    gather_copies = start([push(zin, all_ref.at[me], g_send.at[k], g_recv.at[k], (d, z)) for k, d in enumerate(same_core)])
    relays = start([push(zin, all_ref.at[me], r_send.at[0], r_recv.at[0], (sib, z))])
    own = start([pltpu.make_async_copy(zin, all_ref.at[me], own_sem.at[1])])
    for e in range(own_experts):
        grad_pre = (dot_nt(from_sources(1, e), down[e]) * slopes[e]).astype(jnp.bfloat16)
        to_sources(1, e, dot_nt(grad_pre, up[e]))
    back_copies = send_back(1)
    for k, d in enumerate(same_core):
        weights[k].wait_recv()
        shares += start([push(wqs_ref.at[d], wqs_ref.at[d], v_send.at[k], v_recv.at[k], (sib, z))])
    wait(out_copies)
    expert_out = bin_[:, 0].reshape(flat, width)
    layer_ref[...] = hidden + dot_tn(low, expert_out)
    grad_mix = dot_nt(expert_out, cot[...])
    wait(back_copies)
    grad_mixed = bin_[:, 1].reshape(flat, width)
    product = mix * (grad_mix + dot_nt(grad_mixed, normed))
    grad_logits = product - mix * jnp.sum(product, axis=1, keepdims=True)
    grad_logits = jnp.sum(grad_logits.reshape(experts, groups, rows), axis=1).astype(jnp.bfloat16)
    pad = jnp.zeros((small_in.shape[0] - experts, rows), jnp.bfloat16)
    grad_logits = jnp.concatenate([grad_logits, pad], axis=0)
    grad_normed = dot_tn(jnp.concatenate([low, grad_logits], axis=0), jnp.concatenate([grad_mixed, small_in], axis=0))
    scaled = grad_normed * gain
    mean = jnp.mean(scaled, axis=-1, keepdims=True)
    grad_hidden = cot[...].astype(jnp.float32) + inv_dev * (scaled - mean - unit * jnp.mean(scaled * unit, axis=-1, keepdims=True))
    branch = grad_hidden.astype(jnp.bfloat16)
    grad_heads = dot_nt(branch, weight).astype(jnp.bfloat16)
    for h in range(count):
        at = slice(HEAD * h, HEAD * (h + 1))
        ghead[h] = jnp.concatenate([grad_heads[:half, at], grad_heads[half:, at]], axis=1)
    swap = start([push(ghead.at[d[0]], ghead_ref.at[me], h_send.at[k], h_recv.at[k], d) for k, d in enumerate(c_peers)])
    last = start([pltpu.make_async_copy(ghead.at[me], ghead_ref.at[me], own_sem.at[2])])
    for k, d in enumerate(same_core):
        gather_copies[k].wait_recv()
        relays += start([push(all_ref.at[d], all_ref.at[d], r_send.at[k + 1], r_recv.at[k + 1], (sib, z))])
    ghidden_ref[...] = grad_hidden
    gout_ref[...] = dot_tn(attended, branch).astype(jnp.bfloat16).reshape(gout_ref.shape)
    small_ref[...] = jnp.concatenate(
        [
            dot_nn(grad_logits, normed)[:experts],
            jnp.sum(grad_normed * unit, axis=0, keepdims=True),
            jnp.sum(grad_normed, axis=0, keepdims=True),
            jnp.zeros((small_in.shape[0] - experts - 2, width), jnp.float32),
        ],
        axis=0,
    )
    for copy in gather_copies + weights:
        copy.wait_send()
    wait(own + own_weight + last + relays + shares + swap)


def middle(att, tokens, cot, w_out, pack, gid_row, w_up, w_down, parts, experts, groups):
    rows, width = tokens.shape
    count, owners, own = att.shape[0], pack.shape[0], w_up.shape[0]
    sent = (owners, 2, experts * groups // owners, width)
    dma = pltpu.SemaphoreType.DMA
    low, full = jnp.bfloat16, jnp.float32
    return pl.pallas_call(
        functools.partial(middle_body, experts, groups),
        out_shape=(
            jax.ShapeDtypeStruct((rows, width), full),
            jax.ShapeDtypeStruct((rows, width), full),
            jax.ShapeDtypeStruct((owners, width // owners, width), low),
            jax.ShapeDtypeStruct((pack.shape[1], width), full),
            jax.ShapeDtypeStruct((count,) + sent, low),
            jax.ShapeDtypeStruct(att.shape, low),
            jax.ShapeDtypeStruct((count,) + parts.shape, low),
        ),
        in_specs=[ANY] * 5 + [VMEM] + [ANY] * 2 + [VMEM],
        out_specs=(VMEM,) * 4 + (ANY,) * 3,
        scratch_shapes=[pltpu.VMEM(x.shape, x.dtype) for x in (tokens, cot, w_out, pack, w_up, w_down, att)] + [
            pltpu.VMEM(sent, low), pltpu.VMEM(sent, low), pltpu.VMEM(sent, low), pltpu.VMEM(sent, low), pltpu.VMEM(att.shape, low),
            dma((4 + 2 * own,)), dma((4,)), dma((count - 1,)), dma((count - 1,)), dma((2, owners - 1)), dma((2, owners - 1)),
            dma((2, owners - 1)), dma((2, owners - 1)), dma((3,)), dma((3,)), dma((4,)), dma((4,)), dma((count - 1,)),
            dma((count - 1,)), dma((3,)), dma((3,)), dma((4,)), dma((4,)),
        ],
        compiler_params=pltpu.CompilerParams(collective_id=2, has_side_effects=True, vmem_limit_bytes=LIMIT),
        cost_estimate=cost(35),
        name="middle",
    )(att, tokens, cot, w_out, pack, gid_row, w_up, w_down, parts)


def head_columns(ref, p, index=None):
    columns = []
    for kind in range(3):
        at = slice(HEAD * (2 * kind + p), HEAD * (2 * kind + p + 1))
        columns.append(ref[index, :, at])
    return jnp.concatenate(columns, axis=1)


def closing_body(
    owners, grads_ref, toks_ref, small_in_ref, out_ref, weight_ref, ghidden_ref, gathered_ref, up_ref, down_ref,
    gtok_ref, gq_ref, gout_ref, small_ref, act_ref, gpre_ref,
    held_grads, held_toks, held_small, held_weight, held_hidden, held_mixed, held_up, held_down, act_buf, gpre_buf,
    landing, zsend, zone, total_ref, all_ref, out_zone, out_sum, out_part, out_own, out_all,
    load_sem, store_sem, a_send, a_recv, z_send, z_recv, c_send, c_recv, o_send, o_recv,
):
    me, z = lax.axis_index("ctx"), lax.axis_index("fsdp")
    count, half = grads_ref.shape[0], grads_ref.shape[1]
    width = toks_ref.shape[2]
    own_experts, ffn = up_ref.shape[0], up_ref.shape[2]
    pairs = [
        (grads_ref, held_grads), (toks_ref, held_toks), (small_in_ref, held_small), (gathered_ref, held_mixed), (up_ref, held_up),
        (down_ref, held_down), (ghidden_ref, held_hidden),
    ]
    pairs += [(weight_ref.at[c], held_weight.at[:, c]) for c in range(weight_ref.shape[0])]
    loads = [pltpu.make_async_copy(src, dst, load_sem.at[i]) for i, (src, dst) in enumerate(pairs)]
    for copy in loads:
        copy.start()
    z_peers = [(me, lax.rem(z + k, owners)) for k in range(1, owners)]
    c_peers = [(jnp.bitwise_xor(me, k), z) for k in range(1, count)]
    meet(z_peers + c_peers)
    swaps = []
    for k, device in enumerate(c_peers):
        swaps.append(push(grads_ref.at[device[0]], landing.at[me], a_send.at[k], a_recv.at[k], device))
        swaps[-1].start()
    own_swap = pltpu.make_async_copy(grads_ref.at[me], landing.at[me], store_sem.at[0])
    own_swap.start()
    out_copies = []
    for k, device in enumerate(z_peers):
        out_copies.append(push(out_ref.at[device[1]], out_zone.at[z], o_send.at[0, k], o_recv.at[0, k], device))
        out_copies[-1].start()
    own_out = pltpu.make_async_copy(out_ref.at[z], out_zone.at[z], store_sem.at[1])
    own_out.start()

    loads[0].wait()
    loads[1].wait()
    total = None
    for device in range(count):
        for p in range(2):
            part = dot_tn(head_columns(held_grads, p, device), held_toks[device, p * half:(p + 1) * half, :])
            total = part if total is None else total + part
    loads[2].wait()
    lanes = width // owners
    for c in range(owners):
        at = slice(c * lanes, (c + 1) * lanes)
        zsend[c, :3 * HEAD, :] = total[:, at].astype(jnp.bfloat16)
        zsend[c, 3 * HEAD:, :] = held_small[:, at].astype(jnp.bfloat16)
    z_copies = []
    for k, device in enumerate(z_peers):
        z_copies.append(push(zsend.at[device[1]], zone.at[z], z_send.at[k], z_recv.at[k], device))
        z_copies[-1].start()
    zone[z] = zsend[z]
    for i in (3, 4, 5):
        loads[i].wait()

    step = 512

    def expert_part(own_expert):
        mixed = held_mixed[:, 0, own_expert].reshape(-1, width)
        grad_out = held_mixed[:, 1, own_expert].reshape(-1, width)

        def chunk(i, carry):
            at = pl.ds(pl.multiple_of(i * step, step), step)
            pre = dot_nn(mixed, held_up[own_expert, :, at])
            active, slope = gelu_parts(pre)
            act_buf[own_expert, :, at] = active.astype(jnp.bfloat16)
            gpre_buf[own_expert, :, at] = (dot_nt(grad_out, held_down[own_expert, at, :]) * slope).astype(jnp.bfloat16)
            return carry

        lax.fori_loop(0, ffn // step, chunk, 0)
        stores = [
            pltpu.make_async_copy(act_buf.at[own_expert], act_ref.at[own_expert], store_sem.at[2 + 2 * own_expert]),
            pltpu.make_async_copy(gpre_buf.at[own_expert], gpre_ref.at[own_expert], store_sem.at[3 + 2 * own_expert]),
        ]
        for copy in stores:
            copy.start()
        return stores

    stores = expert_part(0)
    for copy in z_copies:
        copy.wait()
    total = zone[0].astype(jnp.float32)
    for k in range(1, owners):
        total = total + zone[k].astype(jnp.float32)
    total_ref[...] = total.astype(jnp.bfloat16)
    c_copies = []
    for k, device in enumerate(c_peers):
        c_copies.append(push(total_ref, all_ref.at[me], c_send.at[k], c_recv.at[k], device))
        c_copies[-1].start()
    all_ref[me] = total_ref[...]
    own_out.wait()
    for copy in out_copies:
        copy.wait()
    total = out_zone[0].astype(jnp.float32)
    for k in range(1, owners):
        total = total + out_zone[k].astype(jnp.float32)
    per = lanes // count
    out_sum[...] = total.astype(jnp.bfloat16).reshape(out_sum.shape)
    part_copies = []
    for k, device in enumerate(c_peers):
        part_copies.append(push(out_sum.at[device[0]], out_part.at[me], o_send.at[1, k], o_recv.at[1, k], device))
        part_copies[-1].start()
    out_part[me] = out_sum[me]
    for own_expert in range(1, own_experts):
        stores += expert_part(own_expert)
    for copy in part_copies:
        copy.wait()
    total = out_part[0].astype(jnp.float32)
    for k in range(1, count):
        total = total + out_part[k].astype(jnp.float32)
    out_own[...] = total.astype(jnp.bfloat16)
    last_copies = []
    for k, device in enumerate(c_peers):
        last_copies.append(push(out_own, out_all.at[me], o_send.at[2, k], o_recv.at[2, k], device))
        last_copies[-1].start()
    out_all[me] = out_own[...]
    for copy in loads[6:]:
        copy.wait()
    own_swap.wait()
    for copy in swaps:
        copy.wait()
    weight = held_weight[...].reshape(width, -1)
    for p in range(2):
        columns = [landing[h, :, HEAD * (2 * kind + p):HEAD * (2 * kind + p + 1)] for kind in range(3) for h in range(count)]
        at = slice(p * half, (p + 1) * half)
        gtok_ref[at, :] = held_hidden[at, :] + dot_nt(jnp.concatenate(columns, axis=1), weight)
    for copy in c_copies:
        copy.wait()
    small = None
    turned = []
    for c in range(count):
        turned.append(all_ref[c, :3 * HEAD, :].astype(jnp.float32).T)
        part = all_ref[c, 3 * HEAD:, :].astype(jnp.float32)
        small = part if small is None else small + part
    small_ref[...] = small
    for kind in range(3):
        at = slice(HEAD * kind, HEAD * (kind + 1))
        gq_ref[:, HEAD * count * kind:HEAD * count * (kind + 1)] = jnp.concatenate([part[:, at] for part in turned], axis=1)
    for copy in last_copies:
        copy.wait()
    gout_ref[...] = out_all[...].astype(jnp.float32).reshape(gout_ref.shape)
    for copy in stores:
        copy.wait()


def closing(grads, tokens_all, small, gout, weight, ghidden, gathered, w_up, w_down, groups, owners):
    count, width = tokens_all.shape[0], tokens_all.shape[2]
    lanes = width // owners
    height = 3 * HEAD + small.shape[0]
    own_experts, _, ffn = w_up.shape
    sources = gathered.shape[0]
    view = gathered.reshape(sources, 2, own_experts, groups, width)
    wide = (own_experts, sources * groups, ffn)
    dma = pltpu.SemaphoreType.DMA
    held = [grads, tokens_all, small, weight, ghidden, view, w_up, w_down]
    part = (count, lanes // count, width)
    return pl.pallas_call(
        functools.partial(closing_body, owners),
        out_shape=(
            jax.ShapeDtypeStruct(ghidden.shape, jnp.float32),
            jax.ShapeDtypeStruct((lanes, 3 * width), jnp.float32),
            jax.ShapeDtypeStruct((lanes, width), jnp.float32),
            jax.ShapeDtypeStruct((small.shape[0], lanes), jnp.float32),
            jax.ShapeDtypeStruct(wide, jnp.bfloat16),
            jax.ShapeDtypeStruct(wide, jnp.bfloat16),
        ),
        in_specs=[ANY] * 9,
        out_specs=(VMEM,) * 4 + (ANY,) * 2,
        scratch_shapes=[pltpu.VMEM(x.shape, x.dtype) for x in held[:3]]
        + [pltpu.VMEM((owners, count) + weight.shape[2:], jnp.bfloat16)]
        + [pltpu.VMEM(x.shape, x.dtype) for x in held[4:]] + [
            pltpu.VMEM(wide, jnp.bfloat16), pltpu.VMEM(wide, jnp.bfloat16), pltpu.VMEM(grads.shape, jnp.bfloat16),
            pltpu.VMEM((owners, height, lanes), jnp.bfloat16), pltpu.VMEM((owners, height, lanes), jnp.bfloat16),
            pltpu.VMEM((height, lanes), jnp.bfloat16), pltpu.VMEM((count, height, lanes), jnp.bfloat16),
            pltpu.VMEM(gout.shape, jnp.bfloat16), pltpu.VMEM(part, jnp.bfloat16), pltpu.VMEM(part, jnp.bfloat16),
            pltpu.VMEM(part[1:], jnp.bfloat16), pltpu.VMEM(part, jnp.bfloat16),
            dma((7 + count,)), dma((2 + 2 * own_experts,)), dma((count - 1,)), dma((count - 1,)), dma((owners - 1,)), dma((owners - 1,)),
            dma((count - 1,)), dma((count - 1,)), dma((3, count - 1)), dma((3, count - 1)),
        ],
        compiler_params=pltpu.CompilerParams(collective_id=6, has_side_effects=True, vmem_limit_bytes=LIMIT),
        cost_estimate=cost(28),
        name="closing",
    )(*held[:3], gout, *held[3:])


def expert_grad_body(experts, passed, mixed_ref, grad_ref, act_ref, gpre_ref, small_ref, *refs):
    sources, outs = refs[:passed], refs[passed + 5:]
    gup_ref, gdown_ref, router_ref, gain_ref, bias_ref = refs[passed:passed + 5]
    width = gup_ref.shape[1]
    for source, out in zip(sources, outs):
        out[...] = source[...]
    router_ref[...] = small_ref[:experts].T
    gain_ref[...] = small_ref[experts:experts + 1]
    bias_ref[...] = small_ref[experts + 1:experts + 2]
    gup_ref[0] = dot_tn(mixed_ref[...].reshape(-1, width), gpre_ref[0])
    gdown_ref[0] = dot_tn(act_ref[0], grad_ref[...].reshape(-1, width))


def expert_grads(gathered, active, grad_pre, small, passed, groups, experts):
    own, rows, ffn = active.shape
    step = 512
    steps = ffn // step
    sources, width = gathered.shape[0], gathered.shape[3]
    view = gathered.reshape(sources, 2, own, groups, width)
    lanes = small.shape[1]
    full = jnp.float32
    slices = [pl.BlockSpec((x.shape[0] // (own * steps), x.shape[1]), lambda e, f: (e * steps + f, 0)) for x in passed]
    return pl.pallas_call(
        functools.partial(expert_grad_body, experts, len(passed)),
        grid=(own, steps),
        out_shape=[
            jax.ShapeDtypeStruct((own, width, ffn), full), jax.ShapeDtypeStruct((own, ffn, width), full),
            jax.ShapeDtypeStruct((lanes, experts), full), jax.ShapeDtypeStruct((1, lanes), full), jax.ShapeDtypeStruct((1, lanes), full),
        ] + [jax.ShapeDtypeStruct(x.shape, x.dtype) for x in passed],
        in_specs=[
            pl.BlockSpec((sources, 1, 1, groups, width), lambda e, f: (0, 0, e, 0, 0)),
            pl.BlockSpec((sources, 1, 1, groups, width), lambda e, f: (0, 1, e, 0, 0)),
            pl.BlockSpec((1, rows, step), lambda e, f: (e, 0, f)),
            pl.BlockSpec((1, rows, step), lambda e, f: (e, 0, f)),
            pl.BlockSpec(small.shape, lambda e, f: (0, 0)),
        ] + slices,
        out_specs=[
            pl.BlockSpec((1, width, step), lambda e, f: (e, 0, f)), pl.BlockSpec((1, step, width), lambda e, f: (e, f, 0)),
            pl.BlockSpec((lanes, experts), lambda e, f: (0, 0)), pl.BlockSpec((1, lanes), lambda e, f: (0, 0)),
            pl.BlockSpec((1, lanes), lambda e, f: (0, 0)),
        ] + slices,
        compiler_params=pltpu.CompilerParams(vmem_limit_bytes=LIMIT),
        cost_estimate=cost(10),
        name="expert_grads",
    )(view, view, active, grad_pre, small, *passed)


def fast_device(
    tokens, cotangent, block_table, seg_ids, group_ids, w_qkv, w_out, w_router, ln_gain, ln_bias, w_up, w_down
):
    ctx_count, z_count = lax.axis_size("ctx"), lax.axis_size("fsdp")
    tok_rows, cot_rows = tokens[0], cotangent[0]
    rows, width = tok_rows.shape
    experts = w_router.shape[1]
    groups = rows // GROUP_SIZE
    segs = seg_ids[0].reshape(block_table.shape[0], -1)
    tokens_all, head_weights, out_full, pack_full, qkv_parts = gather(
        tok_rows, w_qkv, w_out, w_router, ln_gain, ln_bias, ctx_count, z_count
    )
    att, *saved = attn_fwd(tokens_all.reshape(ctx_count * rows, width), head_weights, block_table, segs)
    layer_out, grad_hidden, gout, small, gathered, grad_heads, qkv_full = middle(
        att, tok_rows, cot_rows, out_full, pack_full, group_ids, w_up, w_down, qkv_parts, experts, groups
    )
    gathered = gathered.reshape((ctx_count * z_count,) + gathered.shape[2:])
    grads = attn_bwd(grad_heads, saved, block_table, segs)
    grad_tokens, grad_qkv, grad_out, small, active, grad_pre = closing(
        grads, tokens_all, small, gout, qkv_full, grad_hidden, gathered, w_up, w_down, groups, z_count
    )
    grad_up, grad_down, grad_router, grad_gain, grad_bias, layer_out, grad_tokens, grad_qkv, grad_out = expert_grads(
        gathered, active, grad_pre, small, [layer_out, grad_tokens, grad_qkv, grad_out], groups, experts
    )
    return (
        layer_out[None],
        grad_tokens[None],
        grad_qkv,
        grad_out,
        grad_router,
        grad_gain[0],
        grad_bias[0],
        grad_up,
        grad_down,
    )


def solution(mesh):
    placed = (
        P("fsdp", "ctx", None),
        P("fsdp", "ctx", None),
        P(),
        P("fsdp", None),
        P("fsdp", "ctx"),
        P("fsdp", None),
        P("fsdp", None),
        P("fsdp", None),
        P("fsdp"),
        P("fsdp"),
        P("fsdp", None, None),
        P("fsdp", None, None),
    )
    step = fast_device if mesh.shape["ctx"] == HEADS else on_device
    return jax.shard_map(
        step,
        mesh=mesh,
        in_specs=placed,
        out_specs=(
            P("fsdp", "ctx", None),
            P("fsdp", "ctx", None),
            P("fsdp", None),
            P("fsdp", None),
            P("fsdp", None),
            P("fsdp"),
            P("fsdp"),
            P("fsdp", None, None),
            P("fsdp", None, None),
        ),
        check_vma=False,
    )
```

```python
import functools

import jax
import jax.numpy as jnp
from jax import lax
from jax.experimental import pallas as pl
from jax.experimental.pallas import tpu as pltpu
from jax.sharding import PartitionSpec as P

HEADS = 8
HEAD = 64
GROUP_SIZE = 32
KEY_BLOCK = 2048


highest = lax.Precision.HIGHEST
neg_large = -1e30
epsilon = 1e-05
gelu_coef = 0.7978845608028654
gelu_cubic = 0.044715


def contract_rows(left, right):
    return lax.dot_general(
        left, right, (((0,), (0,)), ((), ())), preferred_element_type=jnp.float32
    )


def contract_cols(left, right):
    return lax.dot_general(
        left, right, (((1,), (1,)), ((), ())), preferred_element_type=jnp.float32
    )


def gelu_slope(value):
    inner = gelu_coef * (value + gelu_cubic * value * value * value)
    tangent = jnp.tanh(inner)
    return 0.5 * (1.0 + tangent) + 0.5 * value * (1.0 - tangent * tangent) * gelu_coef * (
        1.0 + 3.0 * gelu_cubic * value * value
    )


def expert_forward(mixed_low, up_weight, down_weight):
    pre = jnp.einsum("ged,edh->geh", mixed_low, up_weight, preferred_element_type=jnp.float32)
    active = jax.nn.gelu(pre, approximate=True).astype(jnp.bfloat16)
    result = jnp.einsum("geh,ehd->ged", active, down_weight, preferred_element_type=jnp.float32)
    return (pre, active, result.astype(jnp.bfloat16))


def expert_backward(mixed_low, pre, active, grad_result, up_weight, down_weight):
    grad_act = jnp.einsum(
        "ged,ehd->geh", grad_result, down_weight, preferred_element_type=jnp.float32
    )
    grad_pre = (grad_act * gelu_slope(pre)).astype(jnp.bfloat16)
    grad_down_part = jnp.einsum(
        "geh,ged->ehd", active, grad_result, preferred_element_type=jnp.float32
    )
    grad_up_part = jnp.einsum(
        "ged,geh->edh", mixed_low, grad_pre, preferred_element_type=jnp.float32
    )
    grad_mixed = jnp.einsum("geh,edh->ged", grad_pre, up_weight, preferred_element_type=jnp.float32)
    return (grad_up_part, grad_down_part, grad_mixed.astype(jnp.bfloat16))


def on_device(
    tokens,
    cotangent,
    block_table,
    seg_ids,
    group_ids,
    w_qkv,
    w_out,
    w_router,
    ln_gain,
    ln_bias,
    w_up,
    w_down,
):
    tok_rows = tokens[0]
    tok_count = tok_rows.shape[0]
    width = tok_rows.shape[1]
    expert_count = w_router.shape[1]
    ctx_index = lax.axis_index("ctx")
    full_rows = seg_ids.shape[1]
    block_len = full_rows // block_table.shape[0]
    row_ids = jnp.arange(full_rows, dtype=jnp.int32)
    key_pos = jnp.take(block_table, row_ids // block_len) * block_len + row_ids % block_len
    key_seg = seg_ids[0]
    pos_rows = lax.dynamic_slice_in_dim(key_pos, ctx_index * tok_count, tok_count)
    seg_rows = lax.dynamic_slice_in_dim(key_seg, ctx_index * tok_count, tok_count)
    scale = HEAD ** (-0.5)
    qkv_full, out_full, router_full, gain_full, bias_full = (
        lax.all_gather(w_qkv, "fsdp", axis=0, tiled=True),
        lax.all_gather(w_out, "fsdp", axis=0, tiled=True),
        lax.all_gather(w_router, "fsdp", axis=0, tiled=True),
        lax.all_gather(ln_gain, "fsdp", axis=0, tiled=True),
        lax.all_gather(ln_bias, "fsdp", axis=0, tiled=True),
    )
    qkv = jnp.dot(tok_rows, qkv_full, preferred_element_type=jnp.float32).astype(jnp.bfloat16)
    query_heads = qkv[:, :width].reshape(tok_count, HEADS, HEAD)
    key_all, val_all = (
        lax.all_gather(qkv[:, width : 2 * width], "ctx", axis=0, tiled=True),
        lax.all_gather(qkv[:, 2 * width :], "ctx", axis=0, tiled=True),
    )
    key_heads = key_all.reshape(full_rows, HEADS, HEAD)
    val_heads = val_all.reshape(full_rows, HEADS, HEAD)
    block_count = full_rows // KEY_BLOCK
    block_ids = jnp.arange(block_count, dtype=jnp.int32)

    def block_scores(index):
        start = index * KEY_BLOCK
        key_block = lax.dynamic_slice_in_dim(key_heads, start, KEY_BLOCK, 0)
        val_block = lax.dynamic_slice_in_dim(val_heads, start, KEY_BLOCK, 0)
        pos_block = lax.dynamic_slice_in_dim(key_pos, start, KEY_BLOCK, 0)
        seg_block = lax.dynamic_slice_in_dim(key_seg, start, KEY_BLOCK, 0)
        scores = (
            jnp.einsum("qhd,khd->hqk", query_heads, key_block, preferred_element_type=jnp.float32)
            * scale
        )
        allowed = (pos_block[None, :] <= pos_rows[:, None]) & (
            (seg_block[None, :] == 0) | (seg_block[None, :] == seg_rows[:, None])
        )
        return (scores, allowed[None], key_block, val_block)

    def lse_step(carry, index):
        top, total = carry
        scores, allowed, key_block, val_block = block_scores(index)
        masked = jnp.where(allowed, scores, neg_large)
        new_top = jnp.maximum(top, jnp.max(masked, axis=-1))
        weights = jnp.where(allowed, jnp.exp(masked - new_top[..., None]), 0.0)
        return ((new_top, total * jnp.exp(top - new_top) + jnp.sum(weights, axis=-1)), None)

    start_top = jnp.full((HEADS, tok_count), neg_large, jnp.float32)
    (top, total), unused = lax.scan(
        lse_step, (start_top, jnp.zeros((HEADS, tok_count), jnp.float32)), block_ids
    )
    log_total = top + jnp.log(total)

    def block_probs(index):
        scores, allowed, key_block, val_block = block_scores(index)
        probs = jnp.where(allowed, jnp.exp(scores - log_total[..., None]), 0.0)
        return (probs, key_block, val_block)

    def value_step(accum, index):
        probs, key_block, val_block = block_probs(index)
        return (
            accum
            + jnp.einsum(
                "hqk,khd->qhd",
                probs.astype(jnp.bfloat16),
                val_block,
                preferred_element_type=jnp.float32,
            ),
            None,
        )

    accum, unused = lax.scan(
        value_step, jnp.zeros((tok_count, HEADS, HEAD), jnp.float32), block_ids
    )
    attended = accum.reshape(tok_count, width).astype(jnp.bfloat16)
    hidden = tok_rows.astype(jnp.float32) + jnp.dot(
        attended, out_full, preferred_element_type=jnp.float32
    )
    center = hidden - jnp.mean(hidden, axis=-1, keepdims=True)
    inv_dev = lax.rsqrt(jnp.mean(center * center, axis=-1, keepdims=True) + epsilon)
    unit = center * inv_dev
    gain_f = gain_full.astype(jnp.float32)
    normed_low = (unit * gain_f + bias_full.astype(jnp.float32)).astype(jnp.bfloat16)
    logits = jnp.dot(normed_low, router_full, preferred_element_type=jnp.float32)
    groups_dev = tok_count // GROUP_SIZE
    local_group = group_ids[0] - ctx_index * groups_dev
    member = (local_group[:, None] == jnp.arange(groups_dev, dtype=jnp.int32)[None, :]).astype(
        jnp.float32
    )
    expo = jnp.exp(logits)
    group_total = jnp.dot(member.T, expo, precision=highest)
    mix_weights = expo / jnp.dot(member, group_total, precision=highest)
    weights_low = mix_weights.astype(jnp.bfloat16)
    mixing = member.astype(jnp.bfloat16).T[:, None, :] * weights_low.T[None, :, :]
    mixing_flat = mixing.reshape(groups_dev * expert_count, tok_count)
    mixed_low = jnp.dot(mixing_flat, normed_low, preferred_element_type=jnp.float32).astype(
        jnp.bfloat16
    )
    mixed_low = mixed_low.reshape(groups_dev, expert_count, width)
    owner_mixed = lax.all_to_all(mixed_low, "fsdp", split_axis=1, concat_axis=0, tiled=True)
    pre, active, owner_out = expert_forward(owner_mixed, w_up, w_down)
    expert_out = lax.all_to_all(owner_out, "fsdp", split_axis=0, concat_axis=1, tiled=True)
    expert_flat = expert_out.reshape(groups_dev * expert_count, width)
    spread = contract_rows(mixing_flat, expert_flat)
    layer_out = hidden + spread
    cot_rows = cotangent[0]
    cot_f = cot_rows.astype(jnp.float32)
    grad_expert = jnp.dot(mixing_flat, cot_rows, preferred_element_type=jnp.float32).astype(
        jnp.bfloat16
    )
    grad_expert = grad_expert.reshape(groups_dev, expert_count, width)
    coef = contract_cols(cot_rows, expert_flat).reshape(tok_count, groups_dev, expert_count)
    grad_mix_spread = jnp.sum(coef * member[:, :, None], axis=1)
    owner_grad = lax.all_to_all(grad_expert, "fsdp", split_axis=1, concat_axis=0, tiled=True)
    grad_up_own, grad_down_own, owner_back = expert_backward(
        owner_mixed, pre, active, owner_grad, w_up, w_down
    )
    grad_mixed = lax.all_to_all(owner_back, "fsdp", split_axis=0, concat_axis=1, tiled=True)
    grad_mixed_flat = grad_mixed.reshape(groups_dev * expert_count, width)
    grad_norm_mix = contract_rows(mixing_flat, grad_mixed_flat)
    grad_mixing = contract_cols(grad_mixed_flat, normed_low).reshape(
        groups_dev, expert_count, tok_count
    )
    grad_mix_mixing = jnp.sum(grad_mixing * member.T[:, None, :], axis=0).T
    grad_mix = grad_mix_spread + grad_mix_mixing
    product = mix_weights * grad_mix
    token_dot = jnp.dot(member, jnp.dot(member.T, product, precision=highest), precision=highest)
    grad_logits = (product - mix_weights * token_dot).astype(jnp.bfloat16)
    grad_router_part = contract_rows(normed_low, grad_logits)
    grad_norm_router = contract_cols(grad_logits, router_full)
    grad_normed = grad_norm_mix + grad_norm_router
    grad_gain_part = jnp.sum(grad_normed * unit, axis=0)
    grad_bias_part = jnp.sum(grad_normed, axis=0)
    scaled = grad_normed * gain_f
    grad_hidden = cot_f + inv_dev * (
        scaled
        - jnp.mean(scaled, axis=-1, keepdims=True)
        - unit * jnp.mean(scaled * unit, axis=-1, keepdims=True)
    )
    grad_branch = grad_hidden.astype(jnp.bfloat16)
    grad_out_part = contract_rows(attended, grad_branch)
    grad_heads = (
        contract_cols(grad_branch, out_full).astype(jnp.bfloat16).reshape(tok_count, HEADS, HEAD)
    )
    delta = jnp.sum(grad_heads.astype(jnp.float32) * accum, axis=-1).T

    def grad_step(grad_query, index):
        probs, key_block, val_block = block_probs(index)
        grad_probs = jnp.einsum(
            "qhd,khd->hqk", grad_heads, val_block, preferred_element_type=jnp.float32
        )
        grad_scores = (probs * (grad_probs - delta[..., None])).astype(jnp.bfloat16)
        grad_query = (
            grad_query
            + jnp.einsum("hqk,khd->qhd", grad_scores, key_block, preferred_element_type=jnp.float32)
            * scale
        )
        grad_key = (
            jnp.einsum("hqk,qhd->khd", grad_scores, query_heads, preferred_element_type=jnp.float32)
            * scale
        )
        grad_val = jnp.einsum(
            "hqk,qhd->khd",
            probs.astype(jnp.bfloat16),
            grad_heads,
            preferred_element_type=jnp.float32,
        )
        return (grad_query, (grad_key, grad_val))

    grad_query, (grad_keys, grad_vals) = lax.scan(
        grad_step, jnp.zeros((tok_count, HEADS, HEAD), jnp.float32), block_ids
    )
    grad_key_own, grad_val_own = (
        lax.psum_scatter(
            grad_keys.reshape(full_rows, width), "ctx", scatter_dimension=0, tiled=True
        ),
        lax.psum_scatter(
            grad_vals.reshape(full_rows, width), "ctx", scatter_dimension=0, tiled=True
        ),
    )
    grad_qkv_low = jnp.concatenate(
        [grad_query.reshape(tok_count, width), grad_key_own, grad_val_own], axis=1
    ).astype(jnp.bfloat16)
    grad_qkv_part = contract_rows(tok_rows, grad_qkv_low)
    grad_tokens = grad_hidden + contract_cols(grad_qkv_low, qkv_full)
    dense = (
        lax.psum_scatter(grad_qkv_part, "fsdp", scatter_dimension=0, tiled=True),
        lax.psum_scatter(grad_out_part, "fsdp", scatter_dimension=0, tiled=True),
        lax.psum_scatter(grad_router_part, "fsdp", scatter_dimension=0, tiled=True),
        lax.psum_scatter(grad_gain_part, "fsdp", scatter_dimension=0, tiled=True),
        lax.psum_scatter(grad_bias_part, "fsdp", scatter_dimension=0, tiled=True),
    )
    totals = lax.psum(
        (dense[0], dense[1], dense[2], dense[3], dense[4], grad_up_own, grad_down_own), "ctx"
    )
    return (
        layer_out[None],
        grad_tokens[None],
        totals[0],
        totals[1],
        totals[2],
        totals[3],
        totals[4],
        totals[5],
        totals[6],
    )


def cost(microseconds):
    return pl.CostEstimate(flops=int(microseconds * 1.15e9), bytes_accessed=1 << 20, transcendentals=0)


LOG2E = 1.4426950408889634
HIDE = -1e30
SAFE = 100.0
RUN = 1024
HALF = 512
VMEM = pl.BlockSpec(memory_space=pltpu.VMEM)
SMEM = pl.BlockSpec(memory_space=pltpu.SMEM)
ANY = pl.BlockSpec(memory_space=pl.ANY)
LIMIT = 60 << 20


def dot_nn(left, right):
    return lax.dot_general(left, right, (((1,), (0,)), ((), ())), preferred_element_type=jnp.float32)


def dot_nt(left, right):
    return lax.dot_general(left, right, (((1,), (1,)), ((), ())), preferred_element_type=jnp.float32)


def dot_tn(left, right):
    return lax.dot_general(left, right, (((0,), (0,)), ((), ())), preferred_element_type=jnp.float32)


def split3(value):
    one = value.astype(jnp.bfloat16)
    rest = value - one.astype(jnp.float32)
    two = rest.astype(jnp.bfloat16)
    three = (rest - two.astype(jnp.float32)).astype(jnp.bfloat16)
    return one, two, three


def span(index, size, width=None):
    return pl.ds(pl.multiple_of(index * size, size), size if width is None else width)


def flipped(value):
    return value.astype(jnp.float32).T.astype(value.dtype)


def boundaries(seg_ref, lane):
    segs = seg_ref[...]
    begin = jnp.zeros(lane.shape, jnp.int32)
    end = jnp.zeros(lane.shape, jnp.int32)
    for c in range(1, 10):
        below = (segs < c).astype(jnp.int32)
        total = jnp.sum(jnp.sum(below, axis=1, keepdims=True), axis=0, keepdims=True)
        begin = jnp.where(lane == HEAD - 1 + c, total, begin)
        end = jnp.where(lane == HEAD - 2 + c, total, end)
    return begin, jnp.where(lane == HEAD + 8, 0, end)


def fwd_body(blocks, block_len, table_ref, tok_ref, w_ref, seg_ref, att_ref, qf_ref, kf_ref, vf_ref, stat_ref, vt_ref, inv_ref):
    rows = blocks * block_len
    for t in range(blocks):
        inv_ref[table_ref[t]] = t
    weight = w_ref[...].reshape(w_ref.shape[0] * w_ref.shape[1], w_ref.shape[2])
    weight = jnp.concatenate([weight, jnp.zeros((weight.shape[0], HEAD), weight.dtype)], axis=1)
    lane = lax.broadcasted_iota(jnp.int32, (1, 2 * HEAD), 1)
    begin, end = boundaries(seg_ref, lane)
    is_flag = (lane >= HEAD) & (lane < HEAD + 8)
    is_one = (lane >= HEAD + 8) & (lane < HEAD + 11)
    pair = (lax.broadcasted_iota(jnp.int32, (2 * HEAD, 2 * HEAD), 0) // HEAD == lane // HEAD).astype(jnp.bfloat16)
    ones_v = ((lane >= HEAD) & (lane < HEAD + 3)).astype(jnp.float32)

    def project(s, sizes):
        t = inv_ref[s]
        qkv = dot_nn(tok_ref[span(t, block_len), :], weight)
        both = qkv[:, :2 * HEAD].astype(jnp.bfloat16).astype(jnp.float32)
        turned = pltpu.roll(both, HEAD, 1)
        value = qkv[:, 2 * HEAD:]
        place = lax.broadcasted_iota(jnp.int32, (block_len, 2 * HEAD), 0) + s * block_len
        own = (place >= begin) & (place < end)
        at = span(s, block_len)
        flag_q = jnp.where(is_flag & jnp.logical_not(own), 1.0, 0.0)
        flag_k = jnp.where(own, HIDE, jnp.where(is_one, 1.0, 0.0))
        qf_ref[at, :] = jnp.where(lane < HEAD, both, flag_q).astype(jnp.bfloat16)
        kf_ref[at, :] = jnp.where(lane < HEAD, turned, flag_k).astype(jnp.bfloat16)
        vf_ref[at, :] = (value + ones_v).astype(jnp.bfloat16)
        vt_ref[:, at] = jnp.where(lane < HEAD, value, 1.0).T.astype(jnp.bfloat16)
        return jnp.maximum(sizes, dot_nn((both * both).astype(jnp.bfloat16), pair))

    sizes = lax.fori_loop(0, blocks, project, jnp.zeros((block_len, 2 * HEAD), jnp.float32), unroll=4)
    scale = HEAD ** (-0.5) * LOG2E
    q_size, k_size = jnp.max(sizes[:, :HEAD]), jnp.max(sizes[:, HEAD:])
    small = q_size * k_size <= (SAFE / scale) ** 2
    causal = lax.broadcasted_iota(jnp.int32, (HALF, HALF), 0) <= lax.broadcasted_iota(jnp.int32, (HALF, HALF), 1)

    def query_run(online, run):
        def tile(state, q_at, k_at, diagonal):
            scores = dot_nt(kf_ref[k_at, :], qf_ref[q_at, :]) * scale
            if diagonal:
                scores = jnp.where(causal, scores, HIDE)
            top, acc = state
            if online:
                new_top = jnp.maximum(top, jnp.max(scores, axis=0, keepdims=True))
                acc = acc * jnp.exp2(top - new_top)
                scores, top = scores - new_top, new_top
            return top, acc + dot_nn(vt_ref[:, k_at], jnp.exp2(scores).astype(jnp.bfloat16))

        start = (jnp.full((1, RUN), HIDE if online else 0.0, jnp.float32), jnp.zeros((2 * HEAD, RUN), jnp.float32))
        whole = lax.fori_loop(0, run, lambda n, state: tile(state, span(run, RUN), span(n, RUN), False), start)
        early, late = span(2 * run, HALF), span(2 * run + 1, HALF)
        first = tile([part[:, :HALF] for part in whole], early, early, True)
        second = tile([part[:, HALF:] for part in whole], late, early, False)
        second = tile(second, late, late, True)
        for at, (top, acc) in ((early, first), (late, second)):
            total = acc[HEAD:]
            stat = jnp.concatenate([acc[:HEAD] / total, top + jnp.log2(total)], axis=0).T
            stat_ref[at, :] = stat
            one, two, three = split3(stat * (-1.0 / scale))
            old = qf_ref[at, :]
            old = jnp.where(lane == HEAD + 8, one, old)
            old = jnp.where(lane == HEAD + 9, two, old)
            qf_ref[at, :] = jnp.where(lane == HEAD + 10, three, old)

    for online in (False, True):
        @pl.when(small != online)
        def _():
            @pl.loop(0, rows // RUN)
            def _(run):
                query_run(online, run)

    for c in range(blocks // 2):
        parts = [stat_ref[span(table_ref[2 * c + half], block_len), :HEAD] for half in range(2)]
        att_ref[c] = jnp.concatenate(parts, axis=1).astype(jnp.bfloat16)


def attn_fwd(tokens_all, weight, table, segs):
    rows, blocks = tokens_all.shape[0], table.shape[0]
    block_len = rows // blocks
    low = jnp.bfloat16
    return pl.pallas_call(
        functools.partial(fwd_body, blocks, block_len),
        out_shape=(
            jax.ShapeDtypeStruct((blocks // 2, block_len, 2 * HEAD), low),
            jax.ShapeDtypeStruct((rows, 2 * HEAD), low),
            jax.ShapeDtypeStruct((rows, 2 * HEAD), low),
            jax.ShapeDtypeStruct((rows, 2 * HEAD), low),
            jax.ShapeDtypeStruct((rows, 2 * HEAD), jnp.float32),
        ),
        in_specs=[SMEM, VMEM, VMEM, VMEM],
        out_specs=(VMEM,) * 5,
        scratch_shapes=[pltpu.VMEM((2 * HEAD, rows), low), pltpu.SMEM((blocks,), jnp.int32)],
        compiler_params=pltpu.CompilerParams(vmem_limit_bytes=LIMIT),
        cost_estimate=cost(30),
        name="attention",
    )(table, tokens_all, weight, segs)


MESH = pl.DeviceIdType.MESH


def flip(index, bit):
    return index + bit - 2 * bit * lax.rem(index // bit, 2)


def meet(devices):
    barrier = pltpu.get_barrier_semaphore()
    for device in devices:
        pl.semaphore_signal(barrier, inc=1, device_id=device, device_id_type=MESH)
    pl.semaphore_wait(barrier, len(devices))


def push(src, dst, send_sem, recv_sem, device):
    return pltpu.make_async_remote_copy(
        src_ref=src, dst_ref=dst, send_sem=send_sem, recv_sem=recv_sem, device_id=device, device_id_type=MESH
    )


def gather_body(
    zs, tok_ref, wq_ref, wo_ref, router_ref, gain_ref, bias_ref, toks_ref, heads_ref, wos_ref, packs_ref, parts_ref,
    head_buf, pack_buf, own_sem, z_send, z_recv, far_send, near_send, own_recv, diag_recv, near_recv,
):
    me, z = lax.axis_index("ctx"), lax.axis_index("fsdp")
    sib, xn, yn, diag = flip(me, 1), flip(me, 2), flip(me, 4), flip(flip(me, 2), 4)
    z_peers = [lax.rem(z + k, zs) for k in range(1, zs)]
    meet([(sib, z), (xn, z), (yn, z)] + [(me, other) for other in z_peers])
    half = tok_ref.shape[0] // 2
    count = toks_ref.shape[0]

    def part(device, k):
        return toks_ref.at[device, pl.ds(k * half, half)]

    started, locals_ = [], []

    def go(copy):
        copy.start()
        started.append(copy)

    for k in (0, 1):
        rows = tok_ref.at[pl.ds(k * half, half)]
        go(push(rows, part(me, k), far_send.at[0, k], own_recv.at[0, k], (xn, z)))
        rows = tok_ref.at[pl.ds((1 - k) * half, half)]
        go(push(rows, part(me, 1 - k), far_send.at[1, 1 - k], own_recv.at[1, 1 - k], (yn, z)))

    def share(i, shard, whole):
        for k, other in enumerate(z_peers):
            go(push(shard, whole.at[z], z_send.at[i, k], z_recv.at[i, k], (me, other)))
        locals_.append(pltpu.make_async_copy(shard, whole.at[z], own_sem.at[i]))
        locals_[-1].start()

    depth = wq_ref.shape[0] // count
    width = wq_ref.shape[1] // 3
    for h in range(count):
        @pl.when(me == h)
        def _():
            cols = [wq_ref[:, width * kind + HEAD * h:width * kind + HEAD * (h + 1)] for kind in range(3)]
            head_buf[...] = jnp.concatenate(cols, axis=1)

    share(0, head_buf, heads_ref)
    share(1, wo_ref, wos_ref)
    experts = router_ref.shape[0]
    rows = [router_ref[...].astype(jnp.float32), gain_ref[...].astype(jnp.float32), bias_ref[...].astype(jnp.float32)]
    rows.append(jnp.zeros((pack_buf.shape[0] - experts - 2, pack_buf.shape[1]), jnp.float32))
    pack_buf[...] = jnp.concatenate(rows, axis=0).astype(jnp.bfloat16)
    share(2, pack_buf, packs_ref)
    share(3, wq_ref.at[pl.ds(pl.multiple_of(me * depth, depth), depth)], parts_ref)
    for k in (0, 1):
        rows = tok_ref.at[pl.ds(k * half, half)]
        go(push(rows, part(me, k), near_send.at[0, k], near_recv.at[0, k], (sib, z)))
    locals_.append(pltpu.make_async_copy(tok_ref, toks_ref.at[me], own_sem.at[4]))
    locals_[-1].start()

    def arrived(device, k, sem):
        push(part(device, k), part(device, k), far_send.at[0, 0], sem, (sib, z)).wait_recv()

    def relay(device, k, i):
        go(push(part(device, k), part(device, k), near_send.at[i, k], near_recv.at[i, k], (sib, z)))

    arrived(xn, 0, own_recv.at[0, 0])
    go(push(part(xn, 0), part(xn, 0), far_send.at[2, 0], diag_recv.at[0], (yn, z)))
    relay(xn, 0, 1)
    arrived(yn, 1, own_recv.at[1, 1])
    go(push(part(yn, 1), part(yn, 1), far_send.at[2, 1], diag_recv.at[1], (xn, z)))
    relay(yn, 1, 2)
    arrived(xn, 1, own_recv.at[0, 1])
    relay(xn, 1, 1)
    arrived(yn, 0, own_recv.at[1, 0])
    relay(yn, 0, 2)
    for k in (0, 1):
        arrived(diag, k, diag_recv.at[k])
        relay(diag, k, 3)
    for k in (0, 1):
        for i, device in enumerate((sib, flip(xn, 1), flip(yn, 1), flip(diag, 1))):
            arrived(device, k, near_recv.at[i, k])
    for i, whole in enumerate((heads_ref, wos_ref, packs_ref, parts_ref)):
        for k in range(zs - 1):
            other = lax.rem(z + zs - 1 - k, zs)
            push(whole.at[other], whole.at[other], z_send.at[i, k], z_recv.at[i, k], (me, other)).wait_recv()
    for copy in locals_:
        copy.wait()
    for copy in started:
        copy.wait_send()


def gather(tokens, w_qkv, w_out, w_router, ln_gain, ln_bias, ctx_count, z_count):
    shard, wide = w_qkv.shape
    low = jnp.bfloat16
    outs = [
        (ctx_count,) + tokens.shape, (z_count, shard, 3 * HEAD), (z_count,) + w_out.shape, (z_count, 16, shard),
        (z_count, shard // ctx_count, wide),
    ]
    dma = pltpu.SemaphoreType.DMA
    return pl.pallas_call(
        functools.partial(gather_body, z_count),
        out_shape=[jax.ShapeDtypeStruct(out, low) for out in outs],
        in_specs=[VMEM] * 6,
        out_specs=[ANY] * 5,
        scratch_shapes=[
            pltpu.VMEM((shard, 3 * HEAD), low), pltpu.VMEM((16, shard), low),
            dma((5,)), dma((4, z_count - 1)), dma((4, z_count - 1)), dma((3, 2)), dma((4, 2)), dma((2, 2)), dma((2,)), dma((4, 2)),
        ],
        compiler_params=pltpu.CompilerParams(collective_id=1, has_side_effects=True, vmem_limit_bytes=LIMIT),
        cost_estimate=cost(24),
        name="gather_tokens",
    )(tokens, w_qkv, w_out, w_router.T, ln_gain[None], ln_bias[None])


def gelu_parts(value):
    square = value * value
    tangent = jnp.tanh(value * (square * (gelu_coef * gelu_cubic) + gelu_coef))
    half = 0.5 * tangent + 0.5
    rise = value * (square * (3.0 * gelu_coef * gelu_cubic) + gelu_coef)
    return value * half, half + half * (1.0 - tangent) * rise


def norm_parts(hidden):
    center = hidden - jnp.mean(hidden, axis=-1, keepdims=True)
    inv_dev = lax.rsqrt(jnp.mean(center * center, axis=-1, keepdims=True) + epsilon)
    return center * inv_dev, inv_dev


def middle_body(
    experts, groups, att_ref, tok_ref, cot_ref, wo_ref, pack_ref, gid_ref, up_ref, down_ref,
    layer_ref, ghidden_ref, gout_ref, small_ref, got_ref, ghead_ref,
    tok, cot, wo, pack, up, down, att, zsend, zin, bsend, bin_, ghead,
    load_sem, own_sem, a_send, a_recv, m_send, m_recv, b_send, b_recv, h_send, h_recv,
):
    me, z = lax.axis_index("ctx"), lax.axis_index("fsdp")
    count, half = att_ref.shape[0], att_ref.shape[1]
    rows, width = tok_ref.shape
    owners, own_experts = zsend.shape[0], up_ref.shape[0]
    flat, per = experts * groups, experts * groups // owners
    pairs = [(tok_ref, tok), (wo_ref, wo), (pack_ref, pack), (cot_ref, cot)]
    for e in range(own_experts):
        pairs += [(up_ref.at[e], up.at[e]), (down_ref.at[e], down.at[e])]
    loads = [pltpu.make_async_copy(src, dst, load_sem.at[i]) for i, (src, dst) in enumerate(pairs)]
    for copy in loads:
        copy.start()
    z_peers = [(me, lax.rem(z + k, owners)) for k in range(1, owners)]
    c_peers = [(jnp.bitwise_xor(me, k), z) for k in range(1, count)]
    meet(z_peers + c_peers)

    def start(copies):
        for copy in copies:
            copy.start()
        return copies

    def wait(copies):
        for copy in copies:
            copy.wait()

    swap = start([push(att_ref.at[d[0]], att.at[me], a_send.at[k], a_recv.at[k], d) for k, d in enumerate(c_peers)])
    own = start([pltpu.make_async_copy(att_ref.at[me], att.at[me], own_sem.at[0])])
    small_in = None
    wait(own + swap)
    wait(loads[:4])
    halves = [jnp.concatenate([att[h, :, HEAD * p:HEAD * (p + 1)] for h in range(count)], axis=1) for p in range(2)]
    attended = jnp.concatenate(halves, axis=0)
    weight = wo[...].reshape(width, width)
    hidden = tok[...].astype(jnp.float32) + dot_nn(attended, weight)
    unit, inv_dev = norm_parts(hidden)
    small_in = jnp.concatenate([pack[k] for k in range(owners)], axis=1)
    gain, bias = small_in[experts:experts + 1].astype(jnp.float32), small_in[experts + 1:experts + 2].astype(jnp.float32)
    normed = (unit * gain + bias).astype(jnp.bfloat16)
    expo = jnp.exp(dot_nt(small_in, normed)[:experts])
    expo = jnp.broadcast_to(expo[:, None, :], (experts, groups, rows)).reshape(flat, rows)
    member = lax.rem(lax.broadcasted_iota(jnp.int32, (flat, 1), 0), groups) == lax.rem(gid_ref[...], groups)
    expo = jnp.where(member, expo, 0.0)
    mix = expo / jnp.sum(expo, axis=1, keepdims=True)
    low = mix.astype(jnp.bfloat16)

    def to_owners(kind, value):
        zsend[:, kind] = value.astype(jnp.bfloat16).reshape(owners, per, width)
        zin[z, kind] = zsend[z, kind]
        return start([
            push(zsend.at[d[1], kind], zin.at[z, kind], m_send.at[kind, k], m_recv.at[kind, k], d) for k, d in enumerate(z_peers)
        ])

    mixed_copies = to_owners(0, dot_nn(low, normed))
    grad_experts = dot_nn(low, cot[...])
    wait(loads[4:])
    wait(mixed_copies)
    grad_copies = to_owners(1, grad_experts)

    def from_sources(kind, e):
        return zin[:, kind, e * groups:(e + 1) * groups, :].reshape(owners * groups, width)

    def to_sources(kind, e, value):
        bsend[:, kind, e * groups:(e + 1) * groups, :] = value.astype(jnp.bfloat16).reshape(owners, groups, width)

    def send_back(kind):
        bin_[z, kind] = bsend[z, kind]
        return start([
            push(bsend.at[d[1], kind], bin_.at[z, kind], b_send.at[kind, k], b_recv.at[kind, k], d) for k, d in enumerate(z_peers)
        ])

    slopes = []
    for e in range(own_experts):
        pre = dot_nn(from_sources(0, e), up[e])
        active, slope = gelu_parts(pre)
        slopes.append(slope)
        to_sources(0, e, dot_nn(active.astype(jnp.bfloat16), down[e]))
    out_copies = send_back(0)
    wait(grad_copies)
    got_ref[...] = zin[...]
    for e in range(own_experts):
        grad_pre = (dot_nt(from_sources(1, e), down[e]) * slopes[e]).astype(jnp.bfloat16)
        to_sources(1, e, dot_nt(grad_pre, up[e]))
    back_copies = send_back(1)
    wait(out_copies)
    expert_out = bin_[:, 0].reshape(flat, width)
    layer_ref[...] = hidden + dot_tn(low, expert_out)
    grad_mix = dot_nt(expert_out, cot[...])
    wait(back_copies)
    grad_mixed = bin_[:, 1].reshape(flat, width)
    product = mix * (grad_mix + dot_nt(grad_mixed, normed))
    grad_logits = product - mix * jnp.sum(product, axis=1, keepdims=True)
    grad_logits = jnp.sum(grad_logits.reshape(experts, groups, rows), axis=1).astype(jnp.bfloat16)
    pad = jnp.zeros((small_in.shape[0] - experts, rows), jnp.bfloat16)
    grad_logits = jnp.concatenate([grad_logits, pad], axis=0)
    grad_normed = dot_tn(jnp.concatenate([low, grad_logits], axis=0), jnp.concatenate([grad_mixed, small_in], axis=0))
    scaled = grad_normed * gain
    mean = jnp.mean(scaled, axis=-1, keepdims=True)
    grad_hidden = cot[...].astype(jnp.float32) + inv_dev * (scaled - mean - unit * jnp.mean(scaled * unit, axis=-1, keepdims=True))
    branch = grad_hidden.astype(jnp.bfloat16)
    grad_heads = dot_nt(branch, weight).astype(jnp.bfloat16)
    for h in range(count):
        at = slice(HEAD * h, HEAD * (h + 1))
        ghead[h] = jnp.concatenate([grad_heads[:half, at], grad_heads[half:, at]], axis=1)
    swap = start([push(ghead.at[d[0]], ghead_ref.at[me], h_send.at[k], h_recv.at[k], d) for k, d in enumerate(c_peers)])
    last = start([pltpu.make_async_copy(ghead.at[me], ghead_ref.at[me], own_sem.at[2])])
    ghidden_ref[...] = grad_hidden
    gout_ref[...] = dot_tn(attended, branch).astype(jnp.bfloat16).reshape(gout_ref.shape)
    small_ref[...] = jnp.concatenate(
        [
            dot_nn(grad_logits, normed)[:experts],
            jnp.sum(grad_normed * unit, axis=0, keepdims=True),
            jnp.sum(grad_normed, axis=0, keepdims=True),
            jnp.zeros((small_in.shape[0] - experts - 2, width), jnp.float32),
        ],
        axis=0,
    )
    wait(last + swap)


def middle(att, tokens, cot, w_out, pack, gid_row, w_up, w_down, experts, groups):
    rows, width = tokens.shape
    count, owners, own = att.shape[0], pack.shape[0], w_up.shape[0]
    sent = (owners, 2, experts * groups // owners, width)
    dma = pltpu.SemaphoreType.DMA
    low, full = jnp.bfloat16, jnp.float32
    return pl.pallas_call(
        functools.partial(middle_body, experts, groups),
        out_shape=(
            jax.ShapeDtypeStruct((rows, width), full),
            jax.ShapeDtypeStruct((rows, width), full),
            jax.ShapeDtypeStruct((owners, width // owners, width), low),
            jax.ShapeDtypeStruct((pack.shape[1], width), full),
            jax.ShapeDtypeStruct(sent, low),
            jax.ShapeDtypeStruct(att.shape, low),
        ),
        in_specs=[ANY] * 5 + [VMEM] + [ANY] * 2,
        out_specs=(VMEM,) * 5 + (ANY,),
        scratch_shapes=[pltpu.VMEM(x.shape, x.dtype) for x in (tokens, cot, w_out, pack, w_up, w_down, att)] + [
            pltpu.VMEM(sent, low), pltpu.VMEM(sent, low), pltpu.VMEM(sent, low), pltpu.VMEM(sent, low), pltpu.VMEM(att.shape, low),
            dma((4 + 2 * own,)), dma((3,)), dma((count - 1,)), dma((count - 1,)), dma((2, owners - 1)), dma((2, owners - 1)),
            dma((2, owners - 1)), dma((2, owners - 1)), dma((count - 1,)), dma((count - 1,)),
        ],
        compiler_params=pltpu.CompilerParams(collective_id=2, has_side_effects=True, vmem_limit_bytes=LIMIT),
        cost_estimate=cost(35),
        name="middle",
    )(att, tokens, cot, w_out, pack, gid_row, w_up, w_down)


def backward_body(
    table_ref, ghead_ref, qf_ref, kf_ref, vf_ref, stat_ref, toks_ref, up_ref, down_ref, ghidden_ref, small_ref, gout_ref, part_ref, got_ref,
    gtok_ref, gq_ref, out_ref, sums_ref, act_ref, gpre_ref, all_ref,
    ghead, qf, kf, vf, stat, toks, up, down, ghidden, dof, qt, dot, dq_acc, dk_acc, dv_acc, qk, dv_rows, sorted_dv, head_acc, send, landing,
    weight, mixed_all, act_buf, gpre_buf, zsend, zone, total, totals, out_zone, out_sum, out_part, out_own, out_all,
    load_sem, own_sem, a_send, a_recv, z_send, z_recv, c_send, c_recv, o_send, o_recv, g_send, g_recv, r_send, r_recv,
    w_send, w_recv, v_send, v_recv,
):
    me, z = lax.axis_index("ctx"), lax.axis_index("fsdp")
    count, block_len = ghead_ref.shape[0], ghead_ref.shape[1]
    blocks, owners = 2 * count, gout_ref.shape[0]
    rows, width = blocks * block_len, toks_ref.shape[1]
    own_experts, ffn = up_ref.shape[0], up_ref.shape[2]
    low = jnp.bfloat16

    def start(copies):
        for copy in copies:
            copy.start()
        return copies

    def wait(copies):
        for copy in copies:
            copy.wait()

    pairs = [
        (ghead_ref, ghead), (qf_ref, qf), (stat_ref, stat), (kf_ref, kf), (vf_ref, vf), (toks_ref, toks), (up_ref, up), (down_ref, down),
        (ghidden_ref, ghidden),
    ]
    loads = start([pltpu.make_async_copy(src, dst, load_sem.at[i]) for i, (src, dst) in enumerate(pairs)])
    sib, same_core = flip(me, 1), [flip(me, 2), flip(me, 4), flip(flip(me, 2), 4)]
    z_peers = [(me, lax.rem(z + k, owners)) for k in range(1, owners)]
    c_peers = [(jnp.bitwise_xor(me, k), z) for k in range(1, count)]
    meet(z_peers + c_peers)

    out_copies = start([push(gout_ref.at[d[1]], out_zone.at[z], o_send.at[0, k], o_recv.at[0, k], d) for k, d in enumerate(z_peers)])
    out_zone[z] = gout_ref[z]
    gathers = start([push(got_ref, all_ref.at[me], g_send.at[k], g_recv.at[k], (d, z)) for k, d in enumerate(same_core)])
    relays = start([push(got_ref, all_ref.at[me], r_send.at[3], r_recv.at[3], (sib, z))])
    own_got = start([pltpu.make_async_copy(got_ref, all_ref.at[me], own_sem.at[0])])
    weights = start([push(part_ref, weight.at[:, me], w_send.at[k], w_recv.at[k], (d, z)) for k, d in enumerate(same_core)])
    shares = start([push(part_ref, weight.at[:, me], v_send.at[3], v_recv.at[3], (sib, z))])
    weight[:, me] = part_ref[...]

    def mask(condition):
        return jnp.broadcast_to(jnp.where(condition, 1.0, 0.0), (1, 2 * HEAD))

    firsts = [mask(table_ref[2 * c] < table_ref[2 * c + 1]).astype(low) for c in range(count)]
    lows = [jnp.minimum(table_ref[2 * c], table_ref[2 * c + 1]) for c in range(count)]
    holds = [[mask(lows[c] == j).astype(low) for j in range(count)] for c in range(count)]

    def blend(masks, values):
        out = None
        for weigh, value in zip(masks, values):
            out = weigh * value if out is None else out + weigh * value
        return out

    lane = lax.broadcasted_iota(jnp.int32, (1, 2 * HEAD), 1)

    def prepare(s, both):
        at = slice(s * block_len, (s + 1) * block_len)
        grad = jnp.where(lane < HEAD, both, 0.0)
        delta = jnp.sum(grad * stat[at, :], axis=1, keepdims=True)
        one, two, three = split3(jnp.broadcast_to(-delta, grad.shape))
        wide = jnp.where(lane == HEAD, one, grad.astype(low))
        wide = jnp.where(lane == HEAD + 1, two, wide)
        dof[at, :] = jnp.where(lane == HEAD + 2, three, wide)
        turned = jnp.where(lane < HEAD, both, pltpu.roll(qf[at, :].astype(jnp.float32), HEAD, 1)).T.astype(low)
        dot[:, at] = turned[:HEAD]
        qt[:, at] = turned[HEAD:]

    wait(loads[:3])
    for c in range(count):
        block = ghead[c]
        turned = pltpu.roll(block.astype(jnp.float32), HEAD, 1).astype(low)
        ghead[c] = firsts[c] * block + (1 - firsts[c]) * turned
    for j in range(count):
        both = blend([holds[c][j] for c in range(count)], [ghead[c] for c in range(count)]).astype(jnp.float32)
        prepare(j, both)
        prepare(blocks - 1 - j, pltpu.roll(both, HEAD, 1))
    wait(loads[3:5])
    causal = lax.broadcasted_iota(jnp.int32, (HALF, HALF), 1) <= lax.broadcasted_iota(jnp.int32, (HALF, HALF), 0)
    scale = HEAD ** (-0.5)

    def key_run(run):
        def tile(q_at, k_at, k_low, k_size, diagonal, first_k, first_q):
            scores = dot_nt(qf[q_at, :], kf[k_at, :]) * (scale * LOG2E)
            if diagonal:
                scores = jnp.where(causal, scores, HIDE)
            probs = jnp.exp2(scores)
            grad = (probs * dot_nt(dof[q_at, :], vf[k_at, :])).astype(low)
            dv = dot_nn(dot[:, q_at], probs.astype(low))
            dk = dot_nn(qt[:, q_at], grad)
            dq = dot_nn(grad, kf[k_at, :])
            at = slice(k_low, k_low + k_size)
            if first_k:
                dv_acc[:, at] = dv
                dk_acc[:, at] = dk
            else:
                dv_acc[:, at] += dv
                dk_acc[:, at] += dk
            if first_q:
                @pl.when(run == 0)
                def _():
                    dq_acc[q_at, :] = dq

                @pl.when(run != 0)
                def _():
                    dq_acc[q_at, :] += dq
            else:
                dq_acc[q_at, :] += dq

        early, late = span(2 * run, HALF), span(2 * run + 1, HALF)
        tile(early, early, 0, HALF, True, True, True)
        tile(late, early, 0, HALF, False, False, True)
        tile(late, late, HALF, HALF, True, True, False)

        @pl.loop(run + 1, rows // RUN)
        def _(index):
            tile(span(index, RUN), span(run, RUN), 0, RUN, False, False, True)

        at = span(run, RUN)
        both = jnp.concatenate([dk_acc[...] * scale, dv_acc[...]], axis=0).T
        query = dq_acc[at, :] * scale
        qk[at, :] = jnp.where(lane < HEAD, query, pltpu.roll(both, HEAD, 1)).astype(low)
        dv_rows[at, :] = both.astype(low)

    def send_half(half):
        copies = []
        mid = block_len // 2
        for c in range(count):
            ats = [slice(s * block_len, (s + 1) * block_len) for s in (range(count) if half == 0 else range(blocks - 1, count - 1, -1))]
            send[half, c, :block_len, :] = blend(holds[c], [qk[at, :] for at in ats])
            values = blend(holds[c], [dv_rows[at, :] for at in ats])
            sorted_dv[c] = values
            values = values[:, HEAD:]
            send[half, c, block_len:, :] = jnp.concatenate([values[:mid], values[mid:]], axis=1)
        landing[half, me] = send[half, me]
        for k, d in enumerate(c_peers):
            copies.append(push(send.at[half, d[0]], landing.at[half, me], a_send.at[half, k], a_recv.at[half, k], d))
        return start(copies)

    def head_weights(half):
        first, second = None, None
        for c in range(count):
            order = firsts[c][:, :1] if half == 0 else 1 - firsts[c][:, :1]
            here = order * toks[2 * c * block_len:(2 * c + 1) * block_len, :]
            here = here + (1 - order) * toks[(2 * c + 1) * block_len:(2 * c + 2) * block_len, :]
            one, two = dot_tn(send[half, c, :block_len, :], here), dot_tn(sorted_dv[c], here)
            first, second = (one, two) if first is None else (first + one, second + two)
        both = jnp.concatenate([first, second[HEAD:]], axis=0)
        if half == 0:
            head_acc[...] = both
        else:
            head_acc[...] += both

    @pl.loop(0, 2)
    def _(run):
        key_run(run)

    swaps = send_half(0)

    for k, d in enumerate(same_core):
        gathers[k].wait_recv()
        relays += start([push(all_ref.at[d], all_ref.at[d], r_send.at[k], r_recv.at[k], (sib, z))])
        weights[k].wait_recv()
        shares += start([push(weight.at[:, d], weight.at[:, d], v_send.at[k], v_recv.at[k], (sib, z))])
    wait(out_copies)
    summed = out_zone[0].astype(jnp.float32)
    for k in range(1, owners):
        summed = summed + out_zone[k].astype(jnp.float32)
    out_sum[...] = summed.astype(low).reshape(out_sum.shape)
    part_copies = start([push(out_sum.at[d[0]], out_part.at[me], o_send.at[1, k], o_recv.at[1, k], d) for k, d in enumerate(c_peers)])
    out_part[me] = out_sum[me]
    wait(loads[5:])
    head_weights(0)

    @pl.loop(2, rows // RUN)
    def _(run):
        key_run(run)

    swaps += send_half(1)
    wait(part_copies)
    summed = out_part[0].astype(jnp.float32)
    for k in range(1, count):
        summed = summed + out_part[k].astype(jnp.float32)
    out_own[...] = summed.astype(low)
    last_copies = start([push(out_own, out_all.at[me], o_send.at[2, k], o_recv.at[2, k], d) for k, d in enumerate(c_peers)])
    out_all[me] = out_own[...]
    wait(own_got + relays)
    mixed_load = start([pltpu.make_async_copy(all_ref, mixed_all, own_sem.at[1])])
    head_weights(1)
    lanes = width // owners
    for c in range(owners):
        at = slice(c * lanes, (c + 1) * lanes)
        zsend[c, :3 * HEAD, :] = head_acc[:, at].astype(low)
        zsend[c, 3 * HEAD:, :] = small_ref[:, at].astype(low)
    z_copies = start([push(zsend.at[d[1]], zone.at[z], z_send.at[k], z_recv.at[k], d) for k, d in enumerate(z_peers)])
    zone[z] = zsend[z]
    wait(mixed_load)
    step = 512
    groups = got_ref.shape[2] // own_experts

    def expert_part(e):
        mixed = mixed_all[:, :, 0, e * groups:(e + 1) * groups, :].reshape(-1, width)
        grad_out = mixed_all[:, :, 1, e * groups:(e + 1) * groups, :].reshape(-1, width)

        def chunk(i, carry):
            at = span(i, step)
            active, slope = gelu_parts(dot_nn(mixed, up[e, :, at]))
            act_buf[e, :, at] = active.astype(low)
            gpre_buf[e, :, at] = (dot_nt(grad_out, down[e, at, :]) * slope).astype(low)
            return carry

        lax.fori_loop(0, ffn // step, chunk, 0)
        return start([
            pltpu.make_async_copy(act_buf.at[e], act_ref.at[e], own_sem.at[2 + 2 * e]),
            pltpu.make_async_copy(gpre_buf.at[e], gpre_ref.at[e], own_sem.at[3 + 2 * e]),
        ])

    stores = expert_part(0)
    wait(z_copies)
    summed = zone[0].astype(jnp.float32)
    for k in range(1, owners):
        summed = summed + zone[k].astype(jnp.float32)
    total[...] = summed.astype(low)
    c_copies = start([push(total, totals.at[me], c_send.at[k], c_recv.at[k], d) for k, d in enumerate(c_peers)])
    totals[me] = total[...]
    for e in range(1, own_experts):
        stores += expert_part(e)
    wait(swaps + shares)
    flat = weight[...].reshape(width, -1)
    parts = []
    for half in range(2):
        queries, keys, values = [], [], []
        for h in range(count):
            front, back = landing[half, h, :block_len, :], landing[half, h, block_len:, :]
            queries.append(front[:, :HEAD])
            keys.append(front[:, HEAD:])
            values.append(jnp.concatenate([back[:, :HEAD], back[:, HEAD:]], axis=0))
        parts.append(dot_nt(jnp.concatenate(queries + keys + values, axis=1), flat))
    in_order = mask(table_ref[2 * me] < table_ref[2 * me + 1])[:, :1]
    gtok_ref[:block_len, :] = ghidden[:block_len, :] + (in_order * parts[0] + (1.0 - in_order) * parts[1])
    gtok_ref[block_len:, :] = ghidden[block_len:, :] + (in_order * parts[1] + (1.0 - in_order) * parts[0])
    wait(last_copies)
    out_ref[...] = out_all[...].astype(jnp.float32).reshape(out_ref.shape)
    wait(c_copies)
    small = None
    turned = []
    for c in range(count):
        turned.append(totals[c, :3 * HEAD, :].astype(jnp.float32).T)
        part = totals[c, 3 * HEAD:, :].astype(jnp.float32)
        small = part if small is None else small + part
    sums_ref[...] = small
    for kind in range(3):
        at = slice(HEAD * kind, HEAD * (kind + 1))
        gq_ref[:, HEAD * count * kind:HEAD * count * (kind + 1)] = jnp.concatenate([part[:, at] for part in turned], axis=1)
    wait(stores)
    for copy in gathers + weights:
        copy.wait_send()


def backward(table, grad_heads, saved, tokens_all, small, gout, parts, ghidden, got, w_up, w_down, groups):
    count, block_len = grad_heads.shape[:2]
    qf, kf, vf, stat = saved
    rows, width = qf.shape[0], tokens_all.shape[2]
    owners, lanes = gout.shape[:2]
    own_experts, _, ffn = w_up.shape
    height = 3 * HEAD + small.shape[0]
    wide = (own_experts, count * owners * groups, ffn)
    part = (count, lanes // count, width)
    swap = (2, count, block_len + block_len // 2, 2 * HEAD)
    toks = tokens_all.reshape(rows, width)
    held = [grad_heads, qf, kf, vf, stat, toks, w_up, w_down, ghidden]
    dma = pltpu.SemaphoreType.DMA
    low, full = jnp.bfloat16, jnp.float32
    scratch = [
        ((rows, 2 * HEAD), low), ((HEAD, rows), low), ((HEAD, rows), low), ((rows, 2 * HEAD), full), ((HEAD, RUN), full), ((HEAD, RUN), full),
        ((rows, 2 * HEAD), low), ((rows, 2 * HEAD), low), ((count, block_len, 2 * HEAD), low), ((3 * HEAD, width), full), (swap, low), (swap, low),
        ((owners, count) + parts.shape[1:], low), ((count,) + got.shape, low), (wide, low), (wide, low),
        ((owners, height, lanes), low), ((owners, height, lanes), low), ((height, lanes), low), ((count, height, lanes), low),
        (gout.shape, low), (part, low), (part, low), (part[1:], low), (part, low),
    ]
    sems = [
        (9,), (2 + 2 * own_experts,), (2, count - 1), (2, count - 1), (owners - 1,), (owners - 1,), (count - 1,), (count - 1,),
        (3, count - 1), (3, count - 1), (3,), (3,), (4,), (4,), (3,), (3,), (4,), (4,),
    ]
    return pl.pallas_call(
        backward_body,
        out_shape=(
            jax.ShapeDtypeStruct(ghidden.shape, full),
            jax.ShapeDtypeStruct((lanes, 3 * width), full),
            jax.ShapeDtypeStruct((lanes, width), full),
            jax.ShapeDtypeStruct((small.shape[0], lanes), full),
            jax.ShapeDtypeStruct(wide, low),
            jax.ShapeDtypeStruct(wide, low),
            jax.ShapeDtypeStruct((count,) + got.shape, low),
        ),
        in_specs=[SMEM] + [ANY] * 9 + [VMEM] * 4,
        out_specs=(VMEM,) * 4 + (ANY,) * 3,
        scratch_shapes=[pltpu.VMEM(x.shape, x.dtype) for x in held]
        + [pltpu.VMEM(shape, dtype) for shape, dtype in scratch]
        + [dma(shape) for shape in sems],
        compiler_params=pltpu.CompilerParams(collective_id=6, has_side_effects=True, vmem_limit_bytes=LIMIT),
        cost_estimate=cost(60),
        name="backward",
    )(table, grad_heads, qf, kf, vf, stat, toks, w_up, w_down, ghidden, small, gout, parts, got)


def expert_grad_body(experts, passed, mixed_ref, grad_ref, act_ref, gpre_ref, small_ref, *refs):
    sources, outs = refs[:passed], refs[passed + 5:]
    gup_ref, gdown_ref, router_ref, gain_ref, bias_ref = refs[passed:passed + 5]
    width = gup_ref.shape[1]
    for source, out in zip(sources, outs):
        out[...] = source[...]
    router_ref[...] = small_ref[:experts]
    gain_ref[...] = small_ref[experts:experts + 1]
    bias_ref[...] = small_ref[experts + 1:experts + 2]
    gup_ref[0] = dot_tn(mixed_ref[...].reshape(-1, width), gpre_ref[0])
    gdown_ref[0] = dot_tn(act_ref[0], grad_ref[...].reshape(-1, width))


def expert_grads(gathered, active, grad_pre, small, passed, groups, experts):
    own, rows, ffn = active.shape
    step = 512
    steps = ffn // step
    sources, width = gathered.shape[0], gathered.shape[3]
    view = gathered.reshape(sources, 2, own, groups, width)
    lanes = small.shape[1]
    full = jnp.float32
    slices = [pl.BlockSpec((x.shape[0] // (own * steps), x.shape[1]), lambda e, f: (e * steps + f, 0)) for x in passed]
    return pl.pallas_call(
        functools.partial(expert_grad_body, experts, len(passed)),
        grid=(own, steps),
        out_shape=[
            jax.ShapeDtypeStruct((own, width, ffn), full), jax.ShapeDtypeStruct((own, ffn, width), full),
            jax.ShapeDtypeStruct((experts, lanes), full), jax.ShapeDtypeStruct((1, lanes), full), jax.ShapeDtypeStruct((1, lanes), full),
        ] + [jax.ShapeDtypeStruct(x.shape, x.dtype) for x in passed],
        in_specs=[
            pl.BlockSpec((sources, 1, 1, groups, width), lambda e, f: (0, 0, e, 0, 0)),
            pl.BlockSpec((sources, 1, 1, groups, width), lambda e, f: (0, 1, e, 0, 0)),
            pl.BlockSpec((1, rows, step), lambda e, f: (e, 0, f)),
            pl.BlockSpec((1, rows, step), lambda e, f: (e, 0, f)),
            pl.BlockSpec(small.shape, lambda e, f: (0, 0)),
        ] + slices,
        out_specs=[
            pl.BlockSpec((1, width, step), lambda e, f: (e, 0, f)), pl.BlockSpec((1, step, width), lambda e, f: (e, f, 0)),
            pl.BlockSpec((experts, lanes), lambda e, f: (0, 0)), pl.BlockSpec((1, lanes), lambda e, f: (0, 0)),
            pl.BlockSpec((1, lanes), lambda e, f: (0, 0)),
        ] + slices,
        compiler_params=pltpu.CompilerParams(vmem_limit_bytes=LIMIT),
        cost_estimate=cost(10),
        name="expert_grads",
    )(view, view, active, grad_pre, small, *passed)


def fast_device(
    tokens, cotangent, block_table, seg_ids, group_ids, w_qkv, w_out, w_router, ln_gain, ln_bias, w_up, w_down
):
    ctx_count, z_count = lax.axis_size("ctx"), lax.axis_size("fsdp")
    tok_rows, cot_rows = tokens[0], cotangent[0]
    rows, width = tok_rows.shape
    experts = w_router.shape[1]
    groups = rows // GROUP_SIZE
    tokens_all, head_weights, out_full, pack_full, qkv_parts = gather(
        tok_rows, w_qkv, w_out, w_router, ln_gain, ln_bias, ctx_count, z_count
    )
    att, *saved = attn_fwd(tokens_all.reshape(ctx_count * rows, width), head_weights, block_table, seg_ids)
    layer_out, grad_hidden, gout, small, got, grad_heads = middle(
        att, tok_rows, cot_rows, out_full, pack_full, group_ids, w_up, w_down, experts, groups
    )
    grad_tokens, grad_qkv, grad_out, small, active, grad_pre, gathered = backward(
        block_table, grad_heads, saved, tokens_all, small, gout, qkv_parts, grad_hidden, got, w_up, w_down, groups
    )
    gathered = gathered.reshape((ctx_count * z_count,) + gathered.shape[2:])
    grad_up, grad_down, grad_router, grad_gain, grad_bias, layer_out, grad_tokens, grad_qkv, grad_out = expert_grads(
        gathered, active, grad_pre, small, [layer_out, grad_tokens, grad_qkv, grad_out], groups, experts
    )
    return (
        layer_out[None],
        grad_tokens[None],
        grad_qkv,
        grad_out,
        grad_router.T,
        grad_gain[0],
        grad_bias[0],
        grad_up,
        grad_down,
    )


def solution(mesh):
    placed = (
        P("fsdp", "ctx", None),
        P("fsdp", "ctx", None),
        P(),
        P("fsdp", None),
        P("fsdp", "ctx"),
        P("fsdp", None),
        P("fsdp", None),
        P("fsdp", None),
        P("fsdp"),
        P("fsdp"),
        P("fsdp", None, None),
        P("fsdp", None, None),
    )
    step = fast_device if mesh.shape["ctx"] == HEADS else on_device
    return jax.shard_map(
        step,
        mesh=mesh,
        in_specs=placed,
        out_specs=(
            P("fsdp", "ctx", None),
            P("fsdp", "ctx", None),
            P("fsdp", None),
            P("fsdp", None),
            P("fsdp", None),
            P("fsdp"),
            P("fsdp"),
            P("fsdp", None, None),
            P("fsdp", None, None),
        ),
        check_vma=False,
    )
```

```python
import functools

import jax
import jax.numpy as jnp
from jax import lax
from jax.experimental import pallas as pl
from jax.experimental.pallas import tpu as pltpu
from jax.sharding import PartitionSpec as P

HEADS = 8
HEAD = 64
GROUP_SIZE = 32
KEY_BLOCK = 2048


highest = lax.Precision.HIGHEST
neg_large = -1e30
epsilon = 1e-05
gelu_coef = 0.7978845608028654
gelu_cubic = 0.044715


def contract_rows(left, right):
    return lax.dot_general(
        left, right, (((0,), (0,)), ((), ())), preferred_element_type=jnp.float32
    )


def contract_cols(left, right):
    return lax.dot_general(
        left, right, (((1,), (1,)), ((), ())), preferred_element_type=jnp.float32
    )


def gelu_slope(value):
    inner = gelu_coef * (value + gelu_cubic * value * value * value)
    tangent = jnp.tanh(inner)
    return 0.5 * (1.0 + tangent) + 0.5 * value * (1.0 - tangent * tangent) * gelu_coef * (
        1.0 + 3.0 * gelu_cubic * value * value
    )


def expert_forward(mixed_low, up_weight, down_weight):
    pre = jnp.einsum("ged,edh->geh", mixed_low, up_weight, preferred_element_type=jnp.float32)
    active = jax.nn.gelu(pre, approximate=True).astype(jnp.bfloat16)
    result = jnp.einsum("geh,ehd->ged", active, down_weight, preferred_element_type=jnp.float32)
    return (pre, active, result.astype(jnp.bfloat16))


def expert_backward(mixed_low, pre, active, grad_result, up_weight, down_weight):
    grad_act = jnp.einsum(
        "ged,ehd->geh", grad_result, down_weight, preferred_element_type=jnp.float32
    )
    grad_pre = (grad_act * gelu_slope(pre)).astype(jnp.bfloat16)
    grad_down_part = jnp.einsum(
        "geh,ged->ehd", active, grad_result, preferred_element_type=jnp.float32
    )
    grad_up_part = jnp.einsum(
        "ged,geh->edh", mixed_low, grad_pre, preferred_element_type=jnp.float32
    )
    grad_mixed = jnp.einsum("geh,edh->ged", grad_pre, up_weight, preferred_element_type=jnp.float32)
    return (grad_up_part, grad_down_part, grad_mixed.astype(jnp.bfloat16))


def on_device(
    tokens,
    cotangent,
    block_table,
    seg_ids,
    group_ids,
    w_qkv,
    w_out,
    w_router,
    ln_gain,
    ln_bias,
    w_up,
    w_down,
):
    tok_rows = tokens[0]
    tok_count = tok_rows.shape[0]
    width = tok_rows.shape[1]
    expert_count = w_router.shape[1]
    ctx_index = lax.axis_index("ctx")
    full_rows = seg_ids.shape[1]
    block_len = full_rows // block_table.shape[0]
    row_ids = jnp.arange(full_rows, dtype=jnp.int32)
    key_pos = jnp.take(block_table, row_ids // block_len) * block_len + row_ids % block_len
    key_seg = seg_ids[0]
    pos_rows = lax.dynamic_slice_in_dim(key_pos, ctx_index * tok_count, tok_count)
    seg_rows = lax.dynamic_slice_in_dim(key_seg, ctx_index * tok_count, tok_count)
    scale = HEAD ** (-0.5)
    qkv_full, out_full, router_full, gain_full, bias_full = (
        lax.all_gather(w_qkv, "fsdp", axis=0, tiled=True),
        lax.all_gather(w_out, "fsdp", axis=0, tiled=True),
        lax.all_gather(w_router, "fsdp", axis=0, tiled=True),
        lax.all_gather(ln_gain, "fsdp", axis=0, tiled=True),
        lax.all_gather(ln_bias, "fsdp", axis=0, tiled=True),
    )
    qkv = jnp.dot(tok_rows, qkv_full, preferred_element_type=jnp.float32).astype(jnp.bfloat16)
    query_heads = qkv[:, :width].reshape(tok_count, HEADS, HEAD)
    key_all, val_all = (
        lax.all_gather(qkv[:, width : 2 * width], "ctx", axis=0, tiled=True),
        lax.all_gather(qkv[:, 2 * width :], "ctx", axis=0, tiled=True),
    )
    key_heads = key_all.reshape(full_rows, HEADS, HEAD)
    val_heads = val_all.reshape(full_rows, HEADS, HEAD)
    block_count = full_rows // KEY_BLOCK
    block_ids = jnp.arange(block_count, dtype=jnp.int32)

    def block_scores(index):
        start = index * KEY_BLOCK
        key_block = lax.dynamic_slice_in_dim(key_heads, start, KEY_BLOCK, 0)
        val_block = lax.dynamic_slice_in_dim(val_heads, start, KEY_BLOCK, 0)
        pos_block = lax.dynamic_slice_in_dim(key_pos, start, KEY_BLOCK, 0)
        seg_block = lax.dynamic_slice_in_dim(key_seg, start, KEY_BLOCK, 0)
        scores = (
            jnp.einsum("qhd,khd->hqk", query_heads, key_block, preferred_element_type=jnp.float32)
            * scale
        )
        allowed = (pos_block[None, :] <= pos_rows[:, None]) & (
            (seg_block[None, :] == 0) | (seg_block[None, :] == seg_rows[:, None])
        )
        return (scores, allowed[None], key_block, val_block)

    def lse_step(carry, index):
        top, total = carry
        scores, allowed, key_block, val_block = block_scores(index)
        masked = jnp.where(allowed, scores, neg_large)
        new_top = jnp.maximum(top, jnp.max(masked, axis=-1))
        weights = jnp.where(allowed, jnp.exp(masked - new_top[..., None]), 0.0)
        return ((new_top, total * jnp.exp(top - new_top) + jnp.sum(weights, axis=-1)), None)

    start_top = jnp.full((HEADS, tok_count), neg_large, jnp.float32)
    (top, total), unused = lax.scan(
        lse_step, (start_top, jnp.zeros((HEADS, tok_count), jnp.float32)), block_ids
    )
    log_total = top + jnp.log(total)

    def block_probs(index):
        scores, allowed, key_block, val_block = block_scores(index)
        probs = jnp.where(allowed, jnp.exp(scores - log_total[..., None]), 0.0)
        return (probs, key_block, val_block)

    def value_step(accum, index):
        probs, key_block, val_block = block_probs(index)
        return (
            accum
            + jnp.einsum(
                "hqk,khd->qhd",
                probs.astype(jnp.bfloat16),
                val_block,
                preferred_element_type=jnp.float32,
            ),
            None,
        )

    accum, unused = lax.scan(
        value_step, jnp.zeros((tok_count, HEADS, HEAD), jnp.float32), block_ids
    )
    attended = accum.reshape(tok_count, width).astype(jnp.bfloat16)
    hidden = tok_rows.astype(jnp.float32) + jnp.dot(
        attended, out_full, preferred_element_type=jnp.float32
    )
    center = hidden - jnp.mean(hidden, axis=-1, keepdims=True)
    inv_dev = lax.rsqrt(jnp.mean(center * center, axis=-1, keepdims=True) + epsilon)
    unit = center * inv_dev
    gain_f = gain_full.astype(jnp.float32)
    normed_low = (unit * gain_f + bias_full.astype(jnp.float32)).astype(jnp.bfloat16)
    logits = jnp.dot(normed_low, router_full, preferred_element_type=jnp.float32)
    groups_dev = tok_count // GROUP_SIZE
    local_group = group_ids[0] - ctx_index * groups_dev
    member = (local_group[:, None] == jnp.arange(groups_dev, dtype=jnp.int32)[None, :]).astype(
        jnp.float32
    )
    expo = jnp.exp(logits)
    group_total = jnp.dot(member.T, expo, precision=highest)
    mix_weights = expo / jnp.dot(member, group_total, precision=highest)
    weights_low = mix_weights.astype(jnp.bfloat16)
    mixing = member.astype(jnp.bfloat16).T[:, None, :] * weights_low.T[None, :, :]
    mixing_flat = mixing.reshape(groups_dev * expert_count, tok_count)
    mixed_low = jnp.dot(mixing_flat, normed_low, preferred_element_type=jnp.float32).astype(
        jnp.bfloat16
    )
    mixed_low = mixed_low.reshape(groups_dev, expert_count, width)
    owner_mixed = lax.all_to_all(mixed_low, "fsdp", split_axis=1, concat_axis=0, tiled=True)
    pre, active, owner_out = expert_forward(owner_mixed, w_up, w_down)
    expert_out = lax.all_to_all(owner_out, "fsdp", split_axis=0, concat_axis=1, tiled=True)
    expert_flat = expert_out.reshape(groups_dev * expert_count, width)
    spread = contract_rows(mixing_flat, expert_flat)
    layer_out = hidden + spread
    cot_rows = cotangent[0]
    cot_f = cot_rows.astype(jnp.float32)
    grad_expert = jnp.dot(mixing_flat, cot_rows, preferred_element_type=jnp.float32).astype(
        jnp.bfloat16
    )
    grad_expert = grad_expert.reshape(groups_dev, expert_count, width)
    coef = contract_cols(cot_rows, expert_flat).reshape(tok_count, groups_dev, expert_count)
    grad_mix_spread = jnp.sum(coef * member[:, :, None], axis=1)
    owner_grad = lax.all_to_all(grad_expert, "fsdp", split_axis=1, concat_axis=0, tiled=True)
    grad_up_own, grad_down_own, owner_back = expert_backward(
        owner_mixed, pre, active, owner_grad, w_up, w_down
    )
    grad_mixed = lax.all_to_all(owner_back, "fsdp", split_axis=0, concat_axis=1, tiled=True)
    grad_mixed_flat = grad_mixed.reshape(groups_dev * expert_count, width)
    grad_norm_mix = contract_rows(mixing_flat, grad_mixed_flat)
    grad_mixing = contract_cols(grad_mixed_flat, normed_low).reshape(
        groups_dev, expert_count, tok_count
    )
    grad_mix_mixing = jnp.sum(grad_mixing * member.T[:, None, :], axis=0).T
    grad_mix = grad_mix_spread + grad_mix_mixing
    product = mix_weights * grad_mix
    token_dot = jnp.dot(member, jnp.dot(member.T, product, precision=highest), precision=highest)
    grad_logits = (product - mix_weights * token_dot).astype(jnp.bfloat16)
    grad_router_part = contract_rows(normed_low, grad_logits)
    grad_norm_router = contract_cols(grad_logits, router_full)
    grad_normed = grad_norm_mix + grad_norm_router
    grad_gain_part = jnp.sum(grad_normed * unit, axis=0)
    grad_bias_part = jnp.sum(grad_normed, axis=0)
    scaled = grad_normed * gain_f
    grad_hidden = cot_f + inv_dev * (
        scaled
        - jnp.mean(scaled, axis=-1, keepdims=True)
        - unit * jnp.mean(scaled * unit, axis=-1, keepdims=True)
    )
    grad_branch = grad_hidden.astype(jnp.bfloat16)
    grad_out_part = contract_rows(attended, grad_branch)
    grad_heads = (
        contract_cols(grad_branch, out_full).astype(jnp.bfloat16).reshape(tok_count, HEADS, HEAD)
    )
    delta = jnp.sum(grad_heads.astype(jnp.float32) * accum, axis=-1).T

    def grad_step(grad_query, index):
        probs, key_block, val_block = block_probs(index)
        grad_probs = jnp.einsum(
            "qhd,khd->hqk", grad_heads, val_block, preferred_element_type=jnp.float32
        )
        grad_scores = (probs * (grad_probs - delta[..., None])).astype(jnp.bfloat16)
        grad_query = (
            grad_query
            + jnp.einsum("hqk,khd->qhd", grad_scores, key_block, preferred_element_type=jnp.float32)
            * scale
        )
        grad_key = (
            jnp.einsum("hqk,qhd->khd", grad_scores, query_heads, preferred_element_type=jnp.float32)
            * scale
        )
        grad_val = jnp.einsum(
            "hqk,qhd->khd",
            probs.astype(jnp.bfloat16),
            grad_heads,
            preferred_element_type=jnp.float32,
        )
        return (grad_query, (grad_key, grad_val))

    grad_query, (grad_keys, grad_vals) = lax.scan(
        grad_step, jnp.zeros((tok_count, HEADS, HEAD), jnp.float32), block_ids
    )
    grad_key_own, grad_val_own = (
        lax.psum_scatter(
            grad_keys.reshape(full_rows, width), "ctx", scatter_dimension=0, tiled=True
        ),
        lax.psum_scatter(
            grad_vals.reshape(full_rows, width), "ctx", scatter_dimension=0, tiled=True
        ),
    )
    grad_qkv_low = jnp.concatenate(
        [grad_query.reshape(tok_count, width), grad_key_own, grad_val_own], axis=1
    ).astype(jnp.bfloat16)
    grad_qkv_part = contract_rows(tok_rows, grad_qkv_low)
    grad_tokens = grad_hidden + contract_cols(grad_qkv_low, qkv_full)
    dense = (
        lax.psum_scatter(grad_qkv_part, "fsdp", scatter_dimension=0, tiled=True),
        lax.psum_scatter(grad_out_part, "fsdp", scatter_dimension=0, tiled=True),
        lax.psum_scatter(grad_router_part, "fsdp", scatter_dimension=0, tiled=True),
        lax.psum_scatter(grad_gain_part, "fsdp", scatter_dimension=0, tiled=True),
        lax.psum_scatter(grad_bias_part, "fsdp", scatter_dimension=0, tiled=True),
    )
    totals = lax.psum(
        (dense[0], dense[1], dense[2], dense[3], dense[4], grad_up_own, grad_down_own), "ctx"
    )
    return (
        layer_out[None],
        grad_tokens[None],
        totals[0],
        totals[1],
        totals[2],
        totals[3],
        totals[4],
        totals[5],
        totals[6],
    )


def cost(microseconds):
    return pl.CostEstimate(flops=int(microseconds * 1.15e9), bytes_accessed=1 << 20, transcendentals=0)


LOG2E = 1.4426950408889634
HIDE = -1e30
SAFE = 100.0
RUN = 1024
HALF = 512
VMEM = pl.BlockSpec(memory_space=pltpu.VMEM)
SMEM = pl.BlockSpec(memory_space=pltpu.SMEM)
ANY = pl.BlockSpec(memory_space=pl.ANY)
LIMIT = 60 << 20
CORE_LIMIT = 63 << 20


def dot_nn(left, right):
    return lax.dot_general(left, right, (((1,), (0,)), ((), ())), preferred_element_type=jnp.float32)


def dot_nt(left, right):
    return lax.dot_general(left, right, (((1,), (1,)), ((), ())), preferred_element_type=jnp.float32)


def dot_tn(left, right):
    return lax.dot_general(left, right, (((0,), (0,)), ((), ())), preferred_element_type=jnp.float32)


def split3(value):
    one = value.astype(jnp.bfloat16)
    rest = value - one.astype(jnp.float32)
    two = rest.astype(jnp.bfloat16)
    three = (rest - two.astype(jnp.float32)).astype(jnp.bfloat16)
    return one, two, three


def span(index, size, width=None):
    return pl.ds(pl.multiple_of(index * size, size), size if width is None else width)


def flipped(value):
    return value.astype(jnp.float32).T.astype(value.dtype)


def boundaries(seg_ref, lane):
    segs = seg_ref[...]
    begin = jnp.zeros(lane.shape, jnp.int32)
    end = jnp.zeros(lane.shape, jnp.int32)
    for c in range(1, 10):
        below = (segs < c).astype(jnp.int32)
        total = jnp.sum(jnp.sum(below, axis=1, keepdims=True), axis=0, keepdims=True)
        begin = jnp.where(lane == HEAD - 1 + c, total, begin)
        end = jnp.where(lane == HEAD - 2 + c, total, end)
    return begin, jnp.where(lane == HEAD + 8, 0, end)


def fwd_body(blocks, block_len, table_ref, tok_ref, w_ref, seg_ref, att_ref, qf_ref, kf_ref, vf_ref, stat_ref, vt_ref, inv_ref):
    rows = blocks * block_len
    for t in range(blocks):
        inv_ref[table_ref[t]] = t
    weight = w_ref[...].reshape(w_ref.shape[0] * w_ref.shape[1], w_ref.shape[2])
    weight = jnp.concatenate([weight, jnp.zeros((weight.shape[0], HEAD), weight.dtype)], axis=1)
    lane = lax.broadcasted_iota(jnp.int32, (1, 2 * HEAD), 1)
    begin, end = boundaries(seg_ref, lane)
    is_flag = (lane >= HEAD) & (lane < HEAD + 8)
    is_one = (lane >= HEAD + 8) & (lane < HEAD + 11)
    pair = (lax.broadcasted_iota(jnp.int32, (2 * HEAD, 2 * HEAD), 0) // HEAD == lane // HEAD).astype(jnp.bfloat16)
    ones_v = ((lane >= HEAD) & (lane < HEAD + 3)).astype(jnp.float32)

    def project(s, sizes):
        t = inv_ref[s]
        qkv = dot_nn(tok_ref[span(t, block_len), :], weight)
        both = qkv[:, :2 * HEAD].astype(jnp.bfloat16).astype(jnp.float32)
        turned = pltpu.roll(both, HEAD, 1)
        value = qkv[:, 2 * HEAD:]
        place = lax.broadcasted_iota(jnp.int32, (block_len, 2 * HEAD), 0) + s * block_len
        own = (place >= begin) & (place < end)
        at = span(s, block_len)
        flag_q = jnp.where(is_flag & jnp.logical_not(own), 1.0, 0.0)
        flag_k = jnp.where(own, HIDE, jnp.where(is_one, 1.0, 0.0))
        qf_ref[at, :] = jnp.where(lane < HEAD, both, flag_q).astype(jnp.bfloat16)
        kf_ref[at, :] = jnp.where(lane < HEAD, turned, flag_k).astype(jnp.bfloat16)
        vf_ref[at, :] = (value + ones_v).astype(jnp.bfloat16)
        vt_ref[:, at] = jnp.where(lane < HEAD, value, 1.0).T.astype(jnp.bfloat16)
        return jnp.maximum(sizes, dot_nn((both * both).astype(jnp.bfloat16), pair))

    sizes = lax.fori_loop(0, blocks, project, jnp.zeros((block_len, 2 * HEAD), jnp.float32), unroll=4)
    scale = HEAD ** (-0.5) * LOG2E
    q_size, k_size = jnp.max(sizes[:, :HEAD]), jnp.max(sizes[:, HEAD:])
    small = q_size * k_size <= (SAFE / scale) ** 2
    causal = lax.broadcasted_iota(jnp.int32, (HALF, HALF), 0) <= lax.broadcasted_iota(jnp.int32, (HALF, HALF), 1)

    def query_run(online, run):
        def tile(state, q_at, k_at, diagonal):
            scores = dot_nt(kf_ref[k_at, :], qf_ref[q_at, :]) * scale
            if diagonal:
                scores = jnp.where(causal, scores, HIDE)
            top, acc = state
            if online:
                new_top = jnp.maximum(top, jnp.max(scores, axis=0, keepdims=True))
                acc = acc * jnp.exp2(top - new_top)
                scores, top = scores - new_top, new_top
            return top, acc + dot_nn(vt_ref[:, k_at], jnp.exp2(scores).astype(jnp.bfloat16))

        start = (jnp.full((1, RUN), HIDE if online else 0.0, jnp.float32), jnp.zeros((2 * HEAD, RUN), jnp.float32))
        whole = lax.fori_loop(0, run, lambda n, state: tile(state, span(run, RUN), span(n, RUN), False), start)
        early, late = span(2 * run, HALF), span(2 * run + 1, HALF)
        first = tile([part[:, :HALF] for part in whole], early, early, True)
        second = tile([part[:, HALF:] for part in whole], late, early, False)
        second = tile(second, late, late, True)
        for at, (top, acc) in ((early, first), (late, second)):
            total = acc[HEAD:]
            stat = jnp.concatenate([acc[:HEAD] / total, top + jnp.log2(total)], axis=0).T
            stat_ref[at, :] = stat
            one, two, three = split3(stat * (-1.0 / scale))
            old = qf_ref[at, :]
            old = jnp.where(lane == HEAD + 8, one, old)
            old = jnp.where(lane == HEAD + 9, two, old)
            qf_ref[at, :] = jnp.where(lane == HEAD + 10, three, old)

    for online in (False, True):
        @pl.when(small != online)
        def _():
            @pl.loop(0, rows // RUN)
            def _(run):
                query_run(online, run)

    for c in range(blocks // 2):
        parts = [stat_ref[span(table_ref[2 * c + half], block_len), :HEAD] for half in range(2)]
        att_ref[c] = jnp.concatenate(parts, axis=1).astype(jnp.bfloat16)


def attn_fwd(tokens_all, weight, table, segs):
    rows, blocks = tokens_all.shape[0], table.shape[0]
    block_len = rows // blocks
    low = jnp.bfloat16
    return pl.pallas_call(
        functools.partial(fwd_body, blocks, block_len),
        out_shape=(
            jax.ShapeDtypeStruct((blocks // 2, block_len, 2 * HEAD), low),
            jax.ShapeDtypeStruct((rows, 2 * HEAD), low),
            jax.ShapeDtypeStruct((rows, 2 * HEAD), low),
            jax.ShapeDtypeStruct((rows, 2 * HEAD), low),
            jax.ShapeDtypeStruct((rows, 2 * HEAD), jnp.float32),
        ),
        in_specs=[SMEM, VMEM, VMEM, VMEM],
        out_specs=(VMEM,) * 5,
        scratch_shapes=[pltpu.VMEM((2 * HEAD, rows), low), pltpu.SMEM((blocks,), jnp.int32)],
        compiler_params=pltpu.CompilerParams(vmem_limit_bytes=LIMIT),
        cost_estimate=cost(30),
        name="attention",
    )(table, tokens_all, weight, segs)


MESH = pl.DeviceIdType.MESH


def flip(index, bit):
    return index + bit - 2 * bit * lax.rem(index // bit, 2)


def meet(devices):
    barrier = pltpu.get_barrier_semaphore()
    for device in devices:
        pl.semaphore_signal(barrier, inc=1, device_id=device, device_id_type=MESH)
    pl.semaphore_wait(barrier, len(devices))


def push(src, dst, send_sem, recv_sem, device):
    return pltpu.make_async_remote_copy(
        src_ref=src, dst_ref=dst, send_sem=send_sem, recv_sem=recv_sem, device_id=device, device_id_type=MESH
    )


def gather_body(
    zs, tok_ref, wq_ref, wo_ref, router_ref, gain_ref, bias_ref, toks_ref, heads_ref, wos_ref, packs_ref, parts_ref,
    head_buf, pack_buf, own_sem, z_send, z_recv, far_send, near_send, own_recv, diag_recv, near_recv,
):
    me, z = lax.axis_index("ctx"), lax.axis_index("fsdp")
    sib, xn, yn, diag = flip(me, 1), flip(me, 2), flip(me, 4), flip(flip(me, 2), 4)
    z_peers = [lax.rem(z + k, zs) for k in range(1, zs)]
    meet([(sib, z), (xn, z), (yn, z)] + [(me, other) for other in z_peers])
    half = tok_ref.shape[0] // 2
    count = toks_ref.shape[0]

    def part(device, k):
        return toks_ref.at[device, pl.ds(k * half, half)]

    started, locals_ = [], []

    def go(copy):
        copy.start()
        started.append(copy)

    for k in (0, 1):
        rows = tok_ref.at[pl.ds(k * half, half)]
        go(push(rows, part(me, k), far_send.at[0, k], own_recv.at[0, k], (xn, z)))
        rows = tok_ref.at[pl.ds((1 - k) * half, half)]
        go(push(rows, part(me, 1 - k), far_send.at[1, 1 - k], own_recv.at[1, 1 - k], (yn, z)))

    def share(i, shard, whole):
        for k, other in enumerate(z_peers):
            go(push(shard, whole.at[z], z_send.at[i, k], z_recv.at[i, k], (me, other)))
        locals_.append(pltpu.make_async_copy(shard, whole.at[z], own_sem.at[i]))
        locals_[-1].start()

    depth = wq_ref.shape[0] // count
    width = wq_ref.shape[1] // 3
    for h in range(count):
        @pl.when(me == h)
        def _():
            cols = [wq_ref[:, width * kind + HEAD * h:width * kind + HEAD * (h + 1)] for kind in range(3)]
            head_buf[...] = jnp.concatenate(cols, axis=1)

    share(0, head_buf, heads_ref)
    share(1, wo_ref, wos_ref)
    experts = router_ref.shape[0]
    rows = [router_ref[...].astype(jnp.float32), gain_ref[...].astype(jnp.float32), bias_ref[...].astype(jnp.float32)]
    rows.append(jnp.zeros((pack_buf.shape[0] - experts - 2, pack_buf.shape[1]), jnp.float32))
    pack_buf[...] = jnp.concatenate(rows, axis=0).astype(jnp.bfloat16)
    share(2, pack_buf, packs_ref)
    share(3, wq_ref.at[pl.ds(pl.multiple_of(me * depth, depth), depth)], parts_ref)
    for k in (0, 1):
        rows = tok_ref.at[pl.ds(k * half, half)]
        go(push(rows, part(me, k), near_send.at[0, k], near_recv.at[0, k], (sib, z)))
    locals_.append(pltpu.make_async_copy(tok_ref, toks_ref.at[me], own_sem.at[4]))
    locals_[-1].start()

    def arrived(device, k, sem):
        push(part(device, k), part(device, k), far_send.at[0, 0], sem, (sib, z)).wait_recv()

    def relay(device, k, i):
        go(push(part(device, k), part(device, k), near_send.at[i, k], near_recv.at[i, k], (sib, z)))

    arrived(xn, 0, own_recv.at[0, 0])
    go(push(part(xn, 0), part(xn, 0), far_send.at[2, 0], diag_recv.at[0], (yn, z)))
    relay(xn, 0, 1)
    arrived(yn, 1, own_recv.at[1, 1])
    go(push(part(yn, 1), part(yn, 1), far_send.at[2, 1], diag_recv.at[1], (xn, z)))
    relay(yn, 1, 2)
    arrived(xn, 1, own_recv.at[0, 1])
    relay(xn, 1, 1)
    arrived(yn, 0, own_recv.at[1, 0])
    relay(yn, 0, 2)
    for k in (0, 1):
        arrived(diag, k, diag_recv.at[k])
        relay(diag, k, 3)
    for k in (0, 1):
        for i, device in enumerate((sib, flip(xn, 1), flip(yn, 1), flip(diag, 1))):
            arrived(device, k, near_recv.at[i, k])
    for i, whole in enumerate((heads_ref, wos_ref, packs_ref, parts_ref)):
        for k in range(zs - 1):
            other = lax.rem(z + zs - 1 - k, zs)
            push(whole.at[other], whole.at[other], z_send.at[i, k], z_recv.at[i, k], (me, other)).wait_recv()
    for copy in locals_:
        copy.wait()
    for copy in started:
        copy.wait_send()


def gather(tokens, w_qkv, w_out, w_router, ln_gain, ln_bias, ctx_count, z_count):
    shard, wide = w_qkv.shape
    low = jnp.bfloat16
    outs = [
        (ctx_count,) + tokens.shape, (z_count, shard, 3 * HEAD), (z_count,) + w_out.shape, (z_count, 16, shard),
        (z_count, shard // ctx_count, wide),
    ]
    dma = pltpu.SemaphoreType.DMA
    return pl.pallas_call(
        functools.partial(gather_body, z_count),
        out_shape=[jax.ShapeDtypeStruct(out, low) for out in outs],
        in_specs=[VMEM] * 6,
        out_specs=[ANY] * 5,
        scratch_shapes=[
            pltpu.VMEM((shard, 3 * HEAD), low), pltpu.VMEM((16, shard), low),
            dma((5,)), dma((4, z_count - 1)), dma((4, z_count - 1)), dma((3, 2)), dma((4, 2)), dma((2, 2)), dma((2,)), dma((4, 2)),
        ],
        compiler_params=pltpu.CompilerParams(collective_id=1, has_side_effects=True, vmem_limit_bytes=LIMIT),
        cost_estimate=cost(24),
        name="gather_tokens",
    )(tokens, w_qkv, w_out, w_router.T, ln_gain[None], ln_bias[None])


def norm_parts(hidden):
    center = hidden - jnp.mean(hidden, axis=-1, keepdims=True)
    inv_dev = lax.rsqrt(jnp.mean(center * center, axis=-1, keepdims=True) + epsilon)
    return center * inv_dev, inv_dev


def gelu_parts(value):
    square = value * value
    tangent = jnp.tanh(value * (square * (gelu_coef * gelu_cubic) + gelu_coef))
    half = 0.5 * tangent + 0.5
    rise = value * (square * (3.0 * gelu_coef * gelu_cubic) + gelu_coef)
    return value * half, half + half * (1.0 - tangent) * rise


def core_body(
    experts, groups, table_ref, gid_ref, part_ref, att_ref, tok_ref, cot_ref, wo_ref, pack_ref, qf_ref, kf_ref, vf_ref, stat_ref, toks_ref,
    up_ref, down_ref,
    gq_ref, out_ref, sums_ref, layer_ref, gtok_ref, act_ref, gpre_ref, all_ref,
    tok, cot, wo, pack, att, msend, zin, bsend, bin_, up, down, qf, kf, vf, stat, held, late_held, ghead_out, ghead, wide_out, ghidden,
    dof, qt, dot, dk_acc, dv_acc, sorted_dv, head_acc, send, landing, weight, zsend, zone, total, totals,
    out_mine, out_zone, out_sum, out_part, out_own, out_all,
    load_sem, own_sem, a_send, a_recv, m_send, m_recv, b_send, b_recv, h_send, h_recv, s_send, s_recv, z_send, z_recv, c_send, c_recv,
    o_send, o_recv, g_send, g_recv, r_send, r_recv, w_send, w_recv, v_send, v_recv,
):
    me, z = lax.axis_index("ctx"), lax.axis_index("fsdp")
    count, block_len = att_ref.shape[0], att_ref.shape[1]
    own_rows, width = tok_ref.shape
    owners, own_experts, ffn = msend.shape[0], up_ref.shape[0], up_ref.shape[2]
    flat, per = experts * groups, experts * groups // owners
    blocks = 2 * count
    rows = blocks * block_len
    runs = rows // RUN
    low = jnp.bfloat16
    dq_acc, qk, dv_rows = stat, qf, vf

    def start(copies):
        for copy in copies:
            copy.start()
        return copies

    def wait(copies):
        for copy in copies:
            copy.wait()

    pairs = [(qf_ref, qf), (kf_ref, kf), (tok_ref, tok), (wo_ref, wo), (pack_ref, pack), (cot_ref, cot)]
    for e in range(own_experts):
        pairs += [(up_ref.at[e], up.at[e]), (down_ref.at[e], down.at[e])]
    pairs += [(stat_ref, stat), (vf_ref, vf)]
    loads = start([pltpu.make_async_copy(src, dst, load_sem.at[i]) for i, (src, dst) in enumerate(pairs)])
    sib, same_core = flip(me, 1), [flip(me, 2), flip(me, 4), flip(flip(me, 2), 4)]
    z_peers = [(me, lax.rem(z + k, owners)) for k in range(1, owners)]
    c_peers = [(jnp.bitwise_xor(me, k), z) for k in range(1, count)]
    meet(z_peers + c_peers)
    swap = start([push(att_ref.at[d[0]], att.at[me], a_send.at[k], a_recv.at[k], d) for k, d in enumerate(c_peers)])
    own = start([pltpu.make_async_copy(att_ref.at[me], att.at[me], own_sem.at[0])])

    scale = HEAD ** (-0.5)
    first_diagonal = runs * (runs - 1)

    def slot_of(run, index, part):
        return run * (2 * runs - 1 - run) + 2 * (index - run - 1) + part

    def probabilities(q_at, k_at, visible):
        scores = dot_nt(qf[q_at, :], kf[k_at, :]) * (scale * LOG2E)
        if visible is not None:
            scores = jnp.where(visible, scores, HIDE)
        return jnp.exp2(scores).astype(low)

    def hold_diagonal():
        early = lax.broadcasted_iota(jnp.int32, (RUN, HALF), 1) <= lax.broadcasted_iota(jnp.int32, (RUN, HALF), 0)
        late = lax.broadcasted_iota(jnp.int32, (HALF, HALF), 1) <= lax.broadcasted_iota(jnp.int32, (HALF, HALF), 0)

        @pl.loop(0, runs)
        def _(run):
            held[first_diagonal + run] = probabilities(span(run, RUN), span(2 * run, HALF), early)
            late_held[run] = probabilities(span(2 * run + 1, HALF), span(2 * run + 1, HALF), late)

    def hold(run):
        @pl.loop(run + 1, runs)
        def _(index):
            for part in range(2):
                held[slot_of(run, index, part)] = probabilities(span(index, RUN), span(2 * run + part, HALF), None)

    wait(loads[:2])
    hold_diagonal()

    @pl.loop(1, runs - 1)
    def _(run):
        hold(run)

    wait(own + swap)
    weights = start([push(part_ref, weight.at[:, me], w_send.at[k], w_recv.at[k], (d, z)) for k, d in enumerate(same_core)])
    shares = start([push(part_ref, weight.at[:, me], v_send.at[3], v_recv.at[3], (sib, z))])
    weight[:, me] = part_ref[...]
    wait(loads[2:6])
    halves = [jnp.concatenate([att[h, :, HEAD * p:HEAD * (p + 1)] for h in range(count)], axis=1) for p in range(2)]
    attended = jnp.concatenate(halves, axis=0)
    out_weight = wo[...].reshape(width, width)
    hidden = tok[...].astype(jnp.float32) + dot_nn(attended, out_weight)
    unit, inv_dev = norm_parts(hidden)
    small_in = jnp.concatenate([pack[k] for k in range(owners)], axis=1)
    gain, bias = small_in[experts:experts + 1].astype(jnp.float32), small_in[experts + 1:experts + 2].astype(jnp.float32)
    normed = (unit * gain + bias).astype(low)
    expo = jnp.exp(dot_nt(small_in, normed)[:experts])
    expo = jnp.broadcast_to(expo[:, None, :], (experts, groups, own_rows)).reshape(flat, own_rows)
    member = lax.rem(lax.broadcasted_iota(jnp.int32, (flat, 1), 0), groups) == lax.rem(gid_ref[...], groups)
    expo = jnp.where(member, expo, 0.0)
    mix = expo / jnp.sum(expo, axis=1, keepdims=True)
    mix_low = mix.astype(low)

    def zone_rows(owner, kind):
        return pl.ds(pl.multiple_of((2 * owner + kind) * per, per), per)

    def to_owners(kind, value):
        msend[:, kind] = value.astype(low).reshape(owners, per, width)
        zin[zone_rows(z, kind), :] = msend[z, kind]
        return start([
            push(msend.at[d[1], kind], zin.at[zone_rows(z, kind)], m_send.at[kind, k], m_recv.at[kind, k], d) for k, d in enumerate(z_peers)
        ])

    mixed_copies = to_owners(0, dot_nn(mix_low, normed))
    grad_experts = dot_nn(mix_low, cot[...])
    wait(loads[6:6 + 2 * own_experts])
    wait(mixed_copies)
    grad_copies = to_owners(1, grad_experts)

    def from_sources(kind, e):
        lows_ = [(2 * owner + kind) * per + e * groups for owner in range(owners)]
        return jnp.concatenate([zin[at:at + groups, :] for at in lows_], axis=0)

    def to_sources(kind, e, value):
        bsend[:, kind, e * groups:(e + 1) * groups, :] = value.astype(low).reshape(owners, groups, width)

    def send_back(kind):
        bin_[z, kind] = bsend[z, kind]
        return start([
            push(bsend.at[d[1], kind], bin_.at[z, kind], b_send.at[kind, k], b_recv.at[kind, k], d) for k, d in enumerate(z_peers)
        ])

    slopes = []
    for e in range(own_experts):
        active, slope = gelu_parts(dot_nn(from_sources(0, e), up[e]))
        slopes.append(slope)
        to_sources(0, e, dot_nn(active.astype(low), down[e]))
    out_copies = send_back(0)
    wait(grad_copies)
    gathers = start([push(zin, all_ref.at[me], g_send.at[k], g_recv.at[k], (d, z)) for k, d in enumerate(same_core)])
    relays = start([push(zin, all_ref.at[me], r_send.at[3], r_recv.at[3], (sib, z))])
    own_got = start([pltpu.make_async_copy(zin, all_ref.at[me], own_sem.at[1])])
    for e in range(own_experts):
        grad_pre = (dot_nt(from_sources(1, e), down[e]) * slopes[e]).astype(low)
        to_sources(1, e, dot_nt(grad_pre, up[e]))
    back_copies = send_back(1)
    wait(out_copies)
    expert_out = bin_[:, 0].reshape(flat, width)
    wide_out[...] = hidden + dot_tn(mix_low, expert_out)
    layer_copy = start([pltpu.make_async_copy(wide_out, layer_ref, own_sem.at[2])])
    grad_mix = dot_nt(expert_out, cot[...])
    wait(back_copies)
    grad_mixed = bin_[:, 1].reshape(flat, width)
    product = mix * (grad_mix + dot_nt(grad_mixed, normed))
    grad_logits = product - mix * jnp.sum(product, axis=1, keepdims=True)
    grad_logits = jnp.sum(grad_logits.reshape(experts, groups, own_rows), axis=1).astype(low)
    pad = jnp.zeros((small_in.shape[0] - experts, own_rows), low)
    grad_logits = jnp.concatenate([grad_logits, pad], axis=0)
    grad_normed = dot_tn(jnp.concatenate([mix_low, grad_logits], axis=0), jnp.concatenate([grad_mixed, small_in], axis=0))
    scaled = grad_normed * gain
    mean = jnp.mean(scaled, axis=-1, keepdims=True)
    grad_hidden = cot[...].astype(jnp.float32) + inv_dev * (scaled - mean - unit * jnp.mean(scaled * unit, axis=-1, keepdims=True))
    branch = grad_hidden.astype(low)
    grad_heads = dot_nt(branch, out_weight).astype(low)
    for h in range(count):
        at = slice(HEAD * h, HEAD * (h + 1))
        ghead_out[h] = jnp.concatenate([grad_heads[:block_len, at], grad_heads[block_len:, at]], axis=1)
    swap = start([push(ghead_out.at[d[0]], ghead.at[me], h_send.at[k], h_recv.at[k], d) for k, d in enumerate(c_peers)])
    ghead[me] = ghead_out[me]
    ghidden[...] = grad_hidden
    out_mine[...] = dot_tn(attended, branch).astype(low).reshape(out_mine.shape)
    gout_copies = start([push(out_mine.at[d[1]], out_zone.at[z], o_send.at[0, k], o_recv.at[0, k], d) for k, d in enumerate(z_peers)])
    out_zone[z] = out_mine[z]
    small = jnp.concatenate(
        [
            dot_nn(grad_logits, normed)[:experts],
            jnp.sum(grad_normed * unit, axis=0, keepdims=True),
            jnp.sum(grad_normed, axis=0, keepdims=True),
            jnp.zeros((small_in.shape[0] - experts - 2, width), jnp.float32),
        ],
        axis=0,
    )
    lanes = width // owners
    for c in range(owners):
        zsend[c, 3 * HEAD:, :] = small[:, c * lanes:(c + 1) * lanes].astype(low)
    hold(0)

    def mask(condition):
        return jnp.broadcast_to(jnp.where(condition, 1.0, 0.0), (1, 2 * HEAD))

    firsts = [mask(table_ref[2 * c] < table_ref[2 * c + 1]).astype(low) for c in range(count)]
    lows = [jnp.minimum(table_ref[2 * c], table_ref[2 * c + 1]) for c in range(count)]
    holds = [[mask(lows[c] == j).astype(low) for j in range(count)] for c in range(count)]

    def blend(masks, values):
        out = None
        for weigh, value in zip(masks, values):
            out = weigh * value if out is None else out + weigh * value
        return out

    lane = lax.broadcasted_iota(jnp.int32, (1, 2 * HEAD), 1)

    def prepare(s, both):
        at = slice(s * block_len, (s + 1) * block_len)
        grad = jnp.where(lane < HEAD, both, 0.0)
        delta = jnp.sum(grad * stat[at, :], axis=1, keepdims=True)
        one, two, three = split3(jnp.broadcast_to(-delta, grad.shape))
        wide = jnp.where(lane == HEAD, one, grad.astype(low))
        wide = jnp.where(lane == HEAD + 1, two, wide)
        dof[at, :] = jnp.where(lane == HEAD + 2, three, wide)
        turned = jnp.where(lane < HEAD, both, pltpu.roll(qf[at, :].astype(jnp.float32), HEAD, 1)).T.astype(low)
        dot[:, at] = turned[:HEAD]
        qt[:, at] = turned[HEAD:]

    wait(swap)
    wait(loads[6 + 2 * own_experts:])
    for c in range(count):
        block = ghead[c]
        turned = pltpu.roll(block.astype(jnp.float32), HEAD, 1).astype(low)
        ghead_out[c] = firsts[c] * block + (1 - firsts[c]) * turned
    for j in range(count):
        both = blend([holds[c][j] for c in range(count)], [ghead_out[c] for c in range(count)]).astype(jnp.float32)
        prepare(j, both)
        prepare(blocks - 1 - j, pltpu.roll(both, HEAD, 1))

    tok_loads = [
        pltpu.make_async_copy(toks_ref.at[pl.ds(i * RUN, RUN)], held.at[i], own_sem.at[3 + i]) for i in range(rows // RUN)
    ]

    def key_run(run):
        def tile(q_at, k_at, part, probs, first_k, first_q):
            slope = dot_nt(dof[q_at, :], vf[k_at, :])
            grad = (probs.astype(jnp.float32) * slope).astype(low)
            dv = dot_nn(dot[:, q_at], probs)
            dk = dot_nn(qt[:, q_at], grad)
            dq = dot_nn(grad, kf[k_at, :])
            at = slice(part * HALF, (part + 1) * HALF)
            if first_k:
                dv_acc[:, at] = dv
                dk_acc[:, at] = dk
            else:
                dv_acc[:, at] += dv
                dk_acc[:, at] += dk
            if first_q:
                @pl.when(run == 0)
                def _():
                    dq_acc[q_at, :] = dq

                @pl.when(run != 0)
                def _():
                    dq_acc[q_at, :] += dq
            else:
                dq_acc[q_at, :] += dq

        early, late = span(2 * run, HALF), span(2 * run + 1, HALF)
        tile(span(run, RUN), early, 0, held[first_diagonal + run], True, True)
        tile(late, late, 1, late_held[run], True, False)

        @pl.loop(run + 1, runs)
        def _(index):
            for part in range(2):
                tile(span(index, RUN), span(2 * run + part, HALF), part, held[slot_of(run, index, part)], False, part == 0)

        at = span(run, RUN)
        both = jnp.concatenate([dk_acc[...] * scale, dv_acc[...]], axis=0).T
        query = dq_acc[at, :] * scale
        qk[at, :] = jnp.where(lane < HEAD, query, pltpu.roll(both, HEAD, 1)).astype(low)
        dv_rows[at, :] = both.astype(low)

    def send_half(half):
        mid = block_len // 2
        for c in range(count):
            ats = [slice(s * block_len, (s + 1) * block_len) for s in (range(count) if half == 0 else range(blocks - 1, count - 1, -1))]
            send[half, c, :block_len, :] = blend(holds[c], [qk[at, :] for at in ats])
            values = blend(holds[c], [dv_rows[at, :] for at in ats])
            sorted_dv[c] = values
            values = values[:, HEAD:]
            send[half, c, block_len:, :] = jnp.concatenate([values[:mid], values[mid:]], axis=1)
        landing[half, me] = send[half, me]
        return start([
            push(send.at[half, d[0]], landing.at[half, me], s_send.at[half, k], s_recv.at[half, k], d) for k, d in enumerate(c_peers)
        ])

    def head_weights(half):
        first, second = None, None
        for c in range(count):
            order = firsts[c][:, :1] if half == 0 else 1 - firsts[c][:, :1]
            slot, at = divmod(c * own_rows, RUN)
            here = order * held[slot, at:at + block_len, :] + (1 - order) * held[slot, at + block_len:at + 2 * block_len, :]
            one, two = dot_tn(send[half, c, :block_len, :], here), dot_tn(sorted_dv[c], here)
            first, second = (one, two) if first is None else (first + one, second + two)
        both = jnp.concatenate([first, second[HEAD:]], axis=0)
        if half == 0:
            head_acc[...] = both
        else:
            head_acc[...] += both

    @pl.loop(0, runs // 2)
    def _(run):
        key_run(run)

        @pl.when(run == 0)
        def _():
            start(tok_loads)

    swaps = send_half(0)
    for k, d in enumerate(same_core):
        gathers[k].wait_recv()
        relays += start([push(all_ref.at[d], all_ref.at[d], r_send.at[k], r_recv.at[k], (sib, z))])
        weights[k].wait_recv()
        shares += start([push(weight.at[:, d], weight.at[:, d], v_send.at[k], v_recv.at[k], (sib, z))])
    wait(gout_copies)
    summed = out_zone[0].astype(jnp.float32)
    for k in range(1, owners):
        summed = summed + out_zone[k].astype(jnp.float32)
    out_sum[...] = summed.astype(low).reshape(out_sum.shape)
    part_copies = start([push(out_sum.at[d[0]], out_part.at[me], o_send.at[1, k], o_recv.at[1, k], d) for k, d in enumerate(c_peers)])
    out_part[me] = out_sum[me]
    wait(tok_loads)
    head_weights(0)

    @pl.loop(runs // 2, runs)
    def _(run):
        key_run(run)

    swaps += send_half(1)
    wait(part_copies)
    summed = out_part[0].astype(jnp.float32)
    for k in range(1, count):
        summed = summed + out_part[k].astype(jnp.float32)
    out_own[...] = summed.astype(low)
    last_copies = start([push(out_own, out_all.at[me], o_send.at[2, k], o_recv.at[2, k], d) for k, d in enumerate(c_peers)])
    out_all[me] = out_own[...]
    wait(own_got + relays)

    mixed_slot = rows // RUN
    share = owners * 2 * per
    mixed_loads = []
    for c in range(count):
        slot, at = divmod(c * share, RUN)
        mixed_loads.append(pltpu.make_async_copy(all_ref.at[c], held.at[mixed_slot + slot, pl.ds(at, share)], own_sem.at[3 + rows // RUN + c]))
    start(mixed_loads)
    head_weights(1)
    for c in range(owners):
        zsend[c, :3 * HEAD, :] = head_acc[:, c * lanes:(c + 1) * lanes].astype(low)
    z_copies = start([push(zsend.at[d[1]], zone.at[z], z_send.at[k], z_recv.at[k], d) for k, d in enumerate(z_peers)])
    zone[z] = zsend[z]
    wait(mixed_loads)
    step = HALF
    chunks = ffn // step
    wide_slot = mixed_slot + count * share // RUN

    def of_expert(kind, e):
        parts = []
        for slot in range(mixed_slot, wide_slot):
            value = held[slot].reshape(RUN // share, owners, 2, own_experts, groups, width)
            parts.append(value[:, :, kind, e].reshape(-1, width))
        return jnp.concatenate(parts, axis=0)

    def expert_part(e):
        mixed, grad_out = of_expert(0, e), of_expert(1, e)
        copies = []

        @pl.loop(0, chunks // 2)
        def _(i):
            for part in range(2):
                at = span(2 * i + part, step)
                to = pl.ds(part * step, step)
                active, slope = gelu_parts(dot_nn(mixed, up[e, :, at]))
                held[wide_slot + chunks * e + i, to, :] = active.astype(low)
                slot = wide_slot + chunks * e + chunks // 2 + i
                held[slot, to, :] = (dot_nt(grad_out, down[e, at, :]) * slope).astype(low)

        for i in range(chunks):
            slot = wide_slot + chunks * e + i // 2
            at, to = pl.ds(i * step, step), pl.ds(i % 2 * step, step)
            sem = own_sem.at[3 + rows // RUN + count + 2 * (chunks * e + i)]
            copies.append(pltpu.make_async_copy(held.at[slot, to], act_ref.at[e, :, at], sem))
            sem = own_sem.at[4 + rows // RUN + count + 2 * (chunks * e + i)]
            copies.append(pltpu.make_async_copy(held.at[slot + chunks // 2, to], gpre_ref.at[e, :, at], sem))
        return start(copies)

    stores = expert_part(0)
    wait(z_copies)
    summed = zone[0].astype(jnp.float32)
    for k in range(1, owners):
        summed = summed + zone[k].astype(jnp.float32)
    total[...] = summed.astype(low)
    c_copies = start([push(total, totals.at[me], c_send.at[k], c_recv.at[k], d) for k, d in enumerate(c_peers)])
    totals[me] = total[...]
    for e in range(1, own_experts):
        stores += expert_part(e)
    wait(swaps + shares)
    flat_weight = weight[...].reshape(width, -1)
    parts = []
    for half in range(2):
        queries, keys, values = [], [], []
        for h in range(count):
            front, back = landing[half, h, :block_len, :], landing[half, h, block_len:, :]
            queries.append(front[:, :HEAD])
            keys.append(front[:, HEAD:])
            values.append(jnp.concatenate([back[:, :HEAD], back[:, HEAD:]], axis=0))
        parts.append(dot_nt(jnp.concatenate(queries + keys + values, axis=1), flat_weight))
    in_order = mask(table_ref[2 * me] < table_ref[2 * me + 1])[:, :1]
    wait(layer_copy)
    wide_out[:block_len, :] = ghidden[:block_len, :] + (in_order * parts[0] + (1.0 - in_order) * parts[1])
    wide_out[block_len:, :] = ghidden[block_len:, :] + (in_order * parts[1] + (1.0 - in_order) * parts[0])
    stores += start([pltpu.make_async_copy(wide_out, gtok_ref, own_sem.at[2])])
    wait(last_copies)
    out_ref[...] = out_all[...].astype(jnp.float32).reshape(out_ref.shape)
    wait(c_copies)
    small = None
    turned = []
    for c in range(count):
        turned.append(totals[c, :3 * HEAD, :].astype(jnp.float32).T)
        part = totals[c, 3 * HEAD:, :].astype(jnp.float32)
        small = part if small is None else small + part
    sums_ref[...] = small
    for kind in range(3):
        at = slice(HEAD * kind, HEAD * (kind + 1))
        gq_ref[:, HEAD * count * kind:HEAD * count * (kind + 1)] = jnp.concatenate([part[:, at] for part in turned], axis=1)
    wait(stores)
    for copy in gathers + weights:
        copy.wait_send()


def core(table, gid_row, parts, att, tokens, cot, w_out, pack, saved, tokens_all, w_up, w_down, experts, groups):
    count, block_len = att.shape[:2]
    qf, kf, vf, stat = saved
    rows, (own_rows, width) = qf.shape[0], tokens.shape
    runs = rows // RUN
    own_experts, _, ffn = w_up.shape
    owners, smalls, lanes = pack.shape
    height = 3 * HEAD + smalls
    per = experts * groups // owners
    wide = (own_experts, count * owners * groups, ffn)
    share = (owners * 2 * per, width)
    part = (count, lanes // count, width)
    swap = (2, count, block_len + block_len // 2, 2 * HEAD)
    gout = (owners, lanes, width)
    sent = (owners, 2, per, width)
    low, full = jnp.bfloat16, jnp.float32
    scratch = [
        (tokens.shape, low), (cot.shape, low), (w_out.shape, low), (pack.shape, low), (att.shape, low),
        (sent, low), (share, low), (sent, low), (sent, low), (w_up.shape, low), (w_down.shape, low),
        (qf.shape, low), (kf.shape, low), (vf.shape, low), (stat.shape, full), ((runs * runs, RUN, HALF), low), ((runs, HALF, HALF), low),
        (att.shape, low), (att.shape, low), (tokens.shape, full), (tokens.shape, full),
        ((rows, 2 * HEAD), low), ((HEAD, rows), low), ((HEAD, rows), low), ((HEAD, RUN), full), ((HEAD, RUN), full),
        ((count, block_len, 2 * HEAD), low), ((3 * HEAD, width), full), (swap, low), (swap, low), ((owners, count) + parts.shape[1:], low),
        ((owners, height, lanes), low), ((owners, height, lanes), low), ((height, lanes), low), ((count, height, lanes), low),
        (gout, low), (gout, low), (part, low), (part, low), (part[1:], low), (part, low),
    ]
    owns = 3 + rows // RUN + count + 2 * own_experts * (ffn // HALF)
    to_z, to_c = owners - 1, count - 1
    sems = [
        (8 + 2 * own_experts,), (owns,), (to_c,), (to_c,), (2, to_z), (2, to_z), (2, to_z), (2, to_z), (to_c,), (to_c,), (2, to_c), (2, to_c),
        (to_z,), (to_z,), (to_c,), (to_c,), (3, to_c), (3, to_c), (3,), (3,), (4,), (4,), (3,), (3,), (4,), (4,),
    ]
    return pl.pallas_call(
        functools.partial(core_body, experts, groups),
        out_shape=(
            jax.ShapeDtypeStruct((lanes, 3 * width), full),
            jax.ShapeDtypeStruct((lanes, width), full),
            jax.ShapeDtypeStruct((smalls, lanes), full),
            jax.ShapeDtypeStruct(tokens.shape, full),
            jax.ShapeDtypeStruct(tokens.shape, full),
            jax.ShapeDtypeStruct(wide, low),
            jax.ShapeDtypeStruct(wide, low),
            jax.ShapeDtypeStruct((count,) + share, low),
        ),
        in_specs=[SMEM, VMEM, VMEM] + [ANY] * 12,
        out_specs=(VMEM,) * 3 + (ANY,) * 5,
        scratch_shapes=[pltpu.VMEM(shape, dtype) for shape, dtype in scratch] + [pltpu.SemaphoreType.DMA(shape) for shape in sems],
        compiler_params=pltpu.CompilerParams(collective_id=2, has_side_effects=True, vmem_limit_bytes=CORE_LIMIT),
        cost_estimate=cost(85),
        name="core",
    )(table, gid_row, parts, att, tokens, cot, w_out, pack, qf, kf, vf, stat, tokens_all.reshape(rows, width), w_up, w_down)


def expert_grad_body(experts, passed, mixed_ref, grad_ref, act_ref, gpre_ref, small_ref, *refs):
    sources, outs = refs[:passed], refs[passed + 5:]
    gup_ref, gdown_ref, router_ref, gain_ref, bias_ref = refs[passed:passed + 5]
    width = gup_ref.shape[1]
    for source, out in zip(sources, outs):
        out[...] = source[...]
    router_ref[...] = small_ref[:experts]
    gain_ref[...] = small_ref[experts:experts + 1]
    bias_ref[...] = small_ref[experts + 1:experts + 2]
    gup_ref[0] = dot_tn(mixed_ref[...].reshape(-1, width), gpre_ref[0])
    gdown_ref[0] = dot_tn(act_ref[0], grad_ref[...].reshape(-1, width))


def expert_grads(gathered, active, grad_pre, small, passed, groups, experts):
    own, rows, ffn = active.shape
    step = ffn
    steps = ffn // step
    sources, width = gathered.shape[0], gathered.shape[3]
    view = gathered.reshape(sources, 2, own, groups, width)
    lanes = small.shape[1]
    full = jnp.float32
    slices = [pl.BlockSpec((x.shape[0] // (own * steps), x.shape[1]), lambda e, f: (e * steps + f, 0)) for x in passed]
    return pl.pallas_call(
        functools.partial(expert_grad_body, experts, len(passed)),
        grid=(own, steps),
        out_shape=[
            jax.ShapeDtypeStruct((own, width, ffn), full), jax.ShapeDtypeStruct((own, ffn, width), full),
            jax.ShapeDtypeStruct((experts, lanes), full), jax.ShapeDtypeStruct((1, lanes), full), jax.ShapeDtypeStruct((1, lanes), full),
        ] + [jax.ShapeDtypeStruct(x.shape, x.dtype) for x in passed],
        in_specs=[
            pl.BlockSpec((sources, 1, 1, groups, width), lambda e, f: (0, 0, e, 0, 0)),
            pl.BlockSpec((sources, 1, 1, groups, width), lambda e, f: (0, 1, e, 0, 0)),
            pl.BlockSpec((1, rows, step), lambda e, f: (e, 0, f)),
            pl.BlockSpec((1, rows, step), lambda e, f: (e, 0, f)),
            pl.BlockSpec(small.shape, lambda e, f: (0, 0)),
        ] + slices,
        out_specs=[
            pl.BlockSpec((1, width, step), lambda e, f: (e, 0, f)), pl.BlockSpec((1, step, width), lambda e, f: (e, f, 0)),
            pl.BlockSpec((experts, lanes), lambda e, f: (0, 0)), pl.BlockSpec((1, lanes), lambda e, f: (0, 0)),
            pl.BlockSpec((1, lanes), lambda e, f: (0, 0)),
        ] + slices,
        compiler_params=pltpu.CompilerParams(vmem_limit_bytes=LIMIT),
        cost_estimate=cost(10),
        name="expert_grads",
    )(view, view, active, grad_pre, small, *passed)


def fast_device(
    tokens, cotangent, block_table, seg_ids, group_ids, w_qkv, w_out, w_router, ln_gain, ln_bias, w_up, w_down
):
    ctx_count, z_count = lax.axis_size("ctx"), lax.axis_size("fsdp")
    tok_rows, cot_rows = tokens[0], cotangent[0]
    rows, width = tok_rows.shape
    experts = w_router.shape[1]
    groups = rows // GROUP_SIZE
    tokens_all, head_weights, out_full, pack_full, qkv_parts = gather(
        tok_rows, w_qkv, w_out, w_router, ln_gain, ln_bias, ctx_count, z_count
    )
    att, *saved = attn_fwd(tokens_all.reshape(ctx_count * rows, width), head_weights, block_table, seg_ids)
    grad_qkv, grad_out, small, layer_out, grad_tokens, active, grad_pre, gathered = core(
        block_table, group_ids, qkv_parts, att, tok_rows, cot_rows, out_full, pack_full, saved, tokens_all, w_up, w_down, experts, groups
    )
    gathered = gathered.reshape(ctx_count * z_count, 2, experts * groups // z_count, width)
    grad_up, grad_down, grad_router, grad_gain, grad_bias, layer_out, grad_tokens, grad_qkv, grad_out = expert_grads(
        gathered, active, grad_pre, small, [layer_out, grad_tokens, grad_qkv, grad_out], groups, experts
    )
    return (
        layer_out[None],
        grad_tokens[None],
        grad_qkv,
        grad_out,
        grad_router.T,
        grad_gain[0],
        grad_bias[0],
        grad_up,
        grad_down,
    )


def solution(mesh):
    placed = (
        P("fsdp", "ctx", None),
        P("fsdp", "ctx", None),
        P(),
        P("fsdp", None),
        P("fsdp", "ctx"),
        P("fsdp", None),
        P("fsdp", None),
        P("fsdp", None),
        P("fsdp"),
        P("fsdp"),
        P("fsdp", None, None),
        P("fsdp", None, None),
    )
    step = fast_device if mesh.shape["ctx"] == HEADS else on_device
    return jax.shard_map(
        step,
        mesh=mesh,
        in_specs=placed,
        out_specs=(
            P("fsdp", "ctx", None),
            P("fsdp", "ctx", None),
            P("fsdp", None),
            P("fsdp", None),
            P("fsdp", None),
            P("fsdp"),
            P("fsdp"),
            P("fsdp", None, None),
            P("fsdp", None, None),
        ),
        check_vma=False,
    )
```

```python
import functools

import jax
import jax.numpy as jnp
from jax import lax
from jax.experimental import pallas as pl
from jax.experimental.pallas import tpu as pltpu
from jax.sharding import PartitionSpec as P

HEADS = 8
HEAD = 64
GROUP_SIZE = 32
KEY_BLOCK = 2048


highest = lax.Precision.HIGHEST
neg_large = -1e30
epsilon = 1e-05
gelu_coef = 0.7978845608028654
gelu_cubic = 0.044715


def contract_rows(left, right):
    return lax.dot_general(
        left, right, (((0,), (0,)), ((), ())), preferred_element_type=jnp.float32
    )


def contract_cols(left, right):
    return lax.dot_general(
        left, right, (((1,), (1,)), ((), ())), preferred_element_type=jnp.float32
    )


def gelu_slope(value):
    inner = gelu_coef * (value + gelu_cubic * value * value * value)
    tangent = jnp.tanh(inner)
    return 0.5 * (1.0 + tangent) + 0.5 * value * (1.0 - tangent * tangent) * gelu_coef * (
        1.0 + 3.0 * gelu_cubic * value * value
    )


def expert_forward(mixed_low, up_weight, down_weight):
    pre = jnp.einsum("ged,edh->geh", mixed_low, up_weight, preferred_element_type=jnp.float32)
    active = jax.nn.gelu(pre, approximate=True).astype(jnp.bfloat16)
    result = jnp.einsum("geh,ehd->ged", active, down_weight, preferred_element_type=jnp.float32)
    return (pre, active, result.astype(jnp.bfloat16))


def expert_backward(mixed_low, pre, active, grad_result, up_weight, down_weight):
    grad_act = jnp.einsum(
        "ged,ehd->geh", grad_result, down_weight, preferred_element_type=jnp.float32
    )
    grad_pre = (grad_act * gelu_slope(pre)).astype(jnp.bfloat16)
    grad_down_part = jnp.einsum(
        "geh,ged->ehd", active, grad_result, preferred_element_type=jnp.float32
    )
    grad_up_part = jnp.einsum(
        "ged,geh->edh", mixed_low, grad_pre, preferred_element_type=jnp.float32
    )
    grad_mixed = jnp.einsum("geh,edh->ged", grad_pre, up_weight, preferred_element_type=jnp.float32)
    return (grad_up_part, grad_down_part, grad_mixed.astype(jnp.bfloat16))


def on_device(
    tokens,
    cotangent,
    block_table,
    seg_ids,
    group_ids,
    w_qkv,
    w_out,
    w_router,
    ln_gain,
    ln_bias,
    w_up,
    w_down,
):
    tok_rows = tokens[0]
    tok_count = tok_rows.shape[0]
    width = tok_rows.shape[1]
    expert_count = w_router.shape[1]
    ctx_index = lax.axis_index("ctx")
    full_rows = seg_ids.shape[1]
    block_len = full_rows // block_table.shape[0]
    row_ids = jnp.arange(full_rows, dtype=jnp.int32)
    key_pos = jnp.take(block_table, row_ids // block_len) * block_len + row_ids % block_len
    key_seg = seg_ids[0]
    pos_rows = lax.dynamic_slice_in_dim(key_pos, ctx_index * tok_count, tok_count)
    seg_rows = lax.dynamic_slice_in_dim(key_seg, ctx_index * tok_count, tok_count)
    scale = HEAD ** (-0.5)
    qkv_full, out_full, router_full, gain_full, bias_full = (
        lax.all_gather(w_qkv, "fsdp", axis=0, tiled=True),
        lax.all_gather(w_out, "fsdp", axis=0, tiled=True),
        lax.all_gather(w_router, "fsdp", axis=0, tiled=True),
        lax.all_gather(ln_gain, "fsdp", axis=0, tiled=True),
        lax.all_gather(ln_bias, "fsdp", axis=0, tiled=True),
    )
    qkv = jnp.dot(tok_rows, qkv_full, preferred_element_type=jnp.float32).astype(jnp.bfloat16)
    query_heads = qkv[:, :width].reshape(tok_count, HEADS, HEAD)
    key_all, val_all = (
        lax.all_gather(qkv[:, width : 2 * width], "ctx", axis=0, tiled=True),
        lax.all_gather(qkv[:, 2 * width :], "ctx", axis=0, tiled=True),
    )
    key_heads = key_all.reshape(full_rows, HEADS, HEAD)
    val_heads = val_all.reshape(full_rows, HEADS, HEAD)
    block_count = full_rows // KEY_BLOCK
    block_ids = jnp.arange(block_count, dtype=jnp.int32)

    def block_scores(index):
        start = index * KEY_BLOCK
        key_block = lax.dynamic_slice_in_dim(key_heads, start, KEY_BLOCK, 0)
        val_block = lax.dynamic_slice_in_dim(val_heads, start, KEY_BLOCK, 0)
        pos_block = lax.dynamic_slice_in_dim(key_pos, start, KEY_BLOCK, 0)
        seg_block = lax.dynamic_slice_in_dim(key_seg, start, KEY_BLOCK, 0)
        scores = (
            jnp.einsum("qhd,khd->hqk", query_heads, key_block, preferred_element_type=jnp.float32)
            * scale
        )
        allowed = (pos_block[None, :] <= pos_rows[:, None]) & (
            (seg_block[None, :] == 0) | (seg_block[None, :] == seg_rows[:, None])
        )
        return (scores, allowed[None], key_block, val_block)

    def lse_step(carry, index):
        top, total = carry
        scores, allowed, key_block, val_block = block_scores(index)
        masked = jnp.where(allowed, scores, neg_large)
        new_top = jnp.maximum(top, jnp.max(masked, axis=-1))
        weights = jnp.where(allowed, jnp.exp(masked - new_top[..., None]), 0.0)
        return ((new_top, total * jnp.exp(top - new_top) + jnp.sum(weights, axis=-1)), None)

    start_top = jnp.full((HEADS, tok_count), neg_large, jnp.float32)
    (top, total), unused = lax.scan(
        lse_step, (start_top, jnp.zeros((HEADS, tok_count), jnp.float32)), block_ids
    )
    log_total = top + jnp.log(total)

    def block_probs(index):
        scores, allowed, key_block, val_block = block_scores(index)
        probs = jnp.where(allowed, jnp.exp(scores - log_total[..., None]), 0.0)
        return (probs, key_block, val_block)

    def value_step(accum, index):
        probs, key_block, val_block = block_probs(index)
        return (
            accum
            + jnp.einsum(
                "hqk,khd->qhd",
                probs.astype(jnp.bfloat16),
                val_block,
                preferred_element_type=jnp.float32,
            ),
            None,
        )

    accum, unused = lax.scan(
        value_step, jnp.zeros((tok_count, HEADS, HEAD), jnp.float32), block_ids
    )
    attended = accum.reshape(tok_count, width).astype(jnp.bfloat16)
    hidden = tok_rows.astype(jnp.float32) + jnp.dot(
        attended, out_full, preferred_element_type=jnp.float32
    )
    center = hidden - jnp.mean(hidden, axis=-1, keepdims=True)
    inv_dev = lax.rsqrt(jnp.mean(center * center, axis=-1, keepdims=True) + epsilon)
    unit = center * inv_dev
    gain_f = gain_full.astype(jnp.float32)
    normed_low = (unit * gain_f + bias_full.astype(jnp.float32)).astype(jnp.bfloat16)
    logits = jnp.dot(normed_low, router_full, preferred_element_type=jnp.float32)
    groups_dev = tok_count // GROUP_SIZE
    local_group = group_ids[0] - ctx_index * groups_dev
    member = (local_group[:, None] == jnp.arange(groups_dev, dtype=jnp.int32)[None, :]).astype(
        jnp.float32
    )
    expo = jnp.exp(logits)
    group_total = jnp.dot(member.T, expo, precision=highest)
    mix_weights = expo / jnp.dot(member, group_total, precision=highest)
    weights_low = mix_weights.astype(jnp.bfloat16)
    mixing = member.astype(jnp.bfloat16).T[:, None, :] * weights_low.T[None, :, :]
    mixing_flat = mixing.reshape(groups_dev * expert_count, tok_count)
    mixed_low = jnp.dot(mixing_flat, normed_low, preferred_element_type=jnp.float32).astype(
        jnp.bfloat16
    )
    mixed_low = mixed_low.reshape(groups_dev, expert_count, width)
    owner_mixed = lax.all_to_all(mixed_low, "fsdp", split_axis=1, concat_axis=0, tiled=True)
    pre, active, owner_out = expert_forward(owner_mixed, w_up, w_down)
    expert_out = lax.all_to_all(owner_out, "fsdp", split_axis=0, concat_axis=1, tiled=True)
    expert_flat = expert_out.reshape(groups_dev * expert_count, width)
    spread = contract_rows(mixing_flat, expert_flat)
    layer_out = hidden + spread
    cot_rows = cotangent[0]
    cot_f = cot_rows.astype(jnp.float32)
    grad_expert = jnp.dot(mixing_flat, cot_rows, preferred_element_type=jnp.float32).astype(
        jnp.bfloat16
    )
    grad_expert = grad_expert.reshape(groups_dev, expert_count, width)
    coef = contract_cols(cot_rows, expert_flat).reshape(tok_count, groups_dev, expert_count)
    grad_mix_spread = jnp.sum(coef * member[:, :, None], axis=1)
    owner_grad = lax.all_to_all(grad_expert, "fsdp", split_axis=1, concat_axis=0, tiled=True)
    grad_up_own, grad_down_own, owner_back = expert_backward(
        owner_mixed, pre, active, owner_grad, w_up, w_down
    )
    grad_mixed = lax.all_to_all(owner_back, "fsdp", split_axis=0, concat_axis=1, tiled=True)
    grad_mixed_flat = grad_mixed.reshape(groups_dev * expert_count, width)
    grad_norm_mix = contract_rows(mixing_flat, grad_mixed_flat)
    grad_mixing = contract_cols(grad_mixed_flat, normed_low).reshape(
        groups_dev, expert_count, tok_count
    )
    grad_mix_mixing = jnp.sum(grad_mixing * member.T[:, None, :], axis=0).T
    grad_mix = grad_mix_spread + grad_mix_mixing
    product = mix_weights * grad_mix
    token_dot = jnp.dot(member, jnp.dot(member.T, product, precision=highest), precision=highest)
    grad_logits = (product - mix_weights * token_dot).astype(jnp.bfloat16)
    grad_router_part = contract_rows(normed_low, grad_logits)
    grad_norm_router = contract_cols(grad_logits, router_full)
    grad_normed = grad_norm_mix + grad_norm_router
    grad_gain_part = jnp.sum(grad_normed * unit, axis=0)
    grad_bias_part = jnp.sum(grad_normed, axis=0)
    scaled = grad_normed * gain_f
    grad_hidden = cot_f + inv_dev * (
        scaled
        - jnp.mean(scaled, axis=-1, keepdims=True)
        - unit * jnp.mean(scaled * unit, axis=-1, keepdims=True)
    )
    grad_branch = grad_hidden.astype(jnp.bfloat16)
    grad_out_part = contract_rows(attended, grad_branch)
    grad_heads = (
        contract_cols(grad_branch, out_full).astype(jnp.bfloat16).reshape(tok_count, HEADS, HEAD)
    )
    delta = jnp.sum(grad_heads.astype(jnp.float32) * accum, axis=-1).T

    def grad_step(grad_query, index):
        probs, key_block, val_block = block_probs(index)
        grad_probs = jnp.einsum(
            "qhd,khd->hqk", grad_heads, val_block, preferred_element_type=jnp.float32
        )
        grad_scores = (probs * (grad_probs - delta[..., None])).astype(jnp.bfloat16)
        grad_query = (
            grad_query
            + jnp.einsum("hqk,khd->qhd", grad_scores, key_block, preferred_element_type=jnp.float32)
            * scale
        )
        grad_key = (
            jnp.einsum("hqk,qhd->khd", grad_scores, query_heads, preferred_element_type=jnp.float32)
            * scale
        )
        grad_val = jnp.einsum(
            "hqk,qhd->khd",
            probs.astype(jnp.bfloat16),
            grad_heads,
            preferred_element_type=jnp.float32,
        )
        return (grad_query, (grad_key, grad_val))

    grad_query, (grad_keys, grad_vals) = lax.scan(
        grad_step, jnp.zeros((tok_count, HEADS, HEAD), jnp.float32), block_ids
    )
    grad_key_own, grad_val_own = (
        lax.psum_scatter(
            grad_keys.reshape(full_rows, width), "ctx", scatter_dimension=0, tiled=True
        ),
        lax.psum_scatter(
            grad_vals.reshape(full_rows, width), "ctx", scatter_dimension=0, tiled=True
        ),
    )
    grad_qkv_low = jnp.concatenate(
        [grad_query.reshape(tok_count, width), grad_key_own, grad_val_own], axis=1
    ).astype(jnp.bfloat16)
    grad_qkv_part = contract_rows(tok_rows, grad_qkv_low)
    grad_tokens = grad_hidden + contract_cols(grad_qkv_low, qkv_full)
    dense = (
        lax.psum_scatter(grad_qkv_part, "fsdp", scatter_dimension=0, tiled=True),
        lax.psum_scatter(grad_out_part, "fsdp", scatter_dimension=0, tiled=True),
        lax.psum_scatter(grad_router_part, "fsdp", scatter_dimension=0, tiled=True),
        lax.psum_scatter(grad_gain_part, "fsdp", scatter_dimension=0, tiled=True),
        lax.psum_scatter(grad_bias_part, "fsdp", scatter_dimension=0, tiled=True),
    )
    totals = lax.psum(
        (dense[0], dense[1], dense[2], dense[3], dense[4], grad_up_own, grad_down_own), "ctx"
    )
    return (
        layer_out[None],
        grad_tokens[None],
        totals[0],
        totals[1],
        totals[2],
        totals[3],
        totals[4],
        totals[5],
        totals[6],
    )


def cost(microseconds):
    return pl.CostEstimate(flops=int(microseconds * 1.15e9), bytes_accessed=1 << 20, transcendentals=0)


LOG2E = 1.4426950408889634
HIDE = -1e30
SAFE = 100.0
RUN = 1024
HALF = 512
VMEM = pl.BlockSpec(memory_space=pltpu.VMEM)
SMEM = pl.BlockSpec(memory_space=pltpu.SMEM)
ANY = pl.BlockSpec(memory_space=pl.ANY)
LIMIT = 60 << 20
CORE_LIMIT = 63 << 20


def dot_nn(left, right):
    return lax.dot_general(left, right, (((1,), (0,)), ((), ())), preferred_element_type=jnp.float32)


def dot_nt(left, right):
    return lax.dot_general(left, right, (((1,), (1,)), ((), ())), preferred_element_type=jnp.float32)


def dot_tn(left, right):
    return lax.dot_general(left, right, (((0,), (0,)), ((), ())), preferred_element_type=jnp.float32)


def split3(value):
    one = value.astype(jnp.bfloat16)
    rest = value - one.astype(jnp.float32)
    two = rest.astype(jnp.bfloat16)
    three = (rest - two.astype(jnp.float32)).astype(jnp.bfloat16)
    return one, two, three


def span(index, size, width=None):
    return pl.ds(pl.multiple_of(index * size, size), size if width is None else width)


def flipped(value):
    return value.astype(jnp.float32).T.astype(value.dtype)


def boundaries(seg_ref, lane):
    segs = seg_ref[...]
    begin = jnp.zeros(lane.shape, jnp.int32)
    end = jnp.zeros(lane.shape, jnp.int32)
    for c in range(1, 10):
        below = (segs < c).astype(jnp.int32)
        total = jnp.sum(jnp.sum(below, axis=1, keepdims=True), axis=0, keepdims=True)
        begin = jnp.where(lane == HEAD - 1 + c, total, begin)
        end = jnp.where(lane == HEAD - 2 + c, total, end)
    return begin, jnp.where(lane == HEAD + 8, 0, end)


def fwd_body(blocks, block_len, table_ref, tok_ref, w_ref, seg_ref, att_ref, qf_ref, kf_ref, vf_ref, stat_ref, vt_ref, inv_ref):
    rows = blocks * block_len
    for t in range(blocks):
        inv_ref[table_ref[t]] = t
    weight = w_ref[...].reshape(w_ref.shape[0] * w_ref.shape[1], w_ref.shape[2])
    weight = jnp.concatenate([weight, jnp.zeros((weight.shape[0], HEAD), weight.dtype)], axis=1)
    lane = lax.broadcasted_iota(jnp.int32, (1, 2 * HEAD), 1)
    begin, end = boundaries(seg_ref, lane)
    is_flag = (lane >= HEAD) & (lane < HEAD + 8)
    is_one = (lane >= HEAD + 8) & (lane < HEAD + 11)
    pair = (lax.broadcasted_iota(jnp.int32, (2 * HEAD, 2 * HEAD), 0) // HEAD == lane // HEAD).astype(jnp.bfloat16)
    ones_v = ((lane >= HEAD) & (lane < HEAD + 3)).astype(jnp.float32)

    def project(s, sizes):
        t = inv_ref[s]
        qkv = dot_nn(tok_ref[span(t, block_len), :], weight)
        both = qkv[:, :2 * HEAD].astype(jnp.bfloat16).astype(jnp.float32)
        turned = pltpu.roll(both, HEAD, 1)
        value = qkv[:, 2 * HEAD:]
        place = lax.broadcasted_iota(jnp.int32, (block_len, 2 * HEAD), 0) + s * block_len
        own = (place >= begin) & (place < end)
        at = span(s, block_len)
        flag_q = jnp.where(is_flag & jnp.logical_not(own), 1.0, 0.0)
        flag_k = jnp.where(own, HIDE, jnp.where(is_one, 1.0, 0.0))
        qf_ref[at, :] = jnp.where(lane < HEAD, both, flag_q).astype(jnp.bfloat16)
        kf_ref[at, :] = jnp.where(lane < HEAD, turned, flag_k).astype(jnp.bfloat16)
        vf_ref[at, :] = (value + ones_v).astype(jnp.bfloat16)
        vt_ref[:, at] = jnp.where(lane < HEAD, value, 1.0).T.astype(jnp.bfloat16)
        return jnp.maximum(sizes, dot_nn((both * both).astype(jnp.bfloat16), pair))

    sizes = lax.fori_loop(0, blocks, project, jnp.zeros((block_len, 2 * HEAD), jnp.float32), unroll=4)
    scale = HEAD ** (-0.5) * LOG2E
    q_size, k_size = jnp.max(sizes[:, :HEAD]), jnp.max(sizes[:, HEAD:])
    small = q_size * k_size <= (SAFE / scale) ** 2
    causal = lax.broadcasted_iota(jnp.int32, (HALF, HALF), 0) <= lax.broadcasted_iota(jnp.int32, (HALF, HALF), 1)

    def query_run(online, run):
        def tile(state, q_at, k_at, diagonal):
            scores = dot_nt(kf_ref[k_at, :], qf_ref[q_at, :]) * scale
            if diagonal:
                scores = jnp.where(causal, scores, HIDE)
            top, acc = state
            if online:
                new_top = jnp.maximum(top, jnp.max(scores, axis=0, keepdims=True))
                acc = acc * jnp.exp2(top - new_top)
                scores, top = scores - new_top, new_top
            return top, acc + dot_nn(vt_ref[:, k_at], jnp.exp2(scores).astype(jnp.bfloat16))

        start = (jnp.full((1, RUN), HIDE if online else 0.0, jnp.float32), jnp.zeros((2 * HEAD, RUN), jnp.float32))
        whole = lax.fori_loop(0, run, lambda n, state: tile(state, span(run, RUN), span(n, RUN), False), start)
        early, late = span(2 * run, HALF), span(2 * run + 1, HALF)
        first = tile([part[:, :HALF] for part in whole], early, early, True)
        second = tile([part[:, HALF:] for part in whole], late, early, False)
        second = tile(second, late, late, True)
        for at, (top, acc) in ((early, first), (late, second)):
            total = acc[HEAD:]
            stat = jnp.concatenate([acc[:HEAD] / total, top + jnp.log2(total)], axis=0).T
            stat_ref[at, :] = stat
            one, two, three = split3(stat * (-1.0 / scale))
            old = qf_ref[at, :]
            old = jnp.where(lane == HEAD + 8, one, old)
            old = jnp.where(lane == HEAD + 9, two, old)
            qf_ref[at, :] = jnp.where(lane == HEAD + 10, three, old)

    for online in (False, True):
        @pl.when(small != online)
        def _():
            @pl.loop(0, rows // RUN)
            def _(run):
                query_run(online, run)

    for c in range(blocks // 2):
        parts = [stat_ref[span(table_ref[2 * c + half], block_len), :HEAD] for half in range(2)]
        att_ref[c] = jnp.concatenate(parts, axis=1).astype(jnp.bfloat16)


def attn_fwd(tokens_all, weight, table, segs):
    rows, blocks = tokens_all.shape[0], table.shape[0]
    block_len = rows // blocks
    low = jnp.bfloat16
    return pl.pallas_call(
        functools.partial(fwd_body, blocks, block_len),
        out_shape=(
            jax.ShapeDtypeStruct((blocks // 2, block_len, 2 * HEAD), low),
            jax.ShapeDtypeStruct((rows, 2 * HEAD), low),
            jax.ShapeDtypeStruct((rows, 2 * HEAD), low),
            jax.ShapeDtypeStruct((rows, 2 * HEAD), low),
            jax.ShapeDtypeStruct((rows, 2 * HEAD), jnp.float32),
        ),
        in_specs=[SMEM, VMEM, VMEM, VMEM],
        out_specs=(VMEM,) * 5,
        scratch_shapes=[pltpu.VMEM((2 * HEAD, rows), low), pltpu.SMEM((blocks,), jnp.int32)],
        compiler_params=pltpu.CompilerParams(vmem_limit_bytes=LIMIT),
        cost_estimate=cost(30),
        name="attention",
    )(table, tokens_all, weight, segs)


MESH = pl.DeviceIdType.MESH


def flip(index, bit):
    return index + bit - 2 * bit * lax.rem(index // bit, 2)


def meet(devices):
    barrier = pltpu.get_barrier_semaphore()
    for device in devices:
        pl.semaphore_signal(barrier, inc=1, device_id=device, device_id_type=MESH)
    pl.semaphore_wait(barrier, len(devices))


def push(src, dst, send_sem, recv_sem, device):
    return pltpu.make_async_remote_copy(
        src_ref=src, dst_ref=dst, send_sem=send_sem, recv_sem=recv_sem, device_id=device, device_id_type=MESH
    )


def gather_body(
    zs, tok_ref, wq_ref, wo_ref, router_ref, gain_ref, bias_ref, toks_ref, heads_ref, wos_ref, packs_ref, parts_ref,
    head_buf, pack_buf, own_sem, z_send, z_recv, far_send, near_send, own_recv, diag_recv, near_recv,
):
    me, z = lax.axis_index("ctx"), lax.axis_index("fsdp")
    sib, xn, yn, diag = flip(me, 1), flip(me, 2), flip(me, 4), flip(flip(me, 2), 4)
    z_peers = [lax.rem(z + k, zs) for k in range(1, zs)]
    meet([(sib, z), (xn, z), (yn, z)] + [(me, other) for other in z_peers])
    half = tok_ref.shape[0] // 2
    count = toks_ref.shape[0]

    def part(device, k):
        return toks_ref.at[device, pl.ds(k * half, half)]

    started, locals_ = [], []

    def go(copy):
        copy.start()
        started.append(copy)

    for k in (0, 1):
        rows = tok_ref.at[pl.ds(k * half, half)]
        go(push(rows, part(me, k), far_send.at[0, k], own_recv.at[0, k], (xn, z)))
        rows = tok_ref.at[pl.ds((1 - k) * half, half)]
        go(push(rows, part(me, 1 - k), far_send.at[1, 1 - k], own_recv.at[1, 1 - k], (yn, z)))

    def share(i, shard, whole):
        for k, other in enumerate(z_peers):
            go(push(shard, whole.at[z], z_send.at[i, k], z_recv.at[i, k], (me, other)))
        locals_.append(pltpu.make_async_copy(shard, whole.at[z], own_sem.at[i]))
        locals_[-1].start()

    depth = wq_ref.shape[0] // count
    width = wq_ref.shape[1] // 3
    for h in range(count):
        @pl.when(me == h)
        def _():
            cols = [wq_ref[:, width * kind + HEAD * h:width * kind + HEAD * (h + 1)] for kind in range(3)]
            head_buf[...] = jnp.concatenate(cols, axis=1)

    share(0, head_buf, heads_ref)
    share(1, wo_ref, wos_ref)
    experts = router_ref.shape[0]
    rows = [router_ref[...].astype(jnp.float32), gain_ref[...].astype(jnp.float32), bias_ref[...].astype(jnp.float32)]
    rows.append(jnp.zeros((pack_buf.shape[0] - experts - 2, pack_buf.shape[1]), jnp.float32))
    pack_buf[...] = jnp.concatenate(rows, axis=0).astype(jnp.bfloat16)
    share(2, pack_buf, packs_ref)
    share(3, wq_ref.at[pl.ds(pl.multiple_of(me * depth, depth), depth)], parts_ref)
    for k in (0, 1):
        rows = tok_ref.at[pl.ds(k * half, half)]
        go(push(rows, part(me, k), near_send.at[0, k], near_recv.at[0, k], (sib, z)))
    locals_.append(pltpu.make_async_copy(tok_ref, toks_ref.at[me], own_sem.at[4]))
    locals_[-1].start()

    def arrived(device, k, sem):
        push(part(device, k), part(device, k), far_send.at[0, 0], sem, (sib, z)).wait_recv()

    def relay(device, k, i):
        go(push(part(device, k), part(device, k), near_send.at[i, k], near_recv.at[i, k], (sib, z)))

    arrived(xn, 0, own_recv.at[0, 0])
    go(push(part(xn, 0), part(xn, 0), far_send.at[2, 0], diag_recv.at[0], (yn, z)))
    relay(xn, 0, 1)
    arrived(yn, 1, own_recv.at[1, 1])
    go(push(part(yn, 1), part(yn, 1), far_send.at[2, 1], diag_recv.at[1], (xn, z)))
    relay(yn, 1, 2)
    arrived(xn, 1, own_recv.at[0, 1])
    relay(xn, 1, 1)
    arrived(yn, 0, own_recv.at[1, 0])
    relay(yn, 0, 2)
    for k in (0, 1):
        arrived(diag, k, diag_recv.at[k])
        relay(diag, k, 3)
    for k in (0, 1):
        for i, device in enumerate((sib, flip(xn, 1), flip(yn, 1), flip(diag, 1))):
            arrived(device, k, near_recv.at[i, k])
    for i, whole in enumerate((heads_ref, wos_ref, packs_ref, parts_ref)):
        for k in range(zs - 1):
            other = lax.rem(z + zs - 1 - k, zs)
            push(whole.at[other], whole.at[other], z_send.at[i, k], z_recv.at[i, k], (me, other)).wait_recv()
    for copy in locals_:
        copy.wait()
    for copy in started:
        copy.wait_send()


def gather(tokens, w_qkv, w_out, w_router, ln_gain, ln_bias, ctx_count, z_count):
    shard, wide = w_qkv.shape
    low = jnp.bfloat16
    outs = [
        (ctx_count,) + tokens.shape, (z_count, shard, 3 * HEAD), (z_count,) + w_out.shape, (z_count, 16, shard),
        (z_count, shard // ctx_count, wide),
    ]
    dma = pltpu.SemaphoreType.DMA
    return pl.pallas_call(
        functools.partial(gather_body, z_count),
        out_shape=[jax.ShapeDtypeStruct(out, low) for out in outs],
        in_specs=[VMEM] * 6,
        out_specs=[ANY] * 5,
        scratch_shapes=[
            pltpu.VMEM((shard, 3 * HEAD), low), pltpu.VMEM((16, shard), low),
            dma((5,)), dma((4, z_count - 1)), dma((4, z_count - 1)), dma((3, 2)), dma((4, 2)), dma((2, 2)), dma((2,)), dma((4, 2)),
        ],
        compiler_params=pltpu.CompilerParams(collective_id=1, has_side_effects=True, vmem_limit_bytes=LIMIT),
        cost_estimate=cost(24),
        name="gather_tokens",
    )(tokens, w_qkv, w_out, w_router.T, ln_gain[None], ln_bias[None])


def norm_parts(hidden):
    center = hidden - jnp.mean(hidden, axis=-1, keepdims=True)
    inv_dev = lax.rsqrt(jnp.mean(center * center, axis=-1, keepdims=True) + epsilon)
    return center * inv_dev, inv_dev


def gelu_parts(value):
    square = value * value
    tangent = jnp.tanh(value * (square * (gelu_coef * gelu_cubic) + gelu_coef))
    half = 0.5 * tangent + 0.5
    rise = value * (square * (3.0 * gelu_coef * gelu_cubic) + gelu_coef)
    return value * half, half + half * (1.0 - tangent) * rise


def core_body(
    experts, groups, table_ref, gid_ref, part_ref, att_ref, tok_ref, cot_ref, wo_ref, pack_ref, qf_ref, kf_ref, vf_ref, stat_ref, toks_ref,
    up_ref, down_ref,
    gq_ref, out_ref, sums_ref, layer_ref, gtok_ref, act_ref, gpre_ref, all_ref,
    tok, cot, wo, pack, att, msend, zin, bsend, bin_, up, down, qf, kf, vf, stat, held, late_held, ghead_out, ghead, wide_out, ghidden,
    dof, qt, dot, dk_acc, dv_acc, sorted_dv, head_acc, send, landing, weight, zsend, zone, total, totals,
    out_mine, out_zone, out_sum, out_part, out_own, out_all,
    load_sem, own_sem, a_send, a_recv, m_send, m_recv, b_send, b_recv, h_send, h_recv, s_send, s_recv, z_send, z_recv, c_send, c_recv,
    o_send, o_recv, g_send, g_recv, r_send, r_recv, w_send, w_recv, v_send, v_recv,
):
    me, z = lax.axis_index("ctx"), lax.axis_index("fsdp")
    count, block_len = att_ref.shape[0], att_ref.shape[1]
    own_rows, width = tok_ref.shape
    owners, own_experts, ffn = msend.shape[0], up_ref.shape[0], up_ref.shape[2]
    flat, per = experts * groups, experts * groups // owners
    blocks = 2 * count
    rows = blocks * block_len
    runs = rows // RUN
    low = jnp.bfloat16
    dq_acc, qk, dv_rows = stat, qf, vf

    def start(copies):
        for copy in copies:
            copy.start()
        return copies

    def wait(copies):
        for copy in copies:
            copy.wait()

    pairs = [(qf_ref, qf), (kf_ref, kf), (tok_ref, tok), (wo_ref, wo), (pack_ref, pack), (cot_ref, cot)]
    for e in range(own_experts):
        pairs += [(up_ref.at[e], up.at[e]), (down_ref.at[e], down.at[e])]
    pairs += [(stat_ref, stat), (vf_ref, vf)]
    loads = start([pltpu.make_async_copy(src, dst, load_sem.at[i]) for i, (src, dst) in enumerate(pairs)])
    sib, same_core = flip(me, 1), [flip(me, 2), flip(me, 4), flip(flip(me, 2), 4)]
    z_peers = [(me, lax.rem(z + k, owners)) for k in range(1, owners)]
    c_peers = [(jnp.bitwise_xor(me, k), z) for k in range(1, count)]
    meet(z_peers + c_peers)
    swap = start([push(att_ref.at[d[0]], att.at[me], a_send.at[k], a_recv.at[k], d) for k, d in enumerate(c_peers)])
    own = start([pltpu.make_async_copy(att_ref.at[me], att.at[me], own_sem.at[0])])

    scale = HEAD ** (-0.5)
    first_diagonal = runs * (runs - 1)

    def slot_of(run, index, part):
        return run * (2 * runs - 1 - run) + 2 * (index - run - 1) + part

    def probabilities(q_at, k_at, visible):
        scores = dot_nt(qf[q_at, :], kf[k_at, :]) * (scale * LOG2E)
        if visible is not None:
            scores = jnp.where(visible, scores, HIDE)
        return jnp.exp2(scores).astype(low)

    def hold_diagonal():
        early = lax.broadcasted_iota(jnp.int32, (RUN, HALF), 1) <= lax.broadcasted_iota(jnp.int32, (RUN, HALF), 0)
        late = lax.broadcasted_iota(jnp.int32, (HALF, HALF), 1) <= lax.broadcasted_iota(jnp.int32, (HALF, HALF), 0)

        @pl.loop(0, runs)
        def _(run):
            held[first_diagonal + run] = probabilities(span(run, RUN), span(2 * run, HALF), early)
            late_held[run] = probabilities(span(2 * run + 1, HALF), span(2 * run + 1, HALF), late)

    def hold(run):
        @pl.loop(run + 1, runs)
        def _(index):
            for part in range(2):
                held[slot_of(run, index, part)] = probabilities(span(index, RUN), span(2 * run + part, HALF), None)

    wait(loads[:2])
    hold_diagonal()

    @pl.loop(1, runs - 1)
    def _(run):
        hold(run)

    wait(own + swap)
    weights = start([push(part_ref, weight.at[:, me], w_send.at[k], w_recv.at[k], (d, z)) for k, d in enumerate(same_core)])
    shares = start([push(part_ref, weight.at[:, me], v_send.at[3], v_recv.at[3], (sib, z))])
    weight[:, me] = part_ref[...]
    wait(loads[2:6])
    halves = [jnp.concatenate([att[h, :, HEAD * p:HEAD * (p + 1)] for h in range(count)], axis=1) for p in range(2)]
    attended = jnp.concatenate(halves, axis=0)
    out_weight = wo[...].reshape(width, width)
    hidden = tok[...].astype(jnp.float32) + dot_nn(attended, out_weight)
    unit, inv_dev = norm_parts(hidden)
    small_in = jnp.concatenate([pack[k] for k in range(owners)], axis=1)
    gain, bias = small_in[experts:experts + 1].astype(jnp.float32), small_in[experts + 1:experts + 2].astype(jnp.float32)
    normed = (unit * gain + bias).astype(low)
    expo = jnp.exp(dot_nt(small_in, normed)[:experts])
    expo = jnp.broadcast_to(expo[:, None, :], (experts, groups, own_rows)).reshape(flat, own_rows)
    member = lax.rem(lax.broadcasted_iota(jnp.int32, (flat, 1), 0), groups) == lax.rem(gid_ref[...], groups)
    expo = jnp.where(member, expo, 0.0)
    mix = expo / jnp.sum(expo, axis=1, keepdims=True)
    mix_low = mix.astype(low)

    def zone_rows(owner, kind):
        return pl.ds(pl.multiple_of((2 * owner + kind) * per, per), per)

    def to_owners(kind, value):
        msend[:, kind] = value.astype(low).reshape(owners, per, width)
        zin[zone_rows(z, kind), :] = msend[z, kind]
        return start([
            push(msend.at[d[1], kind], zin.at[zone_rows(z, kind)], m_send.at[kind, k], m_recv.at[kind, k], d) for k, d in enumerate(z_peers)
        ])

    mixed_copies = to_owners(0, dot_nn(mix_low, normed))
    grad_experts = dot_nn(mix_low, cot[...])
    wait(loads[6:6 + 2 * own_experts])
    wait(mixed_copies)
    grad_copies = to_owners(1, grad_experts)

    def from_sources(kind, e):
        lows_ = [(2 * owner + kind) * per + e * groups for owner in range(owners)]
        return jnp.concatenate([zin[at:at + groups, :] for at in lows_], axis=0)

    def to_sources(kind, e, value):
        bsend[:, kind, e * groups:(e + 1) * groups, :] = value.astype(low).reshape(owners, groups, width)

    def send_back(kind):
        bin_[z, kind] = bsend[z, kind]
        return start([
            push(bsend.at[d[1], kind], bin_.at[z, kind], b_send.at[kind, k], b_recv.at[kind, k], d) for k, d in enumerate(z_peers)
        ])

    slopes = []
    for e in range(own_experts):
        active, slope = gelu_parts(dot_nn(from_sources(0, e), up[e]))
        slopes.append(slope)
        to_sources(0, e, dot_nn(active.astype(low), down[e]))
    out_copies = send_back(0)
    wait(grad_copies)
    gathers = start([push(zin, all_ref.at[me], g_send.at[k], g_recv.at[k], (d, z)) for k, d in enumerate(same_core)])
    relays = start([push(zin, all_ref.at[me], r_send.at[3], r_recv.at[3], (sib, z))])
    own_got = start([pltpu.make_async_copy(zin, all_ref.at[me], own_sem.at[1])])
    for e in range(own_experts):
        grad_pre = (dot_nt(from_sources(1, e), down[e]) * slopes[e]).astype(low)
        to_sources(1, e, dot_nt(grad_pre, up[e]))
    back_copies = send_back(1)
    wait(out_copies)
    expert_out = bin_[:, 0].reshape(flat, width)
    wide_out[...] = hidden + dot_tn(mix_low, expert_out)
    layer_copy = start([pltpu.make_async_copy(wide_out, layer_ref, own_sem.at[2])])
    grad_mix = dot_nt(expert_out, cot[...])
    wait(back_copies)
    grad_mixed = bin_[:, 1].reshape(flat, width)
    product = mix * (grad_mix + dot_nt(grad_mixed, normed))
    grad_logits = product - mix * jnp.sum(product, axis=1, keepdims=True)
    grad_logits = jnp.sum(grad_logits.reshape(experts, groups, own_rows), axis=1).astype(low)
    pad = jnp.zeros((small_in.shape[0] - experts, own_rows), low)
    grad_logits = jnp.concatenate([grad_logits, pad], axis=0)
    grad_normed = dot_tn(jnp.concatenate([mix_low, grad_logits], axis=0), jnp.concatenate([grad_mixed, small_in], axis=0))
    scaled = grad_normed * gain
    mean = jnp.mean(scaled, axis=-1, keepdims=True)
    grad_hidden = cot[...].astype(jnp.float32) + inv_dev * (scaled - mean - unit * jnp.mean(scaled * unit, axis=-1, keepdims=True))
    branch = grad_hidden.astype(low)
    grad_heads = dot_nt(branch, out_weight).astype(low)
    for h in range(count):
        at = slice(HEAD * h, HEAD * (h + 1))
        ghead_out[h] = jnp.concatenate([grad_heads[:block_len, at], grad_heads[block_len:, at]], axis=1)
    swap = start([push(ghead_out.at[d[0]], ghead.at[me], h_send.at[k], h_recv.at[k], d) for k, d in enumerate(c_peers)])
    ghead[me] = ghead_out[me]
    ghidden[...] = grad_hidden
    out_mine[...] = dot_tn(attended, branch).astype(low).reshape(out_mine.shape)
    gout_copies = start([push(out_mine.at[d[1]], out_zone.at[z], o_send.at[0, k], o_recv.at[0, k], d) for k, d in enumerate(z_peers)])
    out_zone[z] = out_mine[z]
    small = jnp.concatenate(
        [
            dot_nn(grad_logits, normed)[:experts],
            jnp.sum(grad_normed * unit, axis=0, keepdims=True),
            jnp.sum(grad_normed, axis=0, keepdims=True),
            jnp.zeros((small_in.shape[0] - experts - 2, width), jnp.float32),
        ],
        axis=0,
    )
    lanes = width // owners
    for c in range(owners):
        zsend[c, 3 * HEAD:, :] = small[:, c * lanes:(c + 1) * lanes].astype(low)
    hold(0)

    def mask(condition):
        return jnp.broadcast_to(jnp.where(condition, 1.0, 0.0), (1, 2 * HEAD))

    firsts = [mask(table_ref[2 * c] < table_ref[2 * c + 1]).astype(low) for c in range(count)]
    lows = [jnp.minimum(table_ref[2 * c], table_ref[2 * c + 1]) for c in range(count)]
    holds = [[mask(lows[c] == j).astype(low) for j in range(count)] for c in range(count)]

    def blend(masks, values):
        out = None
        for weigh, value in zip(masks, values):
            out = weigh * value if out is None else out + weigh * value
        return out

    lane = lax.broadcasted_iota(jnp.int32, (1, 2 * HEAD), 1)

    def prepare(s, both):
        at = slice(s * block_len, (s + 1) * block_len)
        grad = jnp.where(lane < HEAD, both, 0.0)
        delta = jnp.sum(grad * stat[at, :], axis=1, keepdims=True)
        one, two, three = split3(jnp.broadcast_to(-delta, grad.shape))
        wide = jnp.where(lane == HEAD, one, grad.astype(low))
        wide = jnp.where(lane == HEAD + 1, two, wide)
        dof[at, :] = jnp.where(lane == HEAD + 2, three, wide)
        turned = jnp.where(lane < HEAD, both, pltpu.roll(qf[at, :].astype(jnp.float32), HEAD, 1)).T.astype(low)
        dot[:, at] = turned[:HEAD]
        qt[:, at] = turned[HEAD:]

    wait(swap)
    wait(loads[6 + 2 * own_experts:])
    for c in range(count):
        block = ghead[c]
        turned = pltpu.roll(block.astype(jnp.float32), HEAD, 1).astype(low)
        ghead_out[c] = firsts[c] * block + (1 - firsts[c]) * turned
    for j in range(count):
        both = blend([holds[c][j] for c in range(count)], [ghead_out[c] for c in range(count)]).astype(jnp.float32)
        prepare(j, both)
        prepare(blocks - 1 - j, pltpu.roll(both, HEAD, 1))

    tok_loads = [
        pltpu.make_async_copy(toks_ref.at[pl.ds(i * RUN, RUN)], held.at[i], own_sem.at[3 + i]) for i in range(rows // RUN)
    ]

    def key_run(run):
        def tile(q_at, k_at, part, probs, first_k, first_q):
            slope = dot_nt(dof[q_at, :], vf[k_at, :])
            grad = (probs.astype(jnp.float32) * slope).astype(low)
            dv = dot_nn(dot[:, q_at], probs)
            dk = dot_nn(qt[:, q_at], grad)
            dq = dot_nn(grad, kf[k_at, :])
            at = slice(part * HALF, (part + 1) * HALF)
            if first_k:
                dv_acc[:, at] = dv
                dk_acc[:, at] = dk
            else:
                dv_acc[:, at] += dv
                dk_acc[:, at] += dk
            if first_q:
                @pl.when(run == 0)
                def _():
                    dq_acc[q_at, :] = dq

                @pl.when(run != 0)
                def _():
                    dq_acc[q_at, :] += dq
            else:
                dq_acc[q_at, :] += dq

        early, late = span(2 * run, HALF), span(2 * run + 1, HALF)
        tile(span(run, RUN), early, 0, held[first_diagonal + run], True, True)
        tile(late, late, 1, late_held[run], True, False)

        @pl.loop(run + 1, runs)
        def _(index):
            for part in range(2):
                tile(span(index, RUN), span(2 * run + part, HALF), part, held[slot_of(run, index, part)], False, part == 0)

        at = span(run, RUN)
        both = jnp.concatenate([dk_acc[...] * scale, dv_acc[...]], axis=0).T
        query = dq_acc[at, :] * scale
        qk[at, :] = jnp.where(lane < HEAD, query, pltpu.roll(both, HEAD, 1)).astype(low)
        dv_rows[at, :] = both.astype(low)

    def send_half(half):
        mid = block_len // 2
        for c in range(count):
            ats = [slice(s * block_len, (s + 1) * block_len) for s in (range(count) if half == 0 else range(blocks - 1, count - 1, -1))]
            send[half, c, :block_len, :] = blend(holds[c], [qk[at, :] for at in ats])
            values = blend(holds[c], [dv_rows[at, :] for at in ats])
            sorted_dv[c] = values
            values = values[:, HEAD:]
            send[half, c, block_len:, :] = jnp.concatenate([values[:mid], values[mid:]], axis=1)
        landing[half, me] = send[half, me]
        return start([
            push(send.at[half, d[0]], landing.at[half, me], s_send.at[half, k], s_recv.at[half, k], d) for k, d in enumerate(c_peers)
        ])

    def head_weights(half):
        first, second = None, None
        for c in range(count):
            order = firsts[c][:, :1] if half == 0 else 1 - firsts[c][:, :1]
            slot, at = divmod(c * own_rows, RUN)
            here = order * held[slot, at:at + block_len, :] + (1 - order) * held[slot, at + block_len:at + 2 * block_len, :]
            one, two = dot_tn(send[half, c, :block_len, :], here), dot_tn(sorted_dv[c], here)
            first, second = (one, two) if first is None else (first + one, second + two)
        both = jnp.concatenate([first, second[HEAD:]], axis=0)
        if half == 0:
            head_acc[...] = both
        else:
            head_acc[...] += both

    @pl.loop(0, runs // 2)
    def _(run):
        key_run(run)

        @pl.when(run == 0)
        def _():
            start(tok_loads)

    swaps = send_half(0)
    for k, d in enumerate(same_core):
        gathers[k].wait_recv()
        relays += start([push(all_ref.at[d], all_ref.at[d], r_send.at[k], r_recv.at[k], (sib, z))])
        weights[k].wait_recv()
        shares += start([push(weight.at[:, d], weight.at[:, d], v_send.at[k], v_recv.at[k], (sib, z))])
    wait(gout_copies)
    summed = out_zone[0].astype(jnp.float32)
    for k in range(1, owners):
        summed = summed + out_zone[k].astype(jnp.float32)
    out_sum[...] = summed.astype(low).reshape(out_sum.shape)
    part_copies = start([push(out_sum.at[d[0]], out_part.at[me], o_send.at[1, k], o_recv.at[1, k], d) for k, d in enumerate(c_peers)])
    out_part[me] = out_sum[me]
    wait(tok_loads)
    head_weights(0)

    @pl.loop(runs // 2, runs)
    def _(run):
        key_run(run)

    swaps += send_half(1)
    wait(part_copies)
    summed = out_part[0].astype(jnp.float32)
    for k in range(1, count):
        summed = summed + out_part[k].astype(jnp.float32)
    out_own[...] = summed.astype(low)
    last_copies = start([push(out_own, out_all.at[me], o_send.at[2, k], o_recv.at[2, k], d) for k, d in enumerate(c_peers)])
    out_all[me] = out_own[...]
    wait(own_got + relays)

    mixed_slot = rows // RUN
    share = owners * 2 * per
    mixed_loads = []
    for c in range(count):
        slot, at = divmod(c * share, RUN)
        mixed_loads.append(pltpu.make_async_copy(all_ref.at[c], held.at[mixed_slot + slot, pl.ds(at, share)], own_sem.at[3 + rows // RUN + c]))
    start(mixed_loads)
    head_weights(1)
    for c in range(owners):
        zsend[c, :3 * HEAD, :] = head_acc[:, c * lanes:(c + 1) * lanes].astype(low)
    z_copies = start([push(zsend.at[d[1]], zone.at[z], z_send.at[k], z_recv.at[k], d) for k, d in enumerate(z_peers)])
    zone[z] = zsend[z]
    wait(mixed_loads)
    step = HALF
    chunks = ffn // step
    wide_slot = mixed_slot + count * share // RUN

    def of_expert(kind, e):
        parts = []
        for slot in range(mixed_slot, wide_slot):
            value = held[slot].reshape(RUN // share, owners, 2, own_experts, groups, width)
            parts.append(value[:, :, kind, e].reshape(-1, width))
        return jnp.concatenate(parts, axis=0)

    def expert_part(e):
        mixed, grad_out = of_expert(0, e), of_expert(1, e)
        copies = []

        @pl.loop(0, chunks // 2)
        def _(i):
            for part in range(2):
                at = span(2 * i + part, step)
                to = pl.ds(part * step, step)
                active, slope = gelu_parts(dot_nn(mixed, up[e, :, at]))
                held[wide_slot + chunks * e + i, to, :] = active.astype(low)
                slot = wide_slot + chunks * e + chunks // 2 + i
                held[slot, to, :] = (dot_nt(grad_out, down[e, at, :]) * slope).astype(low)

        for i in range(chunks):
            slot = wide_slot + chunks * e + i // 2
            at, to = pl.ds(i * step, step), pl.ds(i % 2 * step, step)
            sem = own_sem.at[3 + rows // RUN + count + 2 * (chunks * e + i)]
            copies.append(pltpu.make_async_copy(held.at[slot, to], act_ref.at[e, :, at], sem))
            sem = own_sem.at[4 + rows // RUN + count + 2 * (chunks * e + i)]
            copies.append(pltpu.make_async_copy(held.at[slot + chunks // 2, to], gpre_ref.at[e, :, at], sem))
        return start(copies)

    stores = expert_part(0)
    wait(z_copies)
    summed = zone[0].astype(jnp.float32)
    for k in range(1, owners):
        summed = summed + zone[k].astype(jnp.float32)
    total[...] = summed.astype(low)
    c_copies = start([push(total, totals.at[me], c_send.at[k], c_recv.at[k], d) for k, d in enumerate(c_peers)])
    totals[me] = total[...]
    for e in range(1, own_experts):
        stores += expert_part(e)
    wait(swaps + shares)
    flat_weight = weight[...].reshape(width, -1)
    parts = []
    for half in range(2):
        queries, keys, values = [], [], []
        for h in range(count):
            front, back = landing[half, h, :block_len, :], landing[half, h, block_len:, :]
            queries.append(front[:, :HEAD])
            keys.append(front[:, HEAD:])
            values.append(jnp.concatenate([back[:, :HEAD], back[:, HEAD:]], axis=0))
        parts.append(dot_nt(jnp.concatenate(queries + keys + values, axis=1), flat_weight))
    in_order = mask(table_ref[2 * me] < table_ref[2 * me + 1])[:, :1]
    wait(layer_copy)
    wide_out[:block_len, :] = ghidden[:block_len, :] + (in_order * parts[0] + (1.0 - in_order) * parts[1])
    wide_out[block_len:, :] = ghidden[block_len:, :] + (in_order * parts[1] + (1.0 - in_order) * parts[0])
    stores += start([pltpu.make_async_copy(wide_out, gtok_ref, own_sem.at[2])])
    wait(last_copies)
    out_ref[...] = out_all[...].astype(jnp.float32).reshape(out_ref.shape)
    wait(c_copies)
    small = None
    turned = []
    for c in range(count):
        turned.append(totals[c, :3 * HEAD, :].astype(jnp.float32).T)
        part = totals[c, 3 * HEAD:, :].astype(jnp.float32)
        small = part if small is None else small + part
    sums_ref[...] = small
    for kind in range(3):
        at = slice(HEAD * kind, HEAD * (kind + 1))
        gq_ref[:, HEAD * count * kind:HEAD * count * (kind + 1)] = jnp.concatenate([part[:, at] for part in turned], axis=1)
    wait(stores)
    for copy in gathers + weights:
        copy.wait_send()


def core(table, gid_row, parts, att, tokens, cot, w_out, pack, saved, tokens_all, w_up, w_down, experts, groups):
    count, block_len = att.shape[:2]
    qf, kf, vf, stat = saved
    rows, (own_rows, width) = qf.shape[0], tokens.shape
    runs = rows // RUN
    own_experts, _, ffn = w_up.shape
    owners, smalls, lanes = pack.shape
    height = 3 * HEAD + smalls
    per = experts * groups // owners
    wide = (own_experts, count * owners * groups, ffn)
    share = (owners * 2 * per, width)
    part = (count, lanes // count, width)
    swap = (2, count, block_len + block_len // 2, 2 * HEAD)
    gout = (owners, lanes, width)
    sent = (owners, 2, per, width)
    low, full = jnp.bfloat16, jnp.float32
    scratch = [
        (tokens.shape, low), (cot.shape, low), (w_out.shape, low), (pack.shape, low), (att.shape, low),
        (sent, low), (share, low), (sent, low), (sent, low), (w_up.shape, low), (w_down.shape, low),
        (qf.shape, low), (kf.shape, low), (vf.shape, low), (stat.shape, full), ((runs * runs, RUN, HALF), low), ((runs, HALF, HALF), low),
        (att.shape, low), (att.shape, low), (tokens.shape, full), (tokens.shape, full),
        ((rows, 2 * HEAD), low), ((HEAD, rows), low), ((HEAD, rows), low), ((HEAD, RUN), full), ((HEAD, RUN), full),
        ((count, block_len, 2 * HEAD), low), ((3 * HEAD, width), full), (swap, low), (swap, low), ((owners, count) + parts.shape[1:], low),
        ((owners, height, lanes), low), ((owners, height, lanes), low), ((height, lanes), low), ((count, height, lanes), low),
        (gout, low), (gout, low), (part, low), (part, low), (part[1:], low), (part, low),
    ]
    owns = 3 + rows // RUN + count + 2 * own_experts * (ffn // HALF)
    to_z, to_c = owners - 1, count - 1
    sems = [
        (8 + 2 * own_experts,), (owns,), (to_c,), (to_c,), (2, to_z), (2, to_z), (2, to_z), (2, to_z), (to_c,), (to_c,), (2, to_c), (2, to_c),
        (to_z,), (to_z,), (to_c,), (to_c,), (3, to_c), (3, to_c), (3,), (3,), (4,), (4,), (3,), (3,), (4,), (4,),
    ]
    return pl.pallas_call(
        functools.partial(core_body, experts, groups),
        out_shape=(
            jax.ShapeDtypeStruct((lanes, 3 * width), full),
            jax.ShapeDtypeStruct((lanes, width), full),
            jax.ShapeDtypeStruct((smalls, lanes), full),
            jax.ShapeDtypeStruct(tokens.shape, full),
            jax.ShapeDtypeStruct(tokens.shape, full),
            jax.ShapeDtypeStruct(wide, low),
            jax.ShapeDtypeStruct(wide, low),
            jax.ShapeDtypeStruct((count,) + share, low),
        ),
        in_specs=[SMEM, VMEM, VMEM] + [ANY] * 12,
        out_specs=(VMEM,) * 3 + (ANY,) * 5,
        scratch_shapes=[pltpu.VMEM(shape, dtype) for shape, dtype in scratch] + [pltpu.SemaphoreType.DMA(shape) for shape in sems],
        compiler_params=pltpu.CompilerParams(collective_id=2, has_side_effects=True, vmem_limit_bytes=CORE_LIMIT),
        cost_estimate=cost(85),
        name="core",
    )(table, gid_row, parts, att, tokens, cot, w_out, pack, qf, kf, vf, stat, tokens_all.reshape(rows, width), w_up, w_down)


def expert_grad_body(experts, passed, mixed_ref, grad_ref, act_ref, gpre_ref, small_ref, *refs):
    sources, outs = refs[:passed], refs[passed + 5:]
    gup_ref, gdown_ref, router_ref, gain_ref, bias_ref = refs[passed:passed + 5]
    width = gup_ref.shape[1]
    for source, out in zip(sources, outs):
        out[...] = source[...]
    router_ref[...] = small_ref[:experts]
    gain_ref[...] = small_ref[experts:experts + 1]
    bias_ref[...] = small_ref[experts + 1:experts + 2]
    gup_ref[0] = dot_tn(mixed_ref[...].reshape(-1, width), gpre_ref[0])
    gdown_ref[0] = dot_tn(act_ref[0], grad_ref[...].reshape(-1, width))


def expert_grads(gathered, active, grad_pre, small, passed, groups, experts):
    own, rows, ffn = active.shape
    step = 1024
    steps = ffn // step
    sources, width = gathered.shape[0], gathered.shape[3]
    view = gathered.reshape(sources, 2, own, groups, width)
    lanes = small.shape[1]
    full = jnp.float32
    slices = [pl.BlockSpec((x.shape[0] // (own * steps), x.shape[1]), lambda e, f: (e * steps + f, 0)) for x in passed]
    return pl.pallas_call(
        functools.partial(expert_grad_body, experts, len(passed)),
        grid=(own, steps),
        out_shape=[
            jax.ShapeDtypeStruct((own, width, ffn), full), jax.ShapeDtypeStruct((own, ffn, width), full),
            jax.ShapeDtypeStruct((experts, lanes), full), jax.ShapeDtypeStruct((1, lanes), full), jax.ShapeDtypeStruct((1, lanes), full),
        ] + [jax.ShapeDtypeStruct(x.shape, x.dtype) for x in passed],
        in_specs=[
            pl.BlockSpec((sources, 1, 1, groups, width), lambda e, f: (0, 0, e, 0, 0)),
            pl.BlockSpec((sources, 1, 1, groups, width), lambda e, f: (0, 1, e, 0, 0)),
            pl.BlockSpec((1, rows, step), lambda e, f: (e, 0, f)),
            pl.BlockSpec((1, rows, step), lambda e, f: (e, 0, f)),
            pl.BlockSpec(small.shape, lambda e, f: (0, 0)),
        ] + slices,
        out_specs=[
            pl.BlockSpec((1, width, step), lambda e, f: (e, 0, f)), pl.BlockSpec((1, step, width), lambda e, f: (e, f, 0)),
            pl.BlockSpec((experts, lanes), lambda e, f: (0, 0)), pl.BlockSpec((1, lanes), lambda e, f: (0, 0)),
            pl.BlockSpec((1, lanes), lambda e, f: (0, 0)),
        ] + slices,
        compiler_params=pltpu.CompilerParams(vmem_limit_bytes=LIMIT),
        cost_estimate=cost(10),
        name="expert_grads",
    )(view, view, active, grad_pre, small, *passed)


def fast_device(
    tokens, cotangent, block_table, seg_ids, group_ids, w_qkv, w_out, w_router, ln_gain, ln_bias, w_up, w_down
):
    ctx_count, z_count = lax.axis_size("ctx"), lax.axis_size("fsdp")
    tok_rows, cot_rows = tokens[0], cotangent[0]
    rows, width = tok_rows.shape
    experts = w_router.shape[1]
    groups = rows // GROUP_SIZE
    tokens_all, head_weights, out_full, pack_full, qkv_parts = gather(
        tok_rows, w_qkv, w_out, w_router, ln_gain, ln_bias, ctx_count, z_count
    )
    att, *saved = attn_fwd(tokens_all.reshape(ctx_count * rows, width), head_weights, block_table, seg_ids)
    grad_qkv, grad_out, small, layer_out, grad_tokens, active, grad_pre, gathered = core(
        block_table, group_ids, qkv_parts, att, tok_rows, cot_rows, out_full, pack_full, saved, tokens_all, w_up, w_down, experts, groups
    )
    gathered = gathered.reshape(ctx_count * z_count, 2, experts * groups // z_count, width)
    grad_up, grad_down, grad_router, grad_gain, grad_bias, layer_out, grad_tokens, grad_qkv, grad_out = expert_grads(
        gathered, active, grad_pre, small, [layer_out, grad_tokens, grad_qkv, grad_out], groups, experts
    )
    return (
        layer_out[None],
        grad_tokens[None],
        grad_qkv,
        grad_out,
        grad_router.T,
        grad_gain[0],
        grad_bias[0],
        grad_up,
        grad_down,
    )


def solution(mesh):
    placed = (
        P("fsdp", "ctx", None),
        P("fsdp", "ctx", None),
        P(),
        P("fsdp", None),
        P("fsdp", "ctx"),
        P("fsdp", None),
        P("fsdp", None),
        P("fsdp", None),
        P("fsdp"),
        P("fsdp"),
        P("fsdp", None, None),
        P("fsdp", None, None),
    )
    step = fast_device if mesh.shape["ctx"] == HEADS else on_device
    return jax.shard_map(
        step,
        mesh=mesh,
        in_specs=placed,
        out_specs=(
            P("fsdp", "ctx", None),
            P("fsdp", "ctx", None),
            P("fsdp", None),
            P("fsdp", None),
            P("fsdp", None),
            P("fsdp"),
            P("fsdp"),
            P("fsdp", None, None),
            P("fsdp", None, None),
        ),
        check_vma=False,
    )
```

```python
import functools

import jax
import jax.numpy as jnp
from jax import lax
from jax.experimental import pallas as pl
from jax.experimental.pallas import tpu as pltpu
from jax.sharding import PartitionSpec as P

HEADS = 8
HEAD = 64
GROUP_SIZE = 32
KEY_BLOCK = 2048


highest = lax.Precision.HIGHEST
neg_large = -1e30
epsilon = 1e-05
gelu_coef = 0.7978845608028654
gelu_cubic = 0.044715


def contract_rows(left, right):
    return lax.dot_general(
        left, right, (((0,), (0,)), ((), ())), preferred_element_type=jnp.float32
    )


def contract_cols(left, right):
    return lax.dot_general(
        left, right, (((1,), (1,)), ((), ())), preferred_element_type=jnp.float32
    )


def gelu_slope(value):
    inner = gelu_coef * (value + gelu_cubic * value * value * value)
    tangent = jnp.tanh(inner)
    return 0.5 * (1.0 + tangent) + 0.5 * value * (1.0 - tangent * tangent) * gelu_coef * (
        1.0 + 3.0 * gelu_cubic * value * value
    )


def expert_forward(mixed_low, up_weight, down_weight):
    pre = jnp.einsum("ged,edh->geh", mixed_low, up_weight, preferred_element_type=jnp.float32)
    active = jax.nn.gelu(pre, approximate=True).astype(jnp.bfloat16)
    result = jnp.einsum("geh,ehd->ged", active, down_weight, preferred_element_type=jnp.float32)
    return (pre, active, result.astype(jnp.bfloat16))


def expert_backward(mixed_low, pre, active, grad_result, up_weight, down_weight):
    grad_act = jnp.einsum(
        "ged,ehd->geh", grad_result, down_weight, preferred_element_type=jnp.float32
    )
    grad_pre = (grad_act * gelu_slope(pre)).astype(jnp.bfloat16)
    grad_down_part = jnp.einsum(
        "geh,ged->ehd", active, grad_result, preferred_element_type=jnp.float32
    )
    grad_up_part = jnp.einsum(
        "ged,geh->edh", mixed_low, grad_pre, preferred_element_type=jnp.float32
    )
    grad_mixed = jnp.einsum("geh,edh->ged", grad_pre, up_weight, preferred_element_type=jnp.float32)
    return (grad_up_part, grad_down_part, grad_mixed.astype(jnp.bfloat16))


def on_device(
    tokens,
    cotangent,
    block_table,
    seg_ids,
    group_ids,
    w_qkv,
    w_out,
    w_router,
    ln_gain,
    ln_bias,
    w_up,
    w_down,
):
    tok_rows = tokens[0]
    tok_count = tok_rows.shape[0]
    width = tok_rows.shape[1]
    expert_count = w_router.shape[1]
    ctx_index = lax.axis_index("ctx")
    full_rows = seg_ids.shape[1]
    block_len = full_rows // block_table.shape[0]
    row_ids = jnp.arange(full_rows, dtype=jnp.int32)
    key_pos = jnp.take(block_table, row_ids // block_len) * block_len + row_ids % block_len
    key_seg = seg_ids[0]
    pos_rows = lax.dynamic_slice_in_dim(key_pos, ctx_index * tok_count, tok_count)
    seg_rows = lax.dynamic_slice_in_dim(key_seg, ctx_index * tok_count, tok_count)
    scale = HEAD ** (-0.5)
    qkv_full, out_full, router_full, gain_full, bias_full = (
        lax.all_gather(w_qkv, "fsdp", axis=0, tiled=True),
        lax.all_gather(w_out, "fsdp", axis=0, tiled=True),
        lax.all_gather(w_router, "fsdp", axis=0, tiled=True),
        lax.all_gather(ln_gain, "fsdp", axis=0, tiled=True),
        lax.all_gather(ln_bias, "fsdp", axis=0, tiled=True),
    )
    qkv = jnp.dot(tok_rows, qkv_full, preferred_element_type=jnp.float32).astype(jnp.bfloat16)
    query_heads = qkv[:, :width].reshape(tok_count, HEADS, HEAD)
    key_all, val_all = (
        lax.all_gather(qkv[:, width : 2 * width], "ctx", axis=0, tiled=True),
        lax.all_gather(qkv[:, 2 * width :], "ctx", axis=0, tiled=True),
    )
    key_heads = key_all.reshape(full_rows, HEADS, HEAD)
    val_heads = val_all.reshape(full_rows, HEADS, HEAD)
    block_count = full_rows // KEY_BLOCK
    block_ids = jnp.arange(block_count, dtype=jnp.int32)

    def block_scores(index):
        start = index * KEY_BLOCK
        key_block = lax.dynamic_slice_in_dim(key_heads, start, KEY_BLOCK, 0)
        val_block = lax.dynamic_slice_in_dim(val_heads, start, KEY_BLOCK, 0)
        pos_block = lax.dynamic_slice_in_dim(key_pos, start, KEY_BLOCK, 0)
        seg_block = lax.dynamic_slice_in_dim(key_seg, start, KEY_BLOCK, 0)
        scores = (
            jnp.einsum("qhd,khd->hqk", query_heads, key_block, preferred_element_type=jnp.float32)
            * scale
        )
        allowed = (pos_block[None, :] <= pos_rows[:, None]) & (
            (seg_block[None, :] == 0) | (seg_block[None, :] == seg_rows[:, None])
        )
        return (scores, allowed[None], key_block, val_block)

    def lse_step(carry, index):
        top, total = carry
        scores, allowed, key_block, val_block = block_scores(index)
        masked = jnp.where(allowed, scores, neg_large)
        new_top = jnp.maximum(top, jnp.max(masked, axis=-1))
        weights = jnp.where(allowed, jnp.exp(masked - new_top[..., None]), 0.0)
        return ((new_top, total * jnp.exp(top - new_top) + jnp.sum(weights, axis=-1)), None)

    start_top = jnp.full((HEADS, tok_count), neg_large, jnp.float32)
    (top, total), unused = lax.scan(
        lse_step, (start_top, jnp.zeros((HEADS, tok_count), jnp.float32)), block_ids
    )
    log_total = top + jnp.log(total)

    def block_probs(index):
        scores, allowed, key_block, val_block = block_scores(index)
        probs = jnp.where(allowed, jnp.exp(scores - log_total[..., None]), 0.0)
        return (probs, key_block, val_block)

    def value_step(accum, index):
        probs, key_block, val_block = block_probs(index)
        return (
            accum
            + jnp.einsum(
                "hqk,khd->qhd",
                probs.astype(jnp.bfloat16),
                val_block,
                preferred_element_type=jnp.float32,
            ),
            None,
        )

    accum, unused = lax.scan(
        value_step, jnp.zeros((tok_count, HEADS, HEAD), jnp.float32), block_ids
    )
    attended = accum.reshape(tok_count, width).astype(jnp.bfloat16)
    hidden = tok_rows.astype(jnp.float32) + jnp.dot(
        attended, out_full, preferred_element_type=jnp.float32
    )
    center = hidden - jnp.mean(hidden, axis=-1, keepdims=True)
    inv_dev = lax.rsqrt(jnp.mean(center * center, axis=-1, keepdims=True) + epsilon)
    unit = center * inv_dev
    gain_f = gain_full.astype(jnp.float32)
    normed_low = (unit * gain_f + bias_full.astype(jnp.float32)).astype(jnp.bfloat16)
    logits = jnp.dot(normed_low, router_full, preferred_element_type=jnp.float32)
    groups_dev = tok_count // GROUP_SIZE
    local_group = group_ids[0] - ctx_index * groups_dev
    member = (local_group[:, None] == jnp.arange(groups_dev, dtype=jnp.int32)[None, :]).astype(
        jnp.float32
    )
    expo = jnp.exp(logits)
    group_total = jnp.dot(member.T, expo, precision=highest)
    mix_weights = expo / jnp.dot(member, group_total, precision=highest)
    weights_low = mix_weights.astype(jnp.bfloat16)
    mixing = member.astype(jnp.bfloat16).T[:, None, :] * weights_low.T[None, :, :]
    mixing_flat = mixing.reshape(groups_dev * expert_count, tok_count)
    mixed_low = jnp.dot(mixing_flat, normed_low, preferred_element_type=jnp.float32).astype(
        jnp.bfloat16
    )
    mixed_low = mixed_low.reshape(groups_dev, expert_count, width)
    owner_mixed = lax.all_to_all(mixed_low, "fsdp", split_axis=1, concat_axis=0, tiled=True)
    pre, active, owner_out = expert_forward(owner_mixed, w_up, w_down)
    expert_out = lax.all_to_all(owner_out, "fsdp", split_axis=0, concat_axis=1, tiled=True)
    expert_flat = expert_out.reshape(groups_dev * expert_count, width)
    spread = contract_rows(mixing_flat, expert_flat)
    layer_out = hidden + spread
    cot_rows = cotangent[0]
    cot_f = cot_rows.astype(jnp.float32)
    grad_expert = jnp.dot(mixing_flat, cot_rows, preferred_element_type=jnp.float32).astype(
        jnp.bfloat16
    )
    grad_expert = grad_expert.reshape(groups_dev, expert_count, width)
    coef = contract_cols(cot_rows, expert_flat).reshape(tok_count, groups_dev, expert_count)
    grad_mix_spread = jnp.sum(coef * member[:, :, None], axis=1)
    owner_grad = lax.all_to_all(grad_expert, "fsdp", split_axis=1, concat_axis=0, tiled=True)
    grad_up_own, grad_down_own, owner_back = expert_backward(
        owner_mixed, pre, active, owner_grad, w_up, w_down
    )
    grad_mixed = lax.all_to_all(owner_back, "fsdp", split_axis=0, concat_axis=1, tiled=True)
    grad_mixed_flat = grad_mixed.reshape(groups_dev * expert_count, width)
    grad_norm_mix = contract_rows(mixing_flat, grad_mixed_flat)
    grad_mixing = contract_cols(grad_mixed_flat, normed_low).reshape(
        groups_dev, expert_count, tok_count
    )
    grad_mix_mixing = jnp.sum(grad_mixing * member.T[:, None, :], axis=0).T
    grad_mix = grad_mix_spread + grad_mix_mixing
    product = mix_weights * grad_mix
    token_dot = jnp.dot(member, jnp.dot(member.T, product, precision=highest), precision=highest)
    grad_logits = (product - mix_weights * token_dot).astype(jnp.bfloat16)
    grad_router_part = contract_rows(normed_low, grad_logits)
    grad_norm_router = contract_cols(grad_logits, router_full)
    grad_normed = grad_norm_mix + grad_norm_router
    grad_gain_part = jnp.sum(grad_normed * unit, axis=0)
    grad_bias_part = jnp.sum(grad_normed, axis=0)
    scaled = grad_normed * gain_f
    grad_hidden = cot_f + inv_dev * (
        scaled
        - jnp.mean(scaled, axis=-1, keepdims=True)
        - unit * jnp.mean(scaled * unit, axis=-1, keepdims=True)
    )
    grad_branch = grad_hidden.astype(jnp.bfloat16)
    grad_out_part = contract_rows(attended, grad_branch)
    grad_heads = (
        contract_cols(grad_branch, out_full).astype(jnp.bfloat16).reshape(tok_count, HEADS, HEAD)
    )
    delta = jnp.sum(grad_heads.astype(jnp.float32) * accum, axis=-1).T

    def grad_step(grad_query, index):
        probs, key_block, val_block = block_probs(index)
        grad_probs = jnp.einsum(
            "qhd,khd->hqk", grad_heads, val_block, preferred_element_type=jnp.float32
        )
        grad_scores = (probs * (grad_probs - delta[..., None])).astype(jnp.bfloat16)
        grad_query = (
            grad_query
            + jnp.einsum("hqk,khd->qhd", grad_scores, key_block, preferred_element_type=jnp.float32)
            * scale
        )
        grad_key = (
            jnp.einsum("hqk,qhd->khd", grad_scores, query_heads, preferred_element_type=jnp.float32)
            * scale
        )
        grad_val = jnp.einsum(
            "hqk,qhd->khd",
            probs.astype(jnp.bfloat16),
            grad_heads,
            preferred_element_type=jnp.float32,
        )
        return (grad_query, (grad_key, grad_val))

    grad_query, (grad_keys, grad_vals) = lax.scan(
        grad_step, jnp.zeros((tok_count, HEADS, HEAD), jnp.float32), block_ids
    )
    grad_key_own, grad_val_own = (
        lax.psum_scatter(
            grad_keys.reshape(full_rows, width), "ctx", scatter_dimension=0, tiled=True
        ),
        lax.psum_scatter(
            grad_vals.reshape(full_rows, width), "ctx", scatter_dimension=0, tiled=True
        ),
    )
    grad_qkv_low = jnp.concatenate(
        [grad_query.reshape(tok_count, width), grad_key_own, grad_val_own], axis=1
    ).astype(jnp.bfloat16)
    grad_qkv_part = contract_rows(tok_rows, grad_qkv_low)
    grad_tokens = grad_hidden + contract_cols(grad_qkv_low, qkv_full)
    dense = (
        lax.psum_scatter(grad_qkv_part, "fsdp", scatter_dimension=0, tiled=True),
        lax.psum_scatter(grad_out_part, "fsdp", scatter_dimension=0, tiled=True),
        lax.psum_scatter(grad_router_part, "fsdp", scatter_dimension=0, tiled=True),
        lax.psum_scatter(grad_gain_part, "fsdp", scatter_dimension=0, tiled=True),
        lax.psum_scatter(grad_bias_part, "fsdp", scatter_dimension=0, tiled=True),
    )
    totals = lax.psum(
        (dense[0], dense[1], dense[2], dense[3], dense[4], grad_up_own, grad_down_own), "ctx"
    )
    return (
        layer_out[None],
        grad_tokens[None],
        totals[0],
        totals[1],
        totals[2],
        totals[3],
        totals[4],
        totals[5],
        totals[6],
    )


def cost(microseconds):
    return pl.CostEstimate(flops=int(microseconds * 1.15e9), bytes_accessed=1 << 20, transcendentals=0)


LOG2E = 1.4426950408889634
HIDE = -1e30
SAFE = 100.0
RUN = 1024
HALF = 512
VMEM = pl.BlockSpec(memory_space=pltpu.VMEM)
SMEM = pl.BlockSpec(memory_space=pltpu.SMEM)
ANY = pl.BlockSpec(memory_space=pl.ANY)
LIMIT = 60 << 20
CORE_LIMIT = 60 << 20


def dot_nn(left, right):
    return lax.dot_general(left, right, (((1,), (0,)), ((), ())), preferred_element_type=jnp.float32)


def dot_nt(left, right):
    return lax.dot_general(left, right, (((1,), (1,)), ((), ())), preferred_element_type=jnp.float32)


def dot_tn(left, right):
    return lax.dot_general(left, right, (((0,), (0,)), ((), ())), preferred_element_type=jnp.float32)


def split3(value):
    one = value.astype(jnp.bfloat16)
    rest = value - one.astype(jnp.float32)
    two = rest.astype(jnp.bfloat16)
    three = (rest - two.astype(jnp.float32)).astype(jnp.bfloat16)
    return one, two, three


def span(index, size, width=None):
    return pl.ds(pl.multiple_of(index * size, size), size if width is None else width)


def flipped(value):
    return value.astype(jnp.float32).T.astype(value.dtype)


def boundaries(seg_ref, lane):
    segs = seg_ref[...]
    begin = jnp.zeros(lane.shape, jnp.int32)
    end = jnp.zeros(lane.shape, jnp.int32)
    for c in range(1, 10):
        below = (segs < c).astype(jnp.int32)
        total = jnp.sum(jnp.sum(below, axis=1, keepdims=True), axis=0, keepdims=True)
        begin = jnp.where(lane == HEAD - 1 + c, total, begin)
        end = jnp.where(lane == HEAD - 2 + c, total, end)
    return begin, jnp.where(lane == HEAD + 8, 0, end)


def fwd_body(blocks, block_len, table_ref, tok_ref, w_ref, seg_ref, att_ref, qf_ref, kf_ref, vf_ref, stat_ref, vt_ref, inv_ref):
    rows = blocks * block_len
    for t in range(blocks):
        inv_ref[table_ref[t]] = t
    weight = w_ref[...].reshape(w_ref.shape[0] * w_ref.shape[1], w_ref.shape[2])
    weight = jnp.concatenate([weight, jnp.zeros((weight.shape[0], HEAD), weight.dtype)], axis=1)
    lane = lax.broadcasted_iota(jnp.int32, (1, 2 * HEAD), 1)
    begin, end = boundaries(seg_ref, lane)
    is_flag = (lane >= HEAD) & (lane < HEAD + 8)
    is_one = (lane >= HEAD + 8) & (lane < HEAD + 11)
    pair = (lax.broadcasted_iota(jnp.int32, (2 * HEAD, 2 * HEAD), 0) // HEAD == lane // HEAD).astype(jnp.bfloat16)
    ones_v = ((lane >= HEAD) & (lane < HEAD + 3)).astype(jnp.float32)

    def project(s, sizes):
        t = inv_ref[s]
        qkv = dot_nn(tok_ref[span(t, block_len), :], weight)
        both = qkv[:, :2 * HEAD].astype(jnp.bfloat16).astype(jnp.float32)
        turned = pltpu.roll(both, HEAD, 1)
        value = qkv[:, 2 * HEAD:]
        place = lax.broadcasted_iota(jnp.int32, (block_len, 2 * HEAD), 0) + s * block_len
        own = (place >= begin) & (place < end)
        at = span(s, block_len)
        flag_q = jnp.where(is_flag & jnp.logical_not(own), 1.0, 0.0)
        flag_k = jnp.where(own, HIDE, jnp.where(is_one, 1.0, 0.0))
        qf_ref[at, :] = jnp.where(lane < HEAD, both, flag_q).astype(jnp.bfloat16)
        kf_ref[at, :] = jnp.where(lane < HEAD, turned, flag_k).astype(jnp.bfloat16)
        vf_ref[at, :] = (value + ones_v).astype(jnp.bfloat16)
        vt_ref[:, at] = jnp.where(lane < HEAD, value, 1.0).T.astype(jnp.bfloat16)
        return jnp.maximum(sizes, dot_nn((both * both).astype(jnp.bfloat16), pair))

    sizes = lax.fori_loop(0, blocks, project, jnp.zeros((block_len, 2 * HEAD), jnp.float32), unroll=4)
    scale = HEAD ** (-0.5) * LOG2E
    q_size, k_size = jnp.max(sizes[:, :HEAD]), jnp.max(sizes[:, HEAD:])
    small = q_size * k_size <= (SAFE / scale) ** 2
    causal = lax.broadcasted_iota(jnp.int32, (HALF, HALF), 0) <= lax.broadcasted_iota(jnp.int32, (HALF, HALF), 1)

    def query_run(online, run):
        def tile(state, q_at, k_at, diagonal):
            scores = dot_nt(kf_ref[k_at, :], qf_ref[q_at, :]) * scale
            if diagonal:
                scores = jnp.where(causal, scores, HIDE)
            top, acc = state
            if online:
                new_top = jnp.maximum(top, jnp.max(scores, axis=0, keepdims=True))
                acc = acc * jnp.exp2(top - new_top)
                scores, top = scores - new_top, new_top
            return top, acc + dot_nn(vt_ref[:, k_at], jnp.exp2(scores).astype(jnp.bfloat16))

        start = (jnp.full((1, RUN), HIDE if online else 0.0, jnp.float32), jnp.zeros((2 * HEAD, RUN), jnp.float32))
        whole = lax.fori_loop(0, run, lambda n, state: tile(state, span(run, RUN), span(n, RUN), False), start)
        early, late = span(2 * run, HALF), span(2 * run + 1, HALF)
        first = tile([part[:, :HALF] for part in whole], early, early, True)
        second = tile([part[:, HALF:] for part in whole], late, early, False)
        second = tile(second, late, late, True)
        for at, (top, acc) in ((early, first), (late, second)):
            total = acc[HEAD:]
            stat = jnp.concatenate([acc[:HEAD] / total, top + jnp.log2(total)], axis=0).T
            stat_ref[at, :] = stat
            one, two, three = split3(stat * (-1.0 / scale))
            old = qf_ref[at, :]
            old = jnp.where(lane == HEAD + 8, one, old)
            old = jnp.where(lane == HEAD + 9, two, old)
            qf_ref[at, :] = jnp.where(lane == HEAD + 10, three, old)

    for online in (False, True):
        @pl.when(small != online)
        def _():
            @pl.loop(0, rows // RUN)
            def _(run):
                query_run(online, run)

    for c in range(blocks // 2):
        parts = [stat_ref[span(table_ref[2 * c + half], block_len), :HEAD] for half in range(2)]
        att_ref[c] = jnp.concatenate(parts, axis=1).astype(jnp.bfloat16)


def attn_fwd(tokens_all, weight, table, segs):
    rows, blocks = tokens_all.shape[0], table.shape[0]
    block_len = rows // blocks
    low = jnp.bfloat16
    return pl.pallas_call(
        functools.partial(fwd_body, blocks, block_len),
        out_shape=(
            jax.ShapeDtypeStruct((blocks // 2, block_len, 2 * HEAD), low),
            jax.ShapeDtypeStruct((rows, 2 * HEAD), low),
            jax.ShapeDtypeStruct((rows, 2 * HEAD), low),
            jax.ShapeDtypeStruct((rows, 2 * HEAD), low),
            jax.ShapeDtypeStruct((rows, 2 * HEAD), jnp.float32),
        ),
        in_specs=[SMEM, VMEM, VMEM, VMEM],
        out_specs=(VMEM,) * 5,
        scratch_shapes=[pltpu.VMEM((2 * HEAD, rows), low), pltpu.SMEM((blocks,), jnp.int32)],
        compiler_params=pltpu.CompilerParams(vmem_limit_bytes=LIMIT),
        cost_estimate=cost(30),
        name="attention",
    )(table, tokens_all, weight, segs)


MESH = pl.DeviceIdType.MESH


def flip(index, bit):
    return index + bit - 2 * bit * lax.rem(index // bit, 2)


def meet(devices):
    barrier = pltpu.get_barrier_semaphore()
    for device in devices:
        pl.semaphore_signal(barrier, inc=1, device_id=device, device_id_type=MESH)
    pl.semaphore_wait(barrier, len(devices))


def push(src, dst, send_sem, recv_sem, device):
    return pltpu.make_async_remote_copy(
        src_ref=src, dst_ref=dst, send_sem=send_sem, recv_sem=recv_sem, device_id=device, device_id_type=MESH
    )


def gather_body(
    zs, tok_ref, wq_ref, wo_ref, router_ref, gain_ref, bias_ref, toks_ref, heads_ref, wos_ref, packs_ref, parts_ref,
    head_buf, pack_buf, own_sem, z_send, z_recv, far_send, near_send, own_recv, diag_recv, near_recv,
):
    me, z = lax.axis_index("ctx"), lax.axis_index("fsdp")
    sib, xn, yn, diag = flip(me, 1), flip(me, 2), flip(me, 4), flip(flip(me, 2), 4)
    z_peers = [lax.rem(z + k, zs) for k in range(1, zs)]
    meet([(sib, z), (xn, z), (yn, z)] + [(me, other) for other in z_peers])
    half = tok_ref.shape[0] // 2
    count = toks_ref.shape[0]

    def part(device, k):
        return toks_ref.at[device, pl.ds(k * half, half)]

    started, locals_ = [], []

    def go(copy):
        copy.start()
        started.append(copy)

    for k in (0, 1):
        rows = tok_ref.at[pl.ds(k * half, half)]
        go(push(rows, part(me, k), far_send.at[0, k], own_recv.at[0, k], (xn, z)))
        rows = tok_ref.at[pl.ds((1 - k) * half, half)]
        go(push(rows, part(me, 1 - k), far_send.at[1, 1 - k], own_recv.at[1, 1 - k], (yn, z)))

    def share(i, shard, whole):
        for k, other in enumerate(z_peers):
            go(push(shard, whole.at[z], z_send.at[i, k], z_recv.at[i, k], (me, other)))
        locals_.append(pltpu.make_async_copy(shard, whole.at[z], own_sem.at[i]))
        locals_[-1].start()

    depth = wq_ref.shape[0] // count
    width = wq_ref.shape[1] // 3
    for h in range(count):
        @pl.when(me == h)
        def _():
            cols = [wq_ref[:, width * kind + HEAD * h:width * kind + HEAD * (h + 1)] for kind in range(3)]
            head_buf[...] = jnp.concatenate(cols, axis=1)

    share(0, head_buf, heads_ref)
    share(1, wo_ref, wos_ref)
    experts = router_ref.shape[0]
    rows = [router_ref[...].astype(jnp.float32), gain_ref[...].astype(jnp.float32), bias_ref[...].astype(jnp.float32)]
    rows.append(jnp.zeros((pack_buf.shape[0] - experts - 2, pack_buf.shape[1]), jnp.float32))
    pack_buf[...] = jnp.concatenate(rows, axis=0).astype(jnp.bfloat16)
    share(2, pack_buf, packs_ref)
    share(3, wq_ref.at[pl.ds(pl.multiple_of(me * depth, depth), depth)], parts_ref)
    for k in (0, 1):
        rows = tok_ref.at[pl.ds(k * half, half)]
        go(push(rows, part(me, k), near_send.at[0, k], near_recv.at[0, k], (sib, z)))
    locals_.append(pltpu.make_async_copy(tok_ref, toks_ref.at[me], own_sem.at[4]))
    locals_[-1].start()

    def arrived(device, k, sem):
        push(part(device, k), part(device, k), far_send.at[0, 0], sem, (sib, z)).wait_recv()

    def relay(device, k, i):
        go(push(part(device, k), part(device, k), near_send.at[i, k], near_recv.at[i, k], (sib, z)))

    arrived(xn, 0, own_recv.at[0, 0])
    go(push(part(xn, 0), part(xn, 0), far_send.at[2, 0], diag_recv.at[0], (yn, z)))
    relay(xn, 0, 1)
    arrived(yn, 1, own_recv.at[1, 1])
    go(push(part(yn, 1), part(yn, 1), far_send.at[2, 1], diag_recv.at[1], (xn, z)))
    relay(yn, 1, 2)
    arrived(xn, 1, own_recv.at[0, 1])
    relay(xn, 1, 1)
    arrived(yn, 0, own_recv.at[1, 0])
    relay(yn, 0, 2)
    for k in (0, 1):
        arrived(diag, k, diag_recv.at[k])
        relay(diag, k, 3)
    for k in (0, 1):
        for i, device in enumerate((sib, flip(xn, 1), flip(yn, 1), flip(diag, 1))):
            arrived(device, k, near_recv.at[i, k])
    for i, whole in enumerate((heads_ref, wos_ref, packs_ref, parts_ref)):
        for k in range(zs - 1):
            other = lax.rem(z + zs - 1 - k, zs)
            push(whole.at[other], whole.at[other], z_send.at[i, k], z_recv.at[i, k], (me, other)).wait_recv()
    for copy in locals_:
        copy.wait()
    for copy in started:
        copy.wait_send()


def gather(tokens, w_qkv, w_out, w_router, ln_gain, ln_bias, ctx_count, z_count):
    shard, wide = w_qkv.shape
    low = jnp.bfloat16
    outs = [
        (ctx_count,) + tokens.shape, (z_count, shard, 3 * HEAD), (z_count,) + w_out.shape, (z_count, 16, shard),
        (z_count, shard // ctx_count, wide),
    ]
    dma = pltpu.SemaphoreType.DMA
    return pl.pallas_call(
        functools.partial(gather_body, z_count),
        out_shape=[jax.ShapeDtypeStruct(out, low) for out in outs],
        in_specs=[VMEM] * 6,
        out_specs=[ANY] * 5,
        scratch_shapes=[
            pltpu.VMEM((shard, 3 * HEAD), low), pltpu.VMEM((16, shard), low),
            dma((5,)), dma((4, z_count - 1)), dma((4, z_count - 1)), dma((3, 2)), dma((4, 2)), dma((2, 2)), dma((2,)), dma((4, 2)),
        ],
        compiler_params=pltpu.CompilerParams(collective_id=1, has_side_effects=True, vmem_limit_bytes=LIMIT),
        cost_estimate=cost(24),
        name="gather_tokens",
    )(tokens, w_qkv, w_out, w_router.T, ln_gain[None], ln_bias[None])


def norm_parts(hidden):
    center = hidden - jnp.mean(hidden, axis=-1, keepdims=True)
    inv_dev = lax.rsqrt(jnp.mean(center * center, axis=-1, keepdims=True) + epsilon)
    return center * inv_dev, inv_dev


def gelu_parts(value):
    square = value * value
    tangent = jnp.tanh(value * (square * (gelu_coef * gelu_cubic) + gelu_coef))
    half = 0.5 * tangent + 0.5
    rise = value * (square * (3.0 * gelu_coef * gelu_cubic) + gelu_coef)
    return value * half, half + half * (1.0 - tangent) * rise


def core_body(
    experts, groups, table_ref, gid_ref, part_ref, att_ref, tok_ref, cot_ref, wo_ref, pack_ref, qf_ref, kf_ref, vf_ref, stat_ref, toks_ref,
    up_ref, down_ref,
    gq_ref, out_ref, sums_ref, layer_ref, gtok_ref, act_ref, gpre_ref, all_ref,
    tok, cot, wo, pack, att, msend, zin, bsend, bin_, up, down, qf, kf, vf, stat, held, late_held, ghead_out, ghead, wide_out, ghidden,
    dof, qt, dot, dk_acc, dv_acc, sorted_dv, head_acc, send, landing, weight, zsend, zone, total, totals,
    out_mine, out_zone, out_sum, out_part, out_own, out_all,
    load_sem, own_sem, a_send, a_recv, m_send, m_recv, b_send, b_recv, h_send, h_recv, s_send, s_recv, z_send, z_recv, c_send, c_recv,
    o_send, o_recv, g_send, g_recv, r_send, r_recv, w_send, w_recv, v_send, v_recv,
):
    me, z = lax.axis_index("ctx"), lax.axis_index("fsdp")
    count, block_len = att_ref.shape[0], att_ref.shape[1]
    own_rows, width = tok_ref.shape
    owners, own_experts, ffn = msend.shape[0], up_ref.shape[0], up_ref.shape[2]
    flat, per = experts * groups, experts * groups // owners
    blocks = 2 * count
    rows = blocks * block_len
    runs = rows // RUN
    low = jnp.bfloat16
    dq_acc, qk, dv_rows = stat, qf, vf

    def start(copies):
        for copy in copies:
            copy.start()
        return copies

    def wait(copies):
        for copy in copies:
            copy.wait()

    pairs = [(qf_ref, qf), (kf_ref, kf), (tok_ref, tok), (wo_ref, wo), (pack_ref, pack), (cot_ref, cot)]
    for e in range(own_experts):
        pairs += [(up_ref.at[e], up.at[e]), (down_ref.at[e], down.at[e])]
    pairs += [(stat_ref, stat), (vf_ref, vf)]
    loads = start([pltpu.make_async_copy(src, dst, load_sem.at[i]) for i, (src, dst) in enumerate(pairs)])
    sib, same_core = flip(me, 1), [flip(me, 2), flip(me, 4), flip(flip(me, 2), 4)]
    z_peers = [(me, lax.rem(z + k, owners)) for k in range(1, owners)]
    c_peers = [(jnp.bitwise_xor(me, k), z) for k in range(1, count)]
    meet(z_peers + c_peers)
    swap = start([push(att_ref.at[d[0]], att.at[me], a_send.at[k], a_recv.at[k], d) for k, d in enumerate(c_peers)])
    own = start([pltpu.make_async_copy(att_ref.at[me], att.at[me], own_sem.at[0])])

    scale = HEAD ** (-0.5)
    first_diagonal = runs * (runs - 1)

    def slot_of(run, index, part):
        return run * (2 * runs - 1 - run) + 2 * (index - run - 1) + part

    def probabilities(q_at, k_at, visible):
        scores = dot_nt(qf[q_at, :], kf[k_at, :]) * (scale * LOG2E)
        if visible is not None:
            scores = jnp.where(visible, scores, HIDE)
        return jnp.exp2(scores).astype(low)

    def hold_diagonal():
        early = lax.broadcasted_iota(jnp.int32, (RUN, HALF), 1) <= lax.broadcasted_iota(jnp.int32, (RUN, HALF), 0)
        late = lax.broadcasted_iota(jnp.int32, (HALF, HALF), 1) <= lax.broadcasted_iota(jnp.int32, (HALF, HALF), 0)

        @pl.loop(0, runs)
        def _(run):
            held[first_diagonal + run] = probabilities(span(run, RUN), span(2 * run, HALF), early)
            late_held[run] = probabilities(span(2 * run + 1, HALF), span(2 * run + 1, HALF), late)

    def hold(run):
        @pl.loop(run + 1, runs)
        def _(index):
            for part in range(2):
                held[slot_of(run, index, part)] = probabilities(span(index, RUN), span(2 * run + part, HALF), None)

    wait(loads[:2])
    hold_diagonal()

    @pl.loop(1, runs - 1)
    def _(run):
        hold(run)

    wait(own + swap)
    weights = start([push(part_ref, weight.at[:, me], w_send.at[k], w_recv.at[k], (d, z)) for k, d in enumerate(same_core)])
    shares = start([push(part_ref, weight.at[:, me], v_send.at[3], v_recv.at[3], (sib, z))])
    weight[:, me] = part_ref[...]
    wait(loads[2:6])
    halves = [jnp.concatenate([att[h, :, HEAD * p:HEAD * (p + 1)] for h in range(count)], axis=1) for p in range(2)]
    attended = jnp.concatenate(halves, axis=0)
    out_weight = wo[...].reshape(width, width)
    hidden = tok[...].astype(jnp.float32) + dot_nn(attended, out_weight)
    unit, inv_dev = norm_parts(hidden)
    small_in = jnp.concatenate([pack[k] for k in range(owners)], axis=1)
    gain, bias = small_in[experts:experts + 1].astype(jnp.float32), small_in[experts + 1:experts + 2].astype(jnp.float32)
    normed = (unit * gain + bias).astype(low)
    expo = jnp.exp(dot_nt(small_in, normed)[:experts])
    expo = jnp.broadcast_to(expo[:, None, :], (experts, groups, own_rows)).reshape(flat, own_rows)
    member = lax.rem(lax.broadcasted_iota(jnp.int32, (flat, 1), 0), groups) == lax.rem(gid_ref[...], groups)
    expo = jnp.where(member, expo, 0.0)
    mix = expo / jnp.sum(expo, axis=1, keepdims=True)
    mix_low = mix.astype(low)

    def zone_rows(owner, kind):
        return pl.ds(pl.multiple_of((2 * owner + kind) * per, per), per)

    def to_owners(kind, value):
        msend[:, kind] = value.astype(low).reshape(owners, per, width)
        zin[zone_rows(z, kind), :] = msend[z, kind]
        return start([
            push(msend.at[d[1], kind], zin.at[zone_rows(z, kind)], m_send.at[kind, k], m_recv.at[kind, k], d) for k, d in enumerate(z_peers)
        ])

    mixed_copies = to_owners(0, dot_nn(mix_low, normed))
    grad_experts = dot_nn(mix_low, cot[...])
    wait(loads[6:6 + 2 * own_experts])
    wait(mixed_copies)
    grad_copies = to_owners(1, grad_experts)

    def from_sources(kind, e):
        lows_ = [(2 * owner + kind) * per + e * groups for owner in range(owners)]
        return jnp.concatenate([zin[at:at + groups, :] for at in lows_], axis=0)

    def to_sources(kind, e, value):
        bsend[:, kind, e * groups:(e + 1) * groups, :] = value.astype(low).reshape(owners, groups, width)

    def send_back(kind):
        bin_[z, kind] = bsend[z, kind]
        return start([
            push(bsend.at[d[1], kind], bin_.at[z, kind], b_send.at[kind, k], b_recv.at[kind, k], d) for k, d in enumerate(z_peers)
        ])

    slopes = []
    for e in range(own_experts):
        active, slope = gelu_parts(dot_nn(from_sources(0, e), up[e]))
        slopes.append(slope)
        to_sources(0, e, dot_nn(active.astype(low), down[e]))
    out_copies = send_back(0)
    wait(grad_copies)
    gathers = start([push(zin, all_ref.at[me], g_send.at[k], g_recv.at[k], (d, z)) for k, d in enumerate(same_core)])
    relays = start([push(zin, all_ref.at[me], r_send.at[3], r_recv.at[3], (sib, z))])
    own_got = start([pltpu.make_async_copy(zin, all_ref.at[me], own_sem.at[1])])
    for e in range(own_experts):
        grad_pre = (dot_nt(from_sources(1, e), down[e]) * slopes[e]).astype(low)
        to_sources(1, e, dot_nt(grad_pre, up[e]))
    back_copies = send_back(1)
    wait(out_copies)
    expert_out = bin_[:, 0].reshape(flat, width)
    wide_out[...] = hidden + dot_tn(mix_low, expert_out)
    layer_copy = start([pltpu.make_async_copy(wide_out, layer_ref, own_sem.at[2])])
    grad_mix = dot_nt(expert_out, cot[...])
    wait(back_copies)
    grad_mixed = bin_[:, 1].reshape(flat, width)
    product = mix * (grad_mix + dot_nt(grad_mixed, normed))
    grad_logits = product - mix * jnp.sum(product, axis=1, keepdims=True)
    grad_logits = jnp.sum(grad_logits.reshape(experts, groups, own_rows), axis=1).astype(low)
    pad = jnp.zeros((small_in.shape[0] - experts, own_rows), low)
    grad_logits = jnp.concatenate([grad_logits, pad], axis=0)
    grad_normed = dot_tn(jnp.concatenate([mix_low, grad_logits], axis=0), jnp.concatenate([grad_mixed, small_in], axis=0))
    scaled = grad_normed * gain
    mean = jnp.mean(scaled, axis=-1, keepdims=True)
    grad_hidden = cot[...].astype(jnp.float32) + inv_dev * (scaled - mean - unit * jnp.mean(scaled * unit, axis=-1, keepdims=True))
    branch = grad_hidden.astype(low)
    grad_heads = dot_nt(branch, out_weight).astype(low)
    for h in range(count):
        at = slice(HEAD * h, HEAD * (h + 1))
        ghead_out[h] = jnp.concatenate([grad_heads[:block_len, at], grad_heads[block_len:, at]], axis=1)
    swap = start([push(ghead_out.at[d[0]], ghead.at[me], h_send.at[k], h_recv.at[k], d) for k, d in enumerate(c_peers)])
    ghead[me] = ghead_out[me]
    ghidden[...] = grad_hidden
    out_mine[...] = dot_tn(attended, branch).astype(low).reshape(out_mine.shape)
    gout_copies = start([push(out_mine.at[d[1]], out_zone.at[z], o_send.at[0, k], o_recv.at[0, k], d) for k, d in enumerate(z_peers)])
    out_zone[z] = out_mine[z]
    small = jnp.concatenate(
        [
            dot_nn(grad_logits, normed)[:experts],
            jnp.sum(grad_normed * unit, axis=0, keepdims=True),
            jnp.sum(grad_normed, axis=0, keepdims=True),
            jnp.zeros((small_in.shape[0] - experts - 2, width), jnp.float32),
        ],
        axis=0,
    )
    lanes = width // owners
    for c in range(owners):
        zsend[c, 3 * HEAD:, :] = small[:, c * lanes:(c + 1) * lanes].astype(low)
    hold(0)

    def mask(condition):
        return jnp.broadcast_to(jnp.where(condition, 1.0, 0.0), (1, 2 * HEAD))

    firsts = [mask(table_ref[2 * c] < table_ref[2 * c + 1]).astype(low) for c in range(count)]
    lows = [jnp.minimum(table_ref[2 * c], table_ref[2 * c + 1]) for c in range(count)]
    holds = [[mask(lows[c] == j).astype(low) for j in range(count)] for c in range(count)]

    def blend(masks, values):
        out = None
        for weigh, value in zip(masks, values):
            out = weigh * value if out is None else out + weigh * value
        return out

    lane = lax.broadcasted_iota(jnp.int32, (1, 2 * HEAD), 1)

    def prepare(s, both):
        at = slice(s * block_len, (s + 1) * block_len)
        grad = jnp.where(lane < HEAD, both, 0.0)
        delta = jnp.sum(grad * stat[at, :], axis=1, keepdims=True)
        one, two, three = split3(jnp.broadcast_to(-delta, grad.shape))
        wide = jnp.where(lane == HEAD, one, grad.astype(low))
        wide = jnp.where(lane == HEAD + 1, two, wide)
        dof[at, :] = jnp.where(lane == HEAD + 2, three, wide)
        turned = jnp.where(lane < HEAD, both, pltpu.roll(qf[at, :].astype(jnp.float32), HEAD, 1)).T.astype(low)
        dot[:, at] = turned[:HEAD]
        qt[:, at] = turned[HEAD:]

    wait(swap)
    wait(loads[6 + 2 * own_experts:])
    for c in range(count):
        block = ghead[c]
        turned = pltpu.roll(block.astype(jnp.float32), HEAD, 1).astype(low)
        ghead_out[c] = firsts[c] * block + (1 - firsts[c]) * turned
    for j in range(count):
        both = blend([holds[c][j] for c in range(count)], [ghead_out[c] for c in range(count)]).astype(jnp.float32)
        prepare(j, both)
        prepare(blocks - 1 - j, pltpu.roll(both, HEAD, 1))

    tok_loads = [
        pltpu.make_async_copy(toks_ref.at[pl.ds(i * RUN, RUN)], held.at[i], own_sem.at[3 + i]) for i in range(rows // RUN)
    ]

    def key_run(run):
        def tile(q_at, k_at, part, probs, first_k, first_q):
            slope = dot_nt(dof[q_at, :], vf[k_at, :])
            grad = (probs.astype(jnp.float32) * slope).astype(low)
            dv = dot_nn(dot[:, q_at], probs)
            dk = dot_nn(qt[:, q_at], grad)
            dq = dot_nn(grad, kf[k_at, :])
            at = slice(part * HALF, (part + 1) * HALF)
            if first_k:
                dv_acc[:, at] = dv
                dk_acc[:, at] = dk
            else:
                dv_acc[:, at] += dv
                dk_acc[:, at] += dk
            if first_q:
                @pl.when(run == 0)
                def _():
                    dq_acc[q_at, :] = dq

                @pl.when(run != 0)
                def _():
                    dq_acc[q_at, :] += dq
            else:
                dq_acc[q_at, :] += dq

        early, late = span(2 * run, HALF), span(2 * run + 1, HALF)
        tile(span(run, RUN), early, 0, held[first_diagonal + run], True, True)
        tile(late, late, 1, late_held[run], True, False)

        @pl.loop(run + 1, runs)
        def _(index):
            for part in range(2):
                tile(span(index, RUN), span(2 * run + part, HALF), part, held[slot_of(run, index, part)], False, part == 0)

        at = span(run, RUN)
        both = jnp.concatenate([dk_acc[...] * scale, dv_acc[...]], axis=0).T
        query = dq_acc[at, :] * scale
        qk[at, :] = jnp.where(lane < HEAD, query, pltpu.roll(both, HEAD, 1)).astype(low)
        dv_rows[at, :] = both.astype(low)

    def send_half(half):
        mid = block_len // 2
        for c in range(count):
            ats = [slice(s * block_len, (s + 1) * block_len) for s in (range(count) if half == 0 else range(blocks - 1, count - 1, -1))]
            send[half, c, :block_len, :] = blend(holds[c], [qk[at, :] for at in ats])
            values = blend(holds[c], [dv_rows[at, :] for at in ats])
            sorted_dv[c] = values
            values = values[:, HEAD:]
            send[half, c, block_len:, :] = jnp.concatenate([values[:mid], values[mid:]], axis=1)
        landing[half, me] = send[half, me]
        return start([
            push(send.at[half, d[0]], landing.at[half, me], s_send.at[half, k], s_recv.at[half, k], d) for k, d in enumerate(c_peers)
        ])

    def head_weights(half):
        first, second = None, None
        for c in range(count):
            order = firsts[c][:, :1] if half == 0 else 1 - firsts[c][:, :1]
            slot, at = divmod(c * own_rows, RUN)
            here = order * held[slot, at:at + block_len, :] + (1 - order) * held[slot, at + block_len:at + 2 * block_len, :]
            one, two = dot_tn(send[half, c, :block_len, :], here), dot_tn(sorted_dv[c], here)
            first, second = (one, two) if first is None else (first + one, second + two)
        both = jnp.concatenate([first, second[HEAD:]], axis=0)
        if half == 0:
            head_acc[...] = both
        else:
            head_acc[...] += both

    @pl.loop(0, runs // 2)
    def _(run):
        key_run(run)

        @pl.when(run == 0)
        def _():
            start(tok_loads)

    swaps = send_half(0)
    for k, d in enumerate(same_core):
        gathers[k].wait_recv()
        relays += start([push(all_ref.at[d], all_ref.at[d], r_send.at[k], r_recv.at[k], (sib, z))])
        weights[k].wait_recv()
        shares += start([push(weight.at[:, d], weight.at[:, d], v_send.at[k], v_recv.at[k], (sib, z))])
    wait(gout_copies)
    summed = out_zone[0].astype(jnp.float32)
    for k in range(1, owners):
        summed = summed + out_zone[k].astype(jnp.float32)
    out_sum[...] = summed.astype(low).reshape(out_sum.shape)
    part_copies = start([push(out_sum.at[d[0]], out_part.at[me], o_send.at[1, k], o_recv.at[1, k], d) for k, d in enumerate(c_peers)])
    out_part[me] = out_sum[me]
    wait(tok_loads)
    head_weights(0)

    @pl.loop(runs // 2, runs)
    def _(run):
        key_run(run)

    swaps += send_half(1)
    wait(part_copies)
    summed = out_part[0].astype(jnp.float32)
    for k in range(1, count):
        summed = summed + out_part[k].astype(jnp.float32)
    out_own[...] = summed.astype(low)
    last_copies = start([push(out_own, out_all.at[me], o_send.at[2, k], o_recv.at[2, k], d) for k, d in enumerate(c_peers)])
    out_all[me] = out_own[...]
    wait(own_got + relays)

    mixed_slot = rows // RUN
    share = owners * 2 * per
    mixed_loads = []
    for c in range(count):
        slot, at = divmod(c * share, RUN)
        mixed_loads.append(pltpu.make_async_copy(all_ref.at[c], held.at[mixed_slot + slot, pl.ds(at, share)], own_sem.at[3 + rows // RUN + c]))
    start(mixed_loads)
    head_weights(1)
    for c in range(owners):
        zsend[c, :3 * HEAD, :] = head_acc[:, c * lanes:(c + 1) * lanes].astype(low)
    z_copies = start([push(zsend.at[d[1]], zone.at[z], z_send.at[k], z_recv.at[k], d) for k, d in enumerate(z_peers)])
    zone[z] = zsend[z]
    wait(mixed_loads)
    step = HALF
    chunks = ffn // step
    wide_slot = mixed_slot + count * share // RUN

    def of_expert(kind, e):
        parts = []
        for slot in range(mixed_slot, wide_slot):
            value = held[slot].reshape(RUN // share, owners, 2, own_experts, groups, width)
            parts.append(value[:, :, kind, e].reshape(-1, width))
        return jnp.concatenate(parts, axis=0)

    def expert_part(e):
        mixed, grad_out = of_expert(0, e), of_expert(1, e)
        copies = []

        @pl.loop(0, chunks // 2)
        def _(i):
            for part in range(2):
                at = span(2 * i + part, step)
                to = pl.ds(part * step, step)
                active, slope = gelu_parts(dot_nn(mixed, up[e, :, at]))
                held[wide_slot + chunks * e + i, to, :] = active.astype(low)
                slot = wide_slot + chunks * e + chunks // 2 + i
                held[slot, to, :] = (dot_nt(grad_out, down[e, at, :]) * slope).astype(low)

        for i in range(chunks):
            slot = wide_slot + chunks * e + i // 2
            at, to = pl.ds(i * step, step), pl.ds(i % 2 * step, step)
            sem = own_sem.at[3 + rows // RUN + count + 2 * (chunks * e + i)]
            copies.append(pltpu.make_async_copy(held.at[slot, to], act_ref.at[e, :, at], sem))
            sem = own_sem.at[4 + rows // RUN + count + 2 * (chunks * e + i)]
            copies.append(pltpu.make_async_copy(held.at[slot + chunks // 2, to], gpre_ref.at[e, :, at], sem))
        return start(copies)

    stores = expert_part(0)
    wait(z_copies)
    summed = zone[0].astype(jnp.float32)
    for k in range(1, owners):
        summed = summed + zone[k].astype(jnp.float32)
    total[...] = summed.astype(low)
    c_copies = start([push(total, totals.at[me], c_send.at[k], c_recv.at[k], d) for k, d in enumerate(c_peers)])
    totals[me] = total[...]
    for e in range(1, own_experts):
        stores += expert_part(e)
    wait(swaps + shares)
    flat_weight = weight[...].reshape(width, -1)
    parts = []
    for half in range(2):
        queries, keys, values = [], [], []
        for h in range(count):
            front, back = landing[half, h, :block_len, :], landing[half, h, block_len:, :]
            queries.append(front[:, :HEAD])
            keys.append(front[:, HEAD:])
            values.append(jnp.concatenate([back[:, :HEAD], back[:, HEAD:]], axis=0))
        parts.append(dot_nt(jnp.concatenate(queries + keys + values, axis=1), flat_weight))
    in_order = mask(table_ref[2 * me] < table_ref[2 * me + 1])[:, :1]
    wait(layer_copy)
    wide_out[:block_len, :] = ghidden[:block_len, :] + (in_order * parts[0] + (1.0 - in_order) * parts[1])
    wide_out[block_len:, :] = ghidden[block_len:, :] + (in_order * parts[1] + (1.0 - in_order) * parts[0])
    stores += start([pltpu.make_async_copy(wide_out, gtok_ref, own_sem.at[2])])
    wait(last_copies)
    out_ref[...] = out_all[...].astype(jnp.float32).reshape(out_ref.shape)
    wait(c_copies)
    small = None
    turned = []
    for c in range(count):
        turned.append(totals[c, :3 * HEAD, :].astype(jnp.float32).T)
        part = totals[c, 3 * HEAD:, :].astype(jnp.float32)
        small = part if small is None else small + part
    sums_ref[...] = small
    for kind in range(3):
        at = slice(HEAD * kind, HEAD * (kind + 1))
        gq_ref[:, HEAD * count * kind:HEAD * count * (kind + 1)] = jnp.concatenate([part[:, at] for part in turned], axis=1)
    wait(stores)
    for copy in gathers + weights:
        copy.wait_send()


def core(table, gid_row, parts, att, tokens, cot, w_out, pack, saved, tokens_all, w_up, w_down, experts, groups):
    count, block_len = att.shape[:2]
    qf, kf, vf, stat = saved
    rows, (own_rows, width) = qf.shape[0], tokens.shape
    runs = rows // RUN
    own_experts, _, ffn = w_up.shape
    owners, smalls, lanes = pack.shape
    height = 3 * HEAD + smalls
    per = experts * groups // owners
    wide = (own_experts, count * owners * groups, ffn)
    share = (owners * 2 * per, width)
    part = (count, lanes // count, width)
    swap = (2, count, block_len + block_len // 2, 2 * HEAD)
    gout = (owners, lanes, width)
    sent = (owners, 2, per, width)
    low, full = jnp.bfloat16, jnp.float32
    scratch = [
        (tokens.shape, low), (cot.shape, low), (w_out.shape, low), (pack.shape, low), (att.shape, low),
        (sent, low), (share, low), (sent, low), (sent, low), (w_up.shape, low), (w_down.shape, low),
        (qf.shape, low), (kf.shape, low), (vf.shape, low), (stat.shape, full), ((runs * runs, RUN, HALF), low), ((runs, HALF, HALF), low),
        (att.shape, low), (att.shape, low), (tokens.shape, full), (tokens.shape, full),
        ((rows, 2 * HEAD), low), ((HEAD, rows), low), ((HEAD, rows), low), ((HEAD, RUN), full), ((HEAD, RUN), full),
        ((count, block_len, 2 * HEAD), low), ((3 * HEAD, width), full), (swap, low), (swap, low), ((owners, count) + parts.shape[1:], low),
        ((owners, height, lanes), low), ((owners, height, lanes), low), ((height, lanes), low), ((count, height, lanes), low),
        (gout, low), (gout, low), (part, low), (part, low), (part[1:], low), (part, low),
    ]
    owns = 3 + rows // RUN + count + 2 * own_experts * (ffn // HALF)
    to_z, to_c = owners - 1, count - 1
    sems = [
        (8 + 2 * own_experts,), (owns,), (to_c,), (to_c,), (2, to_z), (2, to_z), (2, to_z), (2, to_z), (to_c,), (to_c,), (2, to_c), (2, to_c),
        (to_z,), (to_z,), (to_c,), (to_c,), (3, to_c), (3, to_c), (3,), (3,), (4,), (4,), (3,), (3,), (4,), (4,),
    ]
    return pl.pallas_call(
        functools.partial(core_body, experts, groups),
        out_shape=(
            jax.ShapeDtypeStruct((lanes, 3 * width), full),
            jax.ShapeDtypeStruct((lanes, width), full),
            jax.ShapeDtypeStruct((smalls, lanes), full),
            jax.ShapeDtypeStruct(tokens.shape, full),
            jax.ShapeDtypeStruct(tokens.shape, full),
            jax.ShapeDtypeStruct(wide, low),
            jax.ShapeDtypeStruct(wide, low),
            jax.ShapeDtypeStruct((count,) + share, low),
        ),
        in_specs=[SMEM, VMEM, VMEM] + [ANY] * 12,
        out_specs=(VMEM,) * 3 + (ANY,) * 5,
        scratch_shapes=[pltpu.VMEM(shape, dtype) for shape, dtype in scratch] + [pltpu.SemaphoreType.DMA(shape) for shape in sems],
        compiler_params=pltpu.CompilerParams(collective_id=2, has_side_effects=True, vmem_limit_bytes=CORE_LIMIT),
        cost_estimate=cost(85),
        name="core",
    )(table, gid_row, parts, att, tokens, cot, w_out, pack, qf, kf, vf, stat, tokens_all.reshape(rows, width), w_up, w_down)


def expert_grad_body(experts, passed, mixed_ref, grad_ref, act_ref, gpre_ref, small_ref, *refs):
    sources, outs = refs[:passed], refs[passed + 5:]
    gup_ref, gdown_ref, router_ref, gain_ref, bias_ref = refs[passed:passed + 5]
    width = gup_ref.shape[1]
    for source, out in zip(sources, outs):
        out[...] = source[...]
    router_ref[...] = small_ref[:experts]
    gain_ref[...] = small_ref[experts:experts + 1]
    bias_ref[...] = small_ref[experts + 1:experts + 2]
    gup_ref[0] = dot_tn(mixed_ref[...].reshape(-1, width), gpre_ref[0])
    gdown_ref[0] = dot_tn(act_ref[0], grad_ref[...].reshape(-1, width))


def expert_grads(gathered, active, grad_pre, small, passed, groups, experts):
    own, rows, ffn = active.shape
    step = ffn
    steps = ffn // step
    sources, width = gathered.shape[0], gathered.shape[3]
    view = gathered.reshape(sources, 2, own, groups, width)
    lanes = small.shape[1]
    full = jnp.float32
    slices = [pl.BlockSpec((x.shape[0] // (own * steps), x.shape[1]), lambda e, f: (e * steps + f, 0)) for x in passed]
    return pl.pallas_call(
        functools.partial(expert_grad_body, experts, len(passed)),
        grid=(own, steps),
        out_shape=[
            jax.ShapeDtypeStruct((own, width, ffn), full), jax.ShapeDtypeStruct((own, ffn, width), full),
            jax.ShapeDtypeStruct((experts, lanes), full), jax.ShapeDtypeStruct((1, lanes), full), jax.ShapeDtypeStruct((1, lanes), full),
        ] + [jax.ShapeDtypeStruct(x.shape, x.dtype) for x in passed],
        in_specs=[
            pl.BlockSpec((sources, 1, 1, groups, width), lambda e, f: (0, 0, e, 0, 0)),
            pl.BlockSpec((sources, 1, 1, groups, width), lambda e, f: (0, 1, e, 0, 0)),
            pl.BlockSpec((1, rows, step), lambda e, f: (e, 0, f)),
            pl.BlockSpec((1, rows, step), lambda e, f: (e, 0, f)),
            pl.BlockSpec(small.shape, lambda e, f: (0, 0)),
        ] + slices,
        out_specs=[
            pl.BlockSpec((1, width, step), lambda e, f: (e, 0, f)), pl.BlockSpec((1, step, width), lambda e, f: (e, f, 0)),
            pl.BlockSpec((experts, lanes), lambda e, f: (0, 0)), pl.BlockSpec((1, lanes), lambda e, f: (0, 0)),
            pl.BlockSpec((1, lanes), lambda e, f: (0, 0)),
        ] + slices,
        compiler_params=pltpu.CompilerParams(vmem_limit_bytes=LIMIT),
        cost_estimate=cost(10),
        name="expert_grads",
    )(view, view, active, grad_pre, small, *passed)


def fast_device(
    tokens, cotangent, block_table, seg_ids, group_ids, w_qkv, w_out, w_router, ln_gain, ln_bias, w_up, w_down
):
    ctx_count, z_count = lax.axis_size("ctx"), lax.axis_size("fsdp")
    tok_rows, cot_rows = tokens[0], cotangent[0]
    rows, width = tok_rows.shape
    experts = w_router.shape[1]
    groups = rows // GROUP_SIZE
    tokens_all, head_weights, out_full, pack_full, qkv_parts = gather(
        tok_rows, w_qkv, w_out, w_router, ln_gain, ln_bias, ctx_count, z_count
    )
    att, *saved = attn_fwd(tokens_all.reshape(ctx_count * rows, width), head_weights, block_table, seg_ids)
    grad_qkv, grad_out, small, layer_out, grad_tokens, active, grad_pre, gathered = core(
        block_table, group_ids, qkv_parts, att, tok_rows, cot_rows, out_full, pack_full, saved, tokens_all, w_up, w_down, experts, groups
    )
    gathered = gathered.reshape(ctx_count * z_count, 2, experts * groups // z_count, width)
    grad_up, grad_down, grad_router, grad_gain, grad_bias, layer_out, grad_tokens, grad_qkv, grad_out = expert_grads(
        gathered, active, grad_pre, small, [layer_out, grad_tokens, grad_qkv, grad_out], groups, experts
    )
    return (
        layer_out[None],
        grad_tokens[None],
        grad_qkv,
        grad_out,
        grad_router.T,
        grad_gain[0],
        grad_bias[0],
        grad_up,
        grad_down,
    )


def solution(mesh):
    placed = (
        P("fsdp", "ctx", None),
        P("fsdp", "ctx", None),
        P(),
        P("fsdp", None),
        P("fsdp", "ctx"),
        P("fsdp", None),
        P("fsdp", None),
        P("fsdp", None),
        P("fsdp"),
        P("fsdp"),
        P("fsdp", None, None),
        P("fsdp", None, None),
    )
    step = fast_device if mesh.shape["ctx"] == HEADS else on_device
    return jax.shard_map(
        step,
        mesh=mesh,
        in_specs=placed,
        out_specs=(
            P("fsdp", "ctx", None),
            P("fsdp", "ctx", None),
            P("fsdp", None),
            P("fsdp", None),
            P("fsdp", None),
            P("fsdp"),
            P("fsdp"),
            P("fsdp", None, None),
            P("fsdp", None, None),
        ),
        check_vma=False,
    )
```

```python
import functools

import jax
import jax.numpy as jnp
from jax import lax
from jax.experimental import pallas as pl
from jax.experimental.pallas import tpu as pltpu
from jax.sharding import PartitionSpec as P

HEADS = 8
HEAD = 64
GROUP_SIZE = 32
KEY_BLOCK = 2048


highest = lax.Precision.HIGHEST
neg_large = -1e30
epsilon = 1e-05
gelu_coef = 0.7978845608028654
gelu_cubic = 0.044715


def contract_rows(left, right):
    return lax.dot_general(
        left, right, (((0,), (0,)), ((), ())), preferred_element_type=jnp.float32
    )


def contract_cols(left, right):
    return lax.dot_general(
        left, right, (((1,), (1,)), ((), ())), preferred_element_type=jnp.float32
    )


def gelu_slope(value):
    inner = gelu_coef * (value + gelu_cubic * value * value * value)
    tangent = jnp.tanh(inner)
    return 0.5 * (1.0 + tangent) + 0.5 * value * (1.0 - tangent * tangent) * gelu_coef * (
        1.0 + 3.0 * gelu_cubic * value * value
    )


def expert_forward(mixed_low, up_weight, down_weight):
    pre = jnp.einsum("ged,edh->geh", mixed_low, up_weight, preferred_element_type=jnp.float32)
    active = jax.nn.gelu(pre, approximate=True).astype(jnp.bfloat16)
    result = jnp.einsum("geh,ehd->ged", active, down_weight, preferred_element_type=jnp.float32)
    return (pre, active, result.astype(jnp.bfloat16))


def expert_backward(mixed_low, pre, active, grad_result, up_weight, down_weight):
    grad_act = jnp.einsum(
        "ged,ehd->geh", grad_result, down_weight, preferred_element_type=jnp.float32
    )
    grad_pre = (grad_act * gelu_slope(pre)).astype(jnp.bfloat16)
    grad_down_part = jnp.einsum(
        "geh,ged->ehd", active, grad_result, preferred_element_type=jnp.float32
    )
    grad_up_part = jnp.einsum(
        "ged,geh->edh", mixed_low, grad_pre, preferred_element_type=jnp.float32
    )
    grad_mixed = jnp.einsum("geh,edh->ged", grad_pre, up_weight, preferred_element_type=jnp.float32)
    return (grad_up_part, grad_down_part, grad_mixed.astype(jnp.bfloat16))


def on_device(
    tokens,
    cotangent,
    block_table,
    seg_ids,
    group_ids,
    w_qkv,
    w_out,
    w_router,
    ln_gain,
    ln_bias,
    w_up,
    w_down,
):
    tok_rows = tokens[0]
    tok_count = tok_rows.shape[0]
    width = tok_rows.shape[1]
    expert_count = w_router.shape[1]
    ctx_index = lax.axis_index("ctx")
    full_rows = seg_ids.shape[1]
    block_len = full_rows // block_table.shape[0]
    row_ids = jnp.arange(full_rows, dtype=jnp.int32)
    key_pos = jnp.take(block_table, row_ids // block_len) * block_len + row_ids % block_len
    key_seg = seg_ids[0]
    pos_rows = lax.dynamic_slice_in_dim(key_pos, ctx_index * tok_count, tok_count)
    seg_rows = lax.dynamic_slice_in_dim(key_seg, ctx_index * tok_count, tok_count)
    scale = HEAD ** (-0.5)
    qkv_full, out_full, router_full, gain_full, bias_full = (
        lax.all_gather(w_qkv, "fsdp", axis=0, tiled=True),
        lax.all_gather(w_out, "fsdp", axis=0, tiled=True),
        lax.all_gather(w_router, "fsdp", axis=0, tiled=True),
        lax.all_gather(ln_gain, "fsdp", axis=0, tiled=True),
        lax.all_gather(ln_bias, "fsdp", axis=0, tiled=True),
    )
    qkv = jnp.dot(tok_rows, qkv_full, preferred_element_type=jnp.float32).astype(jnp.bfloat16)
    query_heads = qkv[:, :width].reshape(tok_count, HEADS, HEAD)
    key_all, val_all = (
        lax.all_gather(qkv[:, width : 2 * width], "ctx", axis=0, tiled=True),
        lax.all_gather(qkv[:, 2 * width :], "ctx", axis=0, tiled=True),
    )
    key_heads = key_all.reshape(full_rows, HEADS, HEAD)
    val_heads = val_all.reshape(full_rows, HEADS, HEAD)
    block_count = full_rows // KEY_BLOCK
    block_ids = jnp.arange(block_count, dtype=jnp.int32)

    def block_scores(index):
        start = index * KEY_BLOCK
        key_block = lax.dynamic_slice_in_dim(key_heads, start, KEY_BLOCK, 0)
        val_block = lax.dynamic_slice_in_dim(val_heads, start, KEY_BLOCK, 0)
        pos_block = lax.dynamic_slice_in_dim(key_pos, start, KEY_BLOCK, 0)
        seg_block = lax.dynamic_slice_in_dim(key_seg, start, KEY_BLOCK, 0)
        scores = (
            jnp.einsum("qhd,khd->hqk", query_heads, key_block, preferred_element_type=jnp.float32)
            * scale
        )
        allowed = (pos_block[None, :] <= pos_rows[:, None]) & (
            (seg_block[None, :] == 0) | (seg_block[None, :] == seg_rows[:, None])
        )
        return (scores, allowed[None], key_block, val_block)

    def lse_step(carry, index):
        top, total = carry
        scores, allowed, key_block, val_block = block_scores(index)
        masked = jnp.where(allowed, scores, neg_large)
        new_top = jnp.maximum(top, jnp.max(masked, axis=-1))
        weights = jnp.where(allowed, jnp.exp(masked - new_top[..., None]), 0.0)
        return ((new_top, total * jnp.exp(top - new_top) + jnp.sum(weights, axis=-1)), None)

    start_top = jnp.full((HEADS, tok_count), neg_large, jnp.float32)
    (top, total), unused = lax.scan(
        lse_step, (start_top, jnp.zeros((HEADS, tok_count), jnp.float32)), block_ids
    )
    log_total = top + jnp.log(total)

    def block_probs(index):
        scores, allowed, key_block, val_block = block_scores(index)
        probs = jnp.where(allowed, jnp.exp(scores - log_total[..., None]), 0.0)
        return (probs, key_block, val_block)

    def value_step(accum, index):
        probs, key_block, val_block = block_probs(index)
        return (
            accum
            + jnp.einsum(
                "hqk,khd->qhd",
                probs.astype(jnp.bfloat16),
                val_block,
                preferred_element_type=jnp.float32,
            ),
            None,
        )

    accum, unused = lax.scan(
        value_step, jnp.zeros((tok_count, HEADS, HEAD), jnp.float32), block_ids
    )
    attended = accum.reshape(tok_count, width).astype(jnp.bfloat16)
    hidden = tok_rows.astype(jnp.float32) + jnp.dot(
        attended, out_full, preferred_element_type=jnp.float32
    )
    center = hidden - jnp.mean(hidden, axis=-1, keepdims=True)
    inv_dev = lax.rsqrt(jnp.mean(center * center, axis=-1, keepdims=True) + epsilon)
    unit = center * inv_dev
    gain_f = gain_full.astype(jnp.float32)
    normed_low = (unit * gain_f + bias_full.astype(jnp.float32)).astype(jnp.bfloat16)
    logits = jnp.dot(normed_low, router_full, preferred_element_type=jnp.float32)
    groups_dev = tok_count // GROUP_SIZE
    local_group = group_ids[0] - ctx_index * groups_dev
    member = (local_group[:, None] == jnp.arange(groups_dev, dtype=jnp.int32)[None, :]).astype(
        jnp.float32
    )
    expo = jnp.exp(logits)
    group_total = jnp.dot(member.T, expo, precision=highest)
    mix_weights = expo / jnp.dot(member, group_total, precision=highest)
    weights_low = mix_weights.astype(jnp.bfloat16)
    mixing = member.astype(jnp.bfloat16).T[:, None, :] * weights_low.T[None, :, :]
    mixing_flat = mixing.reshape(groups_dev * expert_count, tok_count)
    mixed_low = jnp.dot(mixing_flat, normed_low, preferred_element_type=jnp.float32).astype(
        jnp.bfloat16
    )
    mixed_low = mixed_low.reshape(groups_dev, expert_count, width)
    owner_mixed = lax.all_to_all(mixed_low, "fsdp", split_axis=1, concat_axis=0, tiled=True)
    pre, active, owner_out = expert_forward(owner_mixed, w_up, w_down)
    expert_out = lax.all_to_all(owner_out, "fsdp", split_axis=0, concat_axis=1, tiled=True)
    expert_flat = expert_out.reshape(groups_dev * expert_count, width)
    spread = contract_rows(mixing_flat, expert_flat)
    layer_out = hidden + spread
    cot_rows = cotangent[0]
    cot_f = cot_rows.astype(jnp.float32)
    grad_expert = jnp.dot(mixing_flat, cot_rows, preferred_element_type=jnp.float32).astype(
        jnp.bfloat16
    )
    grad_expert = grad_expert.reshape(groups_dev, expert_count, width)
    coef = contract_cols(cot_rows, expert_flat).reshape(tok_count, groups_dev, expert_count)
    grad_mix_spread = jnp.sum(coef * member[:, :, None], axis=1)
    owner_grad = lax.all_to_all(grad_expert, "fsdp", split_axis=1, concat_axis=0, tiled=True)
    grad_up_own, grad_down_own, owner_back = expert_backward(
        owner_mixed, pre, active, owner_grad, w_up, w_down
    )
    grad_mixed = lax.all_to_all(owner_back, "fsdp", split_axis=0, concat_axis=1, tiled=True)
    grad_mixed_flat = grad_mixed.reshape(groups_dev * expert_count, width)
    grad_norm_mix = contract_rows(mixing_flat, grad_mixed_flat)
    grad_mixing = contract_cols(grad_mixed_flat, normed_low).reshape(
        groups_dev, expert_count, tok_count
    )
    grad_mix_mixing = jnp.sum(grad_mixing * member.T[:, None, :], axis=0).T
    grad_mix = grad_mix_spread + grad_mix_mixing
    product = mix_weights * grad_mix
    token_dot = jnp.dot(member, jnp.dot(member.T, product, precision=highest), precision=highest)
    grad_logits = (product - mix_weights * token_dot).astype(jnp.bfloat16)
    grad_router_part = contract_rows(normed_low, grad_logits)
    grad_norm_router = contract_cols(grad_logits, router_full)
    grad_normed = grad_norm_mix + grad_norm_router
    grad_gain_part = jnp.sum(grad_normed * unit, axis=0)
    grad_bias_part = jnp.sum(grad_normed, axis=0)
    scaled = grad_normed * gain_f
    grad_hidden = cot_f + inv_dev * (
        scaled
        - jnp.mean(scaled, axis=-1, keepdims=True)
        - unit * jnp.mean(scaled * unit, axis=-1, keepdims=True)
    )
    grad_branch = grad_hidden.astype(jnp.bfloat16)
    grad_out_part = contract_rows(attended, grad_branch)
    grad_heads = (
        contract_cols(grad_branch, out_full).astype(jnp.bfloat16).reshape(tok_count, HEADS, HEAD)
    )
    delta = jnp.sum(grad_heads.astype(jnp.float32) * accum, axis=-1).T

    def grad_step(grad_query, index):
        probs, key_block, val_block = block_probs(index)
        grad_probs = jnp.einsum(
            "qhd,khd->hqk", grad_heads, val_block, preferred_element_type=jnp.float32
        )
        grad_scores = (probs * (grad_probs - delta[..., None])).astype(jnp.bfloat16)
        grad_query = (
            grad_query
            + jnp.einsum("hqk,khd->qhd", grad_scores, key_block, preferred_element_type=jnp.float32)
            * scale
        )
        grad_key = (
            jnp.einsum("hqk,qhd->khd", grad_scores, query_heads, preferred_element_type=jnp.float32)
            * scale
        )
        grad_val = jnp.einsum(
            "hqk,qhd->khd",
            probs.astype(jnp.bfloat16),
            grad_heads,
            preferred_element_type=jnp.float32,
        )
        return (grad_query, (grad_key, grad_val))

    grad_query, (grad_keys, grad_vals) = lax.scan(
        grad_step, jnp.zeros((tok_count, HEADS, HEAD), jnp.float32), block_ids
    )
    grad_key_own, grad_val_own = (
        lax.psum_scatter(
            grad_keys.reshape(full_rows, width), "ctx", scatter_dimension=0, tiled=True
        ),
        lax.psum_scatter(
            grad_vals.reshape(full_rows, width), "ctx", scatter_dimension=0, tiled=True
        ),
    )
    grad_qkv_low = jnp.concatenate(
        [grad_query.reshape(tok_count, width), grad_key_own, grad_val_own], axis=1
    ).astype(jnp.bfloat16)
    grad_qkv_part = contract_rows(tok_rows, grad_qkv_low)
    grad_tokens = grad_hidden + contract_cols(grad_qkv_low, qkv_full)
    dense = (
        lax.psum_scatter(grad_qkv_part, "fsdp", scatter_dimension=0, tiled=True),
        lax.psum_scatter(grad_out_part, "fsdp", scatter_dimension=0, tiled=True),
        lax.psum_scatter(grad_router_part, "fsdp", scatter_dimension=0, tiled=True),
        lax.psum_scatter(grad_gain_part, "fsdp", scatter_dimension=0, tiled=True),
        lax.psum_scatter(grad_bias_part, "fsdp", scatter_dimension=0, tiled=True),
    )
    totals = lax.psum(
        (dense[0], dense[1], dense[2], dense[3], dense[4], grad_up_own, grad_down_own), "ctx"
    )
    return (
        layer_out[None],
        grad_tokens[None],
        totals[0],
        totals[1],
        totals[2],
        totals[3],
        totals[4],
        totals[5],
        totals[6],
    )


def cost(microseconds):
    return pl.CostEstimate(flops=int(microseconds * 1.15e9), bytes_accessed=1 << 20, transcendentals=0)


LOG2E = 1.4426950408889634
HIDE = -1e30
RUN = 1024
HALF = 512
VMEM = pl.BlockSpec(memory_space=pltpu.VMEM)
SMEM = pl.BlockSpec(memory_space=pltpu.SMEM)
ANY = pl.BlockSpec(memory_space=pl.ANY)
LIMIT = 60 << 20


def dot_nn(left, right):
    return lax.dot_general(left, right, (((1,), (0,)), ((), ())), preferred_element_type=jnp.float32)


def dot_nt(left, right):
    return lax.dot_general(left, right, (((1,), (1,)), ((), ())), preferred_element_type=jnp.float32)


def dot_tn(left, right):
    return lax.dot_general(left, right, (((0,), (0,)), ((), ())), preferred_element_type=jnp.float32)


def split3(value):
    one = value.astype(jnp.bfloat16)
    rest = value - one.astype(jnp.float32)
    two = rest.astype(jnp.bfloat16)
    three = (rest - two.astype(jnp.float32)).astype(jnp.bfloat16)
    return one, two, three


def span(index, size, width=None):
    return pl.ds(pl.multiple_of(index * size, size), size if width is None else width)


MESH = pl.DeviceIdType.MESH


def flip(index, bit):
    return index + bit - 2 * bit * lax.rem(index // bit, 2)


def meet(devices):
    barrier = pltpu.get_barrier_semaphore()
    for device in devices:
        pl.semaphore_signal(barrier, inc=1, device_id=device, device_id_type=MESH)
    pl.semaphore_wait(barrier, len(devices))


def push(src, dst, send_sem, recv_sem, device):
    return pltpu.make_async_remote_copy(
        src_ref=src, dst_ref=dst, send_sem=send_sem, recv_sem=recv_sem, device_id=device, device_id_type=MESH
    )


def norm_parts(hidden):
    center = hidden - jnp.mean(hidden, axis=-1, keepdims=True)
    inv_dev = lax.rsqrt(jnp.mean(center * center, axis=-1, keepdims=True) + epsilon)
    return center * inv_dev, inv_dev


def gelu_parts(value):
    square = value * value
    tangent = jnp.tanh(value * (square * (gelu_coef * gelu_cubic) + gelu_coef))
    half = 0.5 * tangent + 0.5
    rise = value * (square * (3.0 * gelu_coef * gelu_cubic) + gelu_coef)
    return value * half, half + half * (1.0 - tangent) * rise


def boundaries(seg_ref, lane):
    segs = seg_ref[...]
    begin = jnp.zeros(lane.shape, jnp.int32)
    end = jnp.zeros(lane.shape, jnp.int32)
    for c in range(1, 10):
        total = jnp.sum((segs < c).astype(jnp.int32), axis=1, keepdims=True)
        begin = jnp.where(lane == HEAD - 1 + c, total, begin)
        end = jnp.where(lane == HEAD - 2 + c, total, end)
    return begin, jnp.where(lane == HEAD + 8, 0, end)


def layer_body(
    experts, groups, blocks, table_ref, gid_ref, seg_ref, tok_ref, cot_ref, wq_ref, wo_ref, router_ref, gain_ref, bias_ref, up_ref, down_ref,
    gq_ref, out_ref, sums_ref, layer_ref, gtok_ref, act_ref, gpre_ref, all_ref, toks_ref,
    tok, cot, head_buf, pack_buf, heads, wo, pack, zparts, att_send, att, msend, zin, bsend, bin_, up, down, qf, kf, vf, stat, held, late_held,
    ghead_out, ghead, wide_out, ghidden, dof, qt, dot, dk_acc, dv_acc, head_acc, send, landing, weight, zsend, zone, total, totals,
    out_mine, out_zone, out_sum, out_part, out_own, out_all,
    load_sem, own_sem, t_send, t_recv, d_recv, n_send, n_recv, y_send, y_recv, a_send, a_recv, m_send, m_recv, b_send, b_recv,
    h_send, h_recv, s_send, s_recv, z_send, z_recv, c_send, c_recv, o_send, o_recv, g_send, g_recv, r_send, r_recv, w_send, w_recv,
    v_send, v_recv,
):
    me, z = lax.axis_index("ctx"), lax.axis_index("fsdp")
    count, block_len = blocks // 2, tok_ref.shape[0] // 2
    own_rows, width = tok_ref.shape
    owners, own_experts, ffn = msend.shape[0], up_ref.shape[0], up_ref.shape[2]
    flat, per = experts * groups, experts * groups // owners
    rows = blocks * block_len
    runs = rows // RUN
    low = jnp.bfloat16
    dq_acc, qk, dv_rows, sorted_dv = stat, qf, vf, ghead_out

    def start(copies):
        for copy in copies:
            copy.start()
        return copies

    def wait(copies):
        for copy in copies:
            copy.wait()

    loads = []
    for e in range(own_experts):
        loads += [pltpu.make_async_copy(up_ref.at[e], up.at[e], load_sem.at[2 * e])]
        loads += [pltpu.make_async_copy(down_ref.at[e], down.at[e], load_sem.at[2 * e + 1])]
    start(loads)

    def mask(condition):
        return jnp.broadcast_to(jnp.where(condition, 1.0, 0.0), (1, 2 * HEAD))

    lows = [jnp.minimum(table_ref[2 * c], table_ref[2 * c + 1]) for c in range(count)]
    holds = [[mask(lows[c] == j).astype(low) for j in range(count)] for c in range(count)]
    in_order = mask(table_ref[2 * me] < table_ref[2 * me + 1])[:, :1]

    def blend(masks, values):
        out = None
        for weigh, value in zip(masks, values):
            out = weigh * value if out is None else out + weigh * value
        return out

    def ordered(first, second, weigh):
        return weigh * first + (1 - weigh) * second, weigh * second + (1 - weigh) * first

    tok[:block_len, :], tok[block_len:, :] = ordered(tok_ref[:block_len, :], tok_ref[block_len:, :], in_order.astype(low))
    cot[:block_len, :], cot[block_len:, :] = ordered(cot_ref[:block_len, :], cot_ref[block_len:, :], in_order.astype(low))

    sib, xn, yn, diag = flip(me, 1), flip(me, 2), flip(me, 4), flip(flip(me, 2), 4)
    same_core = [xn, yn, diag]
    z_peers = [(me, lax.rem(z + k, owners)) for k in range(1, owners)]
    c_peers = [(jnp.bitwise_xor(me, k), z) for k in range(1, count)]
    meet(z_peers + c_peers)

    piece = block_len // 2
    per_slot = RUN // block_len

    def place(device, half):
        return 2 * half + device // per_slot, lax.rem(device, per_slot) * block_len

    def there(device, half, k):
        slot, at = place(device, half)
        return held.at[slot, pl.ds(pl.multiple_of(at + k * piece, piece), piece)]

    gone = []

    def go(copies):
        gone.extend(start(copies))

    def here(half, k):
        return tok.at[pl.ds(half * block_len + k * piece, piece)]

    def launch(half):
        slot, at = place(me, half)
        held[slot, pl.ds(pl.multiple_of(at, block_len), block_len), :] = tok[half * block_len:(half + 1) * block_len, :]
        for k in (0, 1):
            go([push(here(half, k), there(me, half, k), t_send.at[half, 0, k], t_recv.at[half, 0, k], (xn, z))])
            go([push(here(half, 1 - k), there(me, half, 1 - k), t_send.at[half, 1, 1 - k], t_recv.at[half, 1, 1 - k], (yn, z))])

    def launch_near(half):
        for k in (0, 1):
            go([push(here(half, k), there(me, half, k), n_send.at[half, 0, k], n_recv.at[half, 0, k], (sib, z))])

    def arrived(device, half, k, sem):
        push(there(device, half, k), there(device, half, k), t_send.at[half, 0, 0], sem, (sib, z)).wait_recv()

    def relay(device, half, k, i):
        block = there(device, half, k)
        go([push(block, block, n_send.at[half, i, k], n_recv.at[half, i, k], (sib, z))])

    def forward(half):
        for device, k, i, to in ((xn, 0, 0, yn), (yn, 1, 1, xn)):
            arrived(device, half, k, t_recv.at[half, i, k])
            block = there(device, half, k)
            go([push(block, block, t_send.at[half, 2, k], d_recv.at[half, k], (to, z))])
            relay(device, half, k, i + 1)

    def settle(half):
        arrived(xn, half, 1, t_recv.at[half, 0, 1])
        relay(xn, half, 1, 1)
        arrived(yn, half, 0, t_recv.at[half, 1, 0])
        relay(yn, half, 0, 2)
        for k in (0, 1):
            arrived(diag, half, k, d_recv.at[half, k])
            relay(diag, half, k, 3)
        for k in (0, 1):
            for i, device in enumerate((sib, flip(xn, 1), flip(yn, 1), flip(diag, 1))):
                arrived(device, half, k, n_recv.at[half, i, k])

    launch(0)

    shared = []

    def share(i, shard, whole):
        whole[z] = shard[...]
        shared.append(start([push(shard, whole.at[z], y_send.at[i, k], y_recv.at[i, k], d) for k, d in enumerate(z_peers)]))

    for h in range(count):
        @pl.when(me == h)
        def _():
            cols = [wq_ref[:, width * kind + HEAD * h:width * kind + HEAD * (h + 1)] for kind in range(3)]
            head_buf[...] = jnp.concatenate(cols, axis=1)

    share(0, head_buf, heads)
    launch_near(0)
    parts = [router_ref[...].astype(jnp.float32), gain_ref[...].astype(jnp.float32), bias_ref[...].astype(jnp.float32)]
    parts.append(jnp.zeros((pack_buf.shape[0] - experts - 2, pack_buf.shape[1]), jnp.float32))
    pack_buf[...] = jnp.concatenate(parts, axis=0).astype(low)
    share(1, pack_buf, pack)
    share(2, wo_ref, wo)
    depth = wq_ref.shape[0] // count
    share(3, wq_ref.at[pl.ds(pl.multiple_of(me * depth, depth), depth)], zparts)

    lane = lax.broadcasted_iota(jnp.int32, (1, 2 * HEAD), 1)
    begin, end = boundaries(seg_ref, lane)
    is_flag = (lane >= HEAD) & (lane < HEAD + 8)
    is_one = (lane >= HEAD + 8) & (lane < HEAD + 11)
    ones_v = ((lane >= HEAD) & (lane < HEAD + 3)).astype(jnp.float32)
    scale = HEAD ** (-0.5)

    def projected(half, device):
        at = device % per_slot * block_len
        lanes = device // per_slot * 4 * HEAD
        return held.at[4 + half, at:at + block_len, lanes:lanes + 4 * HEAD]

    def project(half, head_weight):
        for device in range(count):
            slot, at = divmod(device * block_len, RUN)
            projected(half, device)[...] = dot_nn(held[2 * half + slot, at:at + block_len, :], head_weight).astype(low)
        for j in range(count):
            s = j if half == 0 else blocks - 1 - j
            masks = [holds[c][j] for c in range(count)]
            both = blend(masks, [projected(half, c)[:, :2 * HEAD] for c in range(count)]).astype(jnp.float32)
            value = blend(masks, [projected(half, c)[:, 2 * HEAD:] for c in range(count)]).astype(jnp.float32)
            spot = lax.broadcasted_iota(jnp.int32, (block_len, 2 * HEAD), 0) + s * block_len
            mine = (spot >= begin) & (spot < end)
            at = slice(s * block_len, (s + 1) * block_len)
            flag_q = jnp.where(is_flag & jnp.logical_not(mine), 1.0, 0.0)
            flag_k = jnp.where(mine, HIDE, jnp.where(is_one, 1.0, 0.0))
            qf[at, :] = jnp.where(lane < HEAD, both, flag_q).astype(low)
            kf[at, :] = jnp.where(lane < HEAD, pltpu.roll(both, HEAD, 1), flag_k).astype(low)
            vf[at, :] = (value + ones_v).astype(low)
            dot[:, at] = value.T.astype(low)[:HEAD]

    lower = lax.broadcasted_iota(jnp.int32, (HALF, HALF), 0) <= lax.broadcasted_iota(jnp.int32, (HALF, HALF), 1)

    def query_run(run):
        def tile(state, q_at, k_at, size, diagonal):
            scores = dot_nt(kf[k_at, :], qf[q_at, :]) * (scale * LOG2E)
            if diagonal:
                scores = jnp.where(lower, scores, HIDE)
            top, acc = state
            new_top = jnp.maximum(top, jnp.max(scores, axis=0, keepdims=True))
            probs = jnp.exp2(scores - new_top).astype(low)
            values = jnp.concatenate([dot[:, k_at], jnp.ones((HEAD, size), low)], axis=0)
            return new_top, acc * jnp.exp2(top - new_top) + dot_nn(values, probs)

        begin = (jnp.full((1, RUN), HIDE, jnp.float32), jnp.zeros((2 * HEAD, RUN), jnp.float32))
        def both_halves(n, state):
            for part in range(2):
                state = tile(state, span(run, RUN), span(2 * n + part, HALF), HALF, False)
            return state

        whole = lax.fori_loop(0, run, both_halves, begin)
        early, late = span(2 * run, HALF), span(2 * run + 1, HALF)
        first = tile([part[:, :HALF] for part in whole], early, early, HALF, True)
        second = tile([part[:, HALF:] for part in whole], late, early, HALF, False)
        second = tile(second, late, late, HALF, True)
        for at, (top, acc) in ((early, first), (late, second)):
            sums = acc[HEAD:]
            result = jnp.concatenate([acc[:HEAD] / sums, top + jnp.log2(sums)], axis=0).T
            stat[at, :] = result
            one, two, three = split3(result * (-1.0 / (scale * LOG2E)))
            old = qf[at, :]
            old = jnp.where(lane == HEAD + 8, one, old)
            old = jnp.where(lane == HEAD + 9, two, old)
            qf[at, :] = jnp.where(lane == HEAD + 10, three, old)

    def send_attended(half):
        mid = block_len // 2
        for c in range(count):
            ats = [slice(s * block_len, (s + 1) * block_len) for s in (range(count) if half == 0 else range(blocks - 1, count - 1, -1))]
            block = blend(holds[c], [stat[at, :].astype(low) for at in ats])
            att_send[half, c] = jnp.concatenate([block[:mid, :HEAD], block[mid:, :HEAD]], axis=1)
        att[half, me] = att_send[half, me]
        return start([
            push(att_send.at[half, d[0]], att.at[half, me], a_send.at[half, k], a_recv.at[half, k], d) for k, d in enumerate(c_peers)
        ])

    forward(0)
    settle(0)
    launch(1)
    launch_near(1)
    wait(shared[0])
    head_weight = heads[...].reshape(width, 3 * HEAD)
    head_weight = jnp.concatenate([head_weight, jnp.zeros((width, HEAD), low)], axis=1)
    project(0, head_weight)

    @pl.loop(0, 1)
    def _(run):
        query_run(run)

    forward(1)

    @pl.loop(1, runs // 2)
    def _(run):
        query_run(run)

    swap = send_attended(0)
    settle(1)
    saves = start([pltpu.make_async_copy(held.at[i], toks_ref.at[i], own_sem.at[3 + i]) for i in range(rows // RUN)])
    project(1, head_weight)

    @pl.loop(runs // 2, runs)
    def _(run):
        query_run(run)

    swap += send_attended(1)
    for copy in gone:
        copy.wait_send()
    wait(shared[1] + shared[2] + shared[3])

    first_diagonal = runs * (runs - 1)

    def slot_of(run, index, part):
        return run * (2 * runs - 1 - run) + 2 * (index - run - 1) + part

    def probabilities(q_at, k_at, visible):
        scores = dot_nt(qf[q_at, :], kf[k_at, :]) * (scale * LOG2E)
        if visible is not None:
            scores = jnp.where(visible, scores, HIDE)
        return jnp.exp2(scores).astype(low)

    def hold_diagonal():
        early = lax.broadcasted_iota(jnp.int32, (RUN, HALF), 1) <= lax.broadcasted_iota(jnp.int32, (RUN, HALF), 0)
        late = lax.broadcasted_iota(jnp.int32, (HALF, HALF), 1) <= lax.broadcasted_iota(jnp.int32, (HALF, HALF), 0)

        @pl.loop(0, runs)
        def _(run):
            held[first_diagonal + run] = probabilities(span(run, RUN), span(2 * run, HALF), early)
            late_held[run] = probabilities(span(2 * run + 1, HALF), span(2 * run + 1, HALF), late)

    def hold(run):
        @pl.loop(run + 1, runs)
        def _(index):
            for part in range(2):
                held[slot_of(run, index, part)] = probabilities(span(index, RUN), span(2 * run + part, HALF), None)

    hold_diagonal()

    @pl.loop(1, runs - 1)
    def _(run):
        hold(run)

    wait(swap)
    weights = start([push(zparts, weight.at[:, me], w_send.at[k], w_recv.at[k], (d, z)) for k, d in enumerate(same_core)])
    shares = start([push(zparts, weight.at[:, me], v_send.at[3], v_recv.at[3], (sib, z))])
    weight[:, me] = zparts[...]
    quarters = [
        jnp.concatenate([att[half, h, :, HEAD * p:HEAD * (p + 1)] for h in range(count)], axis=1) for half in range(2) for p in range(2)
    ]
    attended = jnp.concatenate(quarters, axis=0)
    out_weight = wo[...].reshape(width, width)
    hidden = tok[...].astype(jnp.float32) + dot_nn(attended, out_weight)
    unit, inv_dev = norm_parts(hidden)
    small_in = jnp.concatenate([pack[k] for k in range(owners)], axis=1)
    gain, bias = small_in[experts:experts + 1].astype(jnp.float32), small_in[experts + 1:experts + 2].astype(jnp.float32)
    normed = (unit * gain + bias).astype(low)
    expo = jnp.exp(dot_nt(small_in, normed)[:experts])
    expo = jnp.broadcast_to(expo[:, None, :], (experts, groups, own_rows)).reshape(flat, own_rows)
    gids = lax.rem(gid_ref[...], groups).astype(jnp.float32)
    gids = jnp.concatenate(ordered(gids[:, :block_len], gids[:, block_len:], in_order), axis=1)
    member = lax.rem(lax.broadcasted_iota(jnp.int32, (flat, 1), 0), groups).astype(jnp.float32) == gids
    expo = jnp.where(member, expo, 0.0)
    mix = expo / jnp.sum(expo, axis=1, keepdims=True)
    mix_low = mix.astype(low)

    def zone_rows(owner, kind):
        return pl.ds(pl.multiple_of((2 * owner + kind) * per, per), per)

    def to_owners(kind, value):
        msend[:, kind] = value.astype(low).reshape(owners, per, width)
        zin[zone_rows(z, kind), :] = msend[z, kind]
        return start([
            push(msend.at[d[1], kind], zin.at[zone_rows(z, kind)], m_send.at[kind, k], m_recv.at[kind, k], d) for k, d in enumerate(z_peers)
        ])

    mixed_copies = to_owners(0, dot_nn(mix_low, normed))
    grad_experts = dot_nn(mix_low, cot[...])
    wait(loads)
    wait(mixed_copies)
    grad_copies = to_owners(1, grad_experts)

    def from_sources(kind, e):
        lows_ = [(2 * owner + kind) * per + e * groups for owner in range(owners)]
        return jnp.concatenate([zin[at:at + groups, :] for at in lows_], axis=0)

    def to_sources(kind, e, value):
        bsend[:, kind, e * groups:(e + 1) * groups, :] = value.astype(low).reshape(owners, groups, width)

    def send_back(kind):
        bin_[z, kind] = bsend[z, kind]
        return start([
            push(bsend.at[d[1], kind], bin_.at[z, kind], b_send.at[kind, k], b_recv.at[kind, k], d) for k, d in enumerate(z_peers)
        ])

    slopes = []
    for e in range(own_experts):
        active, slope = gelu_parts(dot_nn(from_sources(0, e), up[e]))
        slopes.append(slope)
        to_sources(0, e, dot_nn(active.astype(low), down[e]))
    out_copies = send_back(0)
    wait(grad_copies)
    gathers = start([push(zin, all_ref.at[me], g_send.at[k], g_recv.at[k], (d, z)) for k, d in enumerate(same_core)])
    relays = start([push(zin, all_ref.at[me], r_send.at[3], r_recv.at[3], (sib, z))])
    own_got = start([pltpu.make_async_copy(zin, all_ref.at[me], own_sem.at[1])])
    for e in range(own_experts):
        grad_pre = (dot_nt(from_sources(1, e), down[e]) * slopes[e]).astype(low)
        to_sources(1, e, dot_nt(grad_pre, up[e]))
    back_copies = send_back(1)
    wait(out_copies)
    expert_out = bin_[:, 0].reshape(flat, width)
    result = hidden + dot_tn(mix_low, expert_out)
    wide_out[:block_len, :], wide_out[block_len:, :] = ordered(result[:block_len], result[block_len:], in_order)
    layer_copy = start([pltpu.make_async_copy(wide_out, layer_ref, own_sem.at[2])])
    grad_mix = dot_nt(expert_out, cot[...])
    wait(back_copies)
    grad_mixed = bin_[:, 1].reshape(flat, width)
    product = mix * (grad_mix + dot_nt(grad_mixed, normed))
    grad_logits = product - mix * jnp.sum(product, axis=1, keepdims=True)
    grad_logits = jnp.sum(grad_logits.reshape(experts, groups, own_rows), axis=1).astype(low)
    pad = jnp.zeros((small_in.shape[0] - experts, own_rows), low)
    grad_logits = jnp.concatenate([grad_logits, pad], axis=0)
    grad_normed = dot_tn(jnp.concatenate([mix_low, grad_logits], axis=0), jnp.concatenate([grad_mixed, small_in], axis=0))
    scaled = grad_normed * gain
    mean = jnp.mean(scaled, axis=-1, keepdims=True)
    grad_hidden = cot[...].astype(jnp.float32) + inv_dev * (scaled - mean - unit * jnp.mean(scaled * unit, axis=-1, keepdims=True))
    branch = grad_hidden.astype(low)
    grad_heads = dot_nt(branch, out_weight).astype(low)
    for h in range(count):
        at = slice(HEAD * h, HEAD * (h + 1))
        ghead_out[h] = jnp.concatenate([grad_heads[:block_len, at], grad_heads[block_len:, at]], axis=1)
    swap = start([push(ghead_out.at[d[0]], ghead.at[me], h_send.at[k], h_recv.at[k], d) for k, d in enumerate(c_peers)])
    ghead[me] = ghead_out[me]
    ghidden[...] = grad_hidden
    out_mine[...] = dot_tn(attended, branch).astype(low).reshape(out_mine.shape)
    gout_copies = start([push(out_mine.at[d[1]], out_zone.at[z], o_send.at[0, k], o_recv.at[0, k], d) for k, d in enumerate(z_peers)])
    out_zone[z] = out_mine[z]
    small = jnp.concatenate(
        [
            dot_nn(grad_logits, normed)[:experts],
            jnp.sum(grad_normed * unit, axis=0, keepdims=True),
            jnp.sum(grad_normed, axis=0, keepdims=True),
            jnp.zeros((small_in.shape[0] - experts - 2, width), jnp.float32),
        ],
        axis=0,
    )
    lanes = width // owners
    for c in range(owners):
        zsend[c, 3 * HEAD:, :] = small[:, c * lanes:(c + 1) * lanes].astype(low)
    wait(saves)
    hold(0)

    def prepare(s, both):
        at = slice(s * block_len, (s + 1) * block_len)
        grad = jnp.where(lane < HEAD, both, 0.0)
        delta = jnp.sum(grad * stat[at, :], axis=1, keepdims=True)
        one, two, three = split3(jnp.broadcast_to(-delta, grad.shape))
        wide = jnp.where(lane == HEAD, one, grad.astype(low))
        wide = jnp.where(lane == HEAD + 1, two, wide)
        dof[at, :] = jnp.where(lane == HEAD + 2, three, wide)
        turned = jnp.where(lane < HEAD, both, pltpu.roll(qf[at, :].astype(jnp.float32), HEAD, 1)).T.astype(low)
        dot[:, at] = turned[:HEAD]
        qt[:, at] = turned[HEAD:]

    wait(swap)
    for j in range(count):
        both = blend([holds[c][j] for c in range(count)], [ghead[c] for c in range(count)]).astype(jnp.float32)
        prepare(j, both)
        prepare(blocks - 1 - j, pltpu.roll(both, HEAD, 1))

    tok_loads = [
        pltpu.make_async_copy(toks_ref.at[i], held.at[i], own_sem.at[3 + i]) for i in range(rows // RUN)
    ]

    def key_run(run):
        def tile(q_at, k_at, part, probs, first_k, first_q):
            slope = dot_nt(dof[q_at, :], vf[k_at, :])
            grad = (probs.astype(jnp.float32) * slope).astype(low)
            dv = dot_nn(dot[:, q_at], probs)
            dk = dot_nn(qt[:, q_at], grad)
            dq = dot_nn(grad, kf[k_at, :])
            at = slice(part * HALF, (part + 1) * HALF)
            if first_k:
                dv_acc[:, at] = dv
                dk_acc[:, at] = dk
            else:
                dv_acc[:, at] += dv
                dk_acc[:, at] += dk
            if first_q:
                @pl.when(run == 0)
                def _():
                    dq_acc[q_at, :] = dq

                @pl.when(run != 0)
                def _():
                    dq_acc[q_at, :] += dq
            else:
                dq_acc[q_at, :] += dq

        early, late = span(2 * run, HALF), span(2 * run + 1, HALF)
        tile(span(run, RUN), early, 0, held[first_diagonal + run], True, True)
        tile(late, late, 1, late_held[run], True, False)

        @pl.loop(run + 1, runs)
        def _(index):
            for part in range(2):
                tile(span(index, RUN), span(2 * run + part, HALF), part, held[slot_of(run, index, part)], False, part == 0)

        at = span(run, RUN)
        both = jnp.concatenate([dk_acc[...] * scale, dv_acc[...]], axis=0).T
        query = dq_acc[at, :] * scale
        qk[at, :] = jnp.where(lane < HEAD, query, pltpu.roll(both, HEAD, 1)).astype(low)
        dv_rows[at, :] = both.astype(low)

    def send_half(half):
        mid = block_len // 2
        for c in range(count):
            ats = [slice(s * block_len, (s + 1) * block_len) for s in (range(count) if half == 0 else range(blocks - 1, count - 1, -1))]
            send[half, c, :block_len, :] = blend(holds[c], [qk[at, :] for at in ats])
            values = blend(holds[c], [dv_rows[at, :] for at in ats])
            sorted_dv[c] = values
            values = values[:, HEAD:]
            send[half, c, block_len:, :] = jnp.concatenate([values[:mid], values[mid:]], axis=1)
        landing[half, me] = send[half, me]
        return start([
            push(send.at[half, d[0]], landing.at[half, me], s_send.at[half, k], s_recv.at[half, k], d) for k, d in enumerate(c_peers)
        ])

    def head_weights(half):
        first, second = None, None
        for c in range(count):
            slot, at = divmod(c * block_len, RUN)
            here = held[2 * half + slot, at:at + block_len, :]
            one, two = dot_tn(send[half, c, :block_len, :], here), dot_tn(sorted_dv[c], here)
            first, second = (one, two) if first is None else (first + one, second + two)
        both = jnp.concatenate([first, second[HEAD:]], axis=0)
        if half == 0:
            head_acc[...] = both
        else:
            head_acc[...] += both

    @pl.loop(0, runs // 2)
    def _(run):
        key_run(run)

        @pl.when(run == 0)
        def _():
            start(tok_loads)

    swaps = send_half(0)
    for k, d in enumerate(same_core):
        gathers[k].wait_recv()
        relays += start([push(all_ref.at[d], all_ref.at[d], r_send.at[k], r_recv.at[k], (sib, z))])
        weights[k].wait_recv()
        shares += start([push(weight.at[:, d], weight.at[:, d], v_send.at[k], v_recv.at[k], (sib, z))])
    wait(gout_copies)
    summed = out_zone[0].astype(jnp.float32)
    for k in range(1, owners):
        summed = summed + out_zone[k].astype(jnp.float32)
    out_sum[...] = summed.astype(low).reshape(out_sum.shape)
    part_copies = start([push(out_sum.at[d[0]], out_part.at[me], o_send.at[1, k], o_recv.at[1, k], d) for k, d in enumerate(c_peers)])
    out_part[me] = out_sum[me]
    wait(tok_loads)
    head_weights(0)

    @pl.loop(runs // 2, runs)
    def _(run):
        key_run(run)

    swaps += send_half(1)
    wait(part_copies)
    summed = out_part[0].astype(jnp.float32)
    for k in range(1, count):
        summed = summed + out_part[k].astype(jnp.float32)
    out_own[...] = summed.astype(low)
    last_copies = start([push(out_own, out_all.at[me], o_send.at[2, k], o_recv.at[2, k], d) for k, d in enumerate(c_peers)])
    out_all[me] = out_own[...]
    wait(own_got + relays)

    mixed_slot = rows // RUN
    share = owners * 2 * per
    mixed_loads = []
    for c in range(count):
        slot, at = divmod(c * share, RUN)
        mixed_loads.append(pltpu.make_async_copy(all_ref.at[c], held.at[mixed_slot + slot, pl.ds(at, share)], own_sem.at[3 + rows // RUN + c]))
    start(mixed_loads)
    head_weights(1)
    for c in range(owners):
        zsend[c, :3 * HEAD, :] = head_acc[:, c * lanes:(c + 1) * lanes].astype(low)
    z_copies = start([push(zsend.at[d[1]], zone.at[z], z_send.at[k], z_recv.at[k], d) for k, d in enumerate(z_peers)])
    zone[z] = zsend[z]
    wait(mixed_loads)
    step = HALF
    chunks = ffn // step
    wide_slot = mixed_slot + count * share // RUN

    def of_expert(kind, e):
        parts = []
        for slot in range(mixed_slot, wide_slot):
            value = held[slot].reshape(RUN // share, owners, 2, own_experts, groups, width)
            parts.append(value[:, :, kind, e].reshape(-1, width))
        return jnp.concatenate(parts, axis=0)

    def expert_part(e):
        mixed, grad_out = of_expert(0, e), of_expert(1, e)
        copies = []

        @pl.loop(0, chunks // 2)
        def _(i):
            for part in range(2):
                at = span(2 * i + part, step)
                to = pl.ds(part * step, step)
                active, slope = gelu_parts(dot_nn(mixed, up[e, :, at]))
                held[wide_slot + chunks * e + i, to, :] = active.astype(low)
                slot = wide_slot + chunks * e + chunks // 2 + i
                held[slot, to, :] = (dot_nt(grad_out, down[e, at, :]) * slope).astype(low)

        for i in range(chunks):
            slot = wide_slot + chunks * e + i // 2
            at, to = pl.ds(i * step, step), pl.ds(i % 2 * step, step)
            sem = own_sem.at[3 + rows // RUN + count + 2 * (chunks * e + i)]
            copies.append(pltpu.make_async_copy(held.at[slot, to], act_ref.at[e, :, at], sem))
            sem = own_sem.at[4 + rows // RUN + count + 2 * (chunks * e + i)]
            copies.append(pltpu.make_async_copy(held.at[slot + chunks // 2, to], gpre_ref.at[e, :, at], sem))
        return start(copies)

    stores = expert_part(0)
    wait(z_copies)
    summed = zone[0].astype(jnp.float32)
    for k in range(1, owners):
        summed = summed + zone[k].astype(jnp.float32)
    total[...] = summed.astype(low)
    c_copies = start([push(total, totals.at[me], c_send.at[k], c_recv.at[k], d) for k, d in enumerate(c_peers)])
    totals[me] = total[...]
    for e in range(1, own_experts):
        stores += expert_part(e)
    wait(swaps + shares)
    flat_weight = weight[...].reshape(width, -1)
    parts = []
    for half in range(2):
        queries, keys, values = [], [], []
        for h in range(count):
            front, back = landing[half, h, :block_len, :], landing[half, h, block_len:, :]
            queries.append(front[:, :HEAD])
            keys.append(front[:, HEAD:])
            values.append(jnp.concatenate([back[:, :HEAD], back[:, HEAD:]], axis=0))
        parts.append(dot_nt(jnp.concatenate(queries + keys + values, axis=1), flat_weight))
    wait(layer_copy)
    first, second = ghidden[:block_len, :] + parts[0], ghidden[block_len:, :] + parts[1]
    wide_out[:block_len, :], wide_out[block_len:, :] = ordered(first, second, in_order)
    stores += start([pltpu.make_async_copy(wide_out, gtok_ref, own_sem.at[2])])
    wait(last_copies)
    out_ref[...] = out_all[...].astype(jnp.float32).reshape(out_ref.shape)
    wait(c_copies)
    small = None
    turned = []
    for c in range(count):
        turned.append(totals[c, :3 * HEAD, :].astype(jnp.float32).T)
        part = totals[c, 3 * HEAD:, :].astype(jnp.float32)
        small = part if small is None else small + part
    sums_ref[...] = small
    for kind in range(3):
        at = slice(HEAD * kind, HEAD * (kind + 1))
        gq_ref[:, HEAD * count * kind:HEAD * count * (kind + 1)] = jnp.concatenate([part[:, at] for part in turned], axis=1)
    wait(stores)
    for copy in gathers + weights:
        copy.wait_send()


def layer(table, gid_row, segs, tokens, cot, w_qkv, w_out, w_router, ln_gain, ln_bias, w_up, w_down, groups, count, owners):
    own_rows, width = tokens.shape
    experts = w_router.shape[1]
    blocks, block_len = table.shape[0], own_rows // 2
    rows = blocks * block_len
    runs = rows // RUN
    own_experts, _, ffn = w_up.shape
    lanes, wide_qkv = w_qkv.shape
    smalls = 16
    height = 3 * HEAD + smalls
    per = experts * groups // owners
    wide = (own_experts, count * owners * groups, ffn)
    share = (owners * 2 * per, width)
    part = (count, lanes // count, width)
    swap = (2, count, block_len + block_len // 2, 2 * HEAD)
    gout = (owners, lanes, width)
    sent = (owners, 2, per, width)
    attended = (2, count, block_len // 2, 2 * HEAD)
    head_grad = (count, block_len, 2 * HEAD)
    low, full = jnp.bfloat16, jnp.float32
    scratch = [
        (tokens.shape, low), (tokens.shape, low), ((lanes, 3 * HEAD), low), ((smalls, lanes), low), ((owners, lanes, 3 * HEAD), low),
        ((owners,) + w_out.shape, low), ((owners, smalls, lanes), low), ((owners, lanes // count, wide_qkv), low), (attended, low),
        (attended, low), (sent, low), (share, low), (sent, low), (sent, low), (w_up.shape, low), (w_down.shape, low),
        ((rows, 2 * HEAD), low), ((rows, 2 * HEAD), low), ((rows, 2 * HEAD), low), ((rows, 2 * HEAD), full),
        ((runs * runs, RUN, HALF), low), ((runs, HALF, HALF), low), (head_grad, low), (head_grad, low),
        (tokens.shape, full), (tokens.shape, full), ((rows, 2 * HEAD), low), ((HEAD, rows), low), ((HEAD, rows), low),
        ((HEAD, RUN), full), ((HEAD, RUN), full), ((3 * HEAD, width), full), (swap, low), (swap, low),
        ((owners, count, lanes // count, wide_qkv), low), ((owners, height, lanes), low), ((owners, height, lanes), low),
        ((height, lanes), low), ((count, height, lanes), low), (gout, low), (gout, low), (part, low), (part, low), (part[1:], low),
        (part, low),
    ]
    owns = 3 + rows // RUN + count + 2 * own_experts * (ffn // HALF)
    to_z, to_c = owners - 1, count - 1
    sems = [
        (2 * own_experts,), (owns,), (2, 3, 2), (2, 2, 2), (2, 2), (2, 4, 2), (2, 4, 2), (4, to_z), (4, to_z),
        (2, to_c), (2, to_c), (2, to_z), (2, to_z), (2, to_z), (2, to_z), (to_c,), (to_c,), (2, to_c), (2, to_c),
        (to_z,), (to_z,), (to_c,), (to_c,), (3, to_c), (3, to_c), (3,), (3,), (4,), (4,), (3,), (3,), (4,), (4,),
    ]
    return pl.pallas_call(
        functools.partial(layer_body, experts, groups, blocks),
        out_shape=(
            jax.ShapeDtypeStruct((lanes, 3 * width), full),
            jax.ShapeDtypeStruct((lanes, width), full),
            jax.ShapeDtypeStruct((smalls, lanes), full),
            jax.ShapeDtypeStruct(tokens.shape, full),
            jax.ShapeDtypeStruct(tokens.shape, full),
            jax.ShapeDtypeStruct(wide, low),
            jax.ShapeDtypeStruct(wide, low),
            jax.ShapeDtypeStruct((count,) + share, low),
            jax.ShapeDtypeStruct((rows // RUN, RUN, width), low),
        ),
        in_specs=[SMEM] + [VMEM] * 9 + [ANY] * 2,
        out_specs=(VMEM,) * 3 + (ANY,) * 6,
        scratch_shapes=[pltpu.VMEM(shape, dtype) for shape, dtype in scratch] + [pltpu.SemaphoreType.DMA(shape) for shape in sems],
        compiler_params=pltpu.CompilerParams(collective_id=1, has_side_effects=True, vmem_limit_bytes=LIMIT),
        cost_estimate=cost(130),
        name="layer",
    )(table, gid_row, segs, tokens, cot, w_qkv, w_out, w_router.T, ln_gain[None], ln_bias[None], w_up, w_down)


def expert_grad_body(experts, passed, mixed_ref, grad_ref, act_ref, gpre_ref, small_ref, *refs):
    sources, outs = refs[:passed], refs[passed + 5:]
    gup_ref, gdown_ref, router_ref, gain_ref, bias_ref = refs[passed:passed + 5]
    width = gup_ref.shape[1]
    for source, out in zip(sources, outs):
        out[...] = source[...]
    router_ref[...] = small_ref[:experts]
    gain_ref[...] = small_ref[experts:experts + 1]
    bias_ref[...] = small_ref[experts + 1:experts + 2]
    gup_ref[0] = dot_tn(mixed_ref[...].reshape(-1, width), gpre_ref[0])
    gdown_ref[0] = dot_tn(act_ref[0], grad_ref[...].reshape(-1, width))


def expert_grads(gathered, active, grad_pre, small, passed, groups, experts):
    own, rows, ffn = active.shape
    step = ffn
    steps = ffn // step
    sources, width = gathered.shape[0], gathered.shape[3]
    view = gathered.reshape(sources, 2, own, groups, width)
    lanes = small.shape[1]
    full = jnp.float32
    slices = [pl.BlockSpec((x.shape[0] // (own * steps), x.shape[1]), lambda e, f: (e * steps + f, 0)) for x in passed]
    return pl.pallas_call(
        functools.partial(expert_grad_body, experts, len(passed)),
        grid=(own, steps),
        out_shape=[
            jax.ShapeDtypeStruct((own, width, ffn), full), jax.ShapeDtypeStruct((own, ffn, width), full),
            jax.ShapeDtypeStruct((experts, lanes), full), jax.ShapeDtypeStruct((1, lanes), full), jax.ShapeDtypeStruct((1, lanes), full),
        ] + [jax.ShapeDtypeStruct(x.shape, x.dtype) for x in passed],
        in_specs=[
            pl.BlockSpec((sources, 1, 1, groups, width), lambda e, f: (0, 0, e, 0, 0)),
            pl.BlockSpec((sources, 1, 1, groups, width), lambda e, f: (0, 1, e, 0, 0)),
            pl.BlockSpec((1, rows, step), lambda e, f: (e, 0, f)),
            pl.BlockSpec((1, rows, step), lambda e, f: (e, 0, f)),
            pl.BlockSpec(small.shape, lambda e, f: (0, 0)),
        ] + slices,
        out_specs=[
            pl.BlockSpec((1, width, step), lambda e, f: (e, 0, f)), pl.BlockSpec((1, step, width), lambda e, f: (e, f, 0)),
            pl.BlockSpec((experts, lanes), lambda e, f: (0, 0)), pl.BlockSpec((1, lanes), lambda e, f: (0, 0)),
            pl.BlockSpec((1, lanes), lambda e, f: (0, 0)),
        ] + slices,
        compiler_params=pltpu.CompilerParams(vmem_limit_bytes=LIMIT),
        cost_estimate=cost(10),
        name="expert_grads",
    )(view, view, active, grad_pre, small, *passed)


def fast_device(
    tokens, cotangent, block_table, seg_ids, group_ids, w_qkv, w_out, w_router, ln_gain, ln_bias, w_up, w_down
):
    ctx_count, z_count = lax.axis_size("ctx"), lax.axis_size("fsdp")
    tok_rows, cot_rows = tokens[0], cotangent[0]
    rows, width = tok_rows.shape
    experts = w_router.shape[1]
    groups = rows // GROUP_SIZE
    grad_qkv, grad_out, small, layer_out, grad_tokens, active, grad_pre, gathered, unused = layer(
        block_table, group_ids, seg_ids, tok_rows, cot_rows, w_qkv, w_out, w_router, ln_gain, ln_bias, w_up, w_down, groups, ctx_count,
        z_count,
    )
    gathered = gathered.reshape(ctx_count * z_count, 2, experts * groups // z_count, width)
    grad_up, grad_down, grad_router, grad_gain, grad_bias, layer_out, grad_tokens, grad_qkv, grad_out = expert_grads(
        gathered, active, grad_pre, small, [layer_out, grad_tokens, grad_qkv, grad_out], groups, experts
    )
    return (
        layer_out[None],
        grad_tokens[None],
        grad_qkv,
        grad_out,
        grad_router.T,
        grad_gain[0],
        grad_bias[0],
        grad_up,
        grad_down,
    )


def solution(mesh):
    placed = (
        P("fsdp", "ctx", None),
        P("fsdp", "ctx", None),
        P(),
        P("fsdp", None),
        P("fsdp", "ctx"),
        P("fsdp", None),
        P("fsdp", None),
        P("fsdp", None),
        P("fsdp"),
        P("fsdp"),
        P("fsdp", None, None),
        P("fsdp", None, None),
    )
    step = fast_device if mesh.shape["ctx"] == HEADS else on_device
    return jax.shard_map(
        step,
        mesh=mesh,
        in_specs=placed,
        out_specs=(
            P("fsdp", "ctx", None),
            P("fsdp", "ctx", None),
            P("fsdp", None),
            P("fsdp", None),
            P("fsdp", None),
            P("fsdp"),
            P("fsdp"),
            P("fsdp", None, None),
            P("fsdp", None, None),
        ),
        check_vma=False,
    )
```

```python
import functools

import jax
import jax.numpy as jnp
from jax import lax
from jax.experimental import pallas as pl
from jax.experimental.pallas import tpu as pltpu
from jax.sharding import PartitionSpec as P

HEADS = 8
HEAD = 64
GROUP_SIZE = 32
KEY_BLOCK = 2048


highest = lax.Precision.HIGHEST
neg_large = -1e30
epsilon = 1e-05
gelu_coef = 0.7978845608028654
gelu_cubic = 0.044715


def contract_rows(left, right):
    return lax.dot_general(
        left, right, (((0,), (0,)), ((), ())), preferred_element_type=jnp.float32
    )


def contract_cols(left, right):
    return lax.dot_general(
        left, right, (((1,), (1,)), ((), ())), preferred_element_type=jnp.float32
    )


def gelu_slope(value):
    inner = gelu_coef * (value + gelu_cubic * value * value * value)
    tangent = jnp.tanh(inner)
    return 0.5 * (1.0 + tangent) + 0.5 * value * (1.0 - tangent * tangent) * gelu_coef * (
        1.0 + 3.0 * gelu_cubic * value * value
    )


def expert_forward(mixed_low, up_weight, down_weight):
    pre = jnp.einsum("ged,edh->geh", mixed_low, up_weight, preferred_element_type=jnp.float32)
    active = jax.nn.gelu(pre, approximate=True).astype(jnp.bfloat16)
    result = jnp.einsum("geh,ehd->ged", active, down_weight, preferred_element_type=jnp.float32)
    return (pre, active, result.astype(jnp.bfloat16))


def expert_backward(mixed_low, pre, active, grad_result, up_weight, down_weight):
    grad_act = jnp.einsum(
        "ged,ehd->geh", grad_result, down_weight, preferred_element_type=jnp.float32
    )
    grad_pre = (grad_act * gelu_slope(pre)).astype(jnp.bfloat16)
    grad_down_part = jnp.einsum(
        "geh,ged->ehd", active, grad_result, preferred_element_type=jnp.float32
    )
    grad_up_part = jnp.einsum(
        "ged,geh->edh", mixed_low, grad_pre, preferred_element_type=jnp.float32
    )
    grad_mixed = jnp.einsum("geh,edh->ged", grad_pre, up_weight, preferred_element_type=jnp.float32)
    return (grad_up_part, grad_down_part, grad_mixed.astype(jnp.bfloat16))


def on_device(
    tokens,
    cotangent,
    block_table,
    seg_ids,
    group_ids,
    w_qkv,
    w_out,
    w_router,
    ln_gain,
    ln_bias,
    w_up,
    w_down,
):
    tok_rows = tokens[0]
    tok_count = tok_rows.shape[0]
    width = tok_rows.shape[1]
    expert_count = w_router.shape[1]
    ctx_index = lax.axis_index("ctx")
    full_rows = seg_ids.shape[1]
    block_len = full_rows // block_table.shape[0]
    row_ids = jnp.arange(full_rows, dtype=jnp.int32)
    key_pos = jnp.take(block_table, row_ids // block_len) * block_len + row_ids % block_len
    key_seg = seg_ids[0]
    pos_rows = lax.dynamic_slice_in_dim(key_pos, ctx_index * tok_count, tok_count)
    seg_rows = lax.dynamic_slice_in_dim(key_seg, ctx_index * tok_count, tok_count)
    scale = HEAD ** (-0.5)
    qkv_full, out_full, router_full, gain_full, bias_full = (
        lax.all_gather(w_qkv, "fsdp", axis=0, tiled=True),
        lax.all_gather(w_out, "fsdp", axis=0, tiled=True),
        lax.all_gather(w_router, "fsdp", axis=0, tiled=True),
        lax.all_gather(ln_gain, "fsdp", axis=0, tiled=True),
        lax.all_gather(ln_bias, "fsdp", axis=0, tiled=True),
    )
    qkv = jnp.dot(tok_rows, qkv_full, preferred_element_type=jnp.float32).astype(jnp.bfloat16)
    query_heads = qkv[:, :width].reshape(tok_count, HEADS, HEAD)
    key_all, val_all = (
        lax.all_gather(qkv[:, width : 2 * width], "ctx", axis=0, tiled=True),
        lax.all_gather(qkv[:, 2 * width :], "ctx", axis=0, tiled=True),
    )
    key_heads = key_all.reshape(full_rows, HEADS, HEAD)
    val_heads = val_all.reshape(full_rows, HEADS, HEAD)
    block_count = full_rows // KEY_BLOCK
    block_ids = jnp.arange(block_count, dtype=jnp.int32)

    def block_scores(index):
        start = index * KEY_BLOCK
        key_block = lax.dynamic_slice_in_dim(key_heads, start, KEY_BLOCK, 0)
        val_block = lax.dynamic_slice_in_dim(val_heads, start, KEY_BLOCK, 0)
        pos_block = lax.dynamic_slice_in_dim(key_pos, start, KEY_BLOCK, 0)
        seg_block = lax.dynamic_slice_in_dim(key_seg, start, KEY_BLOCK, 0)
        scores = (
            jnp.einsum("qhd,khd->hqk", query_heads, key_block, preferred_element_type=jnp.float32)
            * scale
        )
        allowed = (pos_block[None, :] <= pos_rows[:, None]) & (
            (seg_block[None, :] == 0) | (seg_block[None, :] == seg_rows[:, None])
        )
        return (scores, allowed[None], key_block, val_block)

    def lse_step(carry, index):
        top, total = carry
        scores, allowed, key_block, val_block = block_scores(index)
        masked = jnp.where(allowed, scores, neg_large)
        new_top = jnp.maximum(top, jnp.max(masked, axis=-1))
        weights = jnp.where(allowed, jnp.exp(masked - new_top[..., None]), 0.0)
        return ((new_top, total * jnp.exp(top - new_top) + jnp.sum(weights, axis=-1)), None)

    start_top = jnp.full((HEADS, tok_count), neg_large, jnp.float32)
    (top, total), unused = lax.scan(
        lse_step, (start_top, jnp.zeros((HEADS, tok_count), jnp.float32)), block_ids
    )
    log_total = top + jnp.log(total)

    def block_probs(index):
        scores, allowed, key_block, val_block = block_scores(index)
        probs = jnp.where(allowed, jnp.exp(scores - log_total[..., None]), 0.0)
        return (probs, key_block, val_block)

    def value_step(accum, index):
        probs, key_block, val_block = block_probs(index)
        return (
            accum
            + jnp.einsum(
                "hqk,khd->qhd",
                probs.astype(jnp.bfloat16),
                val_block,
                preferred_element_type=jnp.float32,
            ),
            None,
        )

    accum, unused = lax.scan(
        value_step, jnp.zeros((tok_count, HEADS, HEAD), jnp.float32), block_ids
    )
    attended = accum.reshape(tok_count, width).astype(jnp.bfloat16)
    hidden = tok_rows.astype(jnp.float32) + jnp.dot(
        attended, out_full, preferred_element_type=jnp.float32
    )
    center = hidden - jnp.mean(hidden, axis=-1, keepdims=True)
    inv_dev = lax.rsqrt(jnp.mean(center * center, axis=-1, keepdims=True) + epsilon)
    unit = center * inv_dev
    gain_f = gain_full.astype(jnp.float32)
    normed_low = (unit * gain_f + bias_full.astype(jnp.float32)).astype(jnp.bfloat16)
    logits = jnp.dot(normed_low, router_full, preferred_element_type=jnp.float32)
    groups_dev = tok_count // GROUP_SIZE
    local_group = group_ids[0] - ctx_index * groups_dev
    member = (local_group[:, None] == jnp.arange(groups_dev, dtype=jnp.int32)[None, :]).astype(
        jnp.float32
    )
    expo = jnp.exp(logits)
    group_total = jnp.dot(member.T, expo, precision=highest)
    mix_weights = expo / jnp.dot(member, group_total, precision=highest)
    weights_low = mix_weights.astype(jnp.bfloat16)
    mixing = member.astype(jnp.bfloat16).T[:, None, :] * weights_low.T[None, :, :]
    mixing_flat = mixing.reshape(groups_dev * expert_count, tok_count)
    mixed_low = jnp.dot(mixing_flat, normed_low, preferred_element_type=jnp.float32).astype(
        jnp.bfloat16
    )
    mixed_low = mixed_low.reshape(groups_dev, expert_count, width)
    owner_mixed = lax.all_to_all(mixed_low, "fsdp", split_axis=1, concat_axis=0, tiled=True)
    pre, active, owner_out = expert_forward(owner_mixed, w_up, w_down)
    expert_out = lax.all_to_all(owner_out, "fsdp", split_axis=0, concat_axis=1, tiled=True)
    expert_flat = expert_out.reshape(groups_dev * expert_count, width)
    spread = contract_rows(mixing_flat, expert_flat)
    layer_out = hidden + spread
    cot_rows = cotangent[0]
    cot_f = cot_rows.astype(jnp.float32)
    grad_expert = jnp.dot(mixing_flat, cot_rows, preferred_element_type=jnp.float32).astype(
        jnp.bfloat16
    )
    grad_expert = grad_expert.reshape(groups_dev, expert_count, width)
    coef = contract_cols(cot_rows, expert_flat).reshape(tok_count, groups_dev, expert_count)
    grad_mix_spread = jnp.sum(coef * member[:, :, None], axis=1)
    owner_grad = lax.all_to_all(grad_expert, "fsdp", split_axis=1, concat_axis=0, tiled=True)
    grad_up_own, grad_down_own, owner_back = expert_backward(
        owner_mixed, pre, active, owner_grad, w_up, w_down
    )
    grad_mixed = lax.all_to_all(owner_back, "fsdp", split_axis=0, concat_axis=1, tiled=True)
    grad_mixed_flat = grad_mixed.reshape(groups_dev * expert_count, width)
    grad_norm_mix = contract_rows(mixing_flat, grad_mixed_flat)
    grad_mixing = contract_cols(grad_mixed_flat, normed_low).reshape(
        groups_dev, expert_count, tok_count
    )
    grad_mix_mixing = jnp.sum(grad_mixing * member.T[:, None, :], axis=0).T
    grad_mix = grad_mix_spread + grad_mix_mixing
    product = mix_weights * grad_mix
    token_dot = jnp.dot(member, jnp.dot(member.T, product, precision=highest), precision=highest)
    grad_logits = (product - mix_weights * token_dot).astype(jnp.bfloat16)
    grad_router_part = contract_rows(normed_low, grad_logits)
    grad_norm_router = contract_cols(grad_logits, router_full)
    grad_normed = grad_norm_mix + grad_norm_router
    grad_gain_part = jnp.sum(grad_normed * unit, axis=0)
    grad_bias_part = jnp.sum(grad_normed, axis=0)
    scaled = grad_normed * gain_f
    grad_hidden = cot_f + inv_dev * (
        scaled
        - jnp.mean(scaled, axis=-1, keepdims=True)
        - unit * jnp.mean(scaled * unit, axis=-1, keepdims=True)
    )
    grad_branch = grad_hidden.astype(jnp.bfloat16)
    grad_out_part = contract_rows(attended, grad_branch)
    grad_heads = (
        contract_cols(grad_branch, out_full).astype(jnp.bfloat16).reshape(tok_count, HEADS, HEAD)
    )
    delta = jnp.sum(grad_heads.astype(jnp.float32) * accum, axis=-1).T

    def grad_step(grad_query, index):
        probs, key_block, val_block = block_probs(index)
        grad_probs = jnp.einsum(
            "qhd,khd->hqk", grad_heads, val_block, preferred_element_type=jnp.float32
        )
        grad_scores = (probs * (grad_probs - delta[..., None])).astype(jnp.bfloat16)
        grad_query = (
            grad_query
            + jnp.einsum("hqk,khd->qhd", grad_scores, key_block, preferred_element_type=jnp.float32)
            * scale
        )
        grad_key = (
            jnp.einsum("hqk,qhd->khd", grad_scores, query_heads, preferred_element_type=jnp.float32)
            * scale
        )
        grad_val = jnp.einsum(
            "hqk,qhd->khd",
            probs.astype(jnp.bfloat16),
            grad_heads,
            preferred_element_type=jnp.float32,
        )
        return (grad_query, (grad_key, grad_val))

    grad_query, (grad_keys, grad_vals) = lax.scan(
        grad_step, jnp.zeros((tok_count, HEADS, HEAD), jnp.float32), block_ids
    )
    grad_key_own, grad_val_own = (
        lax.psum_scatter(
            grad_keys.reshape(full_rows, width), "ctx", scatter_dimension=0, tiled=True
        ),
        lax.psum_scatter(
            grad_vals.reshape(full_rows, width), "ctx", scatter_dimension=0, tiled=True
        ),
    )
    grad_qkv_low = jnp.concatenate(
        [grad_query.reshape(tok_count, width), grad_key_own, grad_val_own], axis=1
    ).astype(jnp.bfloat16)
    grad_qkv_part = contract_rows(tok_rows, grad_qkv_low)
    grad_tokens = grad_hidden + contract_cols(grad_qkv_low, qkv_full)
    dense = (
        lax.psum_scatter(grad_qkv_part, "fsdp", scatter_dimension=0, tiled=True),
        lax.psum_scatter(grad_out_part, "fsdp", scatter_dimension=0, tiled=True),
        lax.psum_scatter(grad_router_part, "fsdp", scatter_dimension=0, tiled=True),
        lax.psum_scatter(grad_gain_part, "fsdp", scatter_dimension=0, tiled=True),
        lax.psum_scatter(grad_bias_part, "fsdp", scatter_dimension=0, tiled=True),
    )
    totals = lax.psum(
        (dense[0], dense[1], dense[2], dense[3], dense[4], grad_up_own, grad_down_own), "ctx"
    )
    return (
        layer_out[None],
        grad_tokens[None],
        totals[0],
        totals[1],
        totals[2],
        totals[3],
        totals[4],
        totals[5],
        totals[6],
    )


def cost(microseconds):
    return pl.CostEstimate(flops=int(microseconds * 1.15e9), bytes_accessed=1 << 20, transcendentals=0)


LOG2E = 1.4426950408889634
HIDE = -1e30
RUN = 1024
HALF = 512
VMEM = pl.BlockSpec(memory_space=pltpu.VMEM)
SMEM = pl.BlockSpec(memory_space=pltpu.SMEM)
ANY = pl.BlockSpec(memory_space=pl.ANY)
LIMIT = 60 << 20


def dot_nn(left, right):
    return lax.dot_general(left, right, (((1,), (0,)), ((), ())), preferred_element_type=jnp.float32)


def dot_nt(left, right):
    return lax.dot_general(left, right, (((1,), (1,)), ((), ())), preferred_element_type=jnp.float32)


def dot_tn(left, right):
    return lax.dot_general(left, right, (((0,), (0,)), ((), ())), preferred_element_type=jnp.float32)


def split3(value):
    one = value.astype(jnp.bfloat16)
    rest = value - one.astype(jnp.float32)
    two = rest.astype(jnp.bfloat16)
    three = (rest - two.astype(jnp.float32)).astype(jnp.bfloat16)
    return one, two, three


def span(index, size, width=None):
    return pl.ds(pl.multiple_of(index * size, size), size if width is None else width)


MESH = pl.DeviceIdType.MESH


def flip(index, bit):
    return index + bit - 2 * bit * lax.rem(index // bit, 2)


def meet(devices):
    barrier = pltpu.get_barrier_semaphore()
    for device in devices:
        pl.semaphore_signal(barrier, inc=1, device_id=device, device_id_type=MESH)
    pl.semaphore_wait(barrier, len(devices))


def push(src, dst, send_sem, recv_sem, device):
    return pltpu.make_async_remote_copy(
        src_ref=src, dst_ref=dst, send_sem=send_sem, recv_sem=recv_sem, device_id=device, device_id_type=MESH
    )


def norm_parts(hidden):
    center = hidden - jnp.mean(hidden, axis=-1, keepdims=True)
    inv_dev = lax.rsqrt(jnp.mean(center * center, axis=-1, keepdims=True) + epsilon)
    return center * inv_dev, inv_dev


def gelu_parts(value):
    square = value * value
    tangent = jnp.tanh(value * (square * (gelu_coef * gelu_cubic) + gelu_coef))
    half = 0.5 * tangent + 0.5
    rise = value * (square * (3.0 * gelu_coef * gelu_cubic) + gelu_coef)
    return value * half, half + half * (1.0 - tangent) * rise


def boundaries(seg_ref, lane):
    segs = seg_ref[...]
    begin = jnp.zeros(lane.shape, jnp.int32)
    end = jnp.zeros(lane.shape, jnp.int32)
    for c in range(1, 10):
        total = jnp.sum((segs < c).astype(jnp.int32), axis=1, keepdims=True)
        begin = jnp.where(lane == HEAD - 1 + c, total, begin)
        end = jnp.where(lane == HEAD - 2 + c, total, end)
    return begin, jnp.where(lane == HEAD + 8, 0, end)


def layer_body(
    experts, groups, blocks, table_ref, gid_ref, seg_ref, tok_ref, cot_ref, wq_ref, wo_ref, router_ref, gain_ref, bias_ref, up_ref, down_ref,
    gq_ref, out_ref, sums_ref, layer_ref, gtok_ref, act_ref, gpre_ref, all_ref, toks_ref,
    tok, cot, head_buf, pack_buf, heads, wo, pack, zparts, att_send, att, msend, zin, bsend, bin_, up, down, qf, kf, vf, stat, held, late_held,
    ghead_out, ghead, wide_out, ghidden, dof, qt, dot, dk_acc, dv_acc, head_acc, send, landing, weight, zsend, zone, total, totals,
    out_mine, out_zone, out_sum, out_part, out_own, out_all,
    load_sem, own_sem, t_send, t_recv, d_recv, n_send, n_recv, y_send, y_recv, a_send, a_recv, m_send, m_recv, b_send, b_recv,
    h_send, h_recv, s_send, s_recv, z_send, z_recv, c_send, c_recv, o_send, o_recv, g_send, g_recv, r_send, r_recv, w_send, w_recv,
    v_send, v_recv,
):
    me, z = lax.axis_index("ctx"), lax.axis_index("fsdp")
    count, block_len = blocks // 2, tok_ref.shape[0] // 2
    own_rows, width = tok_ref.shape
    owners, own_experts, ffn = msend.shape[0], up_ref.shape[0], up_ref.shape[2]
    flat, per = experts * groups, experts * groups // owners
    rows = blocks * block_len
    runs = rows // RUN
    low = jnp.bfloat16
    dq_acc, qk, dv_rows, sorted_dv = stat, qf, vf, ghead_out

    def start(copies):
        for copy in copies:
            copy.start()
        return copies

    def wait(copies):
        for copy in copies:
            copy.wait()

    loads = []
    for e in range(own_experts):
        loads += [pltpu.make_async_copy(up_ref.at[e], up.at[e], load_sem.at[2 * e])]
        loads += [pltpu.make_async_copy(down_ref.at[e], down.at[e], load_sem.at[2 * e + 1])]
    start(loads)

    def mask(condition):
        return jnp.broadcast_to(jnp.where(condition, 1.0, 0.0), (1, 2 * HEAD))

    def hold_masks(c=None, j=None):
        pairs = [(c, i) if j is None else (i, j) for i in range(count)]
        return [mask(jnp.minimum(table_ref[2 * c], table_ref[2 * c + 1]) == j).astype(low) for c, j in pairs]

    in_order = mask(table_ref[2 * me] < table_ref[2 * me + 1])[:, :1]

    def blend(masks, values):
        out = None
        for weigh, value in zip(masks, values):
            out = weigh * value if out is None else out + weigh * value
        return out

    def ordered(first, second, weigh):
        return weigh * first + (1 - weigh) * second, weigh * second + (1 - weigh) * first

    tok[:block_len, :], tok[block_len:, :] = ordered(tok_ref[:block_len, :], tok_ref[block_len:, :], in_order.astype(low))
    cot[:block_len, :], cot[block_len:, :] = ordered(cot_ref[:block_len, :], cot_ref[block_len:, :], in_order.astype(low))

    sib, xn, yn, diag = flip(me, 1), flip(me, 2), flip(me, 4), flip(flip(me, 2), 4)
    same_core = [xn, yn, diag]
    z_peers = [(me, lax.rem(z + k, owners)) for k in range(1, owners)]
    c_peers = [(jnp.bitwise_xor(me, k), z) for k in range(1, count)]
    meet(z_peers + c_peers)

    piece = block_len // 2
    per_slot = RUN // block_len

    def place(device, half):
        return 2 * half + device // per_slot, lax.rem(device, per_slot) * block_len

    def there(device, half, k):
        slot, at = place(device, half)
        return held.at[slot, pl.ds(pl.multiple_of(at + k * piece, piece), piece)]

    gone = []

    def go(copies):
        gone.extend(start(copies))

    def here(half, k):
        return tok.at[pl.ds(half * block_len + k * piece, piece)]

    def launch(half):
        slot, at = place(me, half)
        held[slot, pl.ds(pl.multiple_of(at, block_len), block_len), :] = tok[half * block_len:(half + 1) * block_len, :]
        for k in (0, 1):
            go([push(here(half, k), there(me, half, k), t_send.at[half, 0, k], t_recv.at[half, 0, k], (xn, z))])
            go([push(here(half, 1 - k), there(me, half, 1 - k), t_send.at[half, 1, 1 - k], t_recv.at[half, 1, 1 - k], (yn, z))])

    def launch_near(half):
        for k in (0, 1):
            go([push(here(half, k), there(me, half, k), n_send.at[half, 0, k], n_recv.at[half, 0, k], (sib, z))])

    def arrived(device, half, k, sem):
        push(there(device, half, k), there(device, half, k), t_send.at[half, 0, 0], sem, (sib, z)).wait_recv()

    def relay(device, half, k, i):
        block = there(device, half, k)
        go([push(block, block, n_send.at[half, i, k], n_recv.at[half, i, k], (sib, z))])

    def forward(half):
        for device, k, i, to in ((xn, 0, 0, yn), (yn, 1, 1, xn)):
            arrived(device, half, k, t_recv.at[half, i, k])
            block = there(device, half, k)
            go([push(block, block, t_send.at[half, 2, k], d_recv.at[half, k], (to, z))])
            relay(device, half, k, i + 1)

    def settle(half):
        arrived(xn, half, 1, t_recv.at[half, 0, 1])
        relay(xn, half, 1, 1)
        arrived(yn, half, 0, t_recv.at[half, 1, 0])
        relay(yn, half, 0, 2)
        for k in (0, 1):
            arrived(diag, half, k, d_recv.at[half, k])
            relay(diag, half, k, 3)
        for k in (0, 1):
            for i, device in enumerate((sib, flip(xn, 1), flip(yn, 1), flip(diag, 1))):
                arrived(device, half, k, n_recv.at[half, i, k])

    launch(0)

    shared = []

    def share(i, shard, whole):
        whole[z] = shard[...]
        shared.append(start([push(shard, whole.at[z], y_send.at[i, k], y_recv.at[i, k], d) for k, d in enumerate(z_peers)]))

    for h in range(count):
        @pl.when(me == h)
        def _():
            cols = [wq_ref[:, width * kind + HEAD * h:width * kind + HEAD * (h + 1)] for kind in range(3)]
            head_buf[...] = jnp.concatenate(cols, axis=1)

    share(0, head_buf, heads)
    launch_near(0)
    parts = [router_ref[...].astype(jnp.float32), gain_ref[...].astype(jnp.float32), bias_ref[...].astype(jnp.float32)]
    parts.append(jnp.zeros((pack_buf.shape[0] - experts - 2, pack_buf.shape[1]), jnp.float32))
    pack_buf[...] = jnp.concatenate(parts, axis=0).astype(low)
    share(1, pack_buf, pack)
    share(2, wo_ref, wo)
    depth = wq_ref.shape[0] // count
    share(3, wq_ref.at[pl.ds(pl.multiple_of(me * depth, depth), depth)], zparts)

    lane = lax.broadcasted_iota(jnp.int32, (1, 2 * HEAD), 1)
    begin, end = boundaries(seg_ref, lane)
    is_flag = (lane >= HEAD) & (lane < HEAD + 8)
    is_one = (lane >= HEAD + 8) & (lane < HEAD + 11)
    ones_v = ((lane >= HEAD) & (lane < HEAD + 3)).astype(jnp.float32)
    scale = HEAD ** (-0.5)

    def projected(half, device):
        at = device % per_slot * block_len
        lanes = device // per_slot * 4 * HEAD
        return held.at[4 + half, at:at + block_len, lanes:lanes + 4 * HEAD]

    def project(half, head_weight):
        @pl.loop(0, count)
        def _(device):
            slot, at = place(device, half)
            rows_here = held[slot, pl.ds(pl.multiple_of(at, block_len), block_len), :]
            slot, at = 4 + half, pl.ds(pl.multiple_of(at, block_len), block_len)
            to = pl.ds(pl.multiple_of(device // per_slot * 4 * HEAD, 4 * HEAD), 4 * HEAD)
            held[slot, at, to] = dot_nn(rows_here, head_weight).astype(low)

        @pl.loop(0, count)
        def _(j):
            s = j if half == 0 else blocks - 1 - j
            masks = hold_masks(j=j)
            both = blend(masks, [projected(half, c)[:, :2 * HEAD] for c in range(count)]).astype(jnp.float32)
            value = blend(masks, [projected(half, c)[:, 2 * HEAD:] for c in range(count)]).astype(jnp.float32)
            spot = lax.broadcasted_iota(jnp.int32, (block_len, 2 * HEAD), 0) + s * block_len
            mine = (spot >= begin) & (spot < end)
            at = span(s, block_len)
            flag_q = jnp.where(is_flag & jnp.logical_not(mine), 1.0, 0.0)
            flag_k = jnp.where(mine, HIDE, jnp.where(is_one, 1.0, 0.0))
            qf[at, :] = jnp.where(lane < HEAD, both, flag_q).astype(low)
            kf[at, :] = jnp.where(lane < HEAD, pltpu.roll(both, HEAD, 1), flag_k).astype(low)
            vf[at, :] = (value + ones_v).astype(low)
            dot[:, at] = value.T.astype(low)[:HEAD]

    lower = lax.broadcasted_iota(jnp.int32, (HALF, HALF), 0) <= lax.broadcasted_iota(jnp.int32, (HALF, HALF), 1)

    def query_run(run):
        def tile(state, q_at, k_at, size, diagonal):
            scores = dot_nt(kf[k_at, :], qf[q_at, :]) * (scale * LOG2E)
            if diagonal:
                scores = jnp.where(lower, scores, HIDE)
            top, acc = state
            new_top = jnp.maximum(top, jnp.max(scores, axis=0, keepdims=True))
            probs = jnp.exp2(scores - new_top).astype(low)
            values = jnp.concatenate([dot[:, k_at], jnp.ones((HEAD, size), low)], axis=0)
            return new_top, acc * jnp.exp2(top - new_top) + dot_nn(values, probs)

        begin = (jnp.full((1, RUN), HIDE, jnp.float32), jnp.zeros((2 * HEAD, RUN), jnp.float32))
        def both_halves(n, state):
            for part in range(2):
                state = tile(state, span(run, RUN), span(2 * n + part, HALF), HALF, False)
            return state

        whole = lax.fori_loop(0, run, both_halves, begin)
        early, late = span(2 * run, HALF), span(2 * run + 1, HALF)
        first = tile([part[:, :HALF] for part in whole], early, early, HALF, True)
        second = tile([part[:, HALF:] for part in whole], late, early, HALF, False)
        second = tile(second, late, late, HALF, True)
        for at, (top, acc) in ((early, first), (late, second)):
            sums = acc[HEAD:]
            result = jnp.concatenate([acc[:HEAD] / sums, top + jnp.log2(sums)], axis=0).T
            stat[at, :] = result
            one, two, three = split3(result * (-1.0 / (scale * LOG2E)))
            old = qf[at, :]
            old = jnp.where(lane == HEAD + 8, one, old)
            old = jnp.where(lane == HEAD + 9, two, old)
            qf[at, :] = jnp.where(lane == HEAD + 10, three, old)

    def send_attended(half):
        mid = block_len // 2
        ats = [slice(s * block_len, (s + 1) * block_len) for s in (range(count) if half == 0 else range(blocks - 1, count - 1, -1))]

        @pl.loop(0, count)
        def _(c):
            block = blend(hold_masks(c=c), [stat[at, :].astype(low) for at in ats])
            att_send[half, c] = jnp.concatenate([block[:mid, :HEAD], block[mid:, :HEAD]], axis=1)
        att[half, me] = att_send[half, me]
        return start([
            push(att_send.at[half, d[0]], att.at[half, me], a_send.at[half, k], a_recv.at[half, k], d) for k, d in enumerate(c_peers)
        ])

    forward(0)
    settle(0)
    launch(1)
    launch_near(1)
    wait(shared[0])
    head_weight = heads[...].reshape(width, 3 * HEAD)
    head_weight = jnp.concatenate([head_weight, jnp.zeros((width, HEAD), low)], axis=1)
    project(0, head_weight)

    @pl.loop(0, 1)
    def _(run):
        query_run(run)

    forward(1)

    @pl.loop(1, runs // 2)
    def _(run):
        query_run(run)

    swap = send_attended(0)
    settle(1)
    saves = start([pltpu.make_async_copy(held.at[i], toks_ref.at[i], own_sem.at[3 + i]) for i in range(rows // RUN)])
    project(1, head_weight)

    @pl.loop(runs // 2, runs)
    def _(run):
        query_run(run)

    swap += send_attended(1)
    for copy in gone:
        copy.wait_send()
    wait(shared[1] + shared[2] + shared[3])

    first_diagonal = runs * (runs - 1)

    def slot_of(run, index, part):
        return run * (2 * runs - 1 - run) + 2 * (index - run - 1) + part

    def probabilities(q_at, k_at, visible):
        scores = dot_nt(qf[q_at, :], kf[k_at, :]) * (scale * LOG2E)
        if visible is not None:
            scores = jnp.where(visible, scores, HIDE)
        return jnp.exp2(scores).astype(low)

    def hold_diagonal():
        early = lax.broadcasted_iota(jnp.int32, (RUN, HALF), 1) <= lax.broadcasted_iota(jnp.int32, (RUN, HALF), 0)
        late = lax.broadcasted_iota(jnp.int32, (HALF, HALF), 1) <= lax.broadcasted_iota(jnp.int32, (HALF, HALF), 0)

        @pl.loop(0, runs)
        def _(run):
            held[first_diagonal + run] = probabilities(span(run, RUN), span(2 * run, HALF), early)
            late_held[run] = probabilities(span(2 * run + 1, HALF), span(2 * run + 1, HALF), late)

    def hold(run):
        @pl.loop(run + 1, runs)
        def _(index):
            for part in range(2):
                held[slot_of(run, index, part)] = probabilities(span(index, RUN), span(2 * run + part, HALF), None)

    hold_diagonal()

    @pl.loop(1, runs - 1)
    def _(run):
        hold(run)

    wait(swap)
    weights = start([push(zparts, weight.at[:, me], w_send.at[k], w_recv.at[k], (d, z)) for k, d in enumerate(same_core)])
    shares = start([push(zparts, weight.at[:, me], v_send.at[3], v_recv.at[3], (sib, z))])
    weight[:, me] = zparts[...]
    quarters = [
        jnp.concatenate([att[half, h, :, HEAD * p:HEAD * (p + 1)] for h in range(count)], axis=1) for half in range(2) for p in range(2)
    ]
    attended = jnp.concatenate(quarters, axis=0)
    out_weight = wo[...].reshape(width, width)
    hidden = tok[...].astype(jnp.float32) + dot_nn(attended, out_weight)
    unit, inv_dev = norm_parts(hidden)
    small_in = jnp.concatenate([pack[k] for k in range(owners)], axis=1)
    gain, bias = small_in[experts:experts + 1].astype(jnp.float32), small_in[experts + 1:experts + 2].astype(jnp.float32)
    normed = (unit * gain + bias).astype(low)
    expo = jnp.exp(dot_nt(small_in, normed)[:experts])
    expo = jnp.broadcast_to(expo[:, None, :], (experts, groups, own_rows)).reshape(flat, own_rows)
    gids = lax.rem(gid_ref[...], groups).astype(jnp.float32)
    gids = jnp.concatenate(ordered(gids[:, :block_len], gids[:, block_len:], in_order), axis=1)
    member = lax.rem(lax.broadcasted_iota(jnp.int32, (flat, 1), 0), groups).astype(jnp.float32) == gids
    expo = jnp.where(member, expo, 0.0)
    mix = expo / jnp.sum(expo, axis=1, keepdims=True)
    mix_low = mix.astype(low)

    def zone_rows(owner, kind):
        return pl.ds(pl.multiple_of((2 * owner + kind) * per, per), per)

    def to_owners(kind, value):
        msend[:, kind] = value.astype(low).reshape(owners, per, width)
        zin[zone_rows(z, kind), :] = msend[z, kind]
        return start([
            push(msend.at[d[1], kind], zin.at[zone_rows(z, kind)], m_send.at[kind, k], m_recv.at[kind, k], d) for k, d in enumerate(z_peers)
        ])

    mixed_copies = to_owners(0, dot_nn(mix_low, normed))
    grad_experts = dot_nn(mix_low, cot[...])
    wait(loads)
    wait(mixed_copies)
    grad_copies = to_owners(1, grad_experts)

    def from_sources(kind, e):
        lows_ = [(2 * owner + kind) * per + e * groups for owner in range(owners)]
        return jnp.concatenate([zin[at:at + groups, :] for at in lows_], axis=0)

    def to_sources(kind, e, value):
        bsend[:, kind, e * groups:(e + 1) * groups, :] = value.astype(low).reshape(owners, groups, width)

    def send_back(kind):
        bin_[z, kind] = bsend[z, kind]
        return start([
            push(bsend.at[d[1], kind], bin_.at[z, kind], b_send.at[kind, k], b_recv.at[kind, k], d) for k, d in enumerate(z_peers)
        ])

    slopes = []
    for e in range(own_experts):
        active, slope = gelu_parts(dot_nn(from_sources(0, e), up[e]))
        slopes.append(slope)
        to_sources(0, e, dot_nn(active.astype(low), down[e]))
    out_copies = send_back(0)
    wait(grad_copies)
    for e in range(own_experts):
        grad_pre = (dot_nt(from_sources(1, e), down[e]) * slopes[e]).astype(low)
        to_sources(1, e, dot_nt(grad_pre, up[e]))
    back_copies = send_back(1)
    wait(out_copies)
    expert_out = bin_[:, 0].reshape(flat, width)
    result = hidden + dot_tn(mix_low, expert_out)
    wide_out[:block_len, :], wide_out[block_len:, :] = ordered(result[:block_len], result[block_len:], in_order)
    layer_copy = start([pltpu.make_async_copy(wide_out, layer_ref, own_sem.at[2])])
    grad_mix = dot_nt(expert_out, cot[...])
    wait(back_copies)
    grad_mixed = bin_[:, 1].reshape(flat, width)
    product = mix * (grad_mix + dot_nt(grad_mixed, normed))
    grad_logits = product - mix * jnp.sum(product, axis=1, keepdims=True)
    grad_logits = jnp.sum(grad_logits.reshape(experts, groups, own_rows), axis=1).astype(low)
    pad = jnp.zeros((small_in.shape[0] - experts, own_rows), low)
    grad_logits = jnp.concatenate([grad_logits, pad], axis=0)
    grad_normed = dot_tn(jnp.concatenate([mix_low, grad_logits], axis=0), jnp.concatenate([grad_mixed, small_in], axis=0))
    scaled = grad_normed * gain
    mean = jnp.mean(scaled, axis=-1, keepdims=True)
    grad_hidden = cot[...].astype(jnp.float32) + inv_dev * (scaled - mean - unit * jnp.mean(scaled * unit, axis=-1, keepdims=True))
    branch = grad_hidden.astype(low)
    grad_heads = dot_nt(branch, out_weight).astype(low)
    for h in range(count):
        at = slice(HEAD * h, HEAD * (h + 1))
        ghead_out[h] = jnp.concatenate([grad_heads[:block_len, at], grad_heads[block_len:, at]], axis=1)
    swap = start([push(ghead_out.at[d[0]], ghead.at[me], h_send.at[k], h_recv.at[k], d) for k, d in enumerate(c_peers)])
    ghead[me] = ghead_out[me]
    ghidden[...] = grad_hidden
    out_mine[...] = dot_tn(attended, branch).astype(low).reshape(out_mine.shape)
    gout_copies = start([push(out_mine.at[d[1]], out_zone.at[z], o_send.at[0, k], o_recv.at[0, k], d) for k, d in enumerate(z_peers)])
    out_zone[z] = out_mine[z]
    small = jnp.concatenate(
        [
            dot_nn(grad_logits, normed)[:experts],
            jnp.sum(grad_normed * unit, axis=0, keepdims=True),
            jnp.sum(grad_normed, axis=0, keepdims=True),
            jnp.zeros((small_in.shape[0] - experts - 2, width), jnp.float32),
        ],
        axis=0,
    )
    lanes = width // owners
    for c in range(owners):
        zsend[c, 3 * HEAD:, :] = small[:, c * lanes:(c + 1) * lanes].astype(low)
    wait(saves)
    hold(0)

    def prepare(s, both):
        at = span(s, block_len)
        grad = jnp.where(lane < HEAD, both, 0.0)
        delta = jnp.sum(grad * stat[at, :], axis=1, keepdims=True)
        one, two, three = split3(jnp.broadcast_to(-delta, grad.shape))
        wide = jnp.where(lane == HEAD, one, grad.astype(low))
        wide = jnp.where(lane == HEAD + 1, two, wide)
        dof[at, :] = jnp.where(lane == HEAD + 2, three, wide)
        turned = jnp.where(lane < HEAD, both, pltpu.roll(qf[at, :].astype(jnp.float32), HEAD, 1)).T.astype(low)
        dot[:, at] = turned[:HEAD]
        qt[:, at] = turned[HEAD:]

    wait(swap)
    gathers = start([push(zin, all_ref.at[me], g_send.at[k], g_recv.at[k], (d, z)) for k, d in enumerate(same_core)])
    relays = start([push(zin, all_ref.at[me], r_send.at[3], r_recv.at[3], (sib, z))])
    own_got = start([pltpu.make_async_copy(zin, all_ref.at[me], own_sem.at[1])])

    @pl.loop(0, count)
    def _(j):
        both = blend(hold_masks(j=j), [ghead[c] for c in range(count)]).astype(jnp.float32)
        prepare(j, both)
        prepare(blocks - 1 - j, pltpu.roll(both, HEAD, 1))

    tok_loads = [
        pltpu.make_async_copy(toks_ref.at[i], held.at[i], own_sem.at[3 + i]) for i in range(rows // RUN)
    ]

    def key_run(run):
        def tile(q_at, k_at, part, probs, first_k, first_q):
            slope = dot_nt(dof[q_at, :], vf[k_at, :])
            grad = (probs.astype(jnp.float32) * slope).astype(low)
            dv = dot_nn(dot[:, q_at], probs)
            dk = dot_nn(qt[:, q_at], grad)
            dq = dot_nn(grad, kf[k_at, :])
            at = slice(part * HALF, (part + 1) * HALF)
            if first_k:
                dv_acc[:, at] = dv
                dk_acc[:, at] = dk
            else:
                dv_acc[:, at] += dv
                dk_acc[:, at] += dk
            if first_q:
                @pl.when(run == 0)
                def _():
                    dq_acc[q_at, :] = dq

                @pl.when(run != 0)
                def _():
                    dq_acc[q_at, :] += dq
            else:
                dq_acc[q_at, :] += dq

        early, late = span(2 * run, HALF), span(2 * run + 1, HALF)
        tile(span(run, RUN), early, 0, held[first_diagonal + run], True, True)
        tile(late, late, 1, late_held[run], True, False)

        @pl.loop(run + 1, runs)
        def _(index):
            for part in range(2):
                tile(span(index, RUN), span(2 * run + part, HALF), part, held[slot_of(run, index, part)], False, part == 0)

        at = span(run, RUN)
        both = jnp.concatenate([dk_acc[...] * scale, dv_acc[...]], axis=0).T
        query = dq_acc[at, :] * scale
        qk[at, :] = jnp.where(lane < HEAD, query, pltpu.roll(both, HEAD, 1)).astype(low)
        dv_rows[at, :] = both.astype(low)

    def send_half(half):
        mid = block_len // 2
        ats = [slice(s * block_len, (s + 1) * block_len) for s in (range(count) if half == 0 else range(blocks - 1, count - 1, -1))]

        @pl.loop(0, count)
        def _(c):
            masks = hold_masks(c=c)
            send[half, c, :block_len, :] = blend(masks, [qk[at, :] for at in ats])
            values = blend(masks, [dv_rows[at, :] for at in ats])
            sorted_dv[c] = values
            values = values[:, HEAD:]
            send[half, c, block_len:, :] = jnp.concatenate([values[:mid], values[mid:]], axis=1)
        landing[half, me] = send[half, me]
        return start([
            push(send.at[half, d[0]], landing.at[half, me], s_send.at[half, k], s_recv.at[half, k], d) for k, d in enumerate(c_peers)
        ])

    def head_weights(half):
        if half == 0:
            head_acc[...] = jnp.zeros_like(head_acc)

        @pl.loop(0, count // 2)
        def _(i):
            first, second = None, None
            for part in range(2):
                c = 2 * i + part
                slot, at = place(c, half)
                here = held[slot, pl.ds(pl.multiple_of(at, block_len), block_len), :]
                one, two = dot_tn(send[half, c, :block_len, :], here), dot_tn(sorted_dv[c], here)
                first, second = (one, two) if first is None else (first + one, second + two)
            head_acc[:2 * HEAD, :] += first
            head_acc[2 * HEAD:, :] += second[HEAD:]

    @pl.loop(0, runs // 2)
    def _(run):
        key_run(run)

        @pl.when(run == 0)
        def _():
            start(tok_loads)

    swaps = send_half(0)
    for k, d in enumerate(same_core):
        gathers[k].wait_recv()
        relays += start([push(all_ref.at[d], all_ref.at[d], r_send.at[k], r_recv.at[k], (sib, z))])
        weights[k].wait_recv()
        shares += start([push(weight.at[:, d], weight.at[:, d], v_send.at[k], v_recv.at[k], (sib, z))])
    wait(gout_copies)
    summed = out_zone[0].astype(jnp.float32)
    for k in range(1, owners):
        summed = summed + out_zone[k].astype(jnp.float32)
    out_sum[...] = summed.astype(low).reshape(out_sum.shape)
    part_copies = start([push(out_sum.at[d[0]], out_part.at[me], o_send.at[1, k], o_recv.at[1, k], d) for k, d in enumerate(c_peers)])
    out_part[me] = out_sum[me]
    wait(tok_loads)
    head_weights(0)

    @pl.loop(runs // 2, runs)
    def _(run):
        key_run(run)

    swaps += send_half(1)
    wait(part_copies)
    summed = out_part[0].astype(jnp.float32)
    for k in range(1, count):
        summed = summed + out_part[k].astype(jnp.float32)
    out_own[...] = summed.astype(low)
    last_copies = start([push(out_own, out_all.at[me], o_send.at[2, k], o_recv.at[2, k], d) for k, d in enumerate(c_peers)])
    out_all[me] = out_own[...]
    wait(own_got + relays)

    mixed_slot = rows // RUN
    share = owners * 2 * per
    mixed_loads = []
    for c in range(count):
        slot, at = divmod(c * share, RUN)
        mixed_loads.append(pltpu.make_async_copy(all_ref.at[c], held.at[mixed_slot + slot, pl.ds(at, share)], own_sem.at[3 + rows // RUN + c]))
    start(mixed_loads)
    head_weights(1)
    for c in range(owners):
        zsend[c, :3 * HEAD, :] = head_acc[:, c * lanes:(c + 1) * lanes].astype(low)
    z_copies = start([push(zsend.at[d[1]], zone.at[z], z_send.at[k], z_recv.at[k], d) for k, d in enumerate(z_peers)])
    zone[z] = zsend[z]
    wait(mixed_loads)
    step = HALF
    chunks = ffn // step
    wide_slot = mixed_slot + count * share // RUN

    def of_expert(kind, e):
        parts = []
        for slot in range(mixed_slot, wide_slot):
            value = held[slot].reshape(RUN // share, owners, 2, own_experts, groups, width)
            parts.append(value[:, :, kind, e].reshape(-1, width))
        return jnp.concatenate(parts, axis=0)

    def expert_part(e):
        mixed, grad_out = of_expert(0, e), of_expert(1, e)
        copies = []

        @pl.loop(0, chunks)
        def _(i):
            at = span(i, step)
            to = span(lax.rem(i, 2), step)
            active, slope = gelu_parts(dot_nn(mixed, up[e, :, at]))
            held[wide_slot + chunks * e + i // 2, to, :] = active.astype(low)
            slot = wide_slot + chunks * e + chunks // 2 + i // 2
            held[slot, to, :] = (dot_nt(grad_out, down[e, at, :]) * slope).astype(low)

        for i in range(chunks):
            slot = wide_slot + chunks * e + i // 2
            at, to = pl.ds(i * step, step), pl.ds(i % 2 * step, step)
            sem = own_sem.at[3 + rows // RUN + count + 2 * (chunks * e + i)]
            copies.append(pltpu.make_async_copy(held.at[slot, to], act_ref.at[e, :, at], sem))
            sem = own_sem.at[4 + rows // RUN + count + 2 * (chunks * e + i)]
            copies.append(pltpu.make_async_copy(held.at[slot + chunks // 2, to], gpre_ref.at[e, :, at], sem))
        return start(copies)

    stores = expert_part(0)
    wait(z_copies)
    summed = zone[0].astype(jnp.float32)
    for k in range(1, owners):
        summed = summed + zone[k].astype(jnp.float32)
    total[...] = summed.astype(low)
    c_copies = start([push(total, totals.at[me], c_send.at[k], c_recv.at[k], d) for k, d in enumerate(c_peers)])
    totals[me] = total[...]
    for e in range(1, own_experts):
        stores += expert_part(e)
    wait(swaps + shares)
    flat_weight = weight[...].reshape(width, -1)
    parts = []
    for half in range(2):
        queries, keys, values = [], [], []
        for h in range(count):
            front, back = landing[half, h, :block_len, :], landing[half, h, block_len:, :]
            queries.append(front[:, :HEAD])
            keys.append(front[:, HEAD:])
            values.append(jnp.concatenate([back[:, :HEAD], back[:, HEAD:]], axis=0))
        parts.append(dot_nt(jnp.concatenate(queries + keys + values, axis=1), flat_weight))
    wait(layer_copy)
    first, second = ghidden[:block_len, :] + parts[0], ghidden[block_len:, :] + parts[1]
    wide_out[:block_len, :], wide_out[block_len:, :] = ordered(first, second, in_order)
    stores += start([pltpu.make_async_copy(wide_out, gtok_ref, own_sem.at[2])])
    wait(last_copies)
    out_ref[...] = out_all[...].astype(jnp.float32).reshape(out_ref.shape)
    wait(c_copies)
    small = None
    turned = []
    for c in range(count):
        turned.append(totals[c, :3 * HEAD, :].astype(jnp.float32).T)
        part = totals[c, 3 * HEAD:, :].astype(jnp.float32)
        small = part if small is None else small + part
    sums_ref[...] = small
    for kind in range(3):
        at = slice(HEAD * kind, HEAD * (kind + 1))
        gq_ref[:, HEAD * count * kind:HEAD * count * (kind + 1)] = jnp.concatenate([part[:, at] for part in turned], axis=1)
    wait(stores)
    for copy in gathers + weights:
        copy.wait_send()


def layer(table, gid_row, segs, tokens, cot, w_qkv, w_out, w_router, ln_gain, ln_bias, w_up, w_down, groups, count, owners):
    own_rows, width = tokens.shape
    experts = w_router.shape[1]
    blocks, block_len = table.shape[0], own_rows // 2
    rows = blocks * block_len
    runs = rows // RUN
    own_experts, _, ffn = w_up.shape
    lanes, wide_qkv = w_qkv.shape
    smalls = 16
    height = 3 * HEAD + smalls
    per = experts * groups // owners
    wide = (own_experts, count * owners * groups, ffn)
    share = (owners * 2 * per, width)
    part = (count, lanes // count, width)
    swap = (2, count, block_len + block_len // 2, 2 * HEAD)
    gout = (owners, lanes, width)
    sent = (owners, 2, per, width)
    attended = (2, count, block_len // 2, 2 * HEAD)
    head_grad = (count, block_len, 2 * HEAD)
    low, full = jnp.bfloat16, jnp.float32
    scratch = [
        (tokens.shape, low), (tokens.shape, low), ((lanes, 3 * HEAD), low), ((smalls, lanes), low), ((owners, lanes, 3 * HEAD), low),
        ((owners,) + w_out.shape, low), ((owners, smalls, lanes), low), ((owners, lanes // count, wide_qkv), low), (attended, low),
        (attended, low), (sent, low), (share, low), (sent, low), (sent, low), (w_up.shape, low), (w_down.shape, low),
        ((rows, 2 * HEAD), low), ((rows, 2 * HEAD), low), ((rows, 2 * HEAD), low), ((rows, 2 * HEAD), full),
        ((runs * runs, RUN, HALF), low), ((runs, HALF, HALF), low), (head_grad, low), (head_grad, low),
        (tokens.shape, full), (tokens.shape, full), ((rows, 2 * HEAD), low), ((HEAD, rows), low), ((HEAD, rows), low),
        ((HEAD, RUN), full), ((HEAD, RUN), full), ((3 * HEAD, width), full), (swap, low), (swap, low),
        ((owners, count, lanes // count, wide_qkv), low), ((owners, height, lanes), low), ((owners, height, lanes), low),
        ((height, lanes), low), ((count, height, lanes), low), (gout, low), (gout, low), (part, low), (part, low), (part[1:], low),
        (part, low),
    ]
    owns = 3 + rows // RUN + count + 2 * own_experts * (ffn // HALF)
    to_z, to_c = owners - 1, count - 1
    sems = [
        (2 * own_experts,), (owns,), (2, 3, 2), (2, 2, 2), (2, 2), (2, 4, 2), (2, 4, 2), (4, to_z), (4, to_z),
        (2, to_c), (2, to_c), (2, to_z), (2, to_z), (2, to_z), (2, to_z), (to_c,), (to_c,), (2, to_c), (2, to_c),
        (to_z,), (to_z,), (to_c,), (to_c,), (3, to_c), (3, to_c), (3,), (3,), (4,), (4,), (3,), (3,), (4,), (4,),
    ]
    return pl.pallas_call(
        functools.partial(layer_body, experts, groups, blocks),
        out_shape=(
            jax.ShapeDtypeStruct((lanes, 3 * width), full),
            jax.ShapeDtypeStruct((lanes, width), full),
            jax.ShapeDtypeStruct((smalls, lanes), full),
            jax.ShapeDtypeStruct(tokens.shape, full),
            jax.ShapeDtypeStruct(tokens.shape, full),
            jax.ShapeDtypeStruct(wide, low),
            jax.ShapeDtypeStruct(wide, low),
            jax.ShapeDtypeStruct((count,) + share, low),
            jax.ShapeDtypeStruct((rows // RUN, RUN, width), low),
        ),
        in_specs=[SMEM] + [VMEM] * 9 + [ANY] * 2,
        out_specs=(VMEM,) * 3 + (ANY,) * 6,
        scratch_shapes=[pltpu.VMEM(shape, dtype) for shape, dtype in scratch] + [pltpu.SemaphoreType.DMA(shape) for shape in sems],
        compiler_params=pltpu.CompilerParams(collective_id=1, has_side_effects=True, vmem_limit_bytes=LIMIT),
        cost_estimate=cost(130),
        name="layer",
    )(table, gid_row, segs, tokens, cot, w_qkv, w_out, w_router.T, ln_gain[None], ln_bias[None], w_up, w_down)


def expert_grad_body(experts, passed, mixed_ref, grad_ref, act_ref, gpre_ref, small_ref, *refs):
    sources, outs = refs[:passed], refs[passed + 5:]
    gup_ref, gdown_ref, router_ref, gain_ref, bias_ref = refs[passed:passed + 5]
    width = gup_ref.shape[1]
    for source, out in zip(sources, outs):
        out[...] = source[...]
    router_ref[...] = small_ref[:experts]
    gain_ref[...] = small_ref[experts:experts + 1]
    bias_ref[...] = small_ref[experts + 1:experts + 2]
    gup_ref[0] = dot_tn(mixed_ref[...].reshape(-1, width), gpre_ref[0])
    gdown_ref[0] = dot_tn(act_ref[0], grad_ref[...].reshape(-1, width))


def expert_grads(gathered, active, grad_pre, small, passed, groups, experts):
    own, rows, ffn = active.shape
    step = 1024
    steps = ffn // step
    sources, width = gathered.shape[0], gathered.shape[3]
    view = gathered.reshape(sources, 2, own, groups, width)
    lanes = small.shape[1]
    full = jnp.float32
    slices = [pl.BlockSpec((x.shape[0] // (own * steps), x.shape[1]), lambda e, f: (e * steps + f, 0)) for x in passed]
    return pl.pallas_call(
        functools.partial(expert_grad_body, experts, len(passed)),
        grid=(own, steps),
        out_shape=[
            jax.ShapeDtypeStruct((own, width, ffn), full), jax.ShapeDtypeStruct((own, ffn, width), full),
            jax.ShapeDtypeStruct((experts, lanes), full), jax.ShapeDtypeStruct((1, lanes), full), jax.ShapeDtypeStruct((1, lanes), full),
        ] + [jax.ShapeDtypeStruct(x.shape, x.dtype) for x in passed],
        in_specs=[
            pl.BlockSpec((sources, 1, 1, groups, width), lambda e, f: (0, 0, e, 0, 0)),
            pl.BlockSpec((sources, 1, 1, groups, width), lambda e, f: (0, 1, e, 0, 0)),
            pl.BlockSpec((1, rows, step), lambda e, f: (e, 0, f)),
            pl.BlockSpec((1, rows, step), lambda e, f: (e, 0, f)),
            pl.BlockSpec(small.shape, lambda e, f: (0, 0)),
        ] + slices,
        out_specs=[
            pl.BlockSpec((1, width, step), lambda e, f: (e, 0, f)), pl.BlockSpec((1, step, width), lambda e, f: (e, f, 0)),
            pl.BlockSpec((experts, lanes), lambda e, f: (0, 0)), pl.BlockSpec((1, lanes), lambda e, f: (0, 0)),
            pl.BlockSpec((1, lanes), lambda e, f: (0, 0)),
        ] + slices,
        compiler_params=pltpu.CompilerParams(vmem_limit_bytes=LIMIT),
        cost_estimate=cost(10),
        name="expert_grads",
    )(view, view, active, grad_pre, small, *passed)


def fast_device(
    tokens, cotangent, block_table, seg_ids, group_ids, w_qkv, w_out, w_router, ln_gain, ln_bias, w_up, w_down
):
    ctx_count, z_count = lax.axis_size("ctx"), lax.axis_size("fsdp")
    tok_rows, cot_rows = tokens[0], cotangent[0]
    rows, width = tok_rows.shape
    experts = w_router.shape[1]
    groups = rows // GROUP_SIZE
    grad_qkv, grad_out, small, layer_out, grad_tokens, active, grad_pre, gathered, unused = layer(
        block_table, group_ids, seg_ids, tok_rows, cot_rows, w_qkv, w_out, w_router, ln_gain, ln_bias, w_up, w_down, groups, ctx_count,
        z_count,
    )
    gathered = gathered.reshape(ctx_count * z_count, 2, experts * groups // z_count, width)
    grad_up, grad_down, grad_router, grad_gain, grad_bias, layer_out, grad_tokens, grad_qkv, grad_out = expert_grads(
        gathered, active, grad_pre, small, [layer_out, grad_tokens, grad_qkv, grad_out], groups, experts
    )
    return (
        layer_out[None],
        grad_tokens[None],
        grad_qkv,
        grad_out,
        grad_router.T,
        grad_gain[0],
        grad_bias[0],
        grad_up,
        grad_down,
    )


def solution(mesh):
    placed = (
        P("fsdp", "ctx", None),
        P("fsdp", "ctx", None),
        P(),
        P("fsdp", None),
        P("fsdp", "ctx"),
        P("fsdp", None),
        P("fsdp", None),
        P("fsdp", None),
        P("fsdp"),
        P("fsdp"),
        P("fsdp", None, None),
        P("fsdp", None, None),
    )
    step = fast_device if mesh.shape["ctx"] == HEADS else on_device
    return jax.shard_map(
        step,
        mesh=mesh,
        in_specs=placed,
        out_specs=(
            P("fsdp", "ctx", None),
            P("fsdp", "ctx", None),
            P("fsdp", None),
            P("fsdp", None),
            P("fsdp", None),
            P("fsdp"),
            P("fsdp"),
            P("fsdp", None, None),
            P("fsdp", None, None),
        ),
        check_vma=False,
    )
```

```python
import functools

import jax
import jax.numpy as jnp
from jax import lax
from jax.experimental import pallas as pl
from jax.experimental.pallas import tpu as pltpu
from jax.sharding import PartitionSpec as P

HEADS = 8
HEAD = 64
GROUP_SIZE = 32
KEY_BLOCK = 2048


highest = lax.Precision.HIGHEST
neg_large = -1e30
epsilon = 1e-05
gelu_coef = 0.7978845608028654
gelu_cubic = 0.044715


def contract_rows(left, right):
    return lax.dot_general(
        left, right, (((0,), (0,)), ((), ())), preferred_element_type=jnp.float32
    )


def contract_cols(left, right):
    return lax.dot_general(
        left, right, (((1,), (1,)), ((), ())), preferred_element_type=jnp.float32
    )


def gelu_slope(value):
    inner = gelu_coef * (value + gelu_cubic * value * value * value)
    tangent = jnp.tanh(inner)
    return 0.5 * (1.0 + tangent) + 0.5 * value * (1.0 - tangent * tangent) * gelu_coef * (
        1.0 + 3.0 * gelu_cubic * value * value
    )


def expert_forward(mixed_low, up_weight, down_weight):
    pre = jnp.einsum("ged,edh->geh", mixed_low, up_weight, preferred_element_type=jnp.float32)
    active = jax.nn.gelu(pre, approximate=True).astype(jnp.bfloat16)
    result = jnp.einsum("geh,ehd->ged", active, down_weight, preferred_element_type=jnp.float32)
    return (pre, active, result.astype(jnp.bfloat16))


def expert_backward(mixed_low, pre, active, grad_result, up_weight, down_weight):
    grad_act = jnp.einsum(
        "ged,ehd->geh", grad_result, down_weight, preferred_element_type=jnp.float32
    )
    grad_pre = (grad_act * gelu_slope(pre)).astype(jnp.bfloat16)
    grad_down_part = jnp.einsum(
        "geh,ged->ehd", active, grad_result, preferred_element_type=jnp.float32
    )
    grad_up_part = jnp.einsum(
        "ged,geh->edh", mixed_low, grad_pre, preferred_element_type=jnp.float32
    )
    grad_mixed = jnp.einsum("geh,edh->ged", grad_pre, up_weight, preferred_element_type=jnp.float32)
    return (grad_up_part, grad_down_part, grad_mixed.astype(jnp.bfloat16))


def on_device(
    tokens,
    cotangent,
    block_table,
    seg_ids,
    group_ids,
    w_qkv,
    w_out,
    w_router,
    ln_gain,
    ln_bias,
    w_up,
    w_down,
):
    tok_rows = tokens[0]
    tok_count = tok_rows.shape[0]
    width = tok_rows.shape[1]
    expert_count = w_router.shape[1]
    ctx_index = lax.axis_index("ctx")
    full_rows = seg_ids.shape[1]
    block_len = full_rows // block_table.shape[0]
    row_ids = jnp.arange(full_rows, dtype=jnp.int32)
    key_pos = jnp.take(block_table, row_ids // block_len) * block_len + row_ids % block_len
    key_seg = seg_ids[0]
    pos_rows = lax.dynamic_slice_in_dim(key_pos, ctx_index * tok_count, tok_count)
    seg_rows = lax.dynamic_slice_in_dim(key_seg, ctx_index * tok_count, tok_count)
    scale = HEAD ** (-0.5)
    qkv_full, out_full, router_full, gain_full, bias_full = (
        lax.all_gather(w_qkv, "fsdp", axis=0, tiled=True),
        lax.all_gather(w_out, "fsdp", axis=0, tiled=True),
        lax.all_gather(w_router, "fsdp", axis=0, tiled=True),
        lax.all_gather(ln_gain, "fsdp", axis=0, tiled=True),
        lax.all_gather(ln_bias, "fsdp", axis=0, tiled=True),
    )
    qkv = jnp.dot(tok_rows, qkv_full, preferred_element_type=jnp.float32).astype(jnp.bfloat16)
    query_heads = qkv[:, :width].reshape(tok_count, HEADS, HEAD)
    key_all, val_all = (
        lax.all_gather(qkv[:, width : 2 * width], "ctx", axis=0, tiled=True),
        lax.all_gather(qkv[:, 2 * width :], "ctx", axis=0, tiled=True),
    )
    key_heads = key_all.reshape(full_rows, HEADS, HEAD)
    val_heads = val_all.reshape(full_rows, HEADS, HEAD)
    block_count = full_rows // KEY_BLOCK
    block_ids = jnp.arange(block_count, dtype=jnp.int32)

    def block_scores(index):
        start = index * KEY_BLOCK
        key_block = lax.dynamic_slice_in_dim(key_heads, start, KEY_BLOCK, 0)
        val_block = lax.dynamic_slice_in_dim(val_heads, start, KEY_BLOCK, 0)
        pos_block = lax.dynamic_slice_in_dim(key_pos, start, KEY_BLOCK, 0)
        seg_block = lax.dynamic_slice_in_dim(key_seg, start, KEY_BLOCK, 0)
        scores = (
            jnp.einsum("qhd,khd->hqk", query_heads, key_block, preferred_element_type=jnp.float32)
            * scale
        )
        allowed = (pos_block[None, :] <= pos_rows[:, None]) & (
            (seg_block[None, :] == 0) | (seg_block[None, :] == seg_rows[:, None])
        )
        return (scores, allowed[None], key_block, val_block)

    def lse_step(carry, index):
        top, total = carry
        scores, allowed, key_block, val_block = block_scores(index)
        masked = jnp.where(allowed, scores, neg_large)
        new_top = jnp.maximum(top, jnp.max(masked, axis=-1))
        weights = jnp.where(allowed, jnp.exp(masked - new_top[..., None]), 0.0)
        return ((new_top, total * jnp.exp(top - new_top) + jnp.sum(weights, axis=-1)), None)

    start_top = jnp.full((HEADS, tok_count), neg_large, jnp.float32)
    (top, total), unused = lax.scan(
        lse_step, (start_top, jnp.zeros((HEADS, tok_count), jnp.float32)), block_ids
    )
    log_total = top + jnp.log(total)

    def block_probs(index):
        scores, allowed, key_block, val_block = block_scores(index)
        probs = jnp.where(allowed, jnp.exp(scores - log_total[..., None]), 0.0)
        return (probs, key_block, val_block)

    def value_step(accum, index):
        probs, key_block, val_block = block_probs(index)
        return (
            accum
            + jnp.einsum(
                "hqk,khd->qhd",
                probs.astype(jnp.bfloat16),
                val_block,
                preferred_element_type=jnp.float32,
            ),
            None,
        )

    accum, unused = lax.scan(
        value_step, jnp.zeros((tok_count, HEADS, HEAD), jnp.float32), block_ids
    )
    attended = accum.reshape(tok_count, width).astype(jnp.bfloat16)
    hidden = tok_rows.astype(jnp.float32) + jnp.dot(
        attended, out_full, preferred_element_type=jnp.float32
    )
    center = hidden - jnp.mean(hidden, axis=-1, keepdims=True)
    inv_dev = lax.rsqrt(jnp.mean(center * center, axis=-1, keepdims=True) + epsilon)
    unit = center * inv_dev
    gain_f = gain_full.astype(jnp.float32)
    normed_low = (unit * gain_f + bias_full.astype(jnp.float32)).astype(jnp.bfloat16)
    logits = jnp.dot(normed_low, router_full, preferred_element_type=jnp.float32)
    groups_dev = tok_count // GROUP_SIZE
    local_group = group_ids[0] - ctx_index * groups_dev
    member = (local_group[:, None] == jnp.arange(groups_dev, dtype=jnp.int32)[None, :]).astype(
        jnp.float32
    )
    expo = jnp.exp(logits)
    group_total = jnp.dot(member.T, expo, precision=highest)
    mix_weights = expo / jnp.dot(member, group_total, precision=highest)
    weights_low = mix_weights.astype(jnp.bfloat16)
    mixing = member.astype(jnp.bfloat16).T[:, None, :] * weights_low.T[None, :, :]
    mixing_flat = mixing.reshape(groups_dev * expert_count, tok_count)
    mixed_low = jnp.dot(mixing_flat, normed_low, preferred_element_type=jnp.float32).astype(
        jnp.bfloat16
    )
    mixed_low = mixed_low.reshape(groups_dev, expert_count, width)
    owner_mixed = lax.all_to_all(mixed_low, "fsdp", split_axis=1, concat_axis=0, tiled=True)
    pre, active, owner_out = expert_forward(owner_mixed, w_up, w_down)
    expert_out = lax.all_to_all(owner_out, "fsdp", split_axis=0, concat_axis=1, tiled=True)
    expert_flat = expert_out.reshape(groups_dev * expert_count, width)
    spread = contract_rows(mixing_flat, expert_flat)
    layer_out = hidden + spread
    cot_rows = cotangent[0]
    cot_f = cot_rows.astype(jnp.float32)
    grad_expert = jnp.dot(mixing_flat, cot_rows, preferred_element_type=jnp.float32).astype(
        jnp.bfloat16
    )
    grad_expert = grad_expert.reshape(groups_dev, expert_count, width)
    coef = contract_cols(cot_rows, expert_flat).reshape(tok_count, groups_dev, expert_count)
    grad_mix_spread = jnp.sum(coef * member[:, :, None], axis=1)
    owner_grad = lax.all_to_all(grad_expert, "fsdp", split_axis=1, concat_axis=0, tiled=True)
    grad_up_own, grad_down_own, owner_back = expert_backward(
        owner_mixed, pre, active, owner_grad, w_up, w_down
    )
    grad_mixed = lax.all_to_all(owner_back, "fsdp", split_axis=0, concat_axis=1, tiled=True)
    grad_mixed_flat = grad_mixed.reshape(groups_dev * expert_count, width)
    grad_norm_mix = contract_rows(mixing_flat, grad_mixed_flat)
    grad_mixing = contract_cols(grad_mixed_flat, normed_low).reshape(
        groups_dev, expert_count, tok_count
    )
    grad_mix_mixing = jnp.sum(grad_mixing * member.T[:, None, :], axis=0).T
    grad_mix = grad_mix_spread + grad_mix_mixing
    product = mix_weights * grad_mix
    token_dot = jnp.dot(member, jnp.dot(member.T, product, precision=highest), precision=highest)
    grad_logits = (product - mix_weights * token_dot).astype(jnp.bfloat16)
    grad_router_part = contract_rows(normed_low, grad_logits)
    grad_norm_router = contract_cols(grad_logits, router_full)
    grad_normed = grad_norm_mix + grad_norm_router
    grad_gain_part = jnp.sum(grad_normed * unit, axis=0)
    grad_bias_part = jnp.sum(grad_normed, axis=0)
    scaled = grad_normed * gain_f
    grad_hidden = cot_f + inv_dev * (
        scaled
        - jnp.mean(scaled, axis=-1, keepdims=True)
        - unit * jnp.mean(scaled * unit, axis=-1, keepdims=True)
    )
    grad_branch = grad_hidden.astype(jnp.bfloat16)
    grad_out_part = contract_rows(attended, grad_branch)
    grad_heads = (
        contract_cols(grad_branch, out_full).astype(jnp.bfloat16).reshape(tok_count, HEADS, HEAD)
    )
    delta = jnp.sum(grad_heads.astype(jnp.float32) * accum, axis=-1).T

    def grad_step(grad_query, index):
        probs, key_block, val_block = block_probs(index)
        grad_probs = jnp.einsum(
            "qhd,khd->hqk", grad_heads, val_block, preferred_element_type=jnp.float32
        )
        grad_scores = (probs * (grad_probs - delta[..., None])).astype(jnp.bfloat16)
        grad_query = (
            grad_query
            + jnp.einsum("hqk,khd->qhd", grad_scores, key_block, preferred_element_type=jnp.float32)
            * scale
        )
        grad_key = (
            jnp.einsum("hqk,qhd->khd", grad_scores, query_heads, preferred_element_type=jnp.float32)
            * scale
        )
        grad_val = jnp.einsum(
            "hqk,qhd->khd",
            probs.astype(jnp.bfloat16),
            grad_heads,
            preferred_element_type=jnp.float32,
        )
        return (grad_query, (grad_key, grad_val))

    grad_query, (grad_keys, grad_vals) = lax.scan(
        grad_step, jnp.zeros((tok_count, HEADS, HEAD), jnp.float32), block_ids
    )
    grad_key_own, grad_val_own = (
        lax.psum_scatter(
            grad_keys.reshape(full_rows, width), "ctx", scatter_dimension=0, tiled=True
        ),
        lax.psum_scatter(
            grad_vals.reshape(full_rows, width), "ctx", scatter_dimension=0, tiled=True
        ),
    )
    grad_qkv_low = jnp.concatenate(
        [grad_query.reshape(tok_count, width), grad_key_own, grad_val_own], axis=1
    ).astype(jnp.bfloat16)
    grad_qkv_part = contract_rows(tok_rows, grad_qkv_low)
    grad_tokens = grad_hidden + contract_cols(grad_qkv_low, qkv_full)
    dense = (
        lax.psum_scatter(grad_qkv_part, "fsdp", scatter_dimension=0, tiled=True),
        lax.psum_scatter(grad_out_part, "fsdp", scatter_dimension=0, tiled=True),
        lax.psum_scatter(grad_router_part, "fsdp", scatter_dimension=0, tiled=True),
        lax.psum_scatter(grad_gain_part, "fsdp", scatter_dimension=0, tiled=True),
        lax.psum_scatter(grad_bias_part, "fsdp", scatter_dimension=0, tiled=True),
    )
    totals = lax.psum(
        (dense[0], dense[1], dense[2], dense[3], dense[4], grad_up_own, grad_down_own), "ctx"
    )
    return (
        layer_out[None],
        grad_tokens[None],
        totals[0],
        totals[1],
        totals[2],
        totals[3],
        totals[4],
        totals[5],
        totals[6],
    )


def cost(microseconds):
    return pl.CostEstimate(flops=int(microseconds * 1.15e9), bytes_accessed=1 << 20, transcendentals=0)


LOG2E = 1.4426950408889634
HIDE = -1e30
RUN = 1024
HALF = 512
VMEM = pl.BlockSpec(memory_space=pltpu.VMEM)
SMEM = pl.BlockSpec(memory_space=pltpu.SMEM)
ANY = pl.BlockSpec(memory_space=pl.ANY)
LIMIT = 60 << 20


def dot_nn(left, right):
    return lax.dot_general(left, right, (((1,), (0,)), ((), ())), preferred_element_type=jnp.float32)


def dot_nt(left, right):
    return lax.dot_general(left, right, (((1,), (1,)), ((), ())), preferred_element_type=jnp.float32)


def dot_tn(left, right):
    return lax.dot_general(left, right, (((0,), (0,)), ((), ())), preferred_element_type=jnp.float32)


def split3(value):
    one = value.astype(jnp.bfloat16)
    rest = value - one.astype(jnp.float32)
    two = rest.astype(jnp.bfloat16)
    three = (rest - two.astype(jnp.float32)).astype(jnp.bfloat16)
    return one, two, three


def span(index, size, width=None):
    return pl.ds(pl.multiple_of(index * size, size), size if width is None else width)


MESH = pl.DeviceIdType.MESH


def flip(index, bit):
    return index + bit - 2 * bit * lax.rem(index // bit, 2)


def meet(devices):
    barrier = pltpu.get_barrier_semaphore()
    for device in devices:
        pl.semaphore_signal(barrier, inc=1, device_id=device, device_id_type=MESH)
    pl.semaphore_wait(barrier, len(devices))


def push(src, dst, send_sem, recv_sem, device):
    return pltpu.make_async_remote_copy(
        src_ref=src, dst_ref=dst, send_sem=send_sem, recv_sem=recv_sem, device_id=device, device_id_type=MESH
    )


def norm_parts(hidden):
    center = hidden - jnp.mean(hidden, axis=-1, keepdims=True)
    inv_dev = lax.rsqrt(jnp.mean(center * center, axis=-1, keepdims=True) + epsilon)
    return center * inv_dev, inv_dev


def gelu_parts(value):
    square = value * value
    tangent = jnp.tanh(value * (square * (gelu_coef * gelu_cubic) + gelu_coef))
    half = 0.5 * tangent + 0.5
    rise = value * (square * (3.0 * gelu_coef * gelu_cubic) + gelu_coef)
    return value * half, half + half * (1.0 - tangent) * rise


def boundaries(seg_ref, lane):
    segs = seg_ref[...]
    begin = jnp.zeros(lane.shape, jnp.int32)
    end = jnp.zeros(lane.shape, jnp.int32)
    for c in range(1, 10):
        total = jnp.sum((segs < c).astype(jnp.int32), axis=1, keepdims=True)
        begin = jnp.where(lane == HEAD - 1 + c, total, begin)
        end = jnp.where(lane == HEAD - 2 + c, total, end)
    return begin, jnp.where(lane == HEAD + 8, 0, end)


def layer_body(
    experts, groups, blocks, table_ref, gid_ref, seg_ref, tok_ref, cot_ref, wq_ref, wo_ref, router_ref, gain_ref, bias_ref, up_ref, down_ref,
    gq_ref, out_ref, sums_ref, layer_ref, gtok_ref, act_ref, gpre_ref, all_ref, toks_ref,
    tok, cot, head_buf, pack_buf, heads, wo, pack, zparts, att_send, att, msend, zin, bsend, bin_, up, down, qf, kf, vf, stat, held, late_held,
    ghead_out, ghead, wide_out, ghidden, dof, qt, dot, dk_acc, dv_acc, head_acc, send, landing, weight, zsend, zone, total, totals,
    out_mine, out_zone, out_sum, out_part, out_own, out_all,
    load_sem, own_sem, t_send, t_recv, d_recv, n_send, n_recv, y_send, y_recv, a_send, a_recv, m_send, m_recv, b_send, b_recv,
    h_send, h_recv, s_send, s_recv, z_send, z_recv, c_send, c_recv, o_send, o_recv, g_send, g_recv, r_send, r_recv, w_send, w_recv,
    v_send, v_recv,
):
    me, z = lax.axis_index("ctx"), lax.axis_index("fsdp")
    count, block_len = blocks // 2, tok_ref.shape[0] // 2
    own_rows, width = tok_ref.shape
    owners, own_experts, ffn = msend.shape[0], up_ref.shape[0], up_ref.shape[2]
    flat, per = experts * groups, experts * groups // owners
    rows = blocks * block_len
    runs = rows // RUN
    low = jnp.bfloat16
    dq_acc, qk, dv_rows, sorted_dv = stat, qf, vf, ghead_out

    def start(copies):
        for copy in copies:
            copy.start()
        return copies

    def wait(copies):
        for copy in copies:
            copy.wait()

    loads = []
    for e in range(own_experts):
        loads += [pltpu.make_async_copy(up_ref.at[e], up.at[e], load_sem.at[2 * e])]
        loads += [pltpu.make_async_copy(down_ref.at[e], down.at[e], load_sem.at[2 * e + 1])]
    start(loads)

    def mask(condition):
        return jnp.broadcast_to(jnp.where(condition, 1.0, 0.0), (1, 2 * HEAD))

    def hold_masks(c=None, j=None):
        pairs = [(c, i) if j is None else (i, j) for i in range(count)]
        return [mask(jnp.minimum(table_ref[2 * c], table_ref[2 * c + 1]) == j).astype(low) for c, j in pairs]

    in_order = mask(table_ref[2 * me] < table_ref[2 * me + 1])[:, :1]

    def blend(masks, values):
        out = None
        for weigh, value in zip(masks, values):
            out = weigh * value if out is None else out + weigh * value
        return out

    def ordered(first, second, weigh):
        return weigh * first + (1 - weigh) * second, weigh * second + (1 - weigh) * first

    sib, xn, yn, diag = flip(me, 1), flip(me, 2), flip(me, 4), flip(flip(me, 2), 4)
    same_core = [xn, yn, diag]
    z_peers = [(me, lax.rem(z + k, owners)) for k in range(1, owners)]
    c_peers = [(jnp.bitwise_xor(me, k), z) for k in range(1, count)]
    barrier = pltpu.get_barrier_semaphore()
    for d in z_peers + c_peers:
        pl.semaphore_signal(barrier, inc=1, device_id=d, device_id_type=MESH)
    tok[:block_len, :], tok[block_len:, :] = ordered(tok_ref[:block_len, :], tok_ref[block_len:, :], in_order.astype(low))
    pl.semaphore_wait(barrier, len(z_peers + c_peers))

    piece = block_len // 2
    per_slot = RUN // block_len

    def place(device, half):
        return 2 * half + device // per_slot, lax.rem(device, per_slot) * block_len

    def there(device, half, k):
        slot, at = place(device, half)
        return held.at[slot, pl.ds(pl.multiple_of(at + k * piece, piece), piece)]

    gone = []

    def go(copies):
        gone.extend(start(copies))

    def here(half, k):
        return tok.at[pl.ds(half * block_len + k * piece, piece)]

    def launch(half):
        slot, at = place(me, half)
        held[slot, pl.ds(pl.multiple_of(at, block_len), block_len), :] = tok[half * block_len:(half + 1) * block_len, :]
        for k in (0, 1):
            go([push(here(half, k), there(me, half, k), t_send.at[half, 0, k], t_recv.at[half, 0, k], (xn, z))])
            go([push(here(half, 1 - k), there(me, half, 1 - k), t_send.at[half, 1, 1 - k], t_recv.at[half, 1, 1 - k], (yn, z))])

    def launch_near(half):
        for k in (0, 1):
            go([push(here(half, k), there(me, half, k), n_send.at[half, 0, k], n_recv.at[half, 0, k], (sib, z))])

    def arrival(device, half, k, sem):
        return push(there(device, half, k), there(device, half, k), t_send.at[half, 0, 0], sem, (sib, z))

    def relay(device, half, k, i):
        block = there(device, half, k)
        return push(block, block, n_send.at[half, i, k], n_recv.at[half, i, k], (sib, z))

    def forward_plan(half):
        plan = []
        for device, k, i, to in ((xn, 0, 0, yn), (yn, 1, 1, xn)):
            block = there(device, half, k)
            plan.append((
                push(block, block, t_send.at[half, 0, 0], t_recv.at[half, i, k], (sib, z)),
                push(block, block, t_send.at[half, 2, k], d_recv.at[half, k], (to, z)),
                push(block, block, n_send.at[half, i + 1, k], n_recv.at[half, i + 1, k], (sib, z)),
            ))
        return plan

    def forward(plan):
        for came, on, near in plan:
            came.wait_recv()
            start([on, near])

    def settle_plan(half):
        plan = [
            (arrival(xn, half, 1, t_recv.at[half, 0, 1]), relay(xn, half, 1, 1)),
            (arrival(yn, half, 0, t_recv.at[half, 1, 0]), relay(yn, half, 0, 2)),
        ]
        plan += [(arrival(diag, half, k, d_recv.at[half, k]), relay(diag, half, k, 3)) for k in (0, 1)]
        near = []
        for k in (0, 1):
            for i, device in enumerate((sib, flip(xn, 1), flip(yn, 1), flip(diag, 1))):
                near.append(arrival(device, half, k, n_recv.at[half, i, k]))
        return plan, near

    def settle(plan, near):
        for came, on in plan:
            came.wait_recv()
            on.start()
        for came in near:
            came.wait_recv()

    launch(0)

    shared = []

    def share(i, shard, whole):
        whole[z] = shard[...]
        shared.append(start([push(shard, whole.at[z], y_send.at[i, k], y_recv.at[i, k], d) for k, d in enumerate(z_peers)]))

    for h in range(count):
        @pl.when(me == h)
        def _():
            cols = [wq_ref[:, width * kind + HEAD * h:width * kind + HEAD * (h + 1)] for kind in range(3)]
            head_buf[...] = jnp.concatenate(cols, axis=1)

    share(0, head_buf, heads)
    launch_near(0)
    parts = [router_ref[...].astype(jnp.float32), gain_ref[...].astype(jnp.float32), bias_ref[...].astype(jnp.float32)]
    parts.append(jnp.zeros((pack_buf.shape[0] - experts - 2, pack_buf.shape[1]), jnp.float32))
    pack_buf[...] = jnp.concatenate(parts, axis=0).astype(low)
    share(1, pack_buf, pack)
    share(2, wo_ref, wo)
    depth = wq_ref.shape[0] // count
    share(3, wq_ref.at[pl.ds(pl.multiple_of(me * depth, depth), depth)], zparts)

    lane = lax.broadcasted_iota(jnp.int32, (1, 2 * HEAD), 1)
    begin, end = boundaries(seg_ref, lane)
    is_flag = (lane >= HEAD) & (lane < HEAD + 8)
    is_one = (lane >= HEAD + 8) & (lane < HEAD + 11)
    ones_v = ((lane >= HEAD) & (lane < HEAD + 3)).astype(jnp.float32)
    scale = HEAD ** (-0.5)

    def projected(half, device):
        at = device % per_slot * block_len
        lanes = device // per_slot * 4 * HEAD
        return held.at[4 + half, at:at + block_len, lanes:lanes + 4 * HEAD]

    def project(half, head_weight):
        for slot in range(count // per_slot):
            to = slice(4 * HEAD * slot, 4 * HEAD * (slot + 1))
            held[4 + half, :, to] = dot_nn(held[2 * half + slot], head_weight).astype(low)

        @pl.loop(0, count, unroll=4)
        def _(j):
            s = j if half == 0 else blocks - 1 - j
            masks = hold_masks(j=j)
            both = blend(masks, [projected(half, c)[:, :2 * HEAD] for c in range(count)]).astype(jnp.float32)
            value = blend(masks, [projected(half, c)[:, 2 * HEAD:] for c in range(count)]).astype(jnp.float32)
            spot = lax.broadcasted_iota(jnp.int32, (block_len, 2 * HEAD), 0) + s * block_len
            mine = (spot >= begin) & (spot < end)
            at = span(s, block_len)
            flag_q = jnp.where(is_flag & jnp.logical_not(mine), 1.0, 0.0)
            flag_k = jnp.where(mine, HIDE, jnp.where(is_one, 1.0, 0.0))
            qf[at, :] = jnp.where(lane < HEAD, both, flag_q).astype(low)
            kf[at, :] = jnp.where(lane < HEAD, pltpu.roll(both, HEAD, 1), flag_k).astype(low)
            vf[at, :] = (value + ones_v).astype(low)
            dot[:, at] = value.T.astype(low)[:HEAD]

    lower = lax.broadcasted_iota(jnp.int32, (HALF, RUN), 0) <= lax.broadcasted_iota(jnp.int32, (HALF, RUN), 1)

    def query_run(run):
        def tile(state, q_at, k_at, size, diagonal):
            scores = dot_nt(kf[k_at, :], qf[q_at, :]) * (scale * LOG2E)
            if diagonal:
                scores = jnp.where(lower[:, :scores.shape[1]], scores, HIDE)
            top, acc = state
            new_top = jnp.maximum(top, jnp.max(scores, axis=0, keepdims=True))
            probs = jnp.exp2(scores - new_top).astype(low)
            values = jnp.concatenate([dot[:, k_at], jnp.ones((HEAD, size), low)], axis=0)
            return new_top, acc * jnp.exp2(top - new_top) + dot_nn(values, probs)

        begin = (jnp.full((1, RUN), HIDE, jnp.float32), jnp.zeros((2 * HEAD, RUN), jnp.float32))
        def both_halves(n, state):
            for part in range(2):
                state = tile(state, span(run, RUN), span(2 * n + part, HALF), HALF, False)
            return state

        whole = lax.fori_loop(0, run, both_halves, begin)
        early, late = span(2 * run, HALF), span(2 * run + 1, HALF)
        whole = tile(whole, span(run, RUN), early, HALF, True)
        first = [part[:, :HALF] for part in whole]
        second = tile([part[:, HALF:] for part in whole], late, late, HALF, True)
        for at, (top, acc) in ((early, first), (late, second)):
            sums = acc[HEAD:]
            result = jnp.concatenate([acc[:HEAD] / sums, top + jnp.log2(sums)], axis=0).T
            stat[at, :] = result
            one, two, three = split3(result * (-1.0 / (scale * LOG2E)))
            old = qf[at, :]
            old = jnp.where(lane == HEAD + 8, one, old)
            old = jnp.where(lane == HEAD + 9, two, old)
            qf[at, :] = jnp.where(lane == HEAD + 10, three, old)

    def pack_attended(half):
        mid = block_len // 2
        ats = [slice(s * block_len, (s + 1) * block_len) for s in (range(count) if half == 0 else range(blocks - 1, count - 1, -1))]

        @pl.loop(0, count, unroll=4)
        def _(c):
            block = blend(hold_masks(c=c), [stat[at, :].astype(low) for at in ats])
            att_send[half, c] = jnp.concatenate([block[:mid, :HEAD], block[mid:, :HEAD]], axis=1)
        att[half, me] = att_send[half, me]

    swaps = [
        [push(att_send.at[half, d[0]], att.at[half, me], a_send.at[half, k], a_recv.at[half, k], d) for k, d in enumerate(c_peers)]
        for half in range(2)
    ]
    saves = [pltpu.make_async_copy(held.at[i], toks_ref.at[i], own_sem.at[3 + i]) for i in range(rows // RUN)]
    cot[:block_len, :], cot[block_len:, :] = ordered(cot_ref[:block_len, :], cot_ref[block_len:, :], in_order.astype(low))
    plans = [forward_plan(half) for half in range(2)]
    for plan in plans:
        for came, on, near in plan:
            gone.extend([on, near])
    settles = [settle_plan(half) for half in range(2)]
    for plan, near in settles:
        gone.extend([on for came, on in plan])
    forward(plans[0])
    settle(*settles[0])
    launch(1)
    launch_near(1)
    wait(shared[0])
    head_weight = heads[...].reshape(width, 3 * HEAD)
    head_weight = jnp.concatenate([head_weight, jnp.zeros((width, HEAD), low)], axis=1)
    project(0, head_weight)

    @pl.loop(0, runs)
    def _(run):
        query_run(run)

        @pl.when(run == 0)
        def _():
            forward(plans[1])

        @pl.when(run == runs // 2 - 1)
        def _():
            pack_attended(0)
            start(swaps[0])
            settle(*settles[1])
            start(saves)
            project(1, head_weight)

    pack_attended(1)
    start(swaps[1])
    for copy in gone:
        copy.wait_send()
    wait(shared[1] + shared[2] + shared[3])

    first_diagonal = runs * (runs - 1)

    def slot_of(run, index, part):
        return run * (2 * runs - 1 - run) + 2 * (index - run - 1) + part

    def probabilities(q_at, k_at, visible):
        scores = dot_nt(qf[q_at, :], kf[k_at, :]) * (scale * LOG2E)
        if visible is not None:
            scores = jnp.where(visible, scores, HIDE)
        return jnp.exp2(scores).astype(low)

    def hold_diagonal():
        early = lax.broadcasted_iota(jnp.int32, (RUN, HALF), 1) <= lax.broadcasted_iota(jnp.int32, (RUN, HALF), 0)
        late = lax.broadcasted_iota(jnp.int32, (HALF, HALF), 1) <= lax.broadcasted_iota(jnp.int32, (HALF, HALF), 0)

        @pl.loop(0, runs)
        def _(run):
            held[first_diagonal + run] = probabilities(span(run, RUN), span(2 * run, HALF), early)
            late_held[run] = probabilities(span(2 * run + 1, HALF), span(2 * run + 1, HALF), late)

    def hold(run):
        @pl.loop(run + 1, runs)
        def _(index):
            for part in range(2):
                held[slot_of(run, index, part)] = probabilities(span(index, RUN), span(2 * run + part, HALF), None)

    hold_diagonal()
    wait(swaps[0] + swaps[1])
    weights = start([push(zparts, weight.at[:, me], w_send.at[k], w_recv.at[k], (d, z)) for k, d in enumerate(same_core)])
    shares = start([push(zparts, weight.at[:, me], v_send.at[3], v_recv.at[3], (sib, z))])
    weight[:, me] = zparts[...]
    quarters = [
        jnp.concatenate([att[half, h, :, HEAD * p:HEAD * (p + 1)] for h in range(count)], axis=1) for half in range(2) for p in range(2)
    ]
    attended = jnp.concatenate(quarters, axis=0)
    out_weight = wo[...].reshape(width, width)
    hidden = tok[...].astype(jnp.float32) + dot_nn(attended, out_weight)
    unit, inv_dev = norm_parts(hidden)
    small_in = jnp.concatenate([pack[k] for k in range(owners)], axis=1)
    gain, bias = small_in[experts:experts + 1].astype(jnp.float32), small_in[experts + 1:experts + 2].astype(jnp.float32)
    normed = (unit * gain + bias).astype(low)
    expo = jnp.exp(dot_nt(small_in, normed)[:experts])
    expo = jnp.broadcast_to(expo[:, None, :], (experts, groups, own_rows)).reshape(flat, own_rows)
    gids = lax.rem(gid_ref[...], groups).astype(jnp.float32)
    gids = jnp.concatenate(ordered(gids[:, :block_len], gids[:, block_len:], in_order), axis=1)
    member = lax.rem(lax.broadcasted_iota(jnp.int32, (flat, 1), 0), groups).astype(jnp.float32) == gids
    expo = jnp.where(member, expo, 0.0)
    mix = expo / jnp.sum(expo, axis=1, keepdims=True)
    mix_low = mix.astype(low)

    def zone_rows(owner, kind):
        return pl.ds(pl.multiple_of((2 * owner + kind) * per, per), per)

    def to_owners(kind, value):
        msend[:, kind] = value.astype(low).reshape(owners, per, width)
        zin[zone_rows(z, kind), :] = msend[z, kind]
        return start([
            push(msend.at[d[1], kind], zin.at[zone_rows(z, kind)], m_send.at[kind, k], m_recv.at[kind, k], d) for k, d in enumerate(z_peers)
        ])

    mixed_copies = to_owners(0, dot_nn(mix_low, normed))
    grad_experts = dot_nn(mix_low, cot[...])
    wait(loads)
    hold(1)
    grad_copies = to_owners(1, grad_experts)

    @pl.loop(2, runs - 1)
    def _(run):
        hold(run)

    wait(mixed_copies)

    def from_sources(kind, e):
        lows_ = [(2 * owner + kind) * per + e * groups for owner in range(owners)]
        return jnp.concatenate([zin[at:at + groups, :] for at in lows_], axis=0)

    def to_sources(kind, e, value):
        bsend[:, kind, e * groups:(e + 1) * groups, :] = value.astype(low).reshape(owners, groups, width)

    def send_back(kind):
        bin_[z, kind] = bsend[z, kind]
        return start([
            push(bsend.at[d[1], kind], bin_.at[z, kind], b_send.at[kind, k], b_recv.at[kind, k], d) for k, d in enumerate(z_peers)
        ])

    slopes = []
    for e in range(own_experts):
        active, slope = gelu_parts(dot_nn(from_sources(0, e), up[e]))
        slopes.append(slope)
        to_sources(0, e, dot_nn(active.astype(low), down[e]))
    out_copies = send_back(0)
    wait(grad_copies)
    for e in range(own_experts):
        grad_pre = (dot_nt(from_sources(1, e), down[e]) * slopes[e]).astype(low)
        to_sources(1, e, dot_nt(grad_pre, up[e]))
    back_copies = send_back(1)
    wait(out_copies)
    expert_out = bin_[:, 0].reshape(flat, width)
    result = hidden + dot_tn(mix_low, expert_out)
    wide_out[:block_len, :], wide_out[block_len:, :] = ordered(result[:block_len], result[block_len:], in_order)
    layer_copy = start([pltpu.make_async_copy(wide_out, layer_ref, own_sem.at[2])])
    grad_mix = dot_nt(expert_out, cot[...])
    wait(back_copies)
    grad_mixed = bin_[:, 1].reshape(flat, width)
    product = mix * (grad_mix + dot_nt(grad_mixed, normed))
    grad_logits = product - mix * jnp.sum(product, axis=1, keepdims=True)
    grad_logits = jnp.sum(grad_logits.reshape(experts, groups, own_rows), axis=1).astype(low)
    pad = jnp.zeros((small_in.shape[0] - experts, own_rows), low)
    grad_logits = jnp.concatenate([grad_logits, pad], axis=0)
    grad_normed = dot_tn(jnp.concatenate([mix_low, grad_logits], axis=0), jnp.concatenate([grad_mixed, small_in], axis=0))
    scaled = grad_normed * gain
    mean = jnp.mean(scaled, axis=-1, keepdims=True)
    grad_hidden = cot[...].astype(jnp.float32) + inv_dev * (scaled - mean - unit * jnp.mean(scaled * unit, axis=-1, keepdims=True))
    branch = grad_hidden.astype(low)
    grad_heads = dot_nt(branch, out_weight).astype(low)
    for h in range(count):
        at = slice(HEAD * h, HEAD * (h + 1))
        ghead_out[h] = jnp.concatenate([grad_heads[:block_len, at], grad_heads[block_len:, at]], axis=1)
    swap = start([push(ghead_out.at[d[0]], ghead.at[me], h_send.at[k], h_recv.at[k], d) for k, d in enumerate(c_peers)])
    ghead[me] = ghead_out[me]
    ghidden[...] = grad_hidden
    out_mine[...] = dot_tn(attended, branch).astype(low).reshape(out_mine.shape)
    gout_copies = start([push(out_mine.at[d[1]], out_zone.at[z], o_send.at[0, k], o_recv.at[0, k], d) for k, d in enumerate(z_peers)])
    out_zone[z] = out_mine[z]
    small = jnp.concatenate(
        [
            dot_nn(grad_logits, normed)[:experts],
            jnp.sum(grad_normed * unit, axis=0, keepdims=True),
            jnp.sum(grad_normed, axis=0, keepdims=True),
            jnp.zeros((small_in.shape[0] - experts - 2, width), jnp.float32),
        ],
        axis=0,
    )
    lanes = width // owners
    for c in range(owners):
        zsend[c, 3 * HEAD:, :] = small[:, c * lanes:(c + 1) * lanes].astype(low)
    wait(saves)
    hold(0)

    def prepare(s, both):
        at = span(s, block_len)
        grad = jnp.where(lane < HEAD, both, 0.0)
        delta = jnp.sum(grad * stat[at, :], axis=1, keepdims=True)
        one, two, three = split3(jnp.broadcast_to(-delta, grad.shape))
        wide = jnp.where(lane == HEAD, one, grad.astype(low))
        wide = jnp.where(lane == HEAD + 1, two, wide)
        dof[at, :] = jnp.where(lane == HEAD + 2, three, wide)
        turned = jnp.where(lane < HEAD, both, pltpu.roll(qf[at, :].astype(jnp.float32), HEAD, 1)).T.astype(low)
        dot[:, at] = turned[:HEAD]
        qt[:, at] = turned[HEAD:]

    wait(swap)
    gathers = start([push(zin, all_ref.at[me], g_send.at[k], g_recv.at[k], (d, z)) for k, d in enumerate(same_core)])
    own_relay = start([push(zin, all_ref.at[me], r_send.at[3], r_recv.at[3], (sib, z))])
    own_got = start([pltpu.make_async_copy(zin, all_ref.at[me], own_sem.at[1])])

    @pl.loop(0, count, unroll=4)
    def _(j):
        both = blend(hold_masks(j=j), [ghead[c] for c in range(count)]).astype(jnp.float32)
        prepare(j, both)
        prepare(blocks - 1 - j, pltpu.roll(both, HEAD, 1))

    tok_loads = [
        pltpu.make_async_copy(toks_ref.at[i], held.at[i], own_sem.at[3 + i]) for i in range(rows // RUN)
    ]

    def key_run(run):
        def tile(q_at, k_at, part, probs, first_k, first_q):
            slope = dot_nt(dof[q_at, :], vf[k_at, :])
            grad = (probs.astype(jnp.float32) * slope).astype(low)
            dv = dot_nn(dot[:, q_at], probs)
            dk = dot_nn(qt[:, q_at], grad)
            dq = dot_nn(grad, kf[k_at, :])
            at = slice(part * HALF, (part + 1) * HALF)
            if first_k:
                dv_acc[:, at] = dv
                dk_acc[:, at] = dk
            else:
                dv_acc[:, at] += dv
                dk_acc[:, at] += dk
            if first_q:
                @pl.when(run == 0)
                def _():
                    dq_acc[q_at, :] = dq

                @pl.when(run != 0)
                def _():
                    dq_acc[q_at, :] += dq
            else:
                dq_acc[q_at, :] += dq

        early, late = span(2 * run, HALF), span(2 * run + 1, HALF)
        tile(span(run, RUN), early, 0, held[first_diagonal + run], True, True)
        tile(late, late, 1, late_held[run], True, False)

        @pl.loop(run + 1, runs)
        def _(index):
            for part in range(2):
                tile(span(index, RUN), span(2 * run + part, HALF), part, held[slot_of(run, index, part)], False, part == 0)

        at = span(run, RUN)
        both = jnp.concatenate([dk_acc[...] * scale, dv_acc[...]], axis=0).T
        query = dq_acc[at, :] * scale
        qk[at, :] = jnp.where(lane < HEAD, query, pltpu.roll(both, HEAD, 1)).astype(low)
        dv_rows[at, :] = both.astype(low)

    def pack_half(half):
        mid = block_len // 2
        ats = [slice(s * block_len, (s + 1) * block_len) for s in (range(count) if half == 0 else range(blocks - 1, count - 1, -1))]

        @pl.loop(0, count, unroll=4)
        def _(c):
            masks = hold_masks(c=c)
            send[half, c, :block_len, :] = blend(masks, [qk[at, :] for at in ats])
            values = blend(masks, [dv_rows[at, :] for at in ats])
            sorted_dv[c] = values
            values = values[:, HEAD:]
            send[half, c, block_len:, :] = jnp.concatenate([values[:mid], values[mid:]], axis=1)
        landing[half, me] = send[half, me]

    swaps = [
        [push(send.at[half, d[0]], landing.at[half, me], s_send.at[half, k], s_recv.at[half, k], d) for k, d in enumerate(c_peers)]
        for half in range(2)
    ]
    relays = [push(all_ref.at[d], all_ref.at[d], r_send.at[k], r_recv.at[k], (sib, z)) for k, d in enumerate(same_core)]
    others = [push(weight.at[:, d], weight.at[:, d], v_send.at[k], v_recv.at[k], (sib, z)) for k, d in enumerate(same_core)]
    part_copies = [push(out_sum.at[d[0]], out_part.at[me], o_send.at[1, k], o_recv.at[1, k], d) for k, d in enumerate(c_peers)]

    def head_weights(half):
        if half == 0:
            head_acc[...] = jnp.zeros_like(head_acc)

        @pl.loop(0, count // 2)
        def _(i):
            first, second = None, None
            for part in range(2):
                c = 2 * i + part
                slot, at = place(c, half)
                here = held[slot, pl.ds(pl.multiple_of(at, block_len), block_len), :]
                one, two = dot_tn(send[half, c, :block_len, :], here), dot_tn(sorted_dv[c], here)
                first, second = (one, two) if first is None else (first + one, second + two)
            head_acc[:2 * HEAD, :] += first
            head_acc[2 * HEAD:, :] += second[HEAD:]

    @pl.loop(0, runs)
    def _(run):
        key_run(run)

        @pl.when(run == 0)
        def _():
            start(tok_loads)

        @pl.when(run == runs // 2 - 1)
        def _():
            pack_half(0)
            start(swaps[0])
            for k in range(len(same_core)):
                gathers[k].wait_recv()
                relays[k].start()
                weights[k].wait_recv()
                others[k].start()
            wait(gout_copies)
            summed = out_zone[0].astype(jnp.float32)
            for k in range(1, owners):
                summed = summed + out_zone[k].astype(jnp.float32)
            out_sum[...] = summed.astype(low).reshape(out_sum.shape)
            start(part_copies)
            out_part[me] = out_sum[me]
            wait(tok_loads)
            head_weights(0)

    pack_half(1)
    start(swaps[1])
    wait(part_copies)
    summed = out_part[0].astype(jnp.float32)
    for k in range(1, count):
        summed = summed + out_part[k].astype(jnp.float32)
    out_own[...] = summed.astype(low)
    last_copies = start([push(out_own, out_all.at[me], o_send.at[2, k], o_recv.at[2, k], d) for k, d in enumerate(c_peers)])
    out_all[me] = out_own[...]
    wait(own_got + own_relay + relays)

    mixed_slot = rows // RUN
    share = owners * 2 * per
    mixed_loads = []
    for c in range(count):
        slot, at = divmod(c * share, RUN)
        mixed_loads.append(pltpu.make_async_copy(all_ref.at[c], held.at[mixed_slot + slot, pl.ds(at, share)], own_sem.at[3 + rows // RUN + c]))
    start(mixed_loads)
    head_weights(1)
    for c in range(owners):
        zsend[c, :3 * HEAD, :] = head_acc[:, c * lanes:(c + 1) * lanes].astype(low)
    z_copies = start([push(zsend.at[d[1]], zone.at[z], z_send.at[k], z_recv.at[k], d) for k, d in enumerate(z_peers)])
    zone[z] = zsend[z]
    wait(mixed_loads)
    step = HALF
    chunks = ffn // step
    wide_slot = mixed_slot + count * share // RUN

    def of_expert(kind, e):
        parts = []
        for slot in range(mixed_slot, wide_slot):
            value = held[slot].reshape(RUN // share, owners, 2, own_experts, groups, width)
            parts.append(value[:, :, kind, e].reshape(-1, width))
        return jnp.concatenate(parts, axis=0)

    def expert_part(e):
        mixed, grad_out = of_expert(0, e), of_expert(1, e)
        copies = []

        @pl.loop(0, chunks)
        def _(i):
            at = span(i, step)
            to = span(lax.rem(i, 2), step)
            active, slope = gelu_parts(dot_nn(mixed, up[e, :, at]))
            held[wide_slot + chunks * e + i // 2, to, :] = active.astype(low)
            slot = wide_slot + chunks * e + chunks // 2 + i // 2
            held[slot, to, :] = (dot_nt(grad_out, down[e, at, :]) * slope).astype(low)

        for i in range(chunks):
            slot = wide_slot + chunks * e + i // 2
            at, to = pl.ds(i * step, step), pl.ds(i % 2 * step, step)
            sem = own_sem.at[3 + rows // RUN + count + 2 * (chunks * e + i)]
            copies.append(pltpu.make_async_copy(held.at[slot, to], act_ref.at[e, :, at], sem))
            sem = own_sem.at[4 + rows // RUN + count + 2 * (chunks * e + i)]
            copies.append(pltpu.make_async_copy(held.at[slot + chunks // 2, to], gpre_ref.at[e, :, at], sem))
        return start(copies)

    stores = expert_part(0)
    wait(z_copies)
    summed = zone[0].astype(jnp.float32)
    for k in range(1, owners):
        summed = summed + zone[k].astype(jnp.float32)
    total[...] = summed.astype(low)
    c_copies = start([push(total, totals.at[me], c_send.at[k], c_recv.at[k], d) for k, d in enumerate(c_peers)])
    totals[me] = total[...]
    for e in range(1, own_experts):
        stores += expert_part(e)
    wait(swaps[0] + swaps[1] + shares + others)
    flat_weight = weight[...].reshape(width, -1)
    parts = []
    for half in range(2):
        queries, keys, values = [], [], []
        for h in range(count):
            front, back = landing[half, h, :block_len, :], landing[half, h, block_len:, :]
            queries.append(front[:, :HEAD])
            keys.append(front[:, HEAD:])
            values.append(jnp.concatenate([back[:, :HEAD], back[:, HEAD:]], axis=0))
        parts.append(dot_nt(jnp.concatenate(queries + keys + values, axis=1), flat_weight))
    wait(layer_copy)
    first, second = ghidden[:block_len, :] + parts[0], ghidden[block_len:, :] + parts[1]
    wide_out[:block_len, :], wide_out[block_len:, :] = ordered(first, second, in_order)
    stores += start([pltpu.make_async_copy(wide_out, gtok_ref, own_sem.at[2])])
    wait(last_copies)
    out_ref[...] = out_all[...].astype(jnp.float32).reshape(out_ref.shape)
    wait(c_copies)
    small = None
    turned = []
    for c in range(count):
        turned.append(totals[c, :3 * HEAD, :].astype(jnp.float32).T)
        part = totals[c, 3 * HEAD:, :].astype(jnp.float32)
        small = part if small is None else small + part
    sums_ref[...] = small
    for kind in range(3):
        at = slice(HEAD * kind, HEAD * (kind + 1))
        gq_ref[:, HEAD * count * kind:HEAD * count * (kind + 1)] = jnp.concatenate([part[:, at] for part in turned], axis=1)
    wait(stores)
    for copy in gathers + weights:
        copy.wait_send()


def layer(table, gid_row, segs, tokens, cot, w_qkv, w_out, w_router, ln_gain, ln_bias, w_up, w_down, groups, count, owners):
    own_rows, width = tokens.shape
    experts = w_router.shape[1]
    blocks, block_len = table.shape[0], own_rows // 2
    rows = blocks * block_len
    runs = rows // RUN
    own_experts, _, ffn = w_up.shape
    lanes, wide_qkv = w_qkv.shape
    smalls = 16
    height = 3 * HEAD + smalls
    per = experts * groups // owners
    wide = (own_experts, count * owners * groups, ffn)
    share = (owners * 2 * per, width)
    part = (count, lanes // count, width)
    swap = (2, count, block_len + block_len // 2, 2 * HEAD)
    gout = (owners, lanes, width)
    sent = (owners, 2, per, width)
    attended = (2, count, block_len // 2, 2 * HEAD)
    head_grad = (count, block_len, 2 * HEAD)
    low, full = jnp.bfloat16, jnp.float32
    scratch = [
        (tokens.shape, low), (tokens.shape, low), ((lanes, 3 * HEAD), low), ((smalls, lanes), low), ((owners, lanes, 3 * HEAD), low),
        ((owners,) + w_out.shape, low), ((owners, smalls, lanes), low), ((owners, lanes // count, wide_qkv), low), (attended, low),
        (attended, low), (sent, low), (share, low), (sent, low), (sent, low), (w_up.shape, low), (w_down.shape, low),
        ((rows, 2 * HEAD), low), ((rows, 2 * HEAD), low), ((rows, 2 * HEAD), low), ((rows, 2 * HEAD), full),
        ((runs * runs, RUN, HALF), low), ((runs, HALF, HALF), low), (head_grad, low), (head_grad, low),
        (tokens.shape, full), (tokens.shape, full), ((rows, 2 * HEAD), low), ((HEAD, rows), low), ((HEAD, rows), low),
        ((HEAD, RUN), full), ((HEAD, RUN), full), ((3 * HEAD, width), full), (swap, low), (swap, low),
        ((owners, count, lanes // count, wide_qkv), low), ((owners, height, lanes), low), ((owners, height, lanes), low),
        ((height, lanes), low), ((count, height, lanes), low), (gout, low), (gout, low), (part, low), (part, low), (part[1:], low),
        (part, low),
    ]
    owns = 3 + rows // RUN + count + 2 * own_experts * (ffn // HALF)
    to_z, to_c = owners - 1, count - 1
    sems = [
        (2 * own_experts,), (owns,), (2, 3, 2), (2, 2, 2), (2, 2), (2, 4, 2), (2, 4, 2), (4, to_z), (4, to_z),
        (2, to_c), (2, to_c), (2, to_z), (2, to_z), (2, to_z), (2, to_z), (to_c,), (to_c,), (2, to_c), (2, to_c),
        (to_z,), (to_z,), (to_c,), (to_c,), (3, to_c), (3, to_c), (3,), (3,), (4,), (4,), (3,), (3,), (4,), (4,),
    ]
    return pl.pallas_call(
        functools.partial(layer_body, experts, groups, blocks),
        out_shape=(
            jax.ShapeDtypeStruct((lanes, 3 * width), full),
            jax.ShapeDtypeStruct((lanes, width), full),
            jax.ShapeDtypeStruct((smalls, lanes), full),
            jax.ShapeDtypeStruct(tokens.shape, full),
            jax.ShapeDtypeStruct(tokens.shape, full),
            jax.ShapeDtypeStruct(wide, low),
            jax.ShapeDtypeStruct(wide, low),
            jax.ShapeDtypeStruct((count,) + share, low),
            jax.ShapeDtypeStruct((rows // RUN, RUN, width), low),
        ),
        in_specs=[SMEM] + [VMEM] * 9 + [ANY] * 2,
        out_specs=(VMEM,) * 3 + (ANY,) * 6,
        scratch_shapes=[pltpu.VMEM(shape, dtype) for shape, dtype in scratch] + [pltpu.SemaphoreType.DMA(shape) for shape in sems],
        compiler_params=pltpu.CompilerParams(collective_id=1, has_side_effects=True, vmem_limit_bytes=LIMIT),
        cost_estimate=cost(130),
        name="layer",
    )(table, gid_row, segs, tokens, cot, w_qkv, w_out, w_router.T, ln_gain[None], ln_bias[None], w_up, w_down)


def expert_grad_body(experts, passed, mixed_ref, grad_ref, act_ref, gpre_ref, small_ref, *refs):
    sources, outs = refs[:passed], refs[passed + 5:]
    gup_ref, gdown_ref, router_ref, gain_ref, bias_ref = refs[passed:passed + 5]
    width = gup_ref.shape[1]
    for source, out in zip(sources, outs):
        out[...] = source[...]
    router_ref[...] = small_ref[:experts]
    gain_ref[...] = small_ref[experts:experts + 1]
    bias_ref[...] = small_ref[experts + 1:experts + 2]
    gup_ref[0] = dot_tn(mixed_ref[...].reshape(-1, width), gpre_ref[0])
    gdown_ref[0] = dot_tn(act_ref[0], grad_ref[...].reshape(-1, width))


def expert_grads(gathered, active, grad_pre, small, passed, groups, experts):
    own, rows, ffn = active.shape
    step = ffn
    steps = ffn // step
    sources, width = gathered.shape[0], gathered.shape[3]
    view = gathered.reshape(sources, 2, own, groups, width)
    lanes = small.shape[1]
    full = jnp.float32
    slices = [pl.BlockSpec((x.shape[0] // (own * steps), x.shape[1]), lambda e, f: (e * steps + f, 0)) for x in passed]
    return pl.pallas_call(
        functools.partial(expert_grad_body, experts, len(passed)),
        grid=(own, steps),
        out_shape=[
            jax.ShapeDtypeStruct((own, width, ffn), full), jax.ShapeDtypeStruct((own, ffn, width), full),
            jax.ShapeDtypeStruct((experts, lanes), full), jax.ShapeDtypeStruct((1, lanes), full), jax.ShapeDtypeStruct((1, lanes), full),
        ] + [jax.ShapeDtypeStruct(x.shape, x.dtype) for x in passed],
        in_specs=[
            pl.BlockSpec((sources, 1, 1, groups, width), lambda e, f: (0, 0, e, 0, 0)),
            pl.BlockSpec((sources, 1, 1, groups, width), lambda e, f: (0, 1, e, 0, 0)),
            pl.BlockSpec((1, rows, step), lambda e, f: (e, 0, f)),
            pl.BlockSpec((1, rows, step), lambda e, f: (e, 0, f)),
            pl.BlockSpec(small.shape, lambda e, f: (0, 0)),
        ] + slices,
        out_specs=[
            pl.BlockSpec((1, width, step), lambda e, f: (e, 0, f)), pl.BlockSpec((1, step, width), lambda e, f: (e, f, 0)),
            pl.BlockSpec((experts, lanes), lambda e, f: (0, 0)), pl.BlockSpec((1, lanes), lambda e, f: (0, 0)),
            pl.BlockSpec((1, lanes), lambda e, f: (0, 0)),
        ] + slices,
        compiler_params=pltpu.CompilerParams(vmem_limit_bytes=LIMIT),
        cost_estimate=cost(10),
        name="expert_grads",
    )(view, view, active, grad_pre, small, *passed)


def fast_device(
    tokens, cotangent, block_table, seg_ids, group_ids, w_qkv, w_out, w_router, ln_gain, ln_bias, w_up, w_down
):
    ctx_count, z_count = lax.axis_size("ctx"), lax.axis_size("fsdp")
    tok_rows, cot_rows = tokens[0], cotangent[0]
    rows, width = tok_rows.shape
    experts = w_router.shape[1]
    groups = rows // GROUP_SIZE
    grad_qkv, grad_out, small, layer_out, grad_tokens, active, grad_pre, gathered, unused = layer(
        block_table, group_ids, seg_ids, tok_rows, cot_rows, w_qkv, w_out, w_router, ln_gain, ln_bias, w_up, w_down, groups, ctx_count,
        z_count,
    )
    gathered = gathered.reshape(ctx_count * z_count, 2, experts * groups // z_count, width)
    grad_up, grad_down, grad_router, grad_gain, grad_bias, layer_out, grad_tokens, grad_qkv, grad_out = expert_grads(
        gathered, active, grad_pre, small, [layer_out, grad_tokens, grad_qkv, grad_out], groups, experts
    )
    return (
        layer_out[None],
        grad_tokens[None],
        grad_qkv,
        grad_out,
        grad_router.T,
        grad_gain[0],
        grad_bias[0],
        grad_up,
        grad_down,
    )


def solution(mesh):
    placed = (
        P("fsdp", "ctx", None),
        P("fsdp", "ctx", None),
        P(),
        P("fsdp", None),
        P("fsdp", "ctx"),
        P("fsdp", None),
        P("fsdp", None),
        P("fsdp", None),
        P("fsdp"),
        P("fsdp"),
        P("fsdp", None, None),
        P("fsdp", None, None),
    )
    step = fast_device if mesh.shape["ctx"] == HEADS else on_device
    return jax.shard_map(
        step,
        mesh=mesh,
        in_specs=placed,
        out_specs=(
            P("fsdp", "ctx", None),
            P("fsdp", "ctx", None),
            P("fsdp", None),
            P("fsdp", None),
            P("fsdp", None),
            P("fsdp"),
            P("fsdp"),
            P("fsdp", None, None),
            P("fsdp", None, None),
        ),
        check_vma=False,
    )
```

```python
import functools

import jax
import jax.numpy as jnp
from jax import lax
from jax.experimental import pallas as pl
from jax.experimental.pallas import tpu as pltpu
from jax.sharding import PartitionSpec as P

HEADS = 8
HEAD = 64
GROUP_SIZE = 32
KEY_BLOCK = 2048


highest = lax.Precision.HIGHEST
neg_large = -1e30
epsilon = 1e-05
gelu_coef = 0.7978845608028654
gelu_cubic = 0.044715


def contract_rows(left, right):
    return lax.dot_general(
        left, right, (((0,), (0,)), ((), ())), preferred_element_type=jnp.float32
    )


def contract_cols(left, right):
    return lax.dot_general(
        left, right, (((1,), (1,)), ((), ())), preferred_element_type=jnp.float32
    )


def gelu_slope(value):
    inner = gelu_coef * (value + gelu_cubic * value * value * value)
    tangent = jnp.tanh(inner)
    return 0.5 * (1.0 + tangent) + 0.5 * value * (1.0 - tangent * tangent) * gelu_coef * (
        1.0 + 3.0 * gelu_cubic * value * value
    )


def expert_forward(mixed_low, up_weight, down_weight):
    pre = jnp.einsum("ged,edh->geh", mixed_low, up_weight, preferred_element_type=jnp.float32)
    active = jax.nn.gelu(pre, approximate=True).astype(jnp.bfloat16)
    result = jnp.einsum("geh,ehd->ged", active, down_weight, preferred_element_type=jnp.float32)
    return (pre, active, result.astype(jnp.bfloat16))


def expert_backward(mixed_low, pre, active, grad_result, up_weight, down_weight):
    grad_act = jnp.einsum(
        "ged,ehd->geh", grad_result, down_weight, preferred_element_type=jnp.float32
    )
    grad_pre = (grad_act * gelu_slope(pre)).astype(jnp.bfloat16)
    grad_down_part = jnp.einsum(
        "geh,ged->ehd", active, grad_result, preferred_element_type=jnp.float32
    )
    grad_up_part = jnp.einsum(
        "ged,geh->edh", mixed_low, grad_pre, preferred_element_type=jnp.float32
    )
    grad_mixed = jnp.einsum("geh,edh->ged", grad_pre, up_weight, preferred_element_type=jnp.float32)
    return (grad_up_part, grad_down_part, grad_mixed.astype(jnp.bfloat16))


def on_device(
    tokens,
    cotangent,
    block_table,
    seg_ids,
    group_ids,
    w_qkv,
    w_out,
    w_router,
    ln_gain,
    ln_bias,
    w_up,
    w_down,
):
    tok_rows = tokens[0]
    tok_count = tok_rows.shape[0]
    width = tok_rows.shape[1]
    expert_count = w_router.shape[1]
    ctx_index = lax.axis_index("ctx")
    full_rows = seg_ids.shape[1]
    block_len = full_rows // block_table.shape[0]
    row_ids = jnp.arange(full_rows, dtype=jnp.int32)
    key_pos = jnp.take(block_table, row_ids // block_len) * block_len + row_ids % block_len
    key_seg = seg_ids[0]
    pos_rows = lax.dynamic_slice_in_dim(key_pos, ctx_index * tok_count, tok_count)
    seg_rows = lax.dynamic_slice_in_dim(key_seg, ctx_index * tok_count, tok_count)
    scale = HEAD ** (-0.5)
    qkv_full, out_full, router_full, gain_full, bias_full = (
        lax.all_gather(w_qkv, "fsdp", axis=0, tiled=True),
        lax.all_gather(w_out, "fsdp", axis=0, tiled=True),
        lax.all_gather(w_router, "fsdp", axis=0, tiled=True),
        lax.all_gather(ln_gain, "fsdp", axis=0, tiled=True),
        lax.all_gather(ln_bias, "fsdp", axis=0, tiled=True),
    )
    qkv = jnp.dot(tok_rows, qkv_full, preferred_element_type=jnp.float32).astype(jnp.bfloat16)
    query_heads = qkv[:, :width].reshape(tok_count, HEADS, HEAD)
    key_all, val_all = (
        lax.all_gather(qkv[:, width : 2 * width], "ctx", axis=0, tiled=True),
        lax.all_gather(qkv[:, 2 * width :], "ctx", axis=0, tiled=True),
    )
    key_heads = key_all.reshape(full_rows, HEADS, HEAD)
    val_heads = val_all.reshape(full_rows, HEADS, HEAD)
    block_count = full_rows // KEY_BLOCK
    block_ids = jnp.arange(block_count, dtype=jnp.int32)

    def block_scores(index):
        start = index * KEY_BLOCK
        key_block = lax.dynamic_slice_in_dim(key_heads, start, KEY_BLOCK, 0)
        val_block = lax.dynamic_slice_in_dim(val_heads, start, KEY_BLOCK, 0)
        pos_block = lax.dynamic_slice_in_dim(key_pos, start, KEY_BLOCK, 0)
        seg_block = lax.dynamic_slice_in_dim(key_seg, start, KEY_BLOCK, 0)
        scores = (
            jnp.einsum("qhd,khd->hqk", query_heads, key_block, preferred_element_type=jnp.float32)
            * scale
        )
        allowed = (pos_block[None, :] <= pos_rows[:, None]) & (
            (seg_block[None, :] == 0) | (seg_block[None, :] == seg_rows[:, None])
        )
        return (scores, allowed[None], key_block, val_block)

    def lse_step(carry, index):
        top, total = carry
        scores, allowed, key_block, val_block = block_scores(index)
        masked = jnp.where(allowed, scores, neg_large)
        new_top = jnp.maximum(top, jnp.max(masked, axis=-1))
        weights = jnp.where(allowed, jnp.exp(masked - new_top[..., None]), 0.0)
        return ((new_top, total * jnp.exp(top - new_top) + jnp.sum(weights, axis=-1)), None)

    start_top = jnp.full((HEADS, tok_count), neg_large, jnp.float32)
    (top, total), unused = lax.scan(
        lse_step, (start_top, jnp.zeros((HEADS, tok_count), jnp.float32)), block_ids
    )
    log_total = top + jnp.log(total)

    def block_probs(index):
        scores, allowed, key_block, val_block = block_scores(index)
        probs = jnp.where(allowed, jnp.exp(scores - log_total[..., None]), 0.0)
        return (probs, key_block, val_block)

    def value_step(accum, index):
        probs, key_block, val_block = block_probs(index)
        return (
            accum
            + jnp.einsum(
                "hqk,khd->qhd",
                probs.astype(jnp.bfloat16),
                val_block,
                preferred_element_type=jnp.float32,
            ),
            None,
        )

    accum, unused = lax.scan(
        value_step, jnp.zeros((tok_count, HEADS, HEAD), jnp.float32), block_ids
    )
    attended = accum.reshape(tok_count, width).astype(jnp.bfloat16)
    hidden = tok_rows.astype(jnp.float32) + jnp.dot(
        attended, out_full, preferred_element_type=jnp.float32
    )
    center = hidden - jnp.mean(hidden, axis=-1, keepdims=True)
    inv_dev = lax.rsqrt(jnp.mean(center * center, axis=-1, keepdims=True) + epsilon)
    unit = center * inv_dev
    gain_f = gain_full.astype(jnp.float32)
    normed_low = (unit * gain_f + bias_full.astype(jnp.float32)).astype(jnp.bfloat16)
    logits = jnp.dot(normed_low, router_full, preferred_element_type=jnp.float32)
    groups_dev = tok_count // GROUP_SIZE
    local_group = group_ids[0] - ctx_index * groups_dev
    member = (local_group[:, None] == jnp.arange(groups_dev, dtype=jnp.int32)[None, :]).astype(
        jnp.float32
    )
    expo = jnp.exp(logits)
    group_total = jnp.dot(member.T, expo, precision=highest)
    mix_weights = expo / jnp.dot(member, group_total, precision=highest)
    weights_low = mix_weights.astype(jnp.bfloat16)
    mixing = member.astype(jnp.bfloat16).T[:, None, :] * weights_low.T[None, :, :]
    mixing_flat = mixing.reshape(groups_dev * expert_count, tok_count)
    mixed_low = jnp.dot(mixing_flat, normed_low, preferred_element_type=jnp.float32).astype(
        jnp.bfloat16
    )
    mixed_low = mixed_low.reshape(groups_dev, expert_count, width)
    owner_mixed = lax.all_to_all(mixed_low, "fsdp", split_axis=1, concat_axis=0, tiled=True)
    pre, active, owner_out = expert_forward(owner_mixed, w_up, w_down)
    expert_out = lax.all_to_all(owner_out, "fsdp", split_axis=0, concat_axis=1, tiled=True)
    expert_flat = expert_out.reshape(groups_dev * expert_count, width)
    spread = contract_rows(mixing_flat, expert_flat)
    layer_out = hidden + spread
    cot_rows = cotangent[0]
    cot_f = cot_rows.astype(jnp.float32)
    grad_expert = jnp.dot(mixing_flat, cot_rows, preferred_element_type=jnp.float32).astype(
        jnp.bfloat16
    )
    grad_expert = grad_expert.reshape(groups_dev, expert_count, width)
    coef = contract_cols(cot_rows, expert_flat).reshape(tok_count, groups_dev, expert_count)
    grad_mix_spread = jnp.sum(coef * member[:, :, None], axis=1)
    owner_grad = lax.all_to_all(grad_expert, "fsdp", split_axis=1, concat_axis=0, tiled=True)
    grad_up_own, grad_down_own, owner_back = expert_backward(
        owner_mixed, pre, active, owner_grad, w_up, w_down
    )
    grad_mixed = lax.all_to_all(owner_back, "fsdp", split_axis=0, concat_axis=1, tiled=True)
    grad_mixed_flat = grad_mixed.reshape(groups_dev * expert_count, width)
    grad_norm_mix = contract_rows(mixing_flat, grad_mixed_flat)
    grad_mixing = contract_cols(grad_mixed_flat, normed_low).reshape(
        groups_dev, expert_count, tok_count
    )
    grad_mix_mixing = jnp.sum(grad_mixing * member.T[:, None, :], axis=0).T
    grad_mix = grad_mix_spread + grad_mix_mixing
    product = mix_weights * grad_mix
    token_dot = jnp.dot(member, jnp.dot(member.T, product, precision=highest), precision=highest)
    grad_logits = (product - mix_weights * token_dot).astype(jnp.bfloat16)
    grad_router_part = contract_rows(normed_low, grad_logits)
    grad_norm_router = contract_cols(grad_logits, router_full)
    grad_normed = grad_norm_mix + grad_norm_router
    grad_gain_part = jnp.sum(grad_normed * unit, axis=0)
    grad_bias_part = jnp.sum(grad_normed, axis=0)
    scaled = grad_normed * gain_f
    grad_hidden = cot_f + inv_dev * (
        scaled
        - jnp.mean(scaled, axis=-1, keepdims=True)
        - unit * jnp.mean(scaled * unit, axis=-1, keepdims=True)
    )
    grad_branch = grad_hidden.astype(jnp.bfloat16)
    grad_out_part = contract_rows(attended, grad_branch)
    grad_heads = (
        contract_cols(grad_branch, out_full).astype(jnp.bfloat16).reshape(tok_count, HEADS, HEAD)
    )
    delta = jnp.sum(grad_heads.astype(jnp.float32) * accum, axis=-1).T

    def grad_step(grad_query, index):
        probs, key_block, val_block = block_probs(index)
        grad_probs = jnp.einsum(
            "qhd,khd->hqk", grad_heads, val_block, preferred_element_type=jnp.float32
        )
        grad_scores = (probs * (grad_probs - delta[..., None])).astype(jnp.bfloat16)
        grad_query = (
            grad_query
            + jnp.einsum("hqk,khd->qhd", grad_scores, key_block, preferred_element_type=jnp.float32)
            * scale
        )
        grad_key = (
            jnp.einsum("hqk,qhd->khd", grad_scores, query_heads, preferred_element_type=jnp.float32)
            * scale
        )
        grad_val = jnp.einsum(
            "hqk,qhd->khd",
            probs.astype(jnp.bfloat16),
            grad_heads,
            preferred_element_type=jnp.float32,
        )
        return (grad_query, (grad_key, grad_val))

    grad_query, (grad_keys, grad_vals) = lax.scan(
        grad_step, jnp.zeros((tok_count, HEADS, HEAD), jnp.float32), block_ids
    )
    grad_key_own, grad_val_own = (
        lax.psum_scatter(
            grad_keys.reshape(full_rows, width), "ctx", scatter_dimension=0, tiled=True
        ),
        lax.psum_scatter(
            grad_vals.reshape(full_rows, width), "ctx", scatter_dimension=0, tiled=True
        ),
    )
    grad_qkv_low = jnp.concatenate(
        [grad_query.reshape(tok_count, width), grad_key_own, grad_val_own], axis=1
    ).astype(jnp.bfloat16)
    grad_qkv_part = contract_rows(tok_rows, grad_qkv_low)
    grad_tokens = grad_hidden + contract_cols(grad_qkv_low, qkv_full)
    dense = (
        lax.psum_scatter(grad_qkv_part, "fsdp", scatter_dimension=0, tiled=True),
        lax.psum_scatter(grad_out_part, "fsdp", scatter_dimension=0, tiled=True),
        lax.psum_scatter(grad_router_part, "fsdp", scatter_dimension=0, tiled=True),
        lax.psum_scatter(grad_gain_part, "fsdp", scatter_dimension=0, tiled=True),
        lax.psum_scatter(grad_bias_part, "fsdp", scatter_dimension=0, tiled=True),
    )
    totals = lax.psum(
        (dense[0], dense[1], dense[2], dense[3], dense[4], grad_up_own, grad_down_own), "ctx"
    )
    return (
        layer_out[None],
        grad_tokens[None],
        totals[0],
        totals[1],
        totals[2],
        totals[3],
        totals[4],
        totals[5],
        totals[6],
    )


def cost(microseconds):
    return pl.CostEstimate(flops=int(microseconds * 1.15e9), bytes_accessed=1 << 20, transcendentals=0)


LOG2E = 1.4426950408889634
HIDE = -1e30
RUN = 1024
HALF = 512
VMEM = pl.BlockSpec(memory_space=pltpu.VMEM)
SMEM = pl.BlockSpec(memory_space=pltpu.SMEM)
ANY = pl.BlockSpec(memory_space=pl.ANY)
LIMIT = 60 << 20


def dot_nn(left, right):
    return lax.dot_general(left, right, (((1,), (0,)), ((), ())), preferred_element_type=jnp.float32)


def dot_nt(left, right):
    return lax.dot_general(left, right, (((1,), (1,)), ((), ())), preferred_element_type=jnp.float32)


def dot_tn(left, right):
    return lax.dot_general(left, right, (((0,), (0,)), ((), ())), preferred_element_type=jnp.float32)


def split3(value):
    one = value.astype(jnp.bfloat16)
    rest = value - one.astype(jnp.float32)
    two = rest.astype(jnp.bfloat16)
    three = (rest - two.astype(jnp.float32)).astype(jnp.bfloat16)
    return one, two, three


def span(index, size, width=None):
    return pl.ds(pl.multiple_of(index * size, size), size if width is None else width)


MESH = pl.DeviceIdType.MESH


def flip(index, bit):
    return index + bit - 2 * bit * lax.rem(index // bit, 2)


def meet(devices):
    barrier = pltpu.get_barrier_semaphore()
    for device in devices:
        pl.semaphore_signal(barrier, inc=1, device_id=device, device_id_type=MESH)
    pl.semaphore_wait(barrier, len(devices))


def push(src, dst, send_sem, recv_sem, device):
    return pltpu.make_async_remote_copy(
        src_ref=src, dst_ref=dst, send_sem=send_sem, recv_sem=recv_sem, device_id=device, device_id_type=MESH
    )


def norm_parts(hidden):
    center = hidden - jnp.mean(hidden, axis=-1, keepdims=True)
    inv_dev = lax.rsqrt(jnp.mean(center * center, axis=-1, keepdims=True) + epsilon)
    return center * inv_dev, inv_dev


def gelu_parts(value):
    square = value * value
    tangent = jnp.tanh(value * (square * (gelu_coef * gelu_cubic) + gelu_coef))
    half = 0.5 * tangent + 0.5
    rise = value * (square * (3.0 * gelu_coef * gelu_cubic) + gelu_coef)
    return value * half, half + half * (1.0 - tangent) * rise


def boundaries(seg_ref, lane):
    segs = seg_ref[...]
    begin = jnp.zeros(lane.shape, jnp.int32)
    end = jnp.zeros(lane.shape, jnp.int32)
    for c in range(1, 10):
        total = jnp.sum((segs < c).astype(jnp.int32), axis=1, keepdims=True)
        begin = jnp.where(lane == HEAD - 1 + c, total, begin)
        end = jnp.where(lane == HEAD - 2 + c, total, end)
    return begin, jnp.where(lane == HEAD + 8, 0, end)


def layer_body(
    experts, groups, blocks, table_ref, gid_ref, seg_ref, tok_ref, cot_ref, wq_ref, wo_ref, router_ref, gain_ref, bias_ref, up_ref, down_ref,
    gq_ref, out_ref, sums_ref, layer_ref, gtok_ref, act_ref, gpre_ref, all_ref, toks_ref,
    tok, cot, head_buf, pack_buf, heads, wo, pack, zparts, att_send, att, msend, zin, bsend, bin_, up, down, qf, kf, vf, stat, held, late_held,
    ghead_out, ghead, wide_out, ghidden, dof, qt, dot, dk_acc, dv_acc, head_acc, send, landing, weight, zsend, zone, total, totals,
    out_mine, out_zone, out_sum, out_part, out_own, out_all,
    load_sem, own_sem, t_send, t_recv, d_recv, n_send, n_recv, y_send, y_recv, a_send, a_recv, m_send, m_recv, b_send, b_recv,
    h_send, h_recv, s_send, s_recv, z_send, z_recv, c_send, c_recv, o_send, o_recv, g_send, g_recv, r_send, r_recv, w_send, w_recv,
    v_send, v_recv,
):
    me, z = lax.axis_index("ctx"), lax.axis_index("fsdp")
    count, block_len = blocks // 2, tok_ref.shape[0] // 2
    own_rows, width = tok_ref.shape
    owners, own_experts, ffn = msend.shape[0], up_ref.shape[0], up_ref.shape[2]
    flat, per = experts * groups, experts * groups // owners
    rows = blocks * block_len
    runs = rows // RUN
    low = jnp.bfloat16
    dq_acc, qk, dv_rows, sorted_dv = stat, qf, vf, ghead_out

    def start(copies):
        for copy in copies:
            copy.start()
        return copies

    def wait(copies):
        for copy in copies:
            copy.wait()

    loads = []
    for e in range(own_experts):
        loads += [pltpu.make_async_copy(up_ref.at[e], up.at[e], load_sem.at[2 * e])]
        loads += [pltpu.make_async_copy(down_ref.at[e], down.at[e], load_sem.at[2 * e + 1])]
    start(loads)

    def mask(condition):
        return jnp.broadcast_to(jnp.where(condition, 1.0, 0.0), (1, 2 * HEAD))

    def hold_masks(c=None, j=None):
        pairs = [(c, i) if j is None else (i, j) for i in range(count)]
        return [mask(jnp.minimum(table_ref[2 * c], table_ref[2 * c + 1]) == j).astype(low) for c, j in pairs]

    in_order = mask(table_ref[2 * me] < table_ref[2 * me + 1])[:, :1]

    def blend(masks, values):
        out = None
        for weigh, value in zip(masks, values):
            out = weigh * value if out is None else out + weigh * value
        return out

    def ordered(first, second, weigh):
        return weigh * first + (1 - weigh) * second, weigh * second + (1 - weigh) * first

    sib, xn, yn, diag = flip(me, 1), flip(me, 2), flip(me, 4), flip(flip(me, 2), 4)
    same_core = [xn, yn, diag]
    z_peers = [(me, lax.rem(z + k, owners)) for k in range(1, owners)]
    c_peers = [(jnp.bitwise_xor(me, k), z) for k in range(1, count)]
    barrier = pltpu.get_barrier_semaphore()
    for d in z_peers + c_peers:
        pl.semaphore_signal(barrier, inc=1, device_id=d, device_id_type=MESH)
    tok[:block_len, :], tok[block_len:, :] = ordered(tok_ref[:block_len, :], tok_ref[block_len:, :], in_order.astype(low))
    pl.semaphore_wait(barrier, len(z_peers + c_peers))

    piece = block_len // 2
    per_slot = RUN // block_len

    def place(device, half):
        return 2 * half + device // per_slot, lax.rem(device, per_slot) * block_len

    def there(device, half, k):
        slot, at = place(device, half)
        return held.at[slot, pl.ds(pl.multiple_of(at + k * piece, piece), piece)]

    gone = []

    def go(copies):
        gone.extend(start(copies))

    def here(half, k):
        return tok.at[pl.ds(half * block_len + k * piece, piece)]

    def launch(half):
        slot, at = place(me, half)
        held[slot, pl.ds(pl.multiple_of(at, block_len), block_len), :] = tok[half * block_len:(half + 1) * block_len, :]
        for k in (0, 1):
            go([push(here(half, k), there(me, half, k), t_send.at[half, 0, k], t_recv.at[half, 0, k], (xn, z))])
            go([push(here(half, 1 - k), there(me, half, 1 - k), t_send.at[half, 1, 1 - k], t_recv.at[half, 1, 1 - k], (yn, z))])

    def launch_near(half):
        for k in (0, 1):
            go([push(here(half, k), there(me, half, k), n_send.at[half, 0, k], n_recv.at[half, 0, k], (sib, z))])

    def arrival(device, half, k, sem):
        return push(there(device, half, k), there(device, half, k), t_send.at[half, 0, 0], sem, (sib, z))

    def relay(device, half, k, i):
        block = there(device, half, k)
        return push(block, block, n_send.at[half, i, k], n_recv.at[half, i, k], (sib, z))

    def forward_plan(half):
        plan = []
        for device, k, i, to in ((xn, 0, 0, yn), (yn, 1, 1, xn)):
            block = there(device, half, k)
            plan.append((
                push(block, block, t_send.at[half, 0, 0], t_recv.at[half, i, k], (sib, z)),
                push(block, block, t_send.at[half, 2, k], d_recv.at[half, k], (to, z)),
                push(block, block, n_send.at[half, i + 1, k], n_recv.at[half, i + 1, k], (sib, z)),
            ))
        return plan

    def forward(plan):
        for came, on, near in plan:
            came.wait_recv()
            start([on, near])

    def settle_plan(half):
        plan = [
            (arrival(xn, half, 1, t_recv.at[half, 0, 1]), relay(xn, half, 1, 1)),
            (arrival(yn, half, 0, t_recv.at[half, 1, 0]), relay(yn, half, 0, 2)),
        ]
        plan += [(arrival(diag, half, k, d_recv.at[half, k]), relay(diag, half, k, 3)) for k in (0, 1)]
        near = []
        for k in (0, 1):
            for i, device in enumerate((sib, flip(xn, 1), flip(yn, 1), flip(diag, 1))):
                near.append(arrival(device, half, k, n_recv.at[half, i, k]))
        return plan, near

    def settle(plan, near):
        for came, on in plan:
            came.wait_recv()
            on.start()
        for came in near:
            came.wait_recv()

    launch(0)

    shared = []

    def share(i, shard, whole):
        whole[z] = shard[...]
        shared.append(start([push(shard, whole.at[z], y_send.at[i, k], y_recv.at[i, k], d) for k, d in enumerate(z_peers)]))

    for h in range(count):
        @pl.when(me == h)
        def _():
            cols = [wq_ref[:, width * kind + HEAD * h:width * kind + HEAD * (h + 1)] for kind in range(3)]
            head_buf[...] = jnp.concatenate(cols, axis=1)

    share(0, head_buf, heads)
    launch_near(0)
    parts = [router_ref[...].astype(jnp.float32), gain_ref[...].astype(jnp.float32), bias_ref[...].astype(jnp.float32)]
    parts.append(jnp.zeros((pack_buf.shape[0] - experts - 2, pack_buf.shape[1]), jnp.float32))
    pack_buf[...] = jnp.concatenate(parts, axis=0).astype(low)
    share(1, pack_buf, pack)
    share(2, wo_ref, wo)
    depth = wq_ref.shape[0] // count
    share(3, wq_ref.at[pl.ds(pl.multiple_of(me * depth, depth), depth)], zparts)

    lane = lax.broadcasted_iota(jnp.int32, (1, 2 * HEAD), 1)
    begin, end = boundaries(seg_ref, lane)
    is_flag = (lane >= HEAD) & (lane < HEAD + 8)
    is_one = (lane >= HEAD + 8) & (lane < HEAD + 11)
    ones_v = ((lane >= HEAD) & (lane < HEAD + 3)).astype(jnp.float32)
    scale = HEAD ** (-0.5)

    def projected(half, device):
        at = device % per_slot * block_len
        lanes = device // per_slot * 4 * HEAD
        return held.at[4 + half, at:at + block_len, lanes:lanes + 4 * HEAD]

    def project(half, head_weight):
        for slot in range(count // per_slot):
            to = slice(4 * HEAD * slot, 4 * HEAD * (slot + 1))
            held[4 + half, :, to] = dot_nn(held[2 * half + slot], head_weight).astype(low)

        @pl.loop(0, count, unroll=8)
        def _(j):
            s = j if half == 0 else blocks - 1 - j
            masks = hold_masks(j=j)
            both = blend(masks, [projected(half, c)[:, :2 * HEAD] for c in range(count)]).astype(jnp.float32)
            value = blend(masks, [projected(half, c)[:, 2 * HEAD:] for c in range(count)]).astype(jnp.float32)
            spot = lax.broadcasted_iota(jnp.int32, (block_len, 2 * HEAD), 0) + s * block_len
            mine = (spot >= begin) & (spot < end)
            at = span(s, block_len)
            flag_q = jnp.where(is_flag & jnp.logical_not(mine), 1.0, 0.0)
            flag_k = jnp.where(mine, HIDE, jnp.where(is_one, 1.0, 0.0))
            qf[at, :] = jnp.where(lane < HEAD, both, flag_q).astype(low)
            kf[at, :] = jnp.where(lane < HEAD, pltpu.roll(both, HEAD, 1), flag_k).astype(low)
            vf[at, :] = (value + ones_v).astype(low)
            dot[:, at] = value.T.astype(low)[:HEAD]

    lower = lax.broadcasted_iota(jnp.int32, (HALF, RUN), 0) <= lax.broadcasted_iota(jnp.int32, (HALF, RUN), 1)

    def query_run(run):
        def tile(state, q_at, k_at, size, diagonal):
            scores = dot_nt(kf[k_at, :], qf[q_at, :]) * (scale * LOG2E)
            if diagonal:
                scores = jnp.where(lower[:, :scores.shape[1]], scores, HIDE)
            top, acc = state
            new_top = jnp.maximum(top, jnp.max(scores, axis=0, keepdims=True))
            probs = jnp.exp2(scores - new_top).astype(low)
            values = jnp.concatenate([dot[:, k_at], jnp.ones((HEAD, size), low)], axis=0)
            return new_top, acc * jnp.exp2(top - new_top) + dot_nn(values, probs)

        begin = (jnp.full((1, RUN), HIDE, jnp.float32), jnp.zeros((2 * HEAD, RUN), jnp.float32))
        def both_halves(n, state):
            for part in range(2):
                state = tile(state, span(run, RUN), span(2 * n + part, HALF), HALF, False)
            return state

        whole = lax.fori_loop(0, run, both_halves, begin)
        early, late = span(2 * run, HALF), span(2 * run + 1, HALF)
        whole = tile(whole, span(run, RUN), early, HALF, True)
        first = [part[:, :HALF] for part in whole]
        second = tile([part[:, HALF:] for part in whole], late, late, HALF, True)
        for at, (top, acc) in ((early, first), (late, second)):
            sums = acc[HEAD:]
            result = jnp.concatenate([acc[:HEAD] / sums, top + jnp.log2(sums)], axis=0).T
            stat[at, :] = result
            one, two, three = split3(result * (-1.0 / (scale * LOG2E)))
            old = qf[at, :]
            old = jnp.where(lane == HEAD + 8, one, old)
            old = jnp.where(lane == HEAD + 9, two, old)
            qf[at, :] = jnp.where(lane == HEAD + 10, three, old)

    def pack_attended(half):
        mid = block_len // 2
        ats = [slice(s * block_len, (s + 1) * block_len) for s in (range(count) if half == 0 else range(blocks - 1, count - 1, -1))]

        @pl.loop(0, count, unroll=4)
        def _(c):
            block = blend(hold_masks(c=c), [stat[at, :].astype(low) for at in ats])
            att_send[half, c] = jnp.concatenate([block[:mid, :HEAD], block[mid:, :HEAD]], axis=1)
        att[half, me] = att_send[half, me]

    swaps = [
        [push(att_send.at[half, d[0]], att.at[half, me], a_send.at[half, k], a_recv.at[half, k], d) for k, d in enumerate(c_peers)]
        for half in range(2)
    ]
    saves = [pltpu.make_async_copy(held.at[i], toks_ref.at[i], own_sem.at[3 + i]) for i in range(rows // RUN)]
    cot[:block_len, :], cot[block_len:, :] = ordered(cot_ref[:block_len, :], cot_ref[block_len:, :], in_order.astype(low))
    plans = [forward_plan(half) for half in range(2)]
    for plan in plans:
        for came, on, near in plan:
            gone.extend([on, near])
    settles = [settle_plan(half) for half in range(2)]
    for plan, near in settles:
        gone.extend([on for came, on in plan])
    forward(plans[0])
    settle(*settles[0])
    launch(1)
    launch_near(1)
    wait(shared[0])
    head_weight = heads[...].reshape(width, 3 * HEAD)
    head_weight = jnp.concatenate([head_weight, jnp.zeros((width, HEAD), low)], axis=1)
    project(0, head_weight)

    @pl.loop(0, runs)
    def _(run):
        query_run(run)

        @pl.when(run == 0)
        def _():
            forward(plans[1])

        @pl.when(run == runs // 2 - 1)
        def _():
            pack_attended(0)
            start(swaps[0])
            settle(*settles[1])
            start(saves)
            project(1, head_weight)

    pack_attended(1)
    start(swaps[1])
    for copy in gone:
        copy.wait_send()
    wait(shared[1] + shared[2] + shared[3])

    first_diagonal = runs * (runs - 1)

    def slot_of(run, index, part):
        return run * (2 * runs - 1 - run) + 2 * (index - run - 1) + part

    def probabilities(q_at, k_at, visible):
        scores = dot_nt(qf[q_at, :], kf[k_at, :]) * (scale * LOG2E)
        if visible is not None:
            scores = jnp.where(visible, scores, HIDE)
        return jnp.exp2(scores).astype(low)

    def hold_diagonal():
        early = lax.broadcasted_iota(jnp.int32, (RUN, HALF), 1) <= lax.broadcasted_iota(jnp.int32, (RUN, HALF), 0)
        late = lax.broadcasted_iota(jnp.int32, (HALF, HALF), 1) <= lax.broadcasted_iota(jnp.int32, (HALF, HALF), 0)

        @pl.loop(0, runs)
        def _(run):
            held[first_diagonal + run] = probabilities(span(run, RUN), span(2 * run, HALF), early)
            late_held[run] = probabilities(span(2 * run + 1, HALF), span(2 * run + 1, HALF), late)

    def hold(run):
        @pl.loop(run + 1, runs)
        def _(index):
            for part in range(2):
                held[slot_of(run, index, part)] = probabilities(span(index, RUN), span(2 * run + part, HALF), None)

    hold_diagonal()
    wait(swaps[0] + swaps[1])
    weights = start([push(zparts, weight.at[:, me], w_send.at[k], w_recv.at[k], (d, z)) for k, d in enumerate(same_core)])
    shares = start([push(zparts, weight.at[:, me], v_send.at[3], v_recv.at[3], (sib, z))])
    weight[:, me] = zparts[...]
    quarters = [
        jnp.concatenate([att[half, h, :, HEAD * p:HEAD * (p + 1)] for h in range(count)], axis=1) for half in range(2) for p in range(2)
    ]
    attended = jnp.concatenate(quarters, axis=0)
    out_weight = wo[...].reshape(width, width)
    hidden = tok[...].astype(jnp.float32) + dot_nn(attended, out_weight)
    unit, inv_dev = norm_parts(hidden)
    small_in = jnp.concatenate([pack[k] for k in range(owners)], axis=1)
    gain, bias = small_in[experts:experts + 1].astype(jnp.float32), small_in[experts + 1:experts + 2].astype(jnp.float32)
    normed = (unit * gain + bias).astype(low)
    expo = jnp.exp(dot_nt(small_in, normed)[:experts])
    expo = jnp.broadcast_to(expo[:, None, :], (experts, groups, own_rows)).reshape(flat, own_rows)
    gids = lax.rem(gid_ref[...], groups).astype(jnp.float32)
    gids = jnp.concatenate(ordered(gids[:, :block_len], gids[:, block_len:], in_order), axis=1)
    member = lax.rem(lax.broadcasted_iota(jnp.int32, (flat, 1), 0), groups).astype(jnp.float32) == gids
    expo = jnp.where(member, expo, 0.0)
    mix = expo / jnp.sum(expo, axis=1, keepdims=True)
    mix_low = mix.astype(low)

    def zone_rows(owner, kind):
        return pl.ds(pl.multiple_of((2 * owner + kind) * per, per), per)

    def to_owners(kind, value):
        msend[:, kind] = value.astype(low).reshape(owners, per, width)
        zin[zone_rows(z, kind), :] = msend[z, kind]
        return start([
            push(msend.at[d[1], kind], zin.at[zone_rows(z, kind)], m_send.at[kind, k], m_recv.at[kind, k], d) for k, d in enumerate(z_peers)
        ])

    mixed_copies = to_owners(0, dot_nn(mix_low, normed))
    grad_experts = dot_nn(mix_low, cot[...])
    wait(loads)
    hold(1)
    grad_copies = to_owners(1, grad_experts)

    @pl.loop(2, runs - 1)
    def _(run):
        hold(run)

    wait(mixed_copies)

    def from_sources(kind, e):
        lows_ = [(2 * owner + kind) * per + e * groups for owner in range(owners)]
        return jnp.concatenate([zin[at:at + groups, :] for at in lows_], axis=0)

    def to_sources(kind, e, value):
        bsend[:, kind, e * groups:(e + 1) * groups, :] = value.astype(low).reshape(owners, groups, width)

    def send_back(kind, e):
        at = pl.ds(e * groups, groups)
        bin_[z, kind, at, :] = bsend[z, kind, at, :]
        return start([
            push(bsend.at[d[1], kind, at], bin_.at[z, kind, at], b_send.at[kind, e, k], b_recv.at[kind, e, k], d)
            for k, d in enumerate(z_peers)
        ])

    out_copies, back_copies = [], []
    slopes = []
    for e in range(own_experts):
        active, slope = gelu_parts(dot_nn(from_sources(0, e), up[e]))
        slopes.append(slope)
        to_sources(0, e, dot_nn(active.astype(low), down[e]))
        out_copies += send_back(0, e)
    wait(grad_copies)
    for e in range(own_experts):
        grad_pre = (dot_nt(from_sources(1, e), down[e]) * slopes[e]).astype(low)
        to_sources(1, e, dot_nt(grad_pre, up[e]))
        back_copies += send_back(1, e)
    wait(out_copies)
    expert_out = bin_[:, 0].reshape(flat, width)
    result = hidden + dot_tn(mix_low, expert_out)
    wide_out[:block_len, :], wide_out[block_len:, :] = ordered(result[:block_len], result[block_len:], in_order)
    layer_copy = start([pltpu.make_async_copy(wide_out, layer_ref, own_sem.at[2])])
    grad_mix = dot_nt(expert_out, cot[...])
    wait(saves)
    hold(0)
    wait(back_copies)
    grad_mixed = bin_[:, 1].reshape(flat, width)
    product = mix * (grad_mix + dot_nt(grad_mixed, normed))
    grad_logits = product - mix * jnp.sum(product, axis=1, keepdims=True)
    grad_logits = jnp.sum(grad_logits.reshape(experts, groups, own_rows), axis=1).astype(low)
    pad = jnp.zeros((small_in.shape[0] - experts, own_rows), low)
    grad_logits = jnp.concatenate([grad_logits, pad], axis=0)
    grad_normed = dot_tn(jnp.concatenate([mix_low, grad_logits], axis=0), jnp.concatenate([grad_mixed, small_in], axis=0))
    scaled = grad_normed * gain
    mean = jnp.mean(scaled, axis=-1, keepdims=True)
    grad_hidden = cot[...].astype(jnp.float32) + inv_dev * (scaled - mean - unit * jnp.mean(scaled * unit, axis=-1, keepdims=True))
    branch = grad_hidden.astype(low)
    grad_heads = dot_nt(branch, out_weight).astype(low)
    for h in range(count):
        at = slice(HEAD * h, HEAD * (h + 1))
        ghead_out[h] = jnp.concatenate([grad_heads[:block_len, at], grad_heads[block_len:, at]], axis=1)
    swap = start([push(ghead_out.at[d[0]], ghead.at[me], h_send.at[k], h_recv.at[k], d) for k, d in enumerate(c_peers)])
    ghead[me] = ghead_out[me]
    ghidden[...] = grad_hidden
    out_mine[...] = dot_tn(attended, branch).astype(low).reshape(out_mine.shape)
    gout_copies = start([push(out_mine.at[d[1]], out_zone.at[z], o_send.at[0, k], o_recv.at[0, k], d) for k, d in enumerate(z_peers)])
    out_zone[z] = out_mine[z]
    small = jnp.concatenate(
        [
            dot_nn(grad_logits, normed)[:experts],
            jnp.sum(grad_normed * unit, axis=0, keepdims=True),
            jnp.sum(grad_normed, axis=0, keepdims=True),
            jnp.zeros((small_in.shape[0] - experts - 2, width), jnp.float32),
        ],
        axis=0,
    )
    lanes = width // owners
    for c in range(owners):
        zsend[c, 3 * HEAD:, :] = small[:, c * lanes:(c + 1) * lanes].astype(low)

    def prepare(s, both):
        at = span(s, block_len)
        grad = jnp.where(lane < HEAD, both, 0.0)
        delta = jnp.sum(grad * stat[at, :], axis=1, keepdims=True)
        one, two, three = split3(jnp.broadcast_to(-delta, grad.shape))
        wide = jnp.where(lane == HEAD, one, grad.astype(low))
        wide = jnp.where(lane == HEAD + 1, two, wide)
        dof[at, :] = jnp.where(lane == HEAD + 2, three, wide)
        turned = jnp.where(lane < HEAD, both, pltpu.roll(qf[at, :].astype(jnp.float32), HEAD, 1)).T.astype(low)
        dot[:, at] = turned[:HEAD]
        qt[:, at] = turned[HEAD:]

    wait(swap)
    gathers = start([push(zin, all_ref.at[me], g_send.at[k], g_recv.at[k], (d, z)) for k, d in enumerate(same_core)])
    own_relay = start([push(zin, all_ref.at[me], r_send.at[3], r_recv.at[3], (sib, z))])
    own_got = start([pltpu.make_async_copy(zin, all_ref.at[me], own_sem.at[1])])

    @pl.loop(0, count, unroll=4)
    def _(j):
        both = blend(hold_masks(j=j), [ghead[c] for c in range(count)]).astype(jnp.float32)
        prepare(j, both)
        prepare(blocks - 1 - j, pltpu.roll(both, HEAD, 1))

    tok_loads = [
        pltpu.make_async_copy(toks_ref.at[i], held.at[i], own_sem.at[3 + i]) for i in range(rows // RUN)
    ]

    def key_run(run):
        def tile(q_at, k_at, part, probs, first_k, first_q):
            slope = dot_nt(dof[q_at, :], vf[k_at, :])
            grad = (probs.astype(jnp.float32) * slope).astype(low)
            dv = dot_nn(dot[:, q_at], probs)
            dk = dot_nn(qt[:, q_at], grad)
            dq = dot_nn(grad, kf[k_at, :])
            at = slice(part * HALF, (part + 1) * HALF)
            if first_k:
                dv_acc[:, at] = dv
                dk_acc[:, at] = dk
            else:
                dv_acc[:, at] += dv
                dk_acc[:, at] += dk
            if first_q:
                @pl.when(run == 0)
                def _():
                    dq_acc[q_at, :] = dq

                @pl.when(run != 0)
                def _():
                    dq_acc[q_at, :] += dq
            else:
                dq_acc[q_at, :] += dq

        early, late = span(2 * run, HALF), span(2 * run + 1, HALF)
        tile(span(run, RUN), early, 0, held[first_diagonal + run], True, True)
        tile(late, late, 1, late_held[run], True, False)

        @pl.loop(run + 1, runs)
        def _(index):
            for part in range(2):
                tile(span(index, RUN), span(2 * run + part, HALF), part, held[slot_of(run, index, part)], False, part == 0)

        at = span(run, RUN)
        both = jnp.concatenate([dk_acc[...] * scale, dv_acc[...]], axis=0).T
        query = dq_acc[at, :] * scale
        qk[at, :] = jnp.where(lane < HEAD, query, pltpu.roll(both, HEAD, 1)).astype(low)
        dv_rows[at, :] = both.astype(low)

    def pack_half(half):
        mid = block_len // 2
        ats = [slice(s * block_len, (s + 1) * block_len) for s in (range(count) if half == 0 else range(blocks - 1, count - 1, -1))]

        @pl.loop(0, count, unroll=4)
        def _(c):
            masks = hold_masks(c=c)
            send[half, c, :block_len, :] = blend(masks, [qk[at, :] for at in ats])
            values = blend(masks, [dv_rows[at, :] for at in ats])
            sorted_dv[c] = values
            values = values[:, HEAD:]
            send[half, c, block_len:, :] = jnp.concatenate([values[:mid], values[mid:]], axis=1)
        landing[half, me] = send[half, me]

    swaps = [
        [push(send.at[half, d[0]], landing.at[half, me], s_send.at[half, k], s_recv.at[half, k], d) for k, d in enumerate(c_peers)]
        for half in range(2)
    ]
    relays = [push(all_ref.at[d], all_ref.at[d], r_send.at[k], r_recv.at[k], (sib, z)) for k, d in enumerate(same_core)]
    others = [push(weight.at[:, d], weight.at[:, d], v_send.at[k], v_recv.at[k], (sib, z)) for k, d in enumerate(same_core)]
    last_copies = [push(out_own, out_all.at[me], o_send.at[2, k], o_recv.at[2, k], d) for k, d in enumerate(c_peers)]
    part_copies = [push(out_sum.at[d[0]], out_part.at[me], o_send.at[1, k], o_recv.at[1, k], d) for k, d in enumerate(c_peers)]

    def head_weights(half):
        if half == 0:
            head_acc[...] = jnp.zeros_like(head_acc)

        @pl.loop(0, count // 2)
        def _(i):
            first, second = None, None
            for part in range(2):
                c = 2 * i + part
                slot, at = place(c, half)
                here = held[slot, pl.ds(pl.multiple_of(at, block_len), block_len), :]
                one, two = dot_tn(send[half, c, :block_len, :], here), dot_tn(sorted_dv[c], here)
                first, second = (one, two) if first is None else (first + one, second + two)
            head_acc[:2 * HEAD, :] += first
            head_acc[2 * HEAD:, :] += second[HEAD:]

    @pl.loop(0, runs)
    def _(run):
        key_run(run)

        @pl.when(run == 0)
        def _():
            start(tok_loads)

        @pl.when(run == runs // 2 - 1)
        def _():
            wait(gout_copies)
            summed = out_zone[0].astype(jnp.float32)
            for k in range(1, owners):
                summed = summed + out_zone[k].astype(jnp.float32)
            out_sum[...] = summed.astype(low).reshape(out_sum.shape)
            start(part_copies)
            out_part[me] = out_sum[me]
            pack_half(0)
            start(swaps[0])
            for k in range(len(same_core)):
                gathers[k].wait_recv()
                relays[k].start()
                weights[k].wait_recv()
                others[k].start()
            wait(tok_loads)
            head_weights(0)

        @pl.when(run == runs // 2)
        def _():
            wait(part_copies)
            summed = out_part[0].astype(jnp.float32)
            for k in range(1, count):
                summed = summed + out_part[k].astype(jnp.float32)
            out_own[...] = summed.astype(low)
            start(last_copies)
            out_all[me] = out_own[...]

    pack_half(1)
    start(swaps[1])
    wait(own_got + own_relay + relays)

    mixed_slot = rows // RUN
    share = owners * 2 * per
    mixed_loads = []
    for c in range(count):
        slot, at = divmod(c * share, RUN)
        mixed_loads.append(pltpu.make_async_copy(all_ref.at[c], held.at[mixed_slot + slot, pl.ds(at, share)], own_sem.at[3 + rows // RUN + c]))
    start(mixed_loads)
    head_weights(1)
    for c in range(owners):
        zsend[c, :3 * HEAD, :] = head_acc[:, c * lanes:(c + 1) * lanes].astype(low)
    z_copies = start([push(zsend.at[d[1]], zone.at[z], z_send.at[k], z_recv.at[k], d) for k, d in enumerate(z_peers)])
    zone[z] = zsend[z]
    wait(mixed_loads)
    step = HALF
    chunks = ffn // step
    wide_slot = mixed_slot + count * share // RUN

    def of_expert(kind, e):
        parts = []
        for slot in range(mixed_slot, wide_slot):
            value = held[slot].reshape(RUN // share, owners, 2, own_experts, groups, width)
            parts.append(value[:, :, kind, e].reshape(-1, width))
        return jnp.concatenate(parts, axis=0)

    def expert_part(e):
        mixed, grad_out = of_expert(0, e), of_expert(1, e)
        copies = []

        @pl.loop(0, chunks, unroll=2)
        def _(i):
            at = span(i, step)
            to = span(lax.rem(i, 2), step)
            active, slope = gelu_parts(dot_nn(mixed, up[e, :, at]))
            held[wide_slot + chunks * e + i // 2, to, :] = active.astype(low)
            slot = wide_slot + chunks * e + chunks // 2 + i // 2
            held[slot, to, :] = (dot_nt(grad_out, down[e, at, :]) * slope).astype(low)

        for i in range(chunks):
            slot = wide_slot + chunks * e + i // 2
            at, to = pl.ds(i * step, step), pl.ds(i % 2 * step, step)
            sem = own_sem.at[3 + rows // RUN + count + 2 * (chunks * e + i)]
            copies.append(pltpu.make_async_copy(held.at[slot, to], act_ref.at[e, :, at], sem))
            sem = own_sem.at[4 + rows // RUN + count + 2 * (chunks * e + i)]
            copies.append(pltpu.make_async_copy(held.at[slot + chunks // 2, to], gpre_ref.at[e, :, at], sem))
        return start(copies)

    stores = expert_part(0)
    wait(z_copies)
    summed = zone[0].astype(jnp.float32)
    for k in range(1, owners):
        summed = summed + zone[k].astype(jnp.float32)
    total[...] = summed.astype(low)
    c_copies = start([push(total, totals.at[me], c_send.at[k], c_recv.at[k], d) for k, d in enumerate(c_peers)])
    totals[me] = total[...]
    for e in range(1, own_experts):
        stores += expert_part(e)
    wait(swaps[0] + swaps[1] + shares + others)
    flat_weight = weight[...].reshape(width, -1)
    parts = []
    for half in range(2):
        queries, keys, values = [], [], []
        for h in range(count):
            front, back = landing[half, h, :block_len, :], landing[half, h, block_len:, :]
            queries.append(front[:, :HEAD])
            keys.append(front[:, HEAD:])
            values.append(jnp.concatenate([back[:, :HEAD], back[:, HEAD:]], axis=0))
        parts.append(dot_nt(jnp.concatenate(queries + keys + values, axis=1), flat_weight))
    wait(layer_copy)
    first, second = ghidden[:block_len, :] + parts[0], ghidden[block_len:, :] + parts[1]
    wide_out[:block_len, :], wide_out[block_len:, :] = ordered(first, second, in_order)
    stores += start([pltpu.make_async_copy(wide_out, gtok_ref, own_sem.at[2])])
    wait(last_copies)
    out_ref[...] = out_all[...].astype(jnp.float32).reshape(out_ref.shape)
    wait(c_copies)
    small = None
    turned = []
    for c in range(count):
        turned.append(totals[c, :3 * HEAD, :].astype(jnp.float32).T)
        part = totals[c, 3 * HEAD:, :].astype(jnp.float32)
        small = part if small is None else small + part
    sums_ref[...] = small
    for kind in range(3):
        at = slice(HEAD * kind, HEAD * (kind + 1))
        gq_ref[:, HEAD * count * kind:HEAD * count * (kind + 1)] = jnp.concatenate([part[:, at] for part in turned], axis=1)
    wait(stores)
    for copy in gathers + weights:
        copy.wait_send()


def layer(table, gid_row, segs, tokens, cot, w_qkv, w_out, w_router, ln_gain, ln_bias, w_up, w_down, groups, count, owners):
    own_rows, width = tokens.shape
    experts = w_router.shape[1]
    blocks, block_len = table.shape[0], own_rows // 2
    rows = blocks * block_len
    runs = rows // RUN
    own_experts, _, ffn = w_up.shape
    lanes, wide_qkv = w_qkv.shape
    smalls = 16
    height = 3 * HEAD + smalls
    per = experts * groups // owners
    wide = (own_experts, count * owners * groups, ffn)
    share = (owners * 2 * per, width)
    part = (count, lanes // count, width)
    swap = (2, count, block_len + block_len // 2, 2 * HEAD)
    gout = (owners, lanes, width)
    sent = (owners, 2, per, width)
    attended = (2, count, block_len // 2, 2 * HEAD)
    head_grad = (count, block_len, 2 * HEAD)
    low, full = jnp.bfloat16, jnp.float32
    scratch = [
        (tokens.shape, low), (tokens.shape, low), ((lanes, 3 * HEAD), low), ((smalls, lanes), low), ((owners, lanes, 3 * HEAD), low),
        ((owners,) + w_out.shape, low), ((owners, smalls, lanes), low), ((owners, lanes // count, wide_qkv), low), (attended, low),
        (attended, low), (sent, low), (share, low), (sent, low), (sent, low), (w_up.shape, low), (w_down.shape, low),
        ((rows, 2 * HEAD), low), ((rows, 2 * HEAD), low), ((rows, 2 * HEAD), low), ((rows, 2 * HEAD), full),
        ((runs * runs, RUN, HALF), low), ((runs, HALF, HALF), low), (head_grad, low), (head_grad, low),
        (tokens.shape, full), (tokens.shape, full), ((rows, 2 * HEAD), low), ((HEAD, rows), low), ((HEAD, rows), low),
        ((HEAD, RUN), full), ((HEAD, RUN), full), ((3 * HEAD, width), full), (swap, low), (swap, low),
        ((owners, count, lanes // count, wide_qkv), low), ((owners, height, lanes), low), ((owners, height, lanes), low),
        ((height, lanes), low), ((count, height, lanes), low), (gout, low), (gout, low), (part, low), (part, low), (part[1:], low),
        (part, low),
    ]
    owns = 3 + rows // RUN + count + 2 * own_experts * (ffn // HALF)
    to_z, to_c = owners - 1, count - 1
    sems = [
        (2 * own_experts,), (owns,), (2, 3, 2), (2, 2, 2), (2, 2), (2, 4, 2), (2, 4, 2), (4, to_z), (4, to_z),
        (2, to_c), (2, to_c), (2, to_z), (2, to_z), (2, own_experts, to_z), (2, own_experts, to_z), (to_c,), (to_c,), (2, to_c), (2, to_c),
        (to_z,), (to_z,), (to_c,), (to_c,), (3, to_c), (3, to_c), (3,), (3,), (4,), (4,), (3,), (3,), (4,), (4,),
    ]
    return pl.pallas_call(
        functools.partial(layer_body, experts, groups, blocks),
        out_shape=(
            jax.ShapeDtypeStruct((lanes, 3 * width), full),
            jax.ShapeDtypeStruct((lanes, width), full),
            jax.ShapeDtypeStruct((smalls, lanes), full),
            jax.ShapeDtypeStruct(tokens.shape, full),
            jax.ShapeDtypeStruct(tokens.shape, full),
            jax.ShapeDtypeStruct(wide, low),
            jax.ShapeDtypeStruct(wide, low),
            jax.ShapeDtypeStruct((count,) + share, low),
            jax.ShapeDtypeStruct((rows // RUN, RUN, width), low),
        ),
        in_specs=[SMEM] + [VMEM] * 9 + [ANY] * 2,
        out_specs=(VMEM,) * 3 + (ANY,) * 6,
        scratch_shapes=[pltpu.VMEM(shape, dtype) for shape, dtype in scratch] + [pltpu.SemaphoreType.DMA(shape) for shape in sems],
        compiler_params=pltpu.CompilerParams(collective_id=1, has_side_effects=True, vmem_limit_bytes=LIMIT),
        cost_estimate=cost(130),
        name="layer",
    )(table, gid_row, segs, tokens, cot, w_qkv, w_out, w_router.T, ln_gain[None], ln_bias[None], w_up, w_down)


def expert_grad_body(experts, passed, mixed_ref, grad_ref, act_ref, gpre_ref, small_ref, *refs):
    sources, outs = refs[:passed], refs[passed + 5:]
    gup_ref, gdown_ref, router_ref, gain_ref, bias_ref = refs[passed:passed + 5]
    width = gup_ref.shape[1]
    for source, out in zip(sources, outs):
        out[...] = source[...]
    router_ref[...] = small_ref[:experts]
    gain_ref[...] = small_ref[experts:experts + 1]
    bias_ref[...] = small_ref[experts + 1:experts + 2]
    gup_ref[0] = dot_tn(mixed_ref[...].reshape(-1, width), gpre_ref[0])
    gdown_ref[0] = dot_tn(act_ref[0], grad_ref[...].reshape(-1, width))


def expert_grads(gathered, active, grad_pre, small, passed, groups, experts):
    own, rows, ffn = active.shape
    step = ffn
    steps = ffn // step
    sources, width = gathered.shape[0], gathered.shape[3]
    view = gathered.reshape(sources, 2, own, groups, width)
    lanes = small.shape[1]
    full = jnp.float32
    slices = [pl.BlockSpec((x.shape[0] // (own * steps), x.shape[1]), lambda e, f: (e * steps + f, 0)) for x in passed]
    return pl.pallas_call(
        functools.partial(expert_grad_body, experts, len(passed)),
        grid=(own, steps),
        out_shape=[
            jax.ShapeDtypeStruct((own, width, ffn), full), jax.ShapeDtypeStruct((own, ffn, width), full),
            jax.ShapeDtypeStruct((experts, lanes), full), jax.ShapeDtypeStruct((1, lanes), full), jax.ShapeDtypeStruct((1, lanes), full),
        ] + [jax.ShapeDtypeStruct(x.shape, x.dtype) for x in passed],
        in_specs=[
            pl.BlockSpec((sources, 1, 1, groups, width), lambda e, f: (0, 0, e, 0, 0)),
            pl.BlockSpec((sources, 1, 1, groups, width), lambda e, f: (0, 1, e, 0, 0)),
            pl.BlockSpec((1, rows, step), lambda e, f: (e, 0, f)),
            pl.BlockSpec((1, rows, step), lambda e, f: (e, 0, f)),
            pl.BlockSpec(small.shape, lambda e, f: (0, 0)),
        ] + slices,
        out_specs=[
            pl.BlockSpec((1, width, step), lambda e, f: (e, 0, f)), pl.BlockSpec((1, step, width), lambda e, f: (e, f, 0)),
            pl.BlockSpec((experts, lanes), lambda e, f: (0, 0)), pl.BlockSpec((1, lanes), lambda e, f: (0, 0)),
            pl.BlockSpec((1, lanes), lambda e, f: (0, 0)),
        ] + slices,
        compiler_params=pltpu.CompilerParams(vmem_limit_bytes=LIMIT),
        cost_estimate=cost(10),
        name="expert_grads",
    )(view, view, active, grad_pre, small, *passed)


def fast_device(
    tokens, cotangent, block_table, seg_ids, group_ids, w_qkv, w_out, w_router, ln_gain, ln_bias, w_up, w_down
):
    ctx_count, z_count = lax.axis_size("ctx"), lax.axis_size("fsdp")
    tok_rows, cot_rows = tokens[0], cotangent[0]
    rows, width = tok_rows.shape
    experts = w_router.shape[1]
    groups = rows // GROUP_SIZE
    grad_qkv, grad_out, small, layer_out, grad_tokens, active, grad_pre, gathered, unused = layer(
        block_table, group_ids, seg_ids, tok_rows, cot_rows, w_qkv, w_out, w_router, ln_gain, ln_bias, w_up, w_down, groups, ctx_count,
        z_count,
    )
    gathered = gathered.reshape(ctx_count * z_count, 2, experts * groups // z_count, width)
    grad_up, grad_down, grad_router, grad_gain, grad_bias, layer_out, grad_tokens, grad_qkv, grad_out = expert_grads(
        gathered, active, grad_pre, small, [layer_out, grad_tokens, grad_qkv, grad_out], groups, experts
    )
    return (
        layer_out[None],
        grad_tokens[None],
        grad_qkv,
        grad_out,
        grad_router.T,
        grad_gain[0],
        grad_bias[0],
        grad_up,
        grad_down,
    )


def solution(mesh):
    placed = (
        P("fsdp", "ctx", None),
        P("fsdp", "ctx", None),
        P(),
        P("fsdp", None),
        P("fsdp", "ctx"),
        P("fsdp", None),
        P("fsdp", None),
        P("fsdp", None),
        P("fsdp"),
        P("fsdp"),
        P("fsdp", None, None),
        P("fsdp", None, None),
    )
    step = fast_device if mesh.shape["ctx"] == HEADS else on_device
    return jax.shard_map(
        step,
        mesh=mesh,
        in_specs=placed,
        out_specs=(
            P("fsdp", "ctx", None),
            P("fsdp", "ctx", None),
            P("fsdp", None),
            P("fsdp", None),
            P("fsdp", None),
            P("fsdp"),
            P("fsdp"),
            P("fsdp", None, None),
            P("fsdp", None, None),
        ),
        check_vma=False,
    )
```

```python
import functools

import jax
import jax.numpy as jnp
from jax import lax
from jax.experimental import pallas as pl
from jax.experimental.pallas import tpu as pltpu
from jax.sharding import PartitionSpec as P

HEADS = 8
HEAD = 64
GROUP_SIZE = 32
KEY_BLOCK = 2048


highest = lax.Precision.HIGHEST
neg_large = -1e30
epsilon = 1e-05
gelu_coef = 0.7978845608028654
gelu_cubic = 0.044715


def contract_rows(left, right):
    return lax.dot_general(
        left, right, (((0,), (0,)), ((), ())), preferred_element_type=jnp.float32
    )


def contract_cols(left, right):
    return lax.dot_general(
        left, right, (((1,), (1,)), ((), ())), preferred_element_type=jnp.float32
    )


def gelu_slope(value):
    inner = gelu_coef * (value + gelu_cubic * value * value * value)
    tangent = jnp.tanh(inner)
    return 0.5 * (1.0 + tangent) + 0.5 * value * (1.0 - tangent * tangent) * gelu_coef * (
        1.0 + 3.0 * gelu_cubic * value * value
    )


def expert_forward(mixed_low, up_weight, down_weight):
    pre = jnp.einsum("ged,edh->geh", mixed_low, up_weight, preferred_element_type=jnp.float32)
    active = jax.nn.gelu(pre, approximate=True).astype(jnp.bfloat16)
    result = jnp.einsum("geh,ehd->ged", active, down_weight, preferred_element_type=jnp.float32)
    return (pre, active, result.astype(jnp.bfloat16))


def expert_backward(mixed_low, pre, active, grad_result, up_weight, down_weight):
    grad_act = jnp.einsum(
        "ged,ehd->geh", grad_result, down_weight, preferred_element_type=jnp.float32
    )
    grad_pre = (grad_act * gelu_slope(pre)).astype(jnp.bfloat16)
    grad_down_part = jnp.einsum(
        "geh,ged->ehd", active, grad_result, preferred_element_type=jnp.float32
    )
    grad_up_part = jnp.einsum(
        "ged,geh->edh", mixed_low, grad_pre, preferred_element_type=jnp.float32
    )
    grad_mixed = jnp.einsum("geh,edh->ged", grad_pre, up_weight, preferred_element_type=jnp.float32)
    return (grad_up_part, grad_down_part, grad_mixed.astype(jnp.bfloat16))


def on_device(
    tokens,
    cotangent,
    block_table,
    seg_ids,
    group_ids,
    w_qkv,
    w_out,
    w_router,
    ln_gain,
    ln_bias,
    w_up,
    w_down,
):
    tok_rows = tokens[0]
    tok_count = tok_rows.shape[0]
    width = tok_rows.shape[1]
    expert_count = w_router.shape[1]
    ctx_index = lax.axis_index("ctx")
    full_rows = seg_ids.shape[1]
    block_len = full_rows // block_table.shape[0]
    row_ids = jnp.arange(full_rows, dtype=jnp.int32)
    key_pos = jnp.take(block_table, row_ids // block_len) * block_len + row_ids % block_len
    key_seg = seg_ids[0]
    pos_rows = lax.dynamic_slice_in_dim(key_pos, ctx_index * tok_count, tok_count)
    seg_rows = lax.dynamic_slice_in_dim(key_seg, ctx_index * tok_count, tok_count)
    scale = HEAD ** (-0.5)
    qkv_full, out_full, router_full, gain_full, bias_full = (
        lax.all_gather(w_qkv, "fsdp", axis=0, tiled=True),
        lax.all_gather(w_out, "fsdp", axis=0, tiled=True),
        lax.all_gather(w_router, "fsdp", axis=0, tiled=True),
        lax.all_gather(ln_gain, "fsdp", axis=0, tiled=True),
        lax.all_gather(ln_bias, "fsdp", axis=0, tiled=True),
    )
    qkv = jnp.dot(tok_rows, qkv_full, preferred_element_type=jnp.float32).astype(jnp.bfloat16)
    query_heads = qkv[:, :width].reshape(tok_count, HEADS, HEAD)
    key_all, val_all = (
        lax.all_gather(qkv[:, width : 2 * width], "ctx", axis=0, tiled=True),
        lax.all_gather(qkv[:, 2 * width :], "ctx", axis=0, tiled=True),
    )
    key_heads = key_all.reshape(full_rows, HEADS, HEAD)
    val_heads = val_all.reshape(full_rows, HEADS, HEAD)
    block_count = full_rows // KEY_BLOCK
    block_ids = jnp.arange(block_count, dtype=jnp.int32)

    def block_scores(index):
        start = index * KEY_BLOCK
        key_block = lax.dynamic_slice_in_dim(key_heads, start, KEY_BLOCK, 0)
        val_block = lax.dynamic_slice_in_dim(val_heads, start, KEY_BLOCK, 0)
        pos_block = lax.dynamic_slice_in_dim(key_pos, start, KEY_BLOCK, 0)
        seg_block = lax.dynamic_slice_in_dim(key_seg, start, KEY_BLOCK, 0)
        scores = (
            jnp.einsum("qhd,khd->hqk", query_heads, key_block, preferred_element_type=jnp.float32)
            * scale
        )
        allowed = (pos_block[None, :] <= pos_rows[:, None]) & (
            (seg_block[None, :] == 0) | (seg_block[None, :] == seg_rows[:, None])
        )
        return (scores, allowed[None], key_block, val_block)

    def lse_step(carry, index):
        top, total = carry
        scores, allowed, key_block, val_block = block_scores(index)
        masked = jnp.where(allowed, scores, neg_large)
        new_top = jnp.maximum(top, jnp.max(masked, axis=-1))
        weights = jnp.where(allowed, jnp.exp(masked - new_top[..., None]), 0.0)
        return ((new_top, total * jnp.exp(top - new_top) + jnp.sum(weights, axis=-1)), None)

    start_top = jnp.full((HEADS, tok_count), neg_large, jnp.float32)
    (top, total), unused = lax.scan(
        lse_step, (start_top, jnp.zeros((HEADS, tok_count), jnp.float32)), block_ids
    )
    log_total = top + jnp.log(total)

    def block_probs(index):
        scores, allowed, key_block, val_block = block_scores(index)
        probs = jnp.where(allowed, jnp.exp(scores - log_total[..., None]), 0.0)
        return (probs, key_block, val_block)

    def value_step(accum, index):
        probs, key_block, val_block = block_probs(index)
        return (
            accum
            + jnp.einsum(
                "hqk,khd->qhd",
                probs.astype(jnp.bfloat16),
                val_block,
                preferred_element_type=jnp.float32,
            ),
            None,
        )

    accum, unused = lax.scan(
        value_step, jnp.zeros((tok_count, HEADS, HEAD), jnp.float32), block_ids
    )
    attended = accum.reshape(tok_count, width).astype(jnp.bfloat16)
    hidden = tok_rows.astype(jnp.float32) + jnp.dot(
        attended, out_full, preferred_element_type=jnp.float32
    )
    center = hidden - jnp.mean(hidden, axis=-1, keepdims=True)
    inv_dev = lax.rsqrt(jnp.mean(center * center, axis=-1, keepdims=True) + epsilon)
    unit = center * inv_dev
    gain_f = gain_full.astype(jnp.float32)
    normed_low = (unit * gain_f + bias_full.astype(jnp.float32)).astype(jnp.bfloat16)
    logits = jnp.dot(normed_low, router_full, preferred_element_type=jnp.float32)
    groups_dev = tok_count // GROUP_SIZE
    local_group = group_ids[0] - ctx_index * groups_dev
    member = (local_group[:, None] == jnp.arange(groups_dev, dtype=jnp.int32)[None, :]).astype(
        jnp.float32
    )
    expo = jnp.exp(logits)
    group_total = jnp.dot(member.T, expo, precision=highest)
    mix_weights = expo / jnp.dot(member, group_total, precision=highest)
    weights_low = mix_weights.astype(jnp.bfloat16)
    mixing = member.astype(jnp.bfloat16).T[:, None, :] * weights_low.T[None, :, :]
    mixing_flat = mixing.reshape(groups_dev * expert_count, tok_count)
    mixed_low = jnp.dot(mixing_flat, normed_low, preferred_element_type=jnp.float32).astype(
        jnp.bfloat16
    )
    mixed_low = mixed_low.reshape(groups_dev, expert_count, width)
    owner_mixed = lax.all_to_all(mixed_low, "fsdp", split_axis=1, concat_axis=0, tiled=True)
    pre, active, owner_out = expert_forward(owner_mixed, w_up, w_down)
    expert_out = lax.all_to_all(owner_out, "fsdp", split_axis=0, concat_axis=1, tiled=True)
    expert_flat = expert_out.reshape(groups_dev * expert_count, width)
    spread = contract_rows(mixing_flat, expert_flat)
    layer_out = hidden + spread
    cot_rows = cotangent[0]
    cot_f = cot_rows.astype(jnp.float32)
    grad_expert = jnp.dot(mixing_flat, cot_rows, preferred_element_type=jnp.float32).astype(
        jnp.bfloat16
    )
    grad_expert = grad_expert.reshape(groups_dev, expert_count, width)
    coef = contract_cols(cot_rows, expert_flat).reshape(tok_count, groups_dev, expert_count)
    grad_mix_spread = jnp.sum(coef * member[:, :, None], axis=1)
    owner_grad = lax.all_to_all(grad_expert, "fsdp", split_axis=1, concat_axis=0, tiled=True)
    grad_up_own, grad_down_own, owner_back = expert_backward(
        owner_mixed, pre, active, owner_grad, w_up, w_down
    )
    grad_mixed = lax.all_to_all(owner_back, "fsdp", split_axis=0, concat_axis=1, tiled=True)
    grad_mixed_flat = grad_mixed.reshape(groups_dev * expert_count, width)
    grad_norm_mix = contract_rows(mixing_flat, grad_mixed_flat)
    grad_mixing = contract_cols(grad_mixed_flat, normed_low).reshape(
        groups_dev, expert_count, tok_count
    )
    grad_mix_mixing = jnp.sum(grad_mixing * member.T[:, None, :], axis=0).T
    grad_mix = grad_mix_spread + grad_mix_mixing
    product = mix_weights * grad_mix
    token_dot = jnp.dot(member, jnp.dot(member.T, product, precision=highest), precision=highest)
    grad_logits = (product - mix_weights * token_dot).astype(jnp.bfloat16)
    grad_router_part = contract_rows(normed_low, grad_logits)
    grad_norm_router = contract_cols(grad_logits, router_full)
    grad_normed = grad_norm_mix + grad_norm_router
    grad_gain_part = jnp.sum(grad_normed * unit, axis=0)
    grad_bias_part = jnp.sum(grad_normed, axis=0)
    scaled = grad_normed * gain_f
    grad_hidden = cot_f + inv_dev * (
        scaled
        - jnp.mean(scaled, axis=-1, keepdims=True)
        - unit * jnp.mean(scaled * unit, axis=-1, keepdims=True)
    )
    grad_branch = grad_hidden.astype(jnp.bfloat16)
    grad_out_part = contract_rows(attended, grad_branch)
    grad_heads = (
        contract_cols(grad_branch, out_full).astype(jnp.bfloat16).reshape(tok_count, HEADS, HEAD)
    )
    delta = jnp.sum(grad_heads.astype(jnp.float32) * accum, axis=-1).T

    def grad_step(grad_query, index):
        probs, key_block, val_block = block_probs(index)
        grad_probs = jnp.einsum(
            "qhd,khd->hqk", grad_heads, val_block, preferred_element_type=jnp.float32
        )
        grad_scores = (probs * (grad_probs - delta[..., None])).astype(jnp.bfloat16)
        grad_query = (
            grad_query
            + jnp.einsum("hqk,khd->qhd", grad_scores, key_block, preferred_element_type=jnp.float32)
            * scale
        )
        grad_key = (
            jnp.einsum("hqk,qhd->khd", grad_scores, query_heads, preferred_element_type=jnp.float32)
            * scale
        )
        grad_val = jnp.einsum(
            "hqk,qhd->khd",
            probs.astype(jnp.bfloat16),
            grad_heads,
            preferred_element_type=jnp.float32,
        )
        return (grad_query, (grad_key, grad_val))

    grad_query, (grad_keys, grad_vals) = lax.scan(
        grad_step, jnp.zeros((tok_count, HEADS, HEAD), jnp.float32), block_ids
    )
    grad_key_own, grad_val_own = (
        lax.psum_scatter(
            grad_keys.reshape(full_rows, width), "ctx", scatter_dimension=0, tiled=True
        ),
        lax.psum_scatter(
            grad_vals.reshape(full_rows, width), "ctx", scatter_dimension=0, tiled=True
        ),
    )
    grad_qkv_low = jnp.concatenate(
        [grad_query.reshape(tok_count, width), grad_key_own, grad_val_own], axis=1
    ).astype(jnp.bfloat16)
    grad_qkv_part = contract_rows(tok_rows, grad_qkv_low)
    grad_tokens = grad_hidden + contract_cols(grad_qkv_low, qkv_full)
    dense = (
        lax.psum_scatter(grad_qkv_part, "fsdp", scatter_dimension=0, tiled=True),
        lax.psum_scatter(grad_out_part, "fsdp", scatter_dimension=0, tiled=True),
        lax.psum_scatter(grad_router_part, "fsdp", scatter_dimension=0, tiled=True),
        lax.psum_scatter(grad_gain_part, "fsdp", scatter_dimension=0, tiled=True),
        lax.psum_scatter(grad_bias_part, "fsdp", scatter_dimension=0, tiled=True),
    )
    totals = lax.psum(
        (dense[0], dense[1], dense[2], dense[3], dense[4], grad_up_own, grad_down_own), "ctx"
    )
    return (
        layer_out[None],
        grad_tokens[None],
        totals[0],
        totals[1],
        totals[2],
        totals[3],
        totals[4],
        totals[5],
        totals[6],
    )


def cost(microseconds):
    return pl.CostEstimate(flops=int(microseconds * 1.15e9), bytes_accessed=1 << 20, transcendentals=0)


LOG2E = 1.4426950408889634
HIDE = -1e30
RUN = 1024
HALF = 512
VMEM = pl.BlockSpec(memory_space=pltpu.VMEM)
SMEM = pl.BlockSpec(memory_space=pltpu.SMEM)
ANY = pl.BlockSpec(memory_space=pl.ANY)
LIMIT = 60 << 20


def dot_nn(left, right):
    return lax.dot_general(left, right, (((1,), (0,)), ((), ())), preferred_element_type=jnp.float32)


def dot_nt(left, right):
    return lax.dot_general(left, right, (((1,), (1,)), ((), ())), preferred_element_type=jnp.float32)


def dot_tn(left, right):
    return lax.dot_general(left, right, (((0,), (0,)), ((), ())), preferred_element_type=jnp.float32)


def split3(value):
    one = value.astype(jnp.bfloat16)
    rest = value - one.astype(jnp.float32)
    two = rest.astype(jnp.bfloat16)
    three = (rest - two.astype(jnp.float32)).astype(jnp.bfloat16)
    return one, two, three


def span(index, size, width=None):
    return pl.ds(pl.multiple_of(index * size, size), size if width is None else width)


MESH = pl.DeviceIdType.MESH


def flip(index, bit):
    return index + bit - 2 * bit * lax.rem(index // bit, 2)


def meet(devices):
    barrier = pltpu.get_barrier_semaphore()
    for device in devices:
        pl.semaphore_signal(barrier, inc=1, device_id=device, device_id_type=MESH)
    pl.semaphore_wait(barrier, len(devices))


def push(src, dst, send_sem, recv_sem, device):
    return pltpu.make_async_remote_copy(
        src_ref=src, dst_ref=dst, send_sem=send_sem, recv_sem=recv_sem, device_id=device, device_id_type=MESH
    )


def norm_parts(hidden):
    center = hidden - jnp.mean(hidden, axis=-1, keepdims=True)
    inv_dev = lax.rsqrt(jnp.mean(center * center, axis=-1, keepdims=True) + epsilon)
    return center * inv_dev, inv_dev


def gelu_parts(value):
    square = value * value
    tangent = jnp.tanh(value * (square * (gelu_coef * gelu_cubic) + gelu_coef))
    half = 0.5 * tangent + 0.5
    rise = value * (square * (3.0 * gelu_coef * gelu_cubic) + gelu_coef)
    return value * half, half + half * (1.0 - tangent) * rise


def boundaries(seg_ref, lane):
    segs = seg_ref[...]
    begin = jnp.zeros(lane.shape, jnp.int32)
    end = jnp.zeros(lane.shape, jnp.int32)
    for c in range(1, 10):
        total = jnp.sum((segs < c).astype(jnp.int32), axis=1, keepdims=True)
        begin = jnp.where(lane == HEAD - 1 + c, total, begin)
        end = jnp.where(lane == HEAD - 2 + c, total, end)
    return begin, jnp.where(lane == HEAD + 8, 0, end)


def layer_body(
    experts, groups, blocks, table_ref, gid_ref, seg_ref, tok_ref, cot_ref, wq_ref, wo_ref, router_ref, gain_ref, bias_ref, up_ref, down_ref,
    gq_ref, out_ref, sums_ref, layer_ref, gtok_ref, act_ref, gpre_ref, all_ref, toks_ref,
    tok, cot, head_buf, pack_buf, heads, wo, pack, zparts, att_send, att, msend, zin, bsend, bin_, up, down, qf, kf, vf, stat, held, late_held,
    ghead_out, ghead, wide_out, ghidden, dof, qt, dot, dk_acc, dv_acc, head_acc, send, landing, weight, zsend, zone, total, totals,
    out_mine, out_zone, out_sum, out_part, out_own, out_all,
    load_sem, own_sem, t_send, t_recv, d_recv, n_send, n_recv, y_send, y_recv, a_send, a_recv, m_send, m_recv, b_send, b_recv,
    h_send, h_recv, s_send, s_recv, z_send, z_recv, c_send, c_recv, o_send, o_recv, g_send, g_recv, r_send, r_recv, w_send, w_recv,
    v_send, v_recv,
):
    me, z = lax.axis_index("ctx"), lax.axis_index("fsdp")
    count, block_len = blocks // 2, tok_ref.shape[0] // 2
    own_rows, width = tok_ref.shape
    owners, own_experts, ffn = msend.shape[0], up_ref.shape[0], up_ref.shape[2]
    flat, per = experts * groups, experts * groups // owners
    rows = blocks * block_len
    runs = rows // RUN
    low = jnp.bfloat16
    dq_acc, qk, dv_rows, sorted_dv = stat, qf, vf, ghead_out

    def start(copies):
        for copy in copies:
            copy.start()
        return copies

    def wait(copies):
        for copy in copies:
            copy.wait()

    loads = []
    for e in range(own_experts):
        loads += [pltpu.make_async_copy(up_ref.at[e], up.at[e], load_sem.at[2 * e])]
        loads += [pltpu.make_async_copy(down_ref.at[e], down.at[e], load_sem.at[2 * e + 1])]
    start(loads)

    def mask(condition):
        return jnp.broadcast_to(jnp.where(condition, 1.0, 0.0), (1, 2 * HEAD))

    def hold_masks(c=None, j=None):
        pairs = [(c, i) if j is None else (i, j) for i in range(count)]
        return [mask(jnp.minimum(table_ref[2 * c], table_ref[2 * c + 1]) == j).astype(low) for c, j in pairs]

    in_order = mask(table_ref[2 * me] < table_ref[2 * me + 1])[:, :1]

    def blend(masks, values):
        out = None
        for weigh, value in zip(masks, values):
            out = weigh * value if out is None else out + weigh * value
        return out

    def ordered(first, second, weigh):
        return weigh * first + (1 - weigh) * second, weigh * second + (1 - weigh) * first

    sib, xn, yn, diag = flip(me, 1), flip(me, 2), flip(me, 4), flip(flip(me, 2), 4)
    same_core = [xn, yn, diag]
    z_peers = [(me, lax.rem(z + k, owners)) for k in range(1, owners)]
    c_peers = [(jnp.bitwise_xor(me, k), z) for k in range(1, count)]
    barrier = pltpu.get_barrier_semaphore()
    for d in z_peers + c_peers:
        pl.semaphore_signal(barrier, inc=1, device_id=d, device_id_type=MESH)
    tok[:block_len, :], tok[block_len:, :] = ordered(tok_ref[:block_len, :], tok_ref[block_len:, :], in_order.astype(low))
    pl.semaphore_wait(barrier, len(z_peers + c_peers))

    piece = block_len // 2
    per_slot = RUN // block_len

    def place(device, half):
        return 2 * half + device // per_slot, lax.rem(device, per_slot) * block_len

    def there(device, half, k):
        slot, at = place(device, half)
        return held.at[slot, pl.ds(pl.multiple_of(at + k * piece, piece), piece)]

    gone = []

    def go(copies):
        gone.extend(start(copies))

    def here(half, k):
        return tok.at[pl.ds(half * block_len + k * piece, piece)]

    def launch(half):
        slot, at = place(me, half)
        held[slot, pl.ds(pl.multiple_of(at, block_len), block_len), :] = tok[half * block_len:(half + 1) * block_len, :]
        for k in (0, 1):
            go([push(here(half, k), there(me, half, k), t_send.at[half, 0, k], t_recv.at[half, 0, k], (xn, z))])
            go([push(here(half, 1 - k), there(me, half, 1 - k), t_send.at[half, 1, 1 - k], t_recv.at[half, 1, 1 - k], (yn, z))])

    def launch_near(half):
        for k in (0, 1):
            go([push(here(half, k), there(me, half, k), n_send.at[half, 0, k], n_recv.at[half, 0, k], (sib, z))])

    def arrival(device, half, k, sem):
        return push(there(device, half, k), there(device, half, k), t_send.at[half, 0, 0], sem, (sib, z))

    def relay(device, half, k, i):
        block = there(device, half, k)
        return push(block, block, n_send.at[half, i, k], n_recv.at[half, i, k], (sib, z))

    def forward_plan(half):
        plan = []
        for device, k, i, to in ((xn, 0, 0, yn), (yn, 1, 1, xn)):
            block = there(device, half, k)
            plan.append((
                push(block, block, t_send.at[half, 0, 0], t_recv.at[half, i, k], (sib, z)),
                push(block, block, t_send.at[half, 2, k], d_recv.at[half, k], (to, z)),
                push(block, block, n_send.at[half, i + 1, k], n_recv.at[half, i + 1, k], (sib, z)),
            ))
        return plan

    def forward(plan):
        for came, on, near in plan:
            came.wait_recv()
            start([on, near])

    def settle_plan(half):
        plan = [
            (arrival(xn, half, 1, t_recv.at[half, 0, 1]), relay(xn, half, 1, 1)),
            (arrival(yn, half, 0, t_recv.at[half, 1, 0]), relay(yn, half, 0, 2)),
        ]
        plan += [(arrival(diag, half, k, d_recv.at[half, k]), relay(diag, half, k, 3)) for k in (0, 1)]
        near = []
        for k in (0, 1):
            for i, device in enumerate((sib, flip(xn, 1), flip(yn, 1), flip(diag, 1))):
                near.append(arrival(device, half, k, n_recv.at[half, i, k]))
        return plan, near

    def settle(plan, near):
        for came, on in plan:
            came.wait_recv()
            on.start()
        for came in near:
            came.wait_recv()

    launch(0)

    shared = []

    def share(i, shard, whole):
        whole[z] = shard[...]
        shared.append(start([push(shard, whole.at[z], y_send.at[i, k], y_recv.at[i, k], d) for k, d in enumerate(z_peers)]))

    for h in range(count):
        @pl.when(me == h)
        def _():
            cols = [wq_ref[:, width * kind + HEAD * h:width * kind + HEAD * (h + 1)] for kind in range(3)]
            head_buf[...] = jnp.concatenate(cols, axis=1)

    share(0, head_buf, heads)
    launch_near(0)
    parts = [router_ref[...].astype(jnp.float32), gain_ref[...].astype(jnp.float32), bias_ref[...].astype(jnp.float32)]
    parts.append(jnp.zeros((pack_buf.shape[0] - experts - 2, pack_buf.shape[1]), jnp.float32))
    pack_buf[...] = jnp.concatenate(parts, axis=0).astype(low)
    share(1, pack_buf, pack)
    share(2, wo_ref, wo)
    depth = wq_ref.shape[0] // count
    share(3, wq_ref.at[pl.ds(pl.multiple_of(me * depth, depth), depth)], zparts)

    lane = lax.broadcasted_iota(jnp.int32, (1, 2 * HEAD), 1)
    begin, end = boundaries(seg_ref, lane)
    is_flag = (lane >= HEAD) & (lane < HEAD + 8)
    is_one = (lane >= HEAD + 8) & (lane < HEAD + 11)
    ones_v = ((lane >= HEAD) & (lane < HEAD + 3)).astype(jnp.float32)
    scale = HEAD ** (-0.5)

    def projected(half, device):
        at = device % per_slot * block_len
        lanes = device // per_slot * 4 * HEAD
        return held.at[4 + half, at:at + block_len, lanes:lanes + 4 * HEAD]

    def project(half, head_weight):
        for slot in range(count // per_slot):
            to = slice(4 * HEAD * slot, 4 * HEAD * (slot + 1))
            held[4 + half, :, to] = dot_nn(held[2 * half + slot], head_weight).astype(low)

        @pl.loop(0, count, unroll=8)
        def _(j):
            s = j if half == 0 else blocks - 1 - j
            masks = hold_masks(j=j)
            both = blend(masks, [projected(half, c)[:, :2 * HEAD] for c in range(count)]).astype(jnp.float32)
            value = blend(masks, [projected(half, c)[:, 2 * HEAD:] for c in range(count)]).astype(jnp.float32)
            spot = lax.broadcasted_iota(jnp.int32, (block_len, 2 * HEAD), 0) + s * block_len
            mine = (spot >= begin) & (spot < end)
            at = span(s, block_len)
            flag_q = jnp.where(is_flag & jnp.logical_not(mine), 1.0, 0.0)
            flag_k = jnp.where(mine, HIDE, jnp.where(is_one, 1.0, 0.0))
            qf[at, :] = jnp.where(lane < HEAD, both, flag_q).astype(low)
            kf[at, :] = jnp.where(lane < HEAD, pltpu.roll(both, HEAD, 1), flag_k).astype(low)
            vf[at, :] = (value + ones_v).astype(low)
            dot[:, at] = value.T.astype(low)[:HEAD]

    lower = lax.broadcasted_iota(jnp.int32, (HALF, RUN), 0) <= lax.broadcasted_iota(jnp.int32, (HALF, RUN), 1)

    def query_run(run):
        def tile(state, q_at, k_at, size, diagonal):
            scores = dot_nt(kf[k_at, :], qf[q_at, :]) * (scale * LOG2E)
            if diagonal:
                scores = jnp.where(lower[:, :scores.shape[1]], scores, HIDE)
            top, acc = state
            new_top = jnp.maximum(top, jnp.max(scores, axis=0, keepdims=True))
            probs = jnp.exp2(scores - new_top).astype(low)
            values = jnp.concatenate([dot[:, k_at], jnp.ones((HEAD, size), low)], axis=0)
            return new_top, acc * jnp.exp2(top - new_top) + dot_nn(values, probs)

        begin = (jnp.full((1, RUN), HIDE, jnp.float32), jnp.zeros((2 * HEAD, RUN), jnp.float32))
        def both_halves(n, state):
            for part in range(2):
                state = tile(state, span(run, RUN), span(2 * n + part, HALF), HALF, False)
            return state

        whole = lax.fori_loop(0, run, both_halves, begin)
        early, late = span(2 * run, HALF), span(2 * run + 1, HALF)
        whole = tile(whole, span(run, RUN), early, HALF, True)
        first = [part[:, :HALF] for part in whole]
        second = tile([part[:, HALF:] for part in whole], late, late, HALF, True)
        for at, (top, acc) in ((early, first), (late, second)):
            sums = acc[HEAD:]
            result = jnp.concatenate([acc[:HEAD] / sums, top + jnp.log2(sums)], axis=0).T
            stat[at, :] = result
            one, two, three = split3(result * (-1.0 / (scale * LOG2E)))
            old = qf[at, :]
            old = jnp.where(lane == HEAD + 8, one, old)
            old = jnp.where(lane == HEAD + 9, two, old)
            qf[at, :] = jnp.where(lane == HEAD + 10, three, old)

    def pack_attended(half):
        mid = block_len // 2
        ats = [slice(s * block_len, (s + 1) * block_len) for s in (range(count) if half == 0 else range(blocks - 1, count - 1, -1))]

        @pl.loop(0, count, unroll=4)
        def _(c):
            block = blend(hold_masks(c=c), [stat[at, :].astype(low) for at in ats])
            att_send[half, c] = jnp.concatenate([block[:mid, :HEAD], block[mid:, :HEAD]], axis=1)
        att[half, me] = att_send[half, me]

    swaps = [
        [push(att_send.at[half, d[0]], att.at[half, me], a_send.at[half, k], a_recv.at[half, k], d) for k, d in enumerate(c_peers)]
        for half in range(2)
    ]
    saves = [pltpu.make_async_copy(held.at[i], toks_ref.at[i], own_sem.at[3 + i]) for i in range(rows // RUN)]
    cot[:block_len, :], cot[block_len:, :] = ordered(cot_ref[:block_len, :], cot_ref[block_len:, :], in_order.astype(low))
    plans = [forward_plan(half) for half in range(2)]
    for plan in plans:
        for came, on, near in plan:
            gone.extend([on, near])
    settles = [settle_plan(half) for half in range(2)]
    for plan, near in settles:
        gone.extend([on for came, on in plan])
    forward(plans[0])
    settle(*settles[0])
    launch(1)
    launch_near(1)
    wait(shared[0])
    head_weight = heads[...].reshape(width, 3 * HEAD)
    head_weight = jnp.concatenate([head_weight, jnp.zeros((width, HEAD), low)], axis=1)
    project(0, head_weight)

    @pl.loop(0, runs)
    def _(run):
        query_run(run)

        @pl.when(run == 0)
        def _():
            forward(plans[1])

        @pl.when(run == runs // 2 - 1)
        def _():
            pack_attended(0)
            start(swaps[0])
            settle(*settles[1])
            start(saves)
            project(1, head_weight)

    pack_attended(1)
    start(swaps[1])
    for copy in gone:
        copy.wait_send()
    wait(shared[1] + shared[2] + shared[3])

    first_diagonal = runs * (runs - 1)

    def slot_of(run, index, part):
        return run * (2 * runs - 1 - run) + 2 * (index - run - 1) + part

    def probabilities(q_at, k_at, visible):
        scores = dot_nt(qf[q_at, :], kf[k_at, :]) * (scale * LOG2E)
        if visible is not None:
            scores = jnp.where(visible, scores, HIDE)
        return jnp.exp2(scores).astype(low)

    def hold_diagonal():
        early = lax.broadcasted_iota(jnp.int32, (RUN, HALF), 1) <= lax.broadcasted_iota(jnp.int32, (RUN, HALF), 0)
        late = lax.broadcasted_iota(jnp.int32, (HALF, HALF), 1) <= lax.broadcasted_iota(jnp.int32, (HALF, HALF), 0)

        @pl.loop(0, runs)
        def _(run):
            held[first_diagonal + run] = probabilities(span(run, RUN), span(2 * run, HALF), early)
            late_held[run] = probabilities(span(2 * run + 1, HALF), span(2 * run + 1, HALF), late)

    def hold(run):
        @pl.loop(run + 1, runs)
        def _(index):
            for part in range(2):
                held[slot_of(run, index, part)] = probabilities(span(index, RUN), span(2 * run + part, HALF), None)

    hold_diagonal()
    wait(swaps[0] + swaps[1])
    weights = start([push(zparts, weight.at[:, me], w_send.at[k], w_recv.at[k], (d, z)) for k, d in enumerate(same_core)])
    shares = start([push(zparts, weight.at[:, me], v_send.at[3], v_recv.at[3], (sib, z))])
    weight[:, me] = zparts[...]
    quarters = [
        jnp.concatenate([att[half, h, :, HEAD * p:HEAD * (p + 1)] for h in range(count)], axis=1) for half in range(2) for p in range(2)
    ]
    attended = jnp.concatenate(quarters, axis=0)
    out_weight = wo[...].reshape(width, width)
    hidden = tok[...].astype(jnp.float32) + dot_nn(attended, out_weight)
    unit, inv_dev = norm_parts(hidden)
    small_in = jnp.concatenate([pack[k] for k in range(owners)], axis=1)
    gain, bias = small_in[experts:experts + 1].astype(jnp.float32), small_in[experts + 1:experts + 2].astype(jnp.float32)
    normed = (unit * gain + bias).astype(low)
    expo = jnp.exp(dot_nt(small_in, normed)[:experts])
    expo = jnp.broadcast_to(expo[:, None, :], (experts, groups, own_rows)).reshape(flat, own_rows)
    gids = lax.rem(gid_ref[...], groups).astype(jnp.float32)
    gids = jnp.concatenate(ordered(gids[:, :block_len], gids[:, block_len:], in_order), axis=1)
    member = lax.rem(lax.broadcasted_iota(jnp.int32, (flat, 1), 0), groups).astype(jnp.float32) == gids
    expo = jnp.where(member, expo, 0.0)
    mix = expo / jnp.sum(expo, axis=1, keepdims=True)
    mix_low = mix.astype(low)

    def zone_rows(owner, kind):
        return pl.ds(pl.multiple_of((2 * owner + kind) * per, per), per)

    def to_owners(kind, value):
        msend[:, kind] = value.astype(low).reshape(owners, per, width)
        zin[zone_rows(z, kind), :] = msend[z, kind]
        return start([
            push(msend.at[d[1], kind], zin.at[zone_rows(z, kind)], m_send.at[kind, k], m_recv.at[kind, k], d) for k, d in enumerate(z_peers)
        ])

    mixed_copies = to_owners(0, dot_nn(mix_low, normed))
    grad_experts = dot_nn(mix_low, cot[...])
    wait(loads)
    hold(1)
    grad_copies = to_owners(1, grad_experts)

    @pl.loop(2, runs - 1)
    def _(run):
        hold(run)

    wait(mixed_copies)

    def from_sources(kind, e):
        lows_ = [(2 * owner + kind) * per + e * groups for owner in range(owners)]
        return jnp.concatenate([zin[at:at + groups, :] for at in lows_], axis=0)

    def to_sources(kind, e, value):
        bsend[:, kind, e * groups:(e + 1) * groups, :] = value.astype(low).reshape(owners, groups, width)

    def send_back(kind, e):
        at = pl.ds(e * groups, groups)
        bin_[z, kind, at, :] = bsend[z, kind, at, :]
        return start([
            push(bsend.at[d[1], kind, at], bin_.at[z, kind, at], b_send.at[kind, e, k], b_recv.at[kind, e, k], d)
            for k, d in enumerate(z_peers)
        ])

    out_copies, back_copies = [], []
    slopes = []
    for e in range(own_experts):
        active, slope = gelu_parts(dot_nn(from_sources(0, e), up[e]))
        slopes.append(slope)
        to_sources(0, e, dot_nn(active.astype(low), down[e]))
        out_copies += send_back(0, e)
    wait(grad_copies)
    for e in range(own_experts):
        grad_pre = (dot_nt(from_sources(1, e), down[e]) * slopes[e]).astype(low)
        to_sources(1, e, dot_nt(grad_pre, up[e]))
        back_copies += send_back(1, e)
    wait(out_copies)
    expert_out = bin_[:, 0].reshape(flat, width)
    result = hidden + dot_tn(mix_low, expert_out)
    wide_out[:block_len, :], wide_out[block_len:, :] = ordered(result[:block_len], result[block_len:], in_order)
    layer_copy = start([pltpu.make_async_copy(wide_out, layer_ref, own_sem.at[2])])
    grad_mix = dot_nt(expert_out, cot[...])
    wait(saves)
    hold(0)
    wait(back_copies)
    grad_mixed = bin_[:, 1].reshape(flat, width)
    product = mix * (grad_mix + dot_nt(grad_mixed, normed))
    grad_logits = product - mix * jnp.sum(product, axis=1, keepdims=True)
    grad_logits = jnp.sum(grad_logits.reshape(experts, groups, own_rows), axis=1).astype(low)
    pad = jnp.zeros((small_in.shape[0] - experts, own_rows), low)
    grad_logits = jnp.concatenate([grad_logits, pad], axis=0)
    grad_normed = dot_tn(jnp.concatenate([mix_low, grad_logits], axis=0), jnp.concatenate([grad_mixed, small_in], axis=0))
    scaled = grad_normed * gain
    mean = jnp.mean(scaled, axis=-1, keepdims=True)
    grad_hidden = cot[...].astype(jnp.float32) + inv_dev * (scaled - mean - unit * jnp.mean(scaled * unit, axis=-1, keepdims=True))
    branch = grad_hidden.astype(low)
    grad_heads = dot_nt(branch, out_weight).astype(low)
    for h in range(count):
        at = slice(HEAD * h, HEAD * (h + 1))
        ghead_out[h] = jnp.concatenate([grad_heads[:block_len, at], grad_heads[block_len:, at]], axis=1)
    swap = start([push(ghead_out.at[d[0]], ghead.at[me], h_send.at[k], h_recv.at[k], d) for k, d in enumerate(c_peers)])
    ghead[me] = ghead_out[me]
    ghidden[...] = grad_hidden
    out_mine[...] = dot_tn(attended, branch).astype(low).reshape(out_mine.shape)
    gout_copies = start([push(out_mine.at[d[1]], out_zone.at[z], o_send.at[0, k], o_recv.at[0, k], d) for k, d in enumerate(z_peers)])
    out_zone[z] = out_mine[z]
    small = jnp.concatenate(
        [
            dot_nn(grad_logits, normed)[:experts],
            jnp.sum(grad_normed * unit, axis=0, keepdims=True),
            jnp.sum(grad_normed, axis=0, keepdims=True),
            jnp.zeros((small_in.shape[0] - experts - 2, width), jnp.float32),
        ],
        axis=0,
    )
    lanes = width // owners
    for c in range(owners):
        zsend[c, 3 * HEAD:, :] = small[:, c * lanes:(c + 1) * lanes].astype(low)

    def prepare(s, both):
        at = span(s, block_len)
        grad = jnp.where(lane < HEAD, both, 0.0)
        delta = jnp.sum(grad * stat[at, :], axis=1, keepdims=True)
        one, two, three = split3(jnp.broadcast_to(-delta, grad.shape))
        wide = jnp.where(lane == HEAD, one, grad.astype(low))
        wide = jnp.where(lane == HEAD + 1, two, wide)
        dof[at, :] = jnp.where(lane == HEAD + 2, three, wide)
        turned = jnp.where(lane < HEAD, both, pltpu.roll(qf[at, :].astype(jnp.float32), HEAD, 1)).T.astype(low)
        dot[:, at] = turned[:HEAD]
        qt[:, at] = turned[HEAD:]

    wait(swap)
    gathers = start([push(zin, all_ref.at[me], g_send.at[k], g_recv.at[k], (d, z)) for k, d in enumerate(same_core)])
    own_relay = start([push(zin, all_ref.at[me], r_send.at[3], r_recv.at[3], (sib, z))])
    own_got = start([pltpu.make_async_copy(zin, all_ref.at[me], own_sem.at[1])])

    @pl.loop(0, count, unroll=4)
    def _(j):
        both = blend(hold_masks(j=j), [ghead[c] for c in range(count)]).astype(jnp.float32)
        prepare(j, both)
        prepare(blocks - 1 - j, pltpu.roll(both, HEAD, 1))

    tok_loads = [
        pltpu.make_async_copy(toks_ref.at[i], held.at[i], own_sem.at[3 + i]) for i in range(rows // RUN)
    ]

    def key_run(run):
        def tile(q_at, k_at, part, probs, first_k, first_q):
            slope = dot_nt(dof[q_at, :], vf[k_at, :])
            grad = (probs.astype(jnp.float32) * slope).astype(low)
            dv = dot_nn(dot[:, q_at], probs)
            dk = dot_nn(qt[:, q_at], grad)
            dq = dot_nn(grad, kf[k_at, :])
            at = slice(part * HALF, (part + 1) * HALF)
            if first_k:
                dv_acc[:, at] = dv
                dk_acc[:, at] = dk
            else:
                dv_acc[:, at] += dv
                dk_acc[:, at] += dk
            if first_q:
                @pl.when(run == 0)
                def _():
                    dq_acc[q_at, :] = dq

                @pl.when(run != 0)
                def _():
                    dq_acc[q_at, :] += dq
            else:
                dq_acc[q_at, :] += dq

        early, late = span(2 * run, HALF), span(2 * run + 1, HALF)
        tile(span(run, RUN), early, 0, held[first_diagonal + run], True, True)
        tile(late, late, 1, late_held[run], True, False)

        @pl.loop(run + 1, runs)
        def _(index):
            for part in range(2):
                tile(span(index, RUN), span(2 * run + part, HALF), part, held[slot_of(run, index, part)], False, part == 0)

        at = span(run, RUN)
        both = jnp.concatenate([dk_acc[...] * scale, dv_acc[...]], axis=0).T
        query = dq_acc[at, :] * scale
        qk[at, :] = jnp.where(lane < HEAD, query, pltpu.roll(both, HEAD, 1)).astype(low)
        dv_rows[at, :] = both.astype(low)

    def pack_half(half):
        mid = block_len // 2
        ats = [slice(s * block_len, (s + 1) * block_len) for s in (range(count) if half == 0 else range(blocks - 1, count - 1, -1))]

        @pl.loop(0, count, unroll=4)
        def _(c):
            masks = hold_masks(c=c)
            send[half, c, :block_len, :] = blend(masks, [qk[at, :] for at in ats])
            values = blend(masks, [dv_rows[at, :] for at in ats])
            sorted_dv[c] = values
            values = values[:, HEAD:]
            send[half, c, block_len:, :] = jnp.concatenate([values[:mid], values[mid:]], axis=1)
        landing[half, me] = send[half, me]

    swaps = [
        [push(send.at[half, d[0]], landing.at[half, me], s_send.at[half, k], s_recv.at[half, k], d) for k, d in enumerate(c_peers)]
        for half in range(2)
    ]
    relays = [push(all_ref.at[d], all_ref.at[d], r_send.at[k], r_recv.at[k], (sib, z)) for k, d in enumerate(same_core)]
    others = [push(weight.at[:, d], weight.at[:, d], v_send.at[k], v_recv.at[k], (sib, z)) for k, d in enumerate(same_core)]
    last_copies = [push(out_own, out_all.at[me], o_send.at[2, k], o_recv.at[2, k], d) for k, d in enumerate(c_peers)]
    part_copies = [push(out_sum.at[d[0]], out_part.at[me], o_send.at[1, k], o_recv.at[1, k], d) for k, d in enumerate(c_peers)]

    def head_weights(half):
        if half == 0:
            head_acc[...] = jnp.zeros_like(head_acc)

        @pl.loop(0, count // 2)
        def _(i):
            first, second = None, None
            for part in range(2):
                c = 2 * i + part
                slot, at = place(c, half)
                here = held[slot, pl.ds(pl.multiple_of(at, block_len), block_len), :]
                one, two = dot_tn(send[half, c, :block_len, :], here), dot_tn(sorted_dv[c], here)
                first, second = (one, two) if first is None else (first + one, second + two)
            head_acc[:2 * HEAD, :] += first
            head_acc[2 * HEAD:, :] += second[HEAD:]

    @pl.loop(0, runs)
    def _(run):
        key_run(run)

        @pl.when(run == 0)
        def _():
            start(tok_loads)

        @pl.when(run == runs // 2 - 1)
        def _():
            wait(gout_copies)
            summed = out_zone[0].astype(jnp.float32)
            for k in range(1, owners):
                summed = summed + out_zone[k].astype(jnp.float32)
            out_sum[...] = summed.astype(low).reshape(out_sum.shape)
            start(part_copies)
            out_part[me] = out_sum[me]
            pack_half(0)
            start(swaps[0])
            for k in range(len(same_core)):
                gathers[k].wait_recv()
                relays[k].start()
                weights[k].wait_recv()
                others[k].start()
            wait(tok_loads)
            head_weights(0)

        @pl.when(run == runs // 2)
        def _():
            wait(part_copies)
            summed = out_part[0].astype(jnp.float32)
            for k in range(1, count):
                summed = summed + out_part[k].astype(jnp.float32)
            out_own[...] = summed.astype(low)
            start(last_copies)
            out_all[me] = out_own[...]

    pack_half(1)
    start(swaps[1])
    head_weights(1)
    for c in range(owners):
        zsend[c, :3 * HEAD, :] = head_acc[:, c * lanes:(c + 1) * lanes].astype(low)
    z_copies = start([push(zsend.at[d[1]], zone.at[z], z_send.at[k], z_recv.at[k], d) for k, d in enumerate(z_peers)])
    zone[z] = zsend[z]
    wait(own_got + own_relay + relays)

    mixed_slot = rows // RUN
    share = owners * 2 * per
    mixed_loads = []
    for c in range(count):
        slot, at = divmod(c * share, RUN)
        mixed_loads.append(pltpu.make_async_copy(all_ref.at[c], held.at[mixed_slot + slot, pl.ds(at, share)], own_sem.at[3 + rows // RUN + c]))
    start(mixed_loads)
    wait(mixed_loads)
    step = HALF
    chunks = ffn // step
    wide_slot = mixed_slot + count * share // RUN

    def of_expert(kind, e):
        parts = []
        for slot in range(mixed_slot, wide_slot):
            value = held[slot].reshape(RUN // share, owners, 2, own_experts, groups, width)
            parts.append(value[:, :, kind, e].reshape(-1, width))
        return jnp.concatenate(parts, axis=0)

    def expert_part(e):
        mixed, grad_out = of_expert(0, e), of_expert(1, e)
        copies = []

        @pl.loop(0, chunks, unroll=2)
        def _(i):
            at = span(i, step)
            to = span(lax.rem(i, 2), step)
            active, slope = gelu_parts(dot_nn(mixed, up[e, :, at]))
            held[wide_slot + chunks * e + i // 2, to, :] = active.astype(low)
            slot = wide_slot + chunks * e + chunks // 2 + i // 2
            held[slot, to, :] = (dot_nt(grad_out, down[e, at, :]) * slope).astype(low)

        for i in range(chunks):
            slot = wide_slot + chunks * e + i // 2
            at, to = pl.ds(i * step, step), pl.ds(i % 2 * step, step)
            sem = own_sem.at[3 + rows // RUN + count + 2 * (chunks * e + i)]
            copies.append(pltpu.make_async_copy(held.at[slot, to], act_ref.at[e, :, at], sem))
            sem = own_sem.at[4 + rows // RUN + count + 2 * (chunks * e + i)]
            copies.append(pltpu.make_async_copy(held.at[slot + chunks // 2, to], gpre_ref.at[e, :, at], sem))
        return start(copies)

    stores = expert_part(0)
    wait(z_copies)
    summed = zone[0].astype(jnp.float32)
    for k in range(1, owners):
        summed = summed + zone[k].astype(jnp.float32)
    total[...] = summed.astype(low)
    c_copies = start([push(total, totals.at[me], c_send.at[k], c_recv.at[k], d) for k, d in enumerate(c_peers)])
    totals[me] = total[...]
    for e in range(1, own_experts):
        stores += expert_part(e)
    wait(swaps[0] + swaps[1] + shares + others)
    flat_weight = weight[...].reshape(width, -1)
    parts = []
    for half in range(2):
        queries, keys, values = [], [], []
        for h in range(count):
            front, back = landing[half, h, :block_len, :], landing[half, h, block_len:, :]
            queries.append(front[:, :HEAD])
            keys.append(front[:, HEAD:])
            values.append(jnp.concatenate([back[:, :HEAD], back[:, HEAD:]], axis=0))
        parts.append(dot_nt(jnp.concatenate(queries + keys + values, axis=1), flat_weight))
    wait(layer_copy)
    first, second = ghidden[:block_len, :] + parts[0], ghidden[block_len:, :] + parts[1]
    wide_out[:block_len, :], wide_out[block_len:, :] = ordered(first, second, in_order)
    stores += start([pltpu.make_async_copy(wide_out, gtok_ref, own_sem.at[2])])
    wait(last_copies)
    out_ref[...] = out_all[...].reshape(out_ref.shape)
    wait(c_copies)
    small = None
    turned = []
    for c in range(count):
        turned.append(totals[c, :3 * HEAD, :].astype(jnp.float32).T)
        part = totals[c, 3 * HEAD:, :].astype(jnp.float32)
        small = part if small is None else small + part
    sums_ref[...] = small
    for kind in range(3):
        at = slice(HEAD * kind, HEAD * (kind + 1))
        gq_ref[:, HEAD * count * kind:HEAD * count * (kind + 1)] = jnp.concatenate([part[:, at] for part in turned], axis=1).astype(low)
    wait(stores)
    for copy in gathers + weights:
        copy.wait_send()


def layer(table, gid_row, segs, tokens, cot, w_qkv, w_out, w_router, ln_gain, ln_bias, w_up, w_down, groups, count, owners):
    own_rows, width = tokens.shape
    experts = w_router.shape[1]
    blocks, block_len = table.shape[0], own_rows // 2
    rows = blocks * block_len
    runs = rows // RUN
    own_experts, _, ffn = w_up.shape
    lanes, wide_qkv = w_qkv.shape
    smalls = 16
    height = 3 * HEAD + smalls
    per = experts * groups // owners
    wide = (own_experts, count * owners * groups, ffn)
    share = (owners * 2 * per, width)
    part = (count, lanes // count, width)
    swap = (2, count, block_len + block_len // 2, 2 * HEAD)
    gout = (owners, lanes, width)
    sent = (owners, 2, per, width)
    attended = (2, count, block_len // 2, 2 * HEAD)
    head_grad = (count, block_len, 2 * HEAD)
    low, full = jnp.bfloat16, jnp.float32
    scratch = [
        (tokens.shape, low), (tokens.shape, low), ((lanes, 3 * HEAD), low), ((smalls, lanes), low), ((owners, lanes, 3 * HEAD), low),
        ((owners,) + w_out.shape, low), ((owners, smalls, lanes), low), ((owners, lanes // count, wide_qkv), low), (attended, low),
        (attended, low), (sent, low), (share, low), (sent, low), (sent, low), (w_up.shape, low), (w_down.shape, low),
        ((rows, 2 * HEAD), low), ((rows, 2 * HEAD), low), ((rows, 2 * HEAD), low), ((rows, 2 * HEAD), full),
        ((runs * runs, RUN, HALF), low), ((runs, HALF, HALF), low), (head_grad, low), (head_grad, low),
        (tokens.shape, full), (tokens.shape, full), ((rows, 2 * HEAD), low), ((HEAD, rows), low), ((HEAD, rows), low),
        ((HEAD, RUN), full), ((HEAD, RUN), full), ((3 * HEAD, width), full), (swap, low), (swap, low),
        ((owners, count, lanes // count, wide_qkv), low), ((owners, height, lanes), low), ((owners, height, lanes), low),
        ((height, lanes), low), ((count, height, lanes), low), (gout, low), (gout, low), (part, low), (part, low), (part[1:], low),
        (part, low),
    ]
    owns = 3 + rows // RUN + count + 2 * own_experts * (ffn // HALF)
    to_z, to_c = owners - 1, count - 1
    sems = [
        (2 * own_experts,), (owns,), (2, 3, 2), (2, 2, 2), (2, 2), (2, 4, 2), (2, 4, 2), (4, to_z), (4, to_z),
        (2, to_c), (2, to_c), (2, to_z), (2, to_z), (2, own_experts, to_z), (2, own_experts, to_z), (to_c,), (to_c,), (2, to_c), (2, to_c),
        (to_z,), (to_z,), (to_c,), (to_c,), (3, to_c), (3, to_c), (3,), (3,), (4,), (4,), (3,), (3,), (4,), (4,),
    ]
    return pl.pallas_call(
        functools.partial(layer_body, experts, groups, blocks),
        out_shape=(
            jax.ShapeDtypeStruct((lanes, 3 * width), low),
            jax.ShapeDtypeStruct((lanes, width), low),
            jax.ShapeDtypeStruct((smalls, lanes), full),
            jax.ShapeDtypeStruct(tokens.shape, full),
            jax.ShapeDtypeStruct(tokens.shape, full),
            jax.ShapeDtypeStruct(wide, low),
            jax.ShapeDtypeStruct(wide, low),
            jax.ShapeDtypeStruct((count,) + share, low),
            jax.ShapeDtypeStruct((rows // RUN, RUN, width), low),
        ),
        in_specs=[SMEM] + [VMEM] * 9 + [ANY] * 2,
        out_specs=(VMEM,) * 3 + (ANY,) * 6,
        scratch_shapes=[pltpu.VMEM(shape, dtype) for shape, dtype in scratch] + [pltpu.SemaphoreType.DMA(shape) for shape in sems],
        compiler_params=pltpu.CompilerParams(collective_id=1, has_side_effects=True, vmem_limit_bytes=LIMIT),
        cost_estimate=cost(130),
        name="layer",
    )(table, gid_row, segs, tokens, cot, w_qkv, w_out, w_router.T, ln_gain[None], ln_bias[None], w_up, w_down)


def expert_grad_body(experts, passed, mixed_ref, grad_ref, act_ref, gpre_ref, small_ref, *refs):
    sources, outs = refs[:passed], refs[passed + 5:]
    gup_ref, gdown_ref, router_ref, gain_ref, bias_ref = refs[passed:passed + 5]
    width = gup_ref.shape[1]
    for source, out in zip(sources, outs):
        out[...] = source[...].astype(out.dtype)
    router_ref[...] = small_ref[:experts]
    gain_ref[...] = small_ref[experts:experts + 1]
    bias_ref[...] = small_ref[experts + 1:experts + 2]
    gup_ref[0] = dot_tn(mixed_ref[...].reshape(-1, width), gpre_ref[0])
    gdown_ref[0] = dot_tn(act_ref[0], grad_ref[...].reshape(-1, width))


def expert_grads(gathered, active, grad_pre, small, passed, groups, experts):
    own, rows, ffn = active.shape
    step = ffn
    steps = ffn // step
    sources, width = gathered.shape[0], gathered.shape[3]
    view = gathered.reshape(sources, 2, own, groups, width)
    lanes = small.shape[1]
    full = jnp.float32
    slices = [pl.BlockSpec((x.shape[0] // (own * steps), x.shape[1]), lambda e, f: (e * steps + f, 0)) for x in passed]
    return pl.pallas_call(
        functools.partial(expert_grad_body, experts, len(passed)),
        grid=(own, steps),
        out_shape=[
            jax.ShapeDtypeStruct((own, width, ffn), full), jax.ShapeDtypeStruct((own, ffn, width), full),
            jax.ShapeDtypeStruct((experts, lanes), full), jax.ShapeDtypeStruct((1, lanes), full), jax.ShapeDtypeStruct((1, lanes), full),
        ] + [jax.ShapeDtypeStruct(x.shape, full) for x in passed],
        in_specs=[
            pl.BlockSpec((sources, 1, 1, groups, width), lambda e, f: (0, 0, e, 0, 0)),
            pl.BlockSpec((sources, 1, 1, groups, width), lambda e, f: (0, 1, e, 0, 0)),
            pl.BlockSpec((1, rows, step), lambda e, f: (e, 0, f)),
            pl.BlockSpec((1, rows, step), lambda e, f: (e, 0, f)),
            pl.BlockSpec(small.shape, lambda e, f: (0, 0)),
        ] + slices,
        out_specs=[
            pl.BlockSpec((1, width, step), lambda e, f: (e, 0, f)), pl.BlockSpec((1, step, width), lambda e, f: (e, f, 0)),
            pl.BlockSpec((experts, lanes), lambda e, f: (0, 0)), pl.BlockSpec((1, lanes), lambda e, f: (0, 0)),
            pl.BlockSpec((1, lanes), lambda e, f: (0, 0)),
        ] + slices,
        compiler_params=pltpu.CompilerParams(vmem_limit_bytes=LIMIT),
        cost_estimate=cost(10),
        name="expert_grads",
    )(view, view, active, grad_pre, small, *passed)


def fast_device(
    tokens, cotangent, block_table, seg_ids, group_ids, w_qkv, w_out, w_router, ln_gain, ln_bias, w_up, w_down
):
    ctx_count, z_count = lax.axis_size("ctx"), lax.axis_size("fsdp")
    tok_rows, cot_rows = tokens[0], cotangent[0]
    rows, width = tok_rows.shape
    experts = w_router.shape[1]
    groups = rows // GROUP_SIZE
    grad_qkv, grad_out, small, layer_out, grad_tokens, active, grad_pre, gathered, unused = layer(
        block_table, group_ids, seg_ids, tok_rows, cot_rows, w_qkv, w_out, w_router, ln_gain, ln_bias, w_up, w_down, groups, ctx_count,
        z_count,
    )
    gathered = gathered.reshape(ctx_count * z_count, 2, experts * groups // z_count, width)
    grad_up, grad_down, grad_router, grad_gain, grad_bias, layer_out, grad_tokens, grad_qkv, grad_out = expert_grads(
        gathered, active, grad_pre, small, [layer_out, grad_tokens, grad_qkv, grad_out], groups, experts
    )
    return (
        layer_out[None],
        grad_tokens[None],
        grad_qkv,
        grad_out,
        grad_router.T,
        grad_gain[0],
        grad_bias[0],
        grad_up,
        grad_down,
    )


def solution(mesh):
    placed = (
        P("fsdp", "ctx", None),
        P("fsdp", "ctx", None),
        P(),
        P("fsdp", None),
        P("fsdp", "ctx"),
        P("fsdp", None),
        P("fsdp", None),
        P("fsdp", None),
        P("fsdp"),
        P("fsdp"),
        P("fsdp", None, None),
        P("fsdp", None, None),
    )
    step = fast_device if mesh.shape["ctx"] == HEADS else on_device
    return jax.shard_map(
        step,
        mesh=mesh,
        in_specs=placed,
        out_specs=(
            P("fsdp", "ctx", None),
            P("fsdp", "ctx", None),
            P("fsdp", None),
            P("fsdp", None),
            P("fsdp", None),
            P("fsdp"),
            P("fsdp"),
            P("fsdp", None, None),
            P("fsdp", None, None),
        ),
        check_vma=False,
    )
```
